128 devices in a mesh: seq: 64 (over y, z, x_lo, core), tensor: 2 (over x_hi).
Axes of the slice: x: 4 (x_hi: 2, x_lo: 2; x = x_hi * 2 + x_lo), y: 4, z: 4, core: 2. Of those that a mesh axis runs over, the one named last changes fastest.
Arguments:
- tokens: bfloat16 [16384, 1024], P('seq'), may hold values from -6 to 6
- starts: int32 [64], P('seq'), may hold values from 2 to 256, as said below
- gain_one: float32 [1024], replicated, may hold values from 0.1 to 1.9
- in_weight: bfloat16 [1024, 3, 1024], P(None, None, 'tensor'), may hold values from -0.1875 to 0.1875
- conv_weight: float32 [3, 1024], P(None, 'tensor'), may hold values from -3 to 3
- out_weight: bfloat16 [1024, 1024], P('tensor'), may hold values from -0.1875 to 0.1875
- gain_two: float32 [1024], replicated, may hold values from 0.1 to 1.9
- gate_weight: bfloat16 [1024, 4608], P(None, 'tensor'), may hold values from -0.1875 to 0.1875
- up_weight: bfloat16 [1024, 4608], P(None, 'tensor'), may hold values from -0.1875 to 0.1875
- down_weight: bfloat16 [4608, 1024], P('tensor'), may hold values from -0.125 to 0.125
- cotangent: bfloat16 [16384, 1024], P('seq'), may hold values from -16 to 16
Outputs:
- mixed: bfloat16 [16384, 1024], P('seq')
- tokens_grad: float32 [16384, 1024], P('seq')
- gain_one_grad: float32 [1024], replicated
- in_grad: float32 [1024, 3, 1024], P('seq', None, 'tensor')
- conv_grad: float32 [3, 1024], P(None, 'tensor')
- out_grad: float32 [1024, 1024], P('tensor', 'seq')
- gain_two_grad: float32 [1024], replicated
- gate_grad: float32 [1024, 4608], P('seq', 'tensor')
- up_grad: float32 [1024, 4608], P('seq', 'tensor')
- down_grad: float32 [4608, 1024], P('tensor', 'seq')
The draws below stay inside these ranges and needn't reach their ends.
Inputs may be any that keep to these rules, and one draw needn't show every extreme that they name: `starts`: entry j is the offset inside shard j of the only segment start in it, or 256 where the shard has none; shard 0 has none, and the shards that have one lie 16 apart, at a position drawn from the seed.
All inputs are finite; a program needn't handle non-finite values.
Results may differ from the reference program's by a relative error of at most 0.014.
Values may be sent and summed in bfloat16 or wider, within the bound.
No kernel may reach another device: no remote copies, remote signals or barrier semaphores. Data moves between devices by JAX's collectives and lax.ppermute only.
A program may use at most 128 MiB of HBM per device.

```python
import jax
import jax.numpy as jnp
from jax import lax

D = 1024
FF = 4608
TOK_DEV = 256
SHARDS = 64
TOKENS = 16384
RUN = 16


def draw_starts(key, part):
    key = jax.random.fold_in(key, 7)
    phase_key, offset_key = jax.random.split(key)
    phase = jax.random.randint(phase_key, (), 0, RUN)
    offsets = jax.random.randint(offset_key, (SHARDS,), 2, TOK_DEV)
    shard_ids = jnp.arange(SHARDS, dtype=jnp.int32)
    has_start = (shard_ids >= 1) & ((shard_ids + phase) % RUN == 0)
    return jnp.where(has_start, offsets, TOK_DEV).astype(jnp.int32)


def spiked(values, key, source, target, parts, factor):
    owner, partner = [(jnp.arange(values.shape[axis_at]) // (values.shape[axis_at] // parts)).reshape([-1 if axis == axis_at else 1 for axis in range(values.ndim)]) for axis_at in (source, target)]
    chosen = jax.random.permutation(key, parts)[partner]
    strong = (owner == chosen) | (owner == (partner + parts // 2) % parts)
    return jnp.where(strong, factor * values, values)


def block_scale(own_key, extent, cuts, smallest, high):
    def one(position, blocks):
        steps = jax.random.uniform(jax.random.fold_in(jax.random.fold_in(own_key, 6), position), (blocks,), jnp.float32, smallest / len(cuts), high / len(cuts))
        return jnp.repeat(jnp.exp(steps), extent[position] // blocks).reshape((-1,) + (1,) * (len(extent) - position - 1))

    level = one(*cuts[0])
    for cut in cuts[1:]:
        level = level * one(*cut)
    return level


def bell_draw(rng, shape, width, most, shards=(), held_as=jnp.bfloat16):
    values = jax.random.normal(rng, shape, jnp.float32) * width
    if len(shards) > 0:
        values = block_scale(rng, shape, shards, -0.22, 0.18) * values
    return jnp.clip(values, min=-most, max=most).astype(held_as)


def bell_draw_with(own_key, extent, spread, reach, cuts, heavy, kind=jnp.bfloat16):
    array = spread * jax.random.normal(own_key, extent, jnp.float32)
    if cuts:
        array = array * block_scale(own_key, extent, cuts, -0.22, 0.18)
    return jnp.clip(spiked(array, jax.random.fold_in(own_key, 3), *heavy), -reach, reach).astype(kind)


def setup_inputs(seed: int = 0) -> dict:
    keys = jax.random.split(jax.random.key(seed), 12)
    return {
        "tokens": bell_draw(keys[0], (TOKENS, D), 1.0, 6.0, ((0, 64),)),
        "starts": draw_starts(jax.random.fold_in(keys[11], 71), 0),
        "gain_one": jnp.clip(1.0 + 0.18 * jax.random.normal(keys[2], (D,), jnp.float32), 0.1, 1.9),
        "in_weight": bell_draw(keys[3], (D, 3, D), D ** -0.5, 0.1875, ((2, 2),)),
        "conv_weight": bell_draw(keys[4], (3, D), 0.6, 3.0, ((1, 2),), jnp.float32),
        "out_weight": bell_draw(keys[5], (D, D), D ** -0.5, 0.1875, ((0, 2),)),
        "gain_two": jnp.clip(1.0 + 0.18 * jax.random.normal(keys[6], (D,), jnp.float32), 0.1, 1.9),
        "gate_weight": bell_draw(keys[7], (D, FF), D ** -0.5, 0.1875, ((1, 2),)),
        "up_weight": bell_draw(keys[8], (D, FF), D ** -0.5, 0.1875, ((1, 2),)),
        "down_weight": bell_draw(keys[9], (FF, D), (FF // 2) ** -0.5, 0.125, ((0, 2),)),
        "cotangent": bell_draw_with(keys[10], (TOKENS, D), 1.0, 16.0, ((0, 64),), (0, 1, 64, 4.0)),
    }


@jax.custom_vjp
def low(v):
    return lax.optimization_barrier(v.astype(jnp.bfloat16)).astype(jnp.float32)

@jax.custom_vjp
def low_back(v):
    return v

def low_keep(v):
    return (low(v), None)

def low_pass(kept, grad):
    return (grad,)

def back_keep(v):
    return (v, None)

def back_low(kept, grad):
    return (low(grad),)
low.defvjp(low_keep, low_pass)
low_back.defvjp(back_keep, back_low)
EPS = 1e-05

def rms_norm(values, gain):
    return values * lax.rsqrt(lax.optimization_barrier(jnp.mean(values * values, axis=-1, keepdims=True)) + EPS) * gain

def reference(tokens, starts, gain_one, in_weight, conv_weight, out_weight, gain_two, gate_weight, up_weight, down_weight, cotangent):
    highest = lax.Precision.HIGHEST
    flags = (jnp.arange(TOK_DEV, dtype=jnp.int32)[None, :] == starts[:, None]).reshape(-1).astype(jnp.int32)
    segment = jnp.cumsum(flags).astype(jnp.int32)
    lag_masks = []
    for shift_lag in range(3):
        prior = jnp.concatenate([jnp.full((shift_lag,), -1, jnp.int32), segment[:TOKENS - shift_lag]])
        lag_masks.append((prior == segment).astype(jnp.float32)[:, None])

    def forward(inputs, g_one, w_in, w_conv, w_out, g_two, w_gate, w_up, w_down):
        normed_one = low(rms_norm(inputs, g_one))
        projected = low_back(jnp.einsum('td,dkc->tkc', normed_one, w_in, precision=highest))
        b_part, c_part, x_part = (projected[:, 0], projected[:, 1], projected[:, 2])
        gated = low(b_part * x_part)
        conv = jnp.zeros_like(gated)
        for shift_lag in range(3):
            shifted = jnp.concatenate([jnp.zeros((shift_lag, gated.shape[1]), jnp.float32), gated[:TOKENS - shift_lag]], 0)
            conv = conv + w_conv[shift_lag] * shifted * lag_masks[shift_lag]
        ymix = low(c_part * conv)
        branch = low_back(jnp.dot(ymix, w_out, precision=highest))
        resid = inputs + branch
        normed_two = low(rms_norm(resid, g_two))
        gate_act = low_back(jnp.dot(normed_two, w_gate, precision=highest))
        up_act = low_back(jnp.dot(normed_two, w_up, precision=highest))
        hidden = low(jax.nn.silu(gate_act) * up_act)
        down_out = low_back(jnp.dot(hidden, w_down, precision=highest))
        return resid + down_out
    primals = (tokens.astype(jnp.float32), gain_one, in_weight.astype(jnp.float32), conv_weight, out_weight.astype(jnp.float32), gain_two, gate_weight.astype(jnp.float32), up_weight.astype(jnp.float32), down_weight.astype(jnp.float32))
    result, pullback = jax.vjp(forward, *primals)
    grads = pullback(cotangent.astype(jnp.float32))
    return (result.astype(jnp.bfloat16), grads[0], grads[1], grads[2], grads[3], grads[4], grads[5], grads[6], grads[7], grads[8])
```

```python
import jax
import jax.numpy as jnp
from jax import lax
from jax.sharding import PartitionSpec as P

EPS = 1e-05
AXES = ("seq", "tensor")
BF16 = jnp.bfloat16
F32 = jnp.float32


def device_pairs(move):
    def number(y, z, x, core):
        return ((((y % 4) * 4 + z % 4) * 2 + x % 2) * 2 + core) * 2 + (x % 4) // 2

    return [
        (number(y, z, x, core), number(*move(y, z, x, core)))
        for y in range(4)
        for z in range(4)
        for x in range(4)
        for core in range(2)
    ]


ACROSS = device_pairs(lambda y, z, x, core: (y, z, (x + 2) % 4, core))
BESIDE = device_pairs(lambda y, z, x, core: (y, z, x ^ 1, core))
CORES = device_pairs(lambda y, z, x, core: (y, z, x, 1 - core))
PAIRS = {
    "y": (
        device_pairs(lambda y, z, x, core: (y ^ 1, z, x, core)),
        device_pairs(lambda y, z, x, core: (3 - y, z, x, core)),
    ),
    "z": (
        device_pairs(lambda y, z, x, core: (y, z ^ 1, x, core)),
        device_pairs(lambda y, z, x, core: (y, 3 - z, x, core)),
    ),
}


def swap(value, pairs):
    return lax.ppermute(value, AXES, pairs)


def from_behind(value, axis, steps):
    count = lax.axis_size(axis)
    leading, last = (max(0, -steps), min(count, count - steps))
    return lax.ppermute(value, axis, [(source, source + steps) for source in range(leading, last)])


def norm_scale(values):
    return lax.rsqrt(jnp.mean(values * values, axis=1, keepdims=True) + EPS)


def norm_backward(out_grad_rows, values, scale_rows, gain):
    scaled = out_grad_rows * gain
    inner = jnp.mean(scaled * values, axis=1, keepdims=True)
    return scale_rows * (scaled - values * scale_rows * scale_rows * inner)


def pick(value, at, dim):
    return lax.dynamic_index_in_dim(value, at, dim, keepdims=False)


def first_round(value, at, dim, kind):
    near, far = at ^ 1, 3 - at
    one, two = (near, far) if kind == 0 else (far, near)
    one_two = 3 - one if kind == 0 else one ^ 1
    sent = jnp.stack([pick(value, one, dim), pick(value, one_two, dim)], 0)
    kept = jnp.stack([pick(value, at, dim), pick(value, two, dim)], 0)
    return sent, kept


def scatter_rounds(pieces, place):
    state = [piece for piece, _, _ in pieces]
    for leg in range(2):
        names = [axis if leg == 0 else ("z" if axis == "y" else "y") for _, axis, _ in pieces]
        dims = [(0 if name == "y" else 1) if leg == 0 else 0 for name in names]
        sent, kept = zip(
            *(
                first_round(value, place[name], dim, kind)
                for value, name, dim, (_, _, kind) in zip(state, names, dims, pieces)
            )
        )
        got = [
            swap(value, PAIRS[name][kind])
            for value, name, (_, _, kind) in zip(sent, names, pieces)
        ]
        sums = [k.astype(F32) + g.astype(F32) for k, g in zip(kept, got)]
        got = [
            swap(value[1].astype(BF16), PAIRS[name][1 - kind])
            for value, name, (_, _, kind) in zip(sums, names, pieces)
        ]
        state = [s[0] + g.astype(F32) for s, g in zip(sums, got)]
        if leg == 0:
            state = [s.astype(BF16) for s in state]
    return state


def last_rounds(value, place):
    value = value.reshape(2, 2, 16, value.shape[-1])
    got = swap(pick(value, 1 - place["x"], 0).astype(BF16), BESIDE)
    value = pick(value, place["x"], 0) + got.astype(F32)
    mine = pick(value, place["core"], 0)
    other = swap(pick(value, 1 - place["core"], 0), CORES)
    return mine, other


def sum_all(value):
    for pairs in (CORES, BESIDE, *PAIRS["y"], *PAIRS["z"]):
        value = value + swap(value, pairs)
    return value


def on_device(
    tokens,
    starts,
    gain_one,
    in_weight,
    conv_weight,
    out_weight,
    gain_two,
    gate_weight,
    up_weight,
    down_weight,
    cotangent,
):
    count_rows = tokens.shape[0]
    at = lax.axis_index("seq")
    core = at % 2
    place = {"y": at // 16, "z": (at // 4) % 4, "x": (at // 2) % 2, "core": core}

    def share(value):
        return jnp.concatenate([value, swap(value, CORES)], 0)

    def share_columns(value):
        half = value.shape[1] // 2
        mine = lax.dynamic_slice_in_dim(value, core * half, half, 1)
        other = lax.dynamic_slice_in_dim(value, (1 - core) * half, half, 1)
        return jnp.concatenate([mine, swap(other, CORES)], 0)

    def outer(left, right):
        product = jnp.einsum("td,tf->df", left, right, preferred_element_type=F32)
        return product.astype(BF16).reshape(4, 4, 64, right.shape[1])

    inputs = tokens.astype(F32)
    scale_one = norm_scale(inputs)
    normed_one = (inputs * scale_one * gain_one).astype(BF16)
    projected = jnp.einsum("td,dkc->tkc", normed_one, in_weight, preferred_element_type=F32)
    b_part, c_part, x_part = (projected[:, 0], projected[:, 1], projected[:, 2])
    gated = (b_part * x_part).astype(BF16)
    offset = starts[0]
    positions = jnp.arange(count_rows, dtype=jnp.int32)
    tail_positions = positions[count_rows - 2 :]
    keep_mask = jnp.logical_not((tail_positions < offset) & (offset < count_rows)).astype(F32)[
        :, None
    ]
    tail = (gated[count_rows - 2 :].astype(F32) * keep_mask).astype(BF16)
    incoming = from_behind(tail, "seq", 1)
    extended = jnp.concatenate([incoming, gated], 0).astype(F32)
    valid = [jnp.ones((count_rows, 1), F32)]
    for shift_lag in (1, 2):
        valid.append(
            jnp.logical_not((offset <= positions) & (offset > positions - shift_lag)).astype(F32)[
                :, None
            ]
        )
    conv = jnp.zeros_like(b_part)
    for shift_lag in range(3):
        conv = (
            conv
            + conv_weight[shift_lag]
            * extended[2 - shift_lag : 2 - shift_lag + count_rows]
            * valid[shift_lag]
        )
    ymix = (c_part * conv).astype(BF16)
    branch = jnp.dot(ymix, out_weight, preferred_element_type=F32).astype(BF16)
    branch_other = swap(branch, ACROSS)
    hidden_grad = jnp.einsum("td,fd->tf", cotangent, down_weight, preferred_element_type=F32)
    cotangent_chip = share(cotangent)
    normed_one_chip = share(normed_one)
    ymix_chip = share_columns(ymix)
    resid = inputs + (branch.astype(F32) + branch_other.astype(F32))
    scale_two = norm_scale(resid)
    normed_two = (resid * scale_two * gain_two).astype(BF16)
    gate_act = jnp.dot(normed_two, gate_weight, preferred_element_type=F32)
    up_act = jnp.dot(normed_two, up_weight, preferred_element_type=F32)
    sigmoid_gate = jax.nn.sigmoid(gate_act)
    swish = gate_act * sigmoid_gate
    hidden = (swish * up_act).astype(BF16)
    swish_slope = sigmoid_gate * (1.0 + gate_act * (1.0 - sigmoid_gate))
    gate_back = (hidden_grad * up_act * swish_slope).astype(BF16)
    up_back = (hidden_grad * swish).astype(BF16)
    norm_two_part = jnp.einsum("tf,df->td", gate_back, gate_weight, preferred_element_type=F32)
    norm_two_part = norm_two_part + jnp.einsum(
        "tf,df->td", up_back, up_weight, preferred_element_type=F32
    )
    norm_two_part = norm_two_part.astype(BF16)
    norm_two_other = swap(norm_two_part, ACROSS)

    normed_two_chip = share(normed_two)
    down_g = outer(cotangent_chip, share_columns(hidden))
    gate_g = outer(normed_two_chip, share_columns(gate_back))
    up_g = outer(normed_two_chip, share_columns(up_back))
    cut = 896
    rest = jnp.concatenate([down_g[..., cut:], gate_g[..., cut:], up_g[..., cut:]], -1)
    wide = scatter_rounds(
        [
            (down_g[..., :cut], "y", 0),
            (gate_g[..., :cut], "y", 1),
            (up_g[..., :cut], "z", 0),
            (rest, "z", 1),
        ],
        place,
    )

    norm_two_back = norm_two_part.astype(F32) + norm_two_other.astype(F32)
    gain_two_g = jnp.sum(norm_two_back * resid * scale_two, axis=0)
    resid_grad = cotangent.astype(F32) + norm_backward(norm_two_back, resid, scale_two, gain_two)
    resid_low = resid_grad.astype(BF16)
    resid_low_chip = share(resid_low)
    ymix_back = jnp.einsum("td,cd->tc", resid_low, out_weight, preferred_element_type=F32)
    c_back = ymix_back * conv
    conv_back = ymix_back * c_part
    extended_grad = jnp.zeros_like(extended)
    tap_grads = []
    for shift_lag in range(3):
        lag_term = conv_back * valid[shift_lag]
        tap_grads.append(
            jnp.sum(lag_term * extended[2 - shift_lag : 2 - shift_lag + count_rows], axis=0)
        )
        extended_grad = extended_grad + jnp.pad(
            lag_term * conv_weight[shift_lag], ((2 - shift_lag, shift_lag), (0, 0))
        )
    returned = from_behind(extended_grad[:2], "seq", -1)
    gated_back = extended_grad[2:] + jnp.pad(returned * keep_mask, ((count_rows - 2, 0), (0, 0)))
    b_back = (gated_back * x_part).astype(BF16)
    c_back = c_back.astype(BF16)
    x_back = (gated_back * b_part).astype(BF16)
    norm_one_part = sum(
        jnp.einsum("tc,dc->td", back, in_weight[:, k], preferred_element_type=F32)
        for k, back in enumerate((b_back, c_back, x_back))
    )
    norm_one_low = norm_one_part.astype(BF16)
    norm_one_other = swap(norm_one_low, ACROSS)
    gain_one_part = jnp.sum(norm_one_part * inputs * scale_one, axis=0)

    narrow = scatter_rounds(
        [
            (outer(normed_one_chip, share_columns(b_back)), "y", 0),
            (outer(normed_one_chip, share_columns(c_back)), "y", 1),
            (outer(normed_one_chip, share_columns(x_back)), "z", 0),
            (outer(resid_low_chip, ymix_chip), "z", 1),
        ],
        place,
    )
    gain_one_part = gain_one_part.reshape(8, 128)
    gain_one_part = gain_one_part + swap(gain_one_part, ACROSS)
    small = jnp.concatenate(
        [gain_one_part, gain_two_g.reshape(8, 128), jnp.stack(tap_grads, 0).reshape(12, 128)], 0
    )
    small = sum_all(small)
    gain_one_g = small[:8].reshape(-1)
    gain_two_g = small[8:16].reshape(-1)
    conv_g = small[16:].reshape(3, -1)

    mine, other = last_rounds(jnp.concatenate(wide + narrow, -1), place)
    left, right = jnp.where(core == 0, mine, other), jnp.where(core == 0, other, mine)
    both = jnp.stack([left, right], 1)

    def joined(parts):
        return jnp.concatenate(parts, -1).reshape(16, -1)

    low = 3 * cut
    tip = 1152 - cut
    down_g = joined([both[..., :cut], both[..., low : low + tip]]).T
    gate_g = joined([both[..., cut : 2 * cut], both[..., low + tip : low + 2 * tip]])
    up_g = joined([both[..., 2 * cut : low], both[..., low + 2 * tip : low + 3 * tip]])
    base = 3 * 1152
    in_g = jnp.stack(
        [both[..., base + 256 * k : base + 256 * (k + 1)].reshape(16, 512) for k in range(3)], 1
    )
    out_g = both[..., base + 768 :].reshape(16, 512).T

    norm_two_other, down_part = lax.optimization_barrier(
        (norm_two_other, jnp.dot(hidden, down_weight, preferred_element_type=F32).astype(BF16))
    )
    down_other = swap(down_part, ACROSS)
    mixed = (resid + (down_part.astype(F32) + down_other.astype(F32))).astype(BF16)
    norm_one_back = norm_one_low.astype(F32) + norm_one_other.astype(F32)
    tokens_grad = resid_grad + norm_backward(norm_one_back, inputs, scale_one, gain_one)
    return (mixed, tokens_grad, gain_one_g, in_g, conv_g, out_g, gain_two_g, gate_g, up_g, down_g)


def solution(mesh):
    return jax.shard_map(
        on_device,
        mesh=mesh,
        in_specs=(
            P("seq", None),
            P("seq"),
            P(),
            P(None, None, "tensor"),
            P(None, "tensor"),
            P("tensor", None),
            P(),
            P(None, "tensor"),
            P(None, "tensor"),
            P("tensor", None),
            P("seq", None),
        ),
        out_specs=(
            P("seq", None),
            P("seq", None),
            P(),
            P("seq", None, "tensor"),
            P(None, "tensor"),
            P("tensor", "seq"),
            P(),
            P("seq", "tensor"),
            P("seq", "tensor"),
            P("tensor", "seq"),
        ),
        check_vma=False,
    )
```

```python
import functools

import jax
import jax.numpy as jnp
from jax import lax
from jax.experimental import pallas as pl
from jax.experimental.pallas import tpu as pltpu
from jax.sharding import PartitionSpec as P

EPS = 1e-05
AXES = ("seq", "tensor")
BF16 = jnp.bfloat16
F32 = jnp.float32


def device_pairs(move):
    def number(y, z, x, core):
        return ((((y % 4) * 4 + z % 4) * 2 + x % 2) * 2 + core) * 2 + (x % 4) // 2

    return [
        (number(y, z, x, core), number(*move(y, z, x, core)))
        for y in range(4)
        for z in range(4)
        for x in range(4)
        for core in range(2)
    ]


ACROSS = device_pairs(lambda y, z, x, core: (y, z, (x + 2) % 4, core))
BESIDE = device_pairs(lambda y, z, x, core: (y, z, x ^ 1, core))
CORES = device_pairs(lambda y, z, x, core: (y, z, x, 1 - core))
PAIRS = {
    "y": (
        device_pairs(lambda y, z, x, core: (y ^ 1, z, x, core)),
        device_pairs(lambda y, z, x, core: (3 - y, z, x, core)),
    ),
    "z": (
        device_pairs(lambda y, z, x, core: (y, z ^ 1, x, core)),
        device_pairs(lambda y, z, x, core: (y, 3 - z, x, core)),
    ),
}


def swap(value, pairs):
    return lax.ppermute(value, AXES, pairs)


def from_behind(value, axis, steps):
    count = lax.axis_size(axis)
    leading, last = (max(0, -steps), min(count, count - steps))
    return lax.ppermute(value, axis, [(source, source + steps) for source in range(leading, last)])


def norm_scale(values):
    return lax.rsqrt(jnp.mean(values * values, axis=1, keepdims=True) + EPS)


def norm_backward(out_grad_rows, values, scale_rows, gain):
    scaled = out_grad_rows * gain
    inner = jnp.mean(scaled * values, axis=1, keepdims=True)
    return scale_rows * (scaled - values * scale_rows * scale_rows * inner)


MEETS = (
    (("y", 0), ("y", 1), ("z", 0), ("z", 1)),
    (("y", 1), ("y", 0), ("z", 1), ("z", 0)),
    (("z", 0), ("z", 1), ("y", 0), ("y", 1)),
    (("z", 1), ("z", 0), ("y", 1), ("y", 0)),
)
SETS = (("y", 0), ("y", 1), ("z", 0), ("z", 1))
WIDE = (7, 7, 7, 6)
NARROW = (2, 2, 2, 2)
WIDE_COLUMNS = 1152
BLOCK = (64, 128)
COUNTS = (8, 4, 2, 1)


def partners(kind, at):
    near, far = at ^ 1, 3 - at
    return (at, far, near, 3 - near) if kind == 0 else (at, near, far, far ^ 1)


def slot_of(kind, at, chunk):
    own, second, first, _ = partners(kind, at)
    return jnp.where(chunk == own, 0, jnp.where(chunk == second, 1, jnp.where(chunk == first, 2, 3)))


def round_layout(round_at):
    layout = []
    for pairing in SETS:
        entries, total = [], 0
        for family, tiles, step in (("wide", WIDE, round_at), ("narrow", NARROW, round_at - 1)):
            for kind in range(4):
                if 0 <= step < 4 and MEETS[kind][step] == pairing:
                    entries.append((family, kind, step, total))
                    total += COUNTS[step] * tiles[kind]
        layout.append((entries, total))
    return layout


def spot(round_at, family, kind):
    for at, (entries, _) in enumerate(round_layout(round_at)):
        for entry in entries:
            if entry[:2] == (family, kind):
                return at, entry[3]
    return None


def blocks_of(round_at):
    return [
        total + (1 if 1 <= round_at and at == round_at - 1 else 0)
        for at, (_, total) in enumerate(round_layout(round_at))
    ]


def vmem(shape, dtype):
    return jax.ShapeDtypeStruct(shape, dtype)


def call(body, scalars, operands, outs, flops):
    in_specs = [pl.BlockSpec(memory_space=pltpu.SMEM)]
    in_specs += [pl.BlockSpec(memory_space=pltpu.VMEM)] * len(operands)
    size = sum(v.size * v.dtype.itemsize for v in list(operands) + list(outs))
    return pl.pallas_call(
        body,
        out_shape=tuple(outs),
        in_specs=in_specs,
        out_specs=tuple(pl.BlockSpec(memory_space=pltpu.VMEM) for _ in outs),
        compiler_params=pltpu.CompilerParams(vmem_limit_bytes=40 * 2**20),
        cost_estimate=pl.CostEstimate(flops=flops, bytes_accessed=size, transcendentals=0),
    )(scalars, *operands)


def product_columns(left, right):
    return jnp.dot(left[0], right[0], preferred_element_type=F32) + jnp.dot(
        left[1], right[1], preferred_element_type=F32
    )


def store_product(value, tile, kind, tiles, y_chunk, place, send, send_base, keep):
    axis, pairing = MEETS[kind][0]
    count = value.shape[1] // 128
    value = value.astype(BF16)
    for z_chunk in range(4):
        if axis == "y":
            slot, other = slot_of(pairing, place[0], y_chunk), z_chunk
        else:
            slot, other = slot_of(pairing, place[1], z_chunk), y_chunk
        for column in range(count):
            block = value[z_chunk * 64 : z_chunk * 64 + 64, column * 128 : column * 128 + 128]
            inner = other * tiles + tile + column

            @pl.when(slot < 2)
            def _():
                keep[slot * 4 * tiles + inner] = block

            @pl.when(slot >= 2)
            def _():
                send[send_base + (slot - 2) * 4 * tiles + inner] = block


def segments(width, first):
    at = first
    while at < first + width:
        step = min(256, first + width - at)
        yield at, step
        at += step


def wide_kernel(place_ref, two, two_other, cot, cot_other, *refs):
    own, other, (sends, keeps) = refs[:3], refs[3:6], (refs[6:10], refs[10:14])
    place = (place_ref[0], place_ref[1])
    mine = pl.multiple_of(place_ref[3] * WIDE_COLUMNS, 128)
    cut = 896

    def one_chunk(y_chunk, carry):
        lanes = pl.ds(pl.multiple_of(y_chunk * 256, 256), 256)
        left_two = (two[:, lanes].T, two_other[:, lanes].T)
        left_cot = (cot[:, lanes].T, cot_other[:, lanes].T)
        for matrix in range(3):
            left = left_cot if matrix == 0 else left_two
            for kind, first, width, tile in ((matrix, 0, cut, 0), (3, cut, 256, 2 * matrix)):
                for at, step in segments(width, first):
                    right = (
                        own[matrix][:, pl.ds(pl.multiple_of(mine + at, 128), step)],
                        other[matrix][:, at : at + step],
                    )
                    store_product(
                        product_columns(left, right),
                        tile + (at - first) // 128,
                        kind,
                        WIDE[kind],
                        y_chunk,
                        place,
                        sends[SETS.index(MEETS[kind][0])],
                        0,
                        keeps[kind],
                    )
        return carry

    lax.fori_loop(0, 4, one_chunk, 0)


def narrow_chunks(place_ref, one, one_other, low, low_other, backs, backs_other, ymix, ymix_other, sends, keeps):
    place = (place_ref[0], place_ref[1])
    mine = pl.ds(pl.multiple_of(place_ref[3] * 256, 128), 256)

    def one_chunk(y_chunk, carry):
        lanes = pl.ds(pl.multiple_of(y_chunk * 256, 256), 256)
        left_one = (one[:, lanes].T, one_other[:, lanes].T)
        left_low = (low[:, lanes].T, low_other[:, lanes].T)
        for kind in range(4):
            if kind < 3:
                left, right = left_one, (backs[kind, :, mine], backs_other[kind])
            else:
                left, right = left_low, (ymix[:, mine], ymix_other[...])
            at, base = spot(1, "narrow", kind)
            store_product(
                product_columns(left, right), 0, kind, 2, y_chunk, place, sends[at], base, keeps[kind]
            )
        return carry

    lax.fori_loop(0, 4, one_chunk, 0)


def advance(family, kind, step, place_ref, keep, got, got_base, send, send_base, new_keep):
    tiles = (WIDE if family == "wide" else NARROW)[kind]

    def total(at):
        mine = keep[pl.ds(at * tiles, tiles)].astype(F32)
        return mine + got[pl.ds(got_base + at * tiles, tiles)].astype(F32)

    if step == 0:
        for other in range(4):
            new_keep[other * tiles : (other + 1) * tiles] = total(other).astype(BF16)
            send[pl.ds(send_base + other * tiles, tiles)] = total(4 + other).astype(BF16)
    elif step == 1:
        axis, pairing = MEETS[kind][2]
        order = partners(pairing, place_ref[0 if axis == "y" else 1])
        for slot in range(2):
            new_keep[slot * tiles : (slot + 1) * tiles] = total(order[slot]).astype(BF16)
            send[pl.ds(send_base + slot * tiles, tiles)] = total(order[2 + slot]).astype(BF16)
    elif step == 2:
        new_keep[...] = total(0).astype(BF16)
        send[pl.ds(send_base, tiles)] = total(1).astype(BF16)
    else:
        base = 0 if family == "wide" else None
        first = sum((WIDE if family == "wide" else NARROW)[:kind])
        del base
        whole = total(0)
        here = place_ref[2]
        mine, away = whole[:, :32], whole[:, 32:]
        new_keep[first : first + tiles] = jnp.where(here == 0, mine, away)
        send[first : first + tiles] = jnp.where(here == 0, away, mine).astype(BF16)


def small_halves(value):
    high = value.astype(BF16)
    return high, (value - high.astype(F32)).astype(BF16)


def small_pack(value, block_ref, at):
    high, low = small_halves(value)
    block_ref[at, :32] = high
    block_ref[at, 32:] = low


def small_add(value, got_ref, at):
    high, low = small_halves(value)
    mine = high.astype(F32) + low.astype(F32)
    return mine + (got_ref[at, :32].astype(F32) + got_ref[at, 32:].astype(F32))


def round_kernel(round_at, place_ref, *refs):
    refs = list(refs)
    wide_step, narrow_step = round_at, round_at - 1
    take = lambda count: [refs.pop(0) for _ in range(count)]
    gots = take(4)
    keeps = {"wide": take(4) if wide_step < 4 else None, "narrow": take(4) if narrow_step >= 0 else None}
    operands = take(8) if round_at == 0 else None
    small = take(1)[0]
    sends = take(4) if round_at < 4 else None
    outs = {}
    if wide_step < 3:
        outs["wide"] = take(4)
    elif wide_step == 3:
        wide_send, wide_keep = take(2)
    if narrow_step < 3:
        outs["narrow"] = take(4)
    elif narrow_step == 3:
        narrow_send, narrow_keep = take(2)
    new_small = take(1)[0]
    if round_at == 0:
        narrow_chunks(place_ref, *operands, sends, outs["narrow"])
    for family, step in (("wide", wide_step), ("narrow", narrow_step)):
        if not 0 <= step < 4:
            continue
        for kind in range(4):
            got_at, got_base = spot(round_at, family, kind)
            if step < 3:
                send_at, send_base = spot(round_at + 1, family, kind)
                send, new_keep = sends[send_at], outs[family][kind]
            else:
                send, new_keep, send_base = (
                    (wide_send, wide_keep, 0) if family == "wide" else (narrow_send, narrow_keep, 0)
                )
            advance(
                family, kind, step, place_ref, keeps[family][kind], gots[got_at], got_base, send, send_base, new_keep
            )
    value = small[...]
    if round_at >= 1:
        value = small_add(value, gots[round_at - 1], blocks_of(round_at)[round_at - 1] - 1)
    new_small[...] = value
    if round_at < 4:
        small_pack(value, sends[round_at], blocks_of(round_at + 1)[round_at] - 1)


def run_round(round_at, scalars, gots, keeps, operands, small):
    wide_step, narrow_step = round_at, round_at - 1
    arrays = list(gots)
    if wide_step < 4:
        arrays += keeps["wide"]
    if narrow_step >= 0:
        arrays += keeps["narrow"]
    arrays += list(operands) + [small]
    outs, names = [], []

    def add(name, shapes):
        outs.extend(shapes)
        names.append((name, len(shapes)))

    if round_at < 4:
        add("sends", [vmem((count, *BLOCK), BF16) for count in blocks_of(round_at + 1)])
    for family, tiles, step in (("wide", WIDE, wide_step), ("narrow", NARROW, narrow_step)):
        if step < 3:
            add(family, [vmem((COUNTS[step + 1] * count, *BLOCK), BF16) for count in tiles])
        elif step == 3:
            add(family, [vmem((sum(tiles), 32, 128), BF16), vmem((sum(tiles), 32, 128), F32)])
    add("small", [vmem(small.shape, F32)])
    flops = 2 * 512 * 1024 * 1024 if round_at == 0 else 0
    results = list(call(functools.partial(round_kernel, round_at), scalars, arrays, outs, flops))
    return {name: [results.pop(0) for _ in range(count)] for name, count in names}


def swap_round(sends):
    return [swap(value, PAIRS[axis][pairing]) for value, (axis, pairing) in zip(sends, SETS)]


def beside(send, keep):
    return keep + swap(send, BESIDE).astype(F32)


def on_device(
    tokens,
    starts,
    gain_one,
    in_weight,
    conv_weight,
    out_weight,
    gain_two,
    gate_weight,
    up_weight,
    down_weight,
    cotangent,
):
    count_rows = tokens.shape[0]
    at = lax.axis_index("seq")
    core = at % 2
    place = {"y": at // 16, "z": (at // 4) % 4, "x": (at // 2) % 2, "core": core}

    scalars = jnp.stack([place["y"], place["z"], place["x"], core]).astype(jnp.int32)

    def share(value):
        return swap(value, CORES)

    def other_half(value):
        half = value.shape[-1] // 2
        return jnp.where(core == 0, value[..., half:], value[..., :half])

    inputs = tokens.astype(F32)
    scale_one = norm_scale(inputs)
    normed_one = (inputs * scale_one * gain_one).astype(BF16)
    projected = jnp.einsum("td,dkc->tkc", normed_one, in_weight, preferred_element_type=F32)
    b_part, c_part, x_part = (projected[:, 0], projected[:, 1], projected[:, 2])
    gated = (b_part * x_part).astype(BF16)
    offset = starts[0]
    positions = jnp.arange(count_rows, dtype=jnp.int32)
    tail_positions = positions[count_rows - 2 :]
    keep_mask = jnp.logical_not((tail_positions < offset) & (offset < count_rows)).astype(F32)[
        :, None
    ]
    tail = (gated[count_rows - 2 :].astype(F32) * keep_mask).astype(BF16)
    incoming = from_behind(tail, "seq", 1)
    extended = jnp.concatenate([incoming, gated], 0).astype(F32)
    valid = [jnp.ones((count_rows, 1), F32)]
    for shift_lag in (1, 2):
        valid.append(
            jnp.logical_not((offset <= positions) & (offset > positions - shift_lag)).astype(F32)[
                :, None
            ]
        )
    conv = jnp.zeros_like(b_part)
    for shift_lag in range(3):
        conv = (
            conv
            + conv_weight[shift_lag]
            * extended[2 - shift_lag : 2 - shift_lag + count_rows]
            * valid[shift_lag]
        )
    ymix = (c_part * conv).astype(BF16)
    branch = jnp.dot(ymix, out_weight, preferred_element_type=F32).astype(BF16)
    branch_other = swap(branch, ACROSS)
    hidden_grad = jnp.einsum("td,fd->tf", cotangent, down_weight, preferred_element_type=F32)
    cotangent_other = share(cotangent)
    normed_one_other = share(normed_one)
    ymix_other = share(other_half(ymix))
    resid = inputs + (branch.astype(F32) + branch_other.astype(F32))
    scale_two = norm_scale(resid)
    normed_two = (resid * scale_two * gain_two).astype(BF16)
    gate_act = jnp.dot(normed_two, gate_weight, preferred_element_type=F32)
    up_act = jnp.dot(normed_two, up_weight, preferred_element_type=F32)
    sigmoid_gate = jax.nn.sigmoid(gate_act)
    swish = gate_act * sigmoid_gate
    hidden = (swish * up_act).astype(BF16)
    swish_slope = sigmoid_gate * (1.0 + gate_act * (1.0 - sigmoid_gate))
    gate_back = (hidden_grad * up_act * swish_slope).astype(BF16)
    up_back = (hidden_grad * swish).astype(BF16)
    norm_two_part = jnp.einsum("tf,df->td", gate_back, gate_weight, preferred_element_type=F32)
    norm_two_part = norm_two_part + jnp.einsum(
        "tf,df->td", up_back, up_weight, preferred_element_type=F32
    )
    norm_two_part = norm_two_part.astype(BF16)
    norm_two_other = swap(norm_two_part, ACROSS)

    results = call(
        wide_kernel,
        scalars,
        [normed_two, share(normed_two), cotangent, cotangent_other, hidden, gate_back, up_back]
        + [share(other_half(value)) for value in (hidden, gate_back, up_back)],
        [vmem((8 * WIDE[k], *BLOCK), BF16) for k in (0, 1, 2, 3)]
        + [vmem((8 * WIDE[k], *BLOCK), BF16) for k in (0, 1, 2, 3)],
        2 * 512 * 1024 * 3456,
    )
    sends, keeps = list(results[:4]), {"wide": list(results[4:])}
    norm_two_other, keeps["wide"][3] = lax.optimization_barrier((norm_two_other, keeps["wide"][3]))
    gots = swap_round(sends)

    norm_two_back = norm_two_part.astype(F32) + norm_two_other.astype(F32)
    gain_two_g = jnp.sum(norm_two_back * resid * scale_two, axis=0)
    resid_grad = cotangent.astype(F32) + norm_backward(norm_two_back, resid, scale_two, gain_two)
    resid_low = resid_grad.astype(BF16)
    resid_low_other = share(resid_low)
    ymix_back = jnp.einsum("td,cd->tc", resid_low, out_weight, preferred_element_type=F32)
    c_back = ymix_back * conv
    conv_back = ymix_back * c_part
    extended_grad = jnp.zeros_like(extended)
    tap_grads = []
    for shift_lag in range(3):
        lag_term = conv_back * valid[shift_lag]
        tap_grads.append(
            jnp.sum(lag_term * extended[2 - shift_lag : 2 - shift_lag + count_rows], axis=0)
        )
        extended_grad = extended_grad + jnp.pad(
            lag_term * conv_weight[shift_lag], ((2 - shift_lag, shift_lag), (0, 0))
        )
    returned = from_behind(extended_grad[:2], "seq", -1)
    gated_back = extended_grad[2:] + jnp.pad(returned * keep_mask, ((count_rows - 2, 0), (0, 0)))
    b_back = (gated_back * x_part).astype(BF16)
    c_back = c_back.astype(BF16)
    x_back = (gated_back * b_part).astype(BF16)
    norm_one_part = sum(
        jnp.einsum("tc,dc->td", back, in_weight[:, k], preferred_element_type=F32)
        for k, back in enumerate((b_back, c_back, x_back))
    )
    norm_one_low = norm_one_part.astype(BF16)
    norm_one_other = swap(norm_one_low, ACROSS)
    gain_one_part = jnp.sum(norm_one_part * inputs * scale_one, axis=0)

    backs = jnp.stack([b_back, c_back, x_back], 0)
    small = jnp.concatenate(
        [
            gain_one_part.reshape(8, 128),
            gain_two_g.reshape(8, 128),
            jnp.stack(tap_grads, 0).reshape(12, 128),
            jnp.zeros((4, 128), F32),
        ],
        0,
    )
    operands = [
        normed_one,
        normed_one_other,
        resid_low,
        resid_low_other,
        backs,
        share(other_half(backs)),
        ymix,
        ymix_other,
    ]
    state = run_round(0, scalars, gots, keeps, operands, small)
    for round_at in (1, 2, 3):
        gots = swap_round(state["sends"])
        if round_at == 2:
            gots[0], norm_one_other = lax.optimization_barrier((gots[0], norm_one_other))
        state = run_round(round_at, scalars, gots, state, [], state["small"][0])
    wide_send, wide_keep = state["wide"]
    gots = swap_round(state["sends"])
    wide = beside(wide_send, wide_keep)
    state = run_round(4, scalars, gots, state, [], state["small"][0])
    narrow = beside(*state["narrow"])
    small = state["small"][0]
    small = small + swap(small, BESIDE)
    small = small + swap(small, CORES)
    gain_one_g = small[:8] + swap(small[:8], ACROSS)
    gain_one_g = gain_one_g.reshape(-1)
    gain_two_g = small[8:16].reshape(-1)
    conv_g = small[16:28].reshape(3, -1)

    def both_cores(value):
        value = value.reshape(value.shape[0], 2, 16, 128)
        mine = jnp.where(core == 0, value[:, 0], value[:, 1])
        other = swap(jnp.where(core == 0, value[:, 1], value[:, 0]), CORES)
        return jnp.where(core == 0, jnp.stack([mine, other]), jnp.stack([other, mine]))

    def rows(value):
        return value.transpose(2, 0, 1, 3).reshape(16, -1)

    wide = both_cores(wide)
    down_g, gate_g, up_g = (
        rows(jnp.concatenate([wide[:, 7 * k : 7 * k + 7], wide[:, 21 + 2 * k : 23 + 2 * k]], 1))
        for k in range(3)
    )
    down_g = down_g.T
    narrow = both_cores(narrow)
    in_g = jnp.stack([rows(narrow[:, 2 * k : 2 * k + 2]) for k in range(3)], 1)
    out_g = rows(narrow[:, 6:8]).T

    down_part = jnp.dot(hidden, down_weight, preferred_element_type=F32).astype(BF16)
    norm_one_other, down_part = lax.optimization_barrier((norm_one_other, down_part))
    down_other = swap(down_part, ACROSS)
    mixed = (resid + (down_part.astype(F32) + down_other.astype(F32))).astype(BF16)
    norm_one_back = norm_one_low.astype(F32) + norm_one_other.astype(F32)
    tokens_grad = resid_grad + norm_backward(norm_one_back, inputs, scale_one, gain_one)
    return (mixed, tokens_grad, gain_one_g, in_g, conv_g, out_g, gain_two_g, gate_g, up_g, down_g)


def solution(mesh):
    return jax.shard_map(
        on_device,
        mesh=mesh,
        in_specs=(
            P("seq", None),
            P("seq"),
            P(),
            P(None, None, "tensor"),
            P(None, "tensor"),
            P("tensor", None),
            P(),
            P(None, "tensor"),
            P(None, "tensor"),
            P("tensor", None),
            P("seq", None),
        ),
        out_specs=(
            P("seq", None),
            P("seq", None),
            P(),
            P("seq", None, "tensor"),
            P(None, "tensor"),
            P("tensor", "seq"),
            P(),
            P("seq", "tensor"),
            P("seq", "tensor"),
            P("tensor", "seq"),
        ),
        check_vma=False,
    )
```

```python
import functools

import jax
import jax.numpy as jnp
from jax import lax
from jax.experimental import pallas as pl
from jax.experimental.pallas import tpu as pltpu
from jax.sharding import PartitionSpec as P

EPS = 1e-05
AXES = ("seq", "tensor")
BF16 = jnp.bfloat16
F32 = jnp.float32


def device_pairs(move):
    def number(y, z, x, core):
        return ((((y % 4) * 4 + z % 4) * 2 + x % 2) * 2 + core) * 2 + (x % 4) // 2

    return [
        (number(y, z, x, core), number(*move(y, z, x, core)))
        for y in range(4)
        for z in range(4)
        for x in range(4)
        for core in range(2)
    ]


ACROSS = device_pairs(lambda y, z, x, core: (y, z, (x + 2) % 4, core))
BESIDE = device_pairs(lambda y, z, x, core: (y, z, x ^ 1, core))
CORES = device_pairs(lambda y, z, x, core: (y, z, x, 1 - core))


def peer(at, pairing):
    return (at ^ 1, 3 - at, at ^ 2)[pairing]


SETS = (("y", 0), ("y", 1), ("y", 2), ("z", 0), ("z", 1), ("z", 2))
FIRST = (("y", 0), ("y", 1), ("z", 0), ("z", 1))
SECOND = (("y", 1), ("y", 0), ("z", 1), ("z", 0))
PAIRS = {
    (axis, pairing): device_pairs(
        functools.partial(
            lambda axis, pairing, y, z, x, core: (peer(y, pairing), z, x, core)
            if axis == "y"
            else (y, peer(z, pairing), x, core),
            axis,
            pairing,
        )
    )
    for axis, pairing in SETS
}
WIDE = (7, 7, 7, 6)
NARROW = (2, 2, 2, 2)
WIDE_COLUMNS = 1152
CUT = 896
BLOCK = (64, 128)
TILES = sum(WIDE) + sum(NARROW)
OTHER_AXIS = {"y": "z", "z": "y"}


def layouts():
    one, two = [], []
    for axis, pairing in SETS:
        entries, total = {}, 0
        for kind in range(4):
            if SECOND[kind] == (axis, pairing):
                entries["wide", kind] = total
                total += 4 * WIDE[kind]
        for kind in range(4):
            if FIRST[kind][0] == axis:
                entries["narrow", kind] = total
                total += 4 * NARROW[kind]
        if axis == "y":
            entries["small"] = total
            total += 1
        one.append((entries, total))
        entries, total = {}, 0
        for family, tiles in (("wide", WIDE), ("narrow", NARROW)):
            for kind in range(4):
                if FIRST[kind][0] != axis:
                    entries[family, kind] = total
                    total += tiles[kind]
        if axis == "z":
            entries["small"] = total
            total += 1
        two.append((entries, total))
    return one, two


ROUND_ONE, ROUND_TWO = layouts()


def swap(value, pairs):
    return lax.ppermute(value, AXES, pairs)


def from_behind(value, axis, steps):
    count = lax.axis_size(axis)
    leading, last = (max(0, -steps), min(count, count - steps))
    return lax.ppermute(value, axis, [(source, source + steps) for source in range(leading, last)])


def norm_scale(values):
    return lax.rsqrt(jnp.mean(values * values, axis=1, keepdims=True) + EPS)


def norm_backward(out_grad_rows, values, scale_rows, gain):
    scaled = out_grad_rows * gain
    inner = jnp.mean(scaled * values, axis=1, keepdims=True)
    return scale_rows * (scaled - values * scale_rows * scale_rows * inner)


def like(shape, dtype):
    return jax.ShapeDtypeStruct(shape, dtype)


def call(body, *, scalars, operands, outs, scratch=()):
    size = sum(v.size * v.dtype.itemsize for v in list(operands) + list(outs))
    whole = pl.BlockSpec(memory_space=pltpu.VMEM)
    return pl.pallas_call(
        body,
        out_shape=tuple(outs),
        in_specs=[pl.BlockSpec(memory_space=pltpu.SMEM)] + [whole] * len(operands),
        out_specs=tuple(whole for _ in outs),
        scratch_shapes=list(scratch),
        compiler_params=pltpu.CompilerParams(vmem_limit_bytes=min(size + 14 * 2**20, 48 * 2**20)),
        cost_estimate=pl.CostEstimate(flops=0, bytes_accessed=0, transcendentals=0),
    )(scalars, *operands)


def dot(left, right):
    return jnp.dot(left, right, preferred_element_type=F32)


def dot_rows(left, right):
    return lax.dot_general(left, right, (((1,), (1,)), ((), ())), preferred_element_type=F32)


def row_numbers(shape, first=0):
    return lax.broadcasted_iota(jnp.int32, shape, 0) + first


def valid_rows(offset, lag, shape):
    row = row_numbers(shape)
    return jnp.where((offset <= row) & (offset > row - lag), 0.0, 1.0)


def linked_rows(offset, shape, first, count):
    return jnp.where((row_numbers(shape, first) < offset) & (offset < count), 0.0, 1.0)


def tail_kernel(scalars, tokens, gain, weight, tail):
    rows = tokens.shape[0]
    values = tokens[rows - 16 :].astype(F32)
    normed = (values * norm_scale(values) * gain[...]).astype(BF16)
    gated = (dot(normed, weight[0]) * dot(normed, weight[2])).astype(BF16).astype(F32)
    tail[...] = (gated * linked_rows(scalars[4], gated.shape, rows - 16, rows)).astype(BF16)


def project_kernel(scalars, tokens, gain, weight, normed, parts, gated):
    values = tokens[...].astype(F32)
    normed[...] = (values * norm_scale(values) * gain[...]).astype(BF16)
    for k in range(3):
        parts[k] = dot(normed[...], weight[k])
    gated[...] = (parts[0] * parts[2]).astype(BF16)


def behind(gated, incoming, lag):
    moved = pltpu.roll(gated, lag, 0)
    row = row_numbers(gated.shape)
    for at in range(lag):
        moved = jnp.where(row == at, incoming[16 - lag + at : 17 - lag + at], moved)
    return moved


def mix_kernel(scalars, gated, incoming, parts, taps, weight, conv, ymix, ymix_away, branch):
    values = gated[...].astype(F32)
    before = incoming[...].astype(F32)
    total = taps[0:1] * values
    for lag in (1, 2):
        total = total + taps[lag : lag + 1] * behind(values, before, lag) * valid_rows(
            scalars[4], lag, values.shape
        )
    conv[...] = total
    ymix[...] = (parts[1] * total).astype(BF16)
    ymix_away[...] = away_half(ymix[...], scalars[3])
    branch[...] = dot(ymix[...], weight[...]).astype(BF16)


def away_half(value, core):
    half = value.shape[-1] // 2
    return jnp.where(core == 0, value[..., half:], value[..., :half])


def second_norm(part, other, resid, gain, cot):
    back = part.astype(F32) + other.astype(F32)
    scale = norm_scale(resid)
    return back, scale, cot.astype(F32) + norm_backward(back, resid, scale, gain)


def edge_kernel(scalars, part, other, resid, gain, cot, weight, parts, taps, edge):
    top = slice(0, 16)
    _, _, grad = second_norm(part[top], other[top], resid[top], gain[...], cot[top])
    conv_back = dot_rows(grad.astype(BF16), weight[...]) * parts[1, top]
    one = conv_back * valid_rows(scalars[4], 1, conv_back.shape) * taps[1:2]
    two = conv_back * valid_rows(scalars[4], 2, conv_back.shape) * taps[2:3]
    row = row_numbers((8, conv_back.shape[1]))
    edge[...] = jnp.where(row == 6, two[0:1], 0.0) + jnp.where(row == 7, one[0:1] + two[1:2], 0.0)


def middle_kernel(
    scalars, part, other, resid, gain, cot, weight, parts, taps, conv, gated, incoming, grad, low, gain_grad, c_back, gated_back, tap_grads
):
    back, scale, resid_grad = second_norm(part[...], other[...], resid[...], gain[...], cot[...])
    gain_grad[...] = jnp.sum(back * resid[...] * scale, axis=0, keepdims=True)
    grad[...] = resid_grad
    low[...] = resid_grad.astype(BF16)
    ymix_back = dot_rows(low[...], weight[...])
    c_back[...] = (ymix_back * conv[...]).astype(BF16)
    conv_back = ymix_back * parts[1]
    values, before = gated[...].astype(F32), incoming[...].astype(F32)
    rows = values.shape[0]
    tap_grads[0:1] = jnp.sum(conv_back * values, axis=0, keepdims=True)
    total = conv_back * taps[0:1]
    row = row_numbers(values.shape)
    for lag in (1, 2):
        term = conv_back * valid_rows(scalars[4], lag, values.shape)
        tap_grads[lag : lag + 1] = jnp.sum(term * behind(values, before, lag), axis=0, keepdims=True)
        moved = pltpu.roll(term * taps[lag : lag + 1], rows - lag, 0)
        total = total + jnp.where(row < rows - lag, moved, 0.0)
    gated_back[...] = total


def last_kernel(
    scalars, gated_back, returned, parts, c_back, weight, tokens, gain_two_grad, tap_grads, backs, backs_away, low, small
):
    rows = gated_back.shape[0]
    links = linked_rows(scalars[4], returned.shape, rows - 8, rows)
    end = gated_back[rows - 8 :] + returned[...] * links
    total = jnp.concatenate([gated_back[: rows - 8], end], 0)
    backs[0] = (total * parts[2]).astype(BF16)
    backs[1] = c_back[...]
    backs[2] = (total * parts[0]).astype(BF16)
    for k in range(3):
        backs_away[k] = away_half(backs[k], scalars[3])
    grad = dot_rows(backs[0], weight[0]) + dot_rows(backs[1], weight[1]) + dot_rows(backs[2], weight[2])
    low[...] = grad.astype(BF16)
    values = tokens[...].astype(F32)
    gain_grad = jnp.sum(grad * values * norm_scale(values), axis=0, keepdims=True)
    for at in range(8):
        lanes = slice(at * 128, at * 128 + 128)
        small[at : at + 1] = gain_grad[:, lanes]
        small[8 + at : 9 + at] = gain_two_grad[:, lanes]
    for lag in range(3):
        for at in range(4):
            row = 16 + 4 * lag + at
            small[row : row + 1] = tap_grads[lag : lag + 1, at * 128 : at * 128 + 128]
    small[28:32] = jnp.zeros((4, 128), F32)


def fill_transposed(left, own, other):
    for at in range(0, own.shape[1], 256):
        left[at : at + 256, :256] = own[:, at : at + 256].T
        left[at : at + 256, 256:] = other[:, at : at + 256].T


def chunk_rows(left, axis, chunk):
    if axis == "y":
        return left[pl.ds(pl.multiple_of(chunk * 256, 256), 256)]
    return jnp.concatenate(
        [left[pl.ds(pl.multiple_of(at * 256 + chunk * 64, 64), 64)] for at in range(4)], 0
    )


def store_blocks(value, target, base, tiles, tile):
    value = value.astype(BF16)
    for chunk in range(4):
        for column in range(value.shape[1] // 128):
            target[base + chunk * tiles + tile + column] = value[
                chunk * 64 : chunk * 64 + 64, column * 128 : column * 128 + 128
            ]


def position(scalars, axis):
    return scalars[0 if axis == "y" else 1]


def wide_kernel(scalars, two, two_other, cot, cot_other, *refs):
    own, other, sends, keeps = refs[:3], refs[3:6], refs[6:10], refs[10:14]
    left_two, left_cot = refs[14:]
    fill_transposed(left_cot, cot, cot_other)
    fill_transposed(left_two, two, two_other)
    core = scalars[3]
    runs = [(k, k, at, min(256, CUT - at), at // 128) for k in range(3) for at in range(0, CUT, 256)]
    runs += [(3, k, CUT, WIDE_COLUMNS - CUT, 2 * k) for k in range(3)]
    for kind, (axis, pairing) in enumerate(FIRST):
        at = position(scalars, axis)
        first, second = peer(at, pairing), peer(at, 1 - pairing)
        chunks = (at, second, first, peer(first, 1 - pairing))
        for slot, chunk in enumerate(chunks):
            target = keeps[kind] if slot < 2 else sends[kind]
            rows = {}
            for run_kind, matrix, column, width, tile in runs:
                if run_kind != kind:
                    continue
                if (matrix == 0) not in rows:
                    rows[matrix == 0] = chunk_rows(left_cot if matrix == 0 else left_two, axis, chunk)
                left = rows[matrix == 0]
                mine = pl.ds(pl.multiple_of(core * WIDE_COLUMNS + column, 128), width)
                value = dot(left[:, :256], own[matrix][:, mine])
                value = value + dot(left[:, 256:], other[matrix][:, column : column + width])
                store_blocks(value, target, (slot % 2) * 4 * WIDE[kind], WIDE[kind], tile)


def split_small(value, target, at):
    high = value.astype(BF16)
    target[at, :32] = high
    target[at, 32:] = (value - high.astype(F32)).astype(BF16)


def join_small(source, at):
    return source[at, :32].astype(F32) + source[at, 32:].astype(F32)


def rounded_small(value):
    high = value.astype(BF16)
    return high.astype(F32) + (value - high.astype(F32)).astype(BF16).astype(F32)


def sum_small(value, gots, layout, axis):
    near, far, cross = (
        join_small(gots[SETS.index((axis, p))], layout[SETS.index((axis, p))][0]["small"]) for p in range(3)
    )
    return (rounded_small(value) + cross) + (near + far)


def take(refs, *counts):
    out, at = [], 0
    for count in counts:
        out.append(refs[at : at + count])
        at += count
    return out


def first_kernel(scalars, *refs):
    gots, keeps, operands, (small,), sends, wide_keeps, narrow_keeps, lefts = take(refs, 4, 4, 8, 1, 6, 4, 4, 2)
    one, one_other, low, low_other, backs, backs_other, ymix, ymix_other = operands
    left_one, left_low = lefts
    fill_transposed(left_one, one, one_other)
    fill_transposed(left_low, low, low_other)
    mine = pl.ds(pl.multiple_of(scalars[3] * 256, 256), 256)
    for kind in range(4):
        axis = FIRST[kind][0]
        at = position(scalars, axis)
        left, own, other = (
            (left_one, backs[kind, :, mine], backs_other[kind])
            if kind < 3
            else (left_low, ymix[:, mine], ymix_other[...])
        )
        for pairing in (0, 1, 2, None):
            rows = chunk_rows(left, axis, at if pairing is None else peer(at, pairing))
            value = dot(rows[:, :256], own) + dot(rows[:, 256:], other)
            if pairing is None:
                store_blocks(value, narrow_keeps[kind], 0, 2, 0)
            else:
                place = SETS.index((axis, pairing))
                store_blocks(value, sends[place], ROUND_ONE[place][0]["narrow", kind], 2, 0)
    for kind in range(4):
        half = 4 * WIDE[kind]
        place = SETS.index(SECOND[kind])
        base = ROUND_ONE[place][0]["wide", kind]
        wide_keeps[kind][...] = (keeps[kind][:half].astype(F32) + gots[kind][:half].astype(F32)).astype(BF16)
        sends[place][base : base + half] = (
            keeps[kind][half:].astype(F32) + gots[kind][half:].astype(F32)
        ).astype(BF16)
    for pairing in range(3):
        place = SETS.index(("y", pairing))
        split_small(small[...], sends[place], ROUND_ONE[place][0]["small"])


def second_kernel(scalars, *refs):
    gots, wide_in, narrow_in, (small,), sends, wide_keeps, narrow_keeps, (new_small,) = take(refs, 6, 4, 4, 1, 6, 4, 4, 1)
    for family, tiles, keeps, new_keeps in (
        ("narrow", NARROW, narrow_in, narrow_keeps),
        ("wide", WIDE, wide_in, wide_keeps),
    ):
        for kind in range(4):
            axis, count = FIRST[kind][0], tiles[kind]
            came = [SECOND[kind]] if family == "wide" else [(axis, p) for p in range(3)]
            came = [SETS.index(entry) for entry in came]

            def total(chunk):
                value = keeps[kind][pl.ds(chunk * count, count)].astype(F32)
                for place in came:
                    base = ROUND_ONE[place][0][family, kind]
                    value = value + gots[place][pl.ds(base + chunk * count, count)].astype(F32)
                return value.astype(BF16)

            at = position(scalars, OTHER_AXIS[axis])
            new_keeps[kind][...] = total(at)
            for pairing in range(3):
                place = SETS.index((OTHER_AXIS[axis], pairing))
                base = ROUND_TWO[place][0][family, kind]
                sends[place][base : base + count] = total(peer(at, pairing))
    value = sum_small(small[...], gots, ROUND_ONE, "y")
    new_small[...] = value
    for pairing in range(3):
        place = SETS.index(("z", pairing))
        split_small(value, sends[place], ROUND_TWO[place][0]["small"])


def third_kernel(scalars, *refs):
    gots, wide_in, narrow_in, (small,), (send, keep) = take(refs, 6, 4, 4, 1, 2)
    here = scalars[2]
    tile = 0
    for family, tiles, keeps in (("wide", WIDE, wide_in), ("narrow", NARROW, narrow_in)):
        for kind in range(4):
            count = tiles[kind]
            value = keeps[kind][...].astype(F32)
            for pairing in range(3):
                place = SETS.index((OTHER_AXIS[FIRST[kind][0]], pairing))
                base = ROUND_TWO[place][0][family, kind]
                value = value + gots[place][base : base + count].astype(F32)
            zero, one = value[:, :32], value[:, 32:]
            keep[tile : tile + count] = jnp.where(here == 0, zero, one)
            send[tile : tile + count] = jnp.where(here == 0, one, zero).astype(BF16)
            tile += count
    value = sum_small(small[...], gots, ROUND_TWO, "z")
    high = value.astype(BF16)
    low = (value - high.astype(F32)).astype(BF16)
    send[TILES] = high
    send[TILES + 1] = low
    keep[TILES] = high.astype(F32)
    keep[TILES + 1] = low.astype(F32)


def cores_kernel(scalars, keep, got, mine, away):
    core = scalars[3]
    total = keep[:TILES] + got[:TILES].astype(F32)
    zero, one = total[:, :16], total[:, 16:]
    mine[:TILES] = jnp.where(core == 0, zero, one)
    away[:TILES] = jnp.where(core == 0, one, zero)
    small = (keep[TILES] + keep[TILES + 1]) + (got[TILES].astype(F32) + got[TILES + 1].astype(F32))
    for at in range(2):
        mine[TILES + at] = small[at * 16 : at * 16 + 16]
        away[TILES + at] = small[at * 16 : at * 16 + 16]


def outputs_kernel(scalars, mine, got, down, gate, up, inner, out, small):
    core = scalars[3]

    def place(target, tile, column, columns):
        zero, one = jnp.where(core == 0, mine[tile], got[tile]), jnp.where(core == 0, got[tile], mine[tile])
        target[:, column : column + 128] = zero
        target[:, columns + column : columns + column + 128] = one

    for matrix, target in enumerate((down, gate, up)):
        for column in range(0, WIDE_COLUMNS, 128):
            tile = 7 * matrix + column // 128 if column < CUT else 21 + 2 * matrix + (column - CUT) // 128
            place(target, tile, column, WIDE_COLUMNS)
    for kind in range(4):
        for column in range(2):
            place(inner.at[kind] if kind < 3 else out, 27 + 2 * kind + column, column * 128, 256)
    small[:16] = mine[TILES] + got[TILES]
    small[16:] = mine[TILES + 1] + got[TILES + 1]


def swap_round(sends, sets):
    return [swap(value, PAIRS[entry]) for value, entry in zip(sends, sets)]


def blocks(counts):
    return [like((count, *BLOCK), BF16) for count in counts]


def on_device(
    tokens,
    starts,
    gain_one,
    in_weight,
    conv_weight,
    out_weight,
    gain_two,
    gate_weight,
    up_weight,
    down_weight,
    cotangent,
):
    at = lax.axis_index("seq")
    core = at % 2
    scalars = jnp.stack([at // 16, (at // 4) % 4, (at // 2) % 2, core, starts[0]]).astype(jnp.int32)
    run = functools.partial(call, scalars=scalars)
    rows, width = tokens.shape
    channels = conv_weight.shape[1]
    in_parts = in_weight.transpose(1, 0, 2)
    gain_one_row, gain_two_row = gain_one.reshape(1, -1), gain_two.reshape(1, -1)

    def share(value):
        return swap(value, CORES)

    tail = run(tail_kernel, operands=[tokens, gain_one_row, in_parts], outs=[like((16, channels), BF16)])[0]
    incoming = from_behind(tail, "seq", 1)
    normed_one, parts, gated = run(
        project_kernel,
        operands=[tokens, gain_one_row, in_parts],
        outs=[like((rows, width), BF16), like((3, rows, channels), F32), like((rows, channels), BF16)],
    )
    conv, ymix, ymix_away, branch = run(
        mix_kernel,
        operands=[gated, incoming, parts, conv_weight, out_weight],
        outs=[
            like((rows, channels), F32),
            like((rows, channels), BF16),
            like((rows, channels // 2), BF16),
            like((rows, width), BF16),
        ],
    )
    branch_other = swap(branch, ACROSS)
    hidden_grad = jnp.einsum("td,fd->tf", cotangent, down_weight, preferred_element_type=F32)
    cotangent_other = share(cotangent)
    normed_one_other = share(normed_one)
    ymix_other = share(ymix_away)
    resid = tokens.astype(F32) + (branch.astype(F32) + branch_other.astype(F32))
    normed_two = (resid * norm_scale(resid) * gain_two).astype(BF16)
    gate_act = jnp.dot(normed_two, gate_weight, preferred_element_type=F32)
    up_act = jnp.dot(normed_two, up_weight, preferred_element_type=F32)
    sigmoid_gate = jax.nn.sigmoid(gate_act)
    swish = gate_act * sigmoid_gate
    hidden = (swish * up_act).astype(BF16)
    swish_slope = sigmoid_gate * (1.0 + gate_act * (1.0 - sigmoid_gate))
    gate_back = (hidden_grad * up_act * swish_slope).astype(BF16)
    up_back = (hidden_grad * swish).astype(BF16)
    norm_two_part = jnp.einsum("tf,df->td", gate_back, gate_weight, preferred_element_type=F32)
    norm_two_part = norm_two_part + jnp.einsum(
        "tf,df->td", up_back, up_weight, preferred_element_type=F32
    )
    norm_two_part = norm_two_part.astype(BF16)
    norm_two_other = swap(norm_two_part, ACROSS)

    results = run(
        wide_kernel,
        operands=[normed_two, share(normed_two), cotangent, cotangent_other, hidden, gate_back, up_back]
        + [share(away_half(value, core)) for value in (hidden, gate_back, up_back)],
        outs=blocks([8 * count for count in WIDE] * 2),
        scratch=[pltpu.VMEM((width, 2 * rows), BF16)] * 2,
    )
    sends, keeps = list(results[:4]), list(results[4:])
    norm_two_other, keeps[3] = lax.optimization_barrier((norm_two_other, keeps[3]))
    gots = swap_round(sends, FIRST)

    edge_operands = [norm_two_part, norm_two_other, resid, gain_two_row, cotangent, out_weight, parts, conv_weight]
    edge = run(edge_kernel, operands=edge_operands, outs=[like((8, channels), F32)])[0]
    returned = from_behind(edge, "seq", -1)
    resid_grad, resid_low, gain_two_grad, c_back, gated_back, tap_grads = run(
        middle_kernel,
        operands=edge_operands + [conv, gated, incoming],
        outs=[
            like((rows, width), F32),
            like((rows, width), BF16),
            like((1, width), F32),
            like((rows, channels), BF16),
            like((rows, channels), F32),
            like((3, channels), F32),
        ],
    )
    resid_low_other = share(resid_low)
    backs, backs_away, norm_one_low, small = run(
        last_kernel,
        operands=[gated_back, returned, parts, c_back, in_parts, tokens, gain_two_grad, tap_grads],
        outs=[
            like((3, rows, channels), BF16),
            like((3, rows, channels // 2), BF16),
            like((rows, width), BF16),
            like((32, 128), F32),
        ],
    )
    norm_one_other = swap(norm_one_low, ACROSS)
    results = run(
        first_kernel,
        operands=gots
        + keeps
        + [normed_one, normed_one_other, resid_low, resid_low_other, backs, share(backs_away), ymix, ymix_other]
        + [small],
        outs=blocks([total for _, total in ROUND_ONE])
        + blocks([4 * count for count in WIDE])
        + blocks([4 * count for count in NARROW]),
        scratch=[pltpu.VMEM((width, 2 * rows), BF16)] * 2,
    )
    sends, keeps = list(results[:6]), list(results[6:])
    gots = swap_round(sends, SETS)
    gots[0], norm_one_other = lax.optimization_barrier((gots[0], norm_one_other))
    results = run(
        second_kernel,
        operands=gots + keeps + [small],
        outs=blocks([total for _, total in ROUND_TWO]) + blocks(WIDE) + blocks(NARROW) + [like((32, 128), F32)],
    )
    sends, keeps, small = list(results[:6]), list(results[6:14]), results[14]
    down_part = jnp.dot(hidden, down_weight, preferred_element_type=F32).astype(BF16)
    norm_one_other, down_part = lax.optimization_barrier((norm_one_other, down_part))
    down_other = swap(down_part, ACROSS)
    gots = swap_round(sends, SETS)
    gots[0], down_other = lax.optimization_barrier((gots[0], down_other))
    beside, kept = run(
        third_kernel,
        operands=gots + keeps + [small],
        outs=[like((TILES + 2, 32, 128), BF16), like((TILES + 2, 32, 128), F32)],
    )
    mine, away = run(
        cores_kernel,
        operands=[kept, swap(beside, BESIDE)],
        outs=[like((TILES + 2, 16, 128), F32)] * 2,
    )
    down_g, gate_g, up_g, in_g, out_g, small = run(
        outputs_kernel,
        operands=[mine, swap(away, CORES)],
        outs=[like((16, 2 * WIDE_COLUMNS), F32)] * 3
        + [like((3, 16, channels), F32), like((16, channels), F32), like((32, 128), F32)],
    )
    in_g = in_g.transpose(1, 0, 2)
    gain_one_g = (small[:8] + swap(small[:8], ACROSS)).reshape(-1)
    gain_two_g = small[8:16].reshape(-1)
    conv_g = small[16:28].reshape(3, -1)

    mixed = (resid + (down_part.astype(F32) + down_other.astype(F32))).astype(BF16)
    inputs = tokens.astype(F32)
    norm_one_back = norm_one_low.astype(F32) + norm_one_other.astype(F32)
    tokens_grad = resid_grad + norm_backward(norm_one_back, inputs, norm_scale(inputs), gain_one)
    return (mixed, tokens_grad, gain_one_g, in_g, conv_g, out_g.T, gain_two_g, gate_g, up_g, down_g.T)


def solution(mesh):
    return jax.shard_map(
        on_device,
        mesh=mesh,
        in_specs=(
            P("seq", None),
            P("seq"),
            P(),
            P(None, None, "tensor"),
            P(None, "tensor"),
            P("tensor", None),
            P(),
            P(None, "tensor"),
            P(None, "tensor"),
            P("tensor", None),
            P("seq", None),
        ),
        out_specs=(
            P("seq", None),
            P("seq", None),
            P(),
            P("seq", None, "tensor"),
            P(None, "tensor"),
            P("tensor", "seq"),
            P(),
            P("seq", "tensor"),
            P("seq", "tensor"),
            P("tensor", "seq"),
        ),
        check_vma=False,
    )
```

```python
import functools

import jax
import jax.numpy as jnp
from jax import lax
from jax.experimental import pallas as pl
from jax.experimental.pallas import tpu as pltpu
from jax.sharding import PartitionSpec as P

EPS = 1e-05
AXES = ("seq", "tensor")
BF16 = jnp.bfloat16
F32 = jnp.float32


def device_pairs(move):
    def number(y, z, x, core):
        return ((((y % 4) * 4 + z % 4) * 2 + x % 2) * 2 + core) * 2 + (x % 4) // 2

    return [
        (number(y, z, x, core), number(*move(y, z, x, core)))
        for y in range(4)
        for z in range(4)
        for x in range(4)
        for core in range(2)
    ]


ACROSS = device_pairs(lambda y, z, x, core: (y, z, (x + 2) % 4, core))
BESIDE = device_pairs(lambda y, z, x, core: (y, z, x ^ 1, core))
SKEW = device_pairs(lambda y, z, x, core: (y, z, (x ^ 1) ^ 2, core))
CORES = device_pairs(lambda y, z, x, core: (y, z, x, 1 - core))


def peer(at, pairing):
    return (at ^ 1, 3 - at, at ^ 2)[pairing]


SETS = (("y", 0), ("y", 1), ("y", 2), ("z", 0), ("z", 1), ("z", 2))
FIRST = (("y", 0), ("y", 1), ("z", 0), ("z", 1))
SECOND = (("y", 1), ("y", 0), ("z", 1), ("z", 0))
PAIRS = {
    (axis, pairing): device_pairs(
        functools.partial(
            lambda axis, pairing, y, z, x, core: (peer(y, pairing), z, x, core)
            if axis == "y"
            else (y, peer(z, pairing), x, core),
            axis,
            pairing,
        )
    )
    for axis, pairing in SETS
}
WIDE = (7, 7, 7, 6)
NARROW = (2, 2, 2, 2)
WIDE_COLUMNS = 1152
CUT = 896
BLOCK = (64, 128)
TILES = sum(WIDE) + sum(NARROW)
OTHER_AXIS = {"y": "z", "z": "y"}


def layouts():
    one, two = [], []
    for axis, pairing in SETS:
        entries, total = {}, 0
        for kind in range(4):
            if SECOND[kind] == (axis, pairing):
                entries["wide", kind] = total
                total += 4 * WIDE[kind]
        for kind in range(4):
            if FIRST[kind][0] == axis:
                entries["narrow", kind] = total
                total += 4 * NARROW[kind]
        if axis == "y":
            entries["small"] = total
            total += 1
        one.append((entries, total))
        entries, total = {}, 0
        for family, tiles in (("wide", WIDE), ("narrow", NARROW)):
            for kind in range(4):
                if FIRST[kind][0] != axis:
                    entries[family, kind] = total
                    total += tiles[kind]
        if axis == "z":
            entries["small"] = total
            total += 1
        two.append((entries, total))
    return one, two


ROUND_ONE, ROUND_TWO = layouts()


def swap(value, pairs):
    return lax.ppermute(value, AXES, pairs)


def from_behind(value, axis, steps):
    count = lax.axis_size(axis)
    leading, last = (max(0, -steps), min(count, count - steps))
    return lax.ppermute(value, axis, [(source, source + steps) for source in range(leading, last)])


def norm_scale(values):
    return lax.rsqrt(jnp.mean(values * values, axis=1, keepdims=True) + EPS)


def norm_backward(out_grad_rows, values, scale_rows, gain):
    scaled = out_grad_rows * gain
    inner = jnp.mean(scaled * values, axis=1, keepdims=True)
    return scale_rows * (scaled - values * scale_rows * scale_rows * inner)


def like(shape, dtype):
    return jax.ShapeDtypeStruct(shape, dtype)


def call(body, *, scalars, operands, outs, scratch=()):
    whole = pl.BlockSpec(memory_space=pltpu.VMEM)
    return pl.pallas_call(
        body,
        out_shape=tuple(outs),
        in_specs=[pl.BlockSpec(memory_space=pltpu.SMEM)] + [whole] * len(operands),
        out_specs=tuple(whole for _ in outs),
        scratch_shapes=list(scratch),
        compiler_params=pltpu.CompilerParams(vmem_limit_bytes=16 * 2**20),
        cost_estimate=pl.CostEstimate(flops=0, bytes_accessed=0, transcendentals=0),
    )(scalars, *operands)


def dot(left, right):
    return jnp.dot(left, right, preferred_element_type=F32)


def dot_rows(left, right):
    return lax.dot_general(left, right, (((1,), (1,)), ((), ())), preferred_element_type=F32)


def row_numbers(shape, first=0):
    return lax.broadcasted_iota(jnp.int32, shape, 0) + first


def valid_rows(offset, lag, shape):
    row = row_numbers(shape)
    return jnp.where((offset <= row) & (offset > row - lag), 0.0, 1.0)


def linked_rows(offset, shape, first, count):
    return jnp.where((row_numbers(shape, first) < offset) & (offset < count), 0.0, 1.0)


def tail_kernel(scalars, tokens, gain, weight, tail):
    rows = tokens.shape[0]
    values = tokens[rows - 16 :].astype(F32)
    normed = (values * norm_scale(values) * gain[...]).astype(BF16)
    gated = (dot(normed, weight[0]) * dot(normed, weight[2])).astype(BF16).astype(F32)
    tail[...] = (gated * linked_rows(scalars[4], gated.shape, rows - 16, rows)).astype(BF16)


def project_kernel(scalars, tokens, gain, weight, normed, parts, gated):
    values = tokens[...].astype(F32)
    normed[...] = (values * norm_scale(values) * gain[...]).astype(BF16)
    for k in range(3):
        parts[k] = dot(normed[...], weight[k])
    gated[...] = (parts[0] * parts[2]).astype(BF16)


def behind(gated, incoming, lag):
    moved = pltpu.roll(gated, lag, 0)
    row = row_numbers(gated.shape)
    for at in range(lag):
        moved = jnp.where(row == at, incoming[16 - lag + at : 17 - lag + at], moved)
    return moved


def mix_kernel(scalars, gated, incoming, parts, taps, weight, normed, conv, ymix, shared, branch):
    values = gated[...].astype(F32)
    before = incoming[...].astype(F32)
    total = taps[0:1] * values
    for lag in (1, 2):
        total = total + taps[lag : lag + 1] * behind(values, before, lag) * valid_rows(
            scalars[4], lag, values.shape
        )
    conv[...] = total
    ymix[...] = (parts[1] * total).astype(BF16)
    shared[:, : normed.shape[1]] = normed[...]
    shared[:, normed.shape[1] :] = away_half(ymix[...], scalars[3])
    branch[...] = dot(ymix[...], weight[...]).astype(BF16)


def away_half(value, core):
    half = value.shape[-1] // 2
    return jnp.where(core == 0, value[..., half:], value[..., :half])


def second_norm(part, other, resid, gain, cot):
    back = part.astype(F32) + other.astype(F32)
    scale = norm_scale(resid)
    return back, scale, cot.astype(F32) + norm_backward(back, resid, scale, gain)


def edge_kernel(scalars, part, other, resid, gain, cot, weight, parts, taps, edge):
    top = slice(0, 16)
    _, _, grad = second_norm(part[top], other[top], resid[top], gain[...], cot[top])
    conv_back = dot_rows(grad.astype(BF16), weight[...]) * parts[1, top]
    one = conv_back * valid_rows(scalars[4], 1, conv_back.shape) * taps[1:2]
    two = conv_back * valid_rows(scalars[4], 2, conv_back.shape) * taps[2:3]
    row = row_numbers((8, conv_back.shape[1]))
    edge[...] = jnp.where(row == 6, two[0:1], 0.0) + jnp.where(row == 7, one[0:1] + two[1:2], 0.0)


def middle_kernel(
    scalars, part, other, resid, gain, cot, weight, parts, taps, conv, gated, incoming, grad, low, gain_grad, c_back, gated_back, tap_grads
):
    back, scale, resid_grad = second_norm(part[...], other[...], resid[...], gain[...], cot[...])
    gain_grad[...] = jnp.sum(back * resid[...] * scale, axis=0, keepdims=True)
    grad[...] = resid_grad
    low[...] = resid_grad.astype(BF16)
    ymix_back = dot_rows(low[...], weight[...])
    c_back[...] = (ymix_back * conv[...]).astype(BF16)
    conv_back = ymix_back * parts[1]
    values, before = gated[...].astype(F32), incoming[...].astype(F32)
    rows = values.shape[0]
    tap_grads[0:1] = jnp.sum(conv_back * values, axis=0, keepdims=True)
    total = conv_back * taps[0:1]
    row = row_numbers(values.shape)
    for lag in (1, 2):
        term = conv_back * valid_rows(scalars[4], lag, values.shape)
        tap_grads[lag : lag + 1] = jnp.sum(term * behind(values, before, lag), axis=0, keepdims=True)
        moved = pltpu.roll(term * taps[lag : lag + 1], rows - lag, 0)
        total = total + jnp.where(row < rows - lag, moved, 0.0)
    gated_back[...] = total


def last_kernel(
    scalars,
    gated_back,
    returned,
    parts,
    c_back,
    weight,
    tokens,
    gain_two_grad,
    tap_grads,
    resid_low,
    down_part,
    backs,
    shared,
    sums,
    small,
):
    rows = gated_back.shape[0]
    links = linked_rows(scalars[4], returned.shape, rows - 8, rows)
    end = gated_back[rows - 8 :] + returned[...] * links
    total = jnp.concatenate([gated_back[: rows - 8], end], 0)
    backs[0] = (total * parts[2]).astype(BF16)
    backs[1] = c_back[...]
    backs[2] = (total * parts[0]).astype(BF16)
    for k in range(3):
        shared[4 + k] = away_half(backs[k], scalars[3])
    for at in range(4):
        shared[at] = resid_low[:, at * 256 : at * 256 + 256]
    grad = dot_rows(backs[0], weight[0]) + dot_rows(backs[1], weight[1]) + dot_rows(backs[2], weight[2])
    sums[0] = grad.astype(BF16)
    sums[1] = down_part[...]
    values = tokens[...].astype(F32)
    gain_grad = jnp.sum(grad * values * norm_scale(values), axis=0, keepdims=True)
    for at in range(8):
        lanes = slice(at * 128, at * 128 + 128)
        small[at : at + 1] = gain_grad[:, lanes]
        small[8 + at : 9 + at] = gain_two_grad[:, lanes]
    for lag in range(3):
        for at in range(4):
            row = 16 + 4 * lag + at
            small[row : row + 1] = tap_grads[lag : lag + 1, at * 128 : at * 128 + 128]
    small[28:32] = jnp.zeros((4, 128), F32)


def fill_transposed(left, own, other):
    for at in range(0, own.shape[1], 256):
        left[at : at + 256, :256] = own[:, at : at + 256].T
        left[at : at + 256, 256:] = other[:, at : at + 256].T


def chunk_rows(left, axis, chunk):
    if axis == "y":
        return left[pl.ds(pl.multiple_of(chunk * 256, 256), 256)]
    return jnp.concatenate(
        [left[pl.ds(pl.multiple_of(at * 256 + chunk * 64, 64), 64)] for at in range(4)], 0
    )


def store_blocks(value, target, base, tiles, tile):
    value = value.astype(BF16)
    for chunk in range(4):
        for column in range(value.shape[1] // 128):
            target[base + chunk * tiles + tile + column] = value[
                chunk * 64 : chunk * 64 + 64, column * 128 : column * 128 + 128
            ]


def position(scalars, axis):
    return scalars[0 if axis == "y" else 1]


def wide_kernel(scalars, two, two_other, cot, cot_other, *refs):
    own, other, sends, keeps = refs[:3], refs[3:6], refs[6:10], refs[10:14]
    left_two, left_cot = refs[14:]
    fill_transposed(left_cot, cot, cot_other)
    fill_transposed(left_two, two, two_other)
    core = scalars[3]
    runs = [(k, k, at, min(256, CUT - at), at // 128) for k in range(3) for at in range(0, CUT, 256)]
    runs += [(3, k, CUT, WIDE_COLUMNS - CUT, 2 * k) for k in range(3)]
    for kind, (axis, pairing) in enumerate(FIRST):
        at = position(scalars, axis)
        first, second = peer(at, pairing), peer(at, 1 - pairing)
        chunks = (at, second, first, peer(first, 1 - pairing))
        for slot, chunk in enumerate(chunks):
            target = keeps[kind] if slot < 2 else sends[kind]
            rows = {}
            for run_kind, matrix, column, width, tile in runs:
                if run_kind != kind:
                    continue
                if (matrix == 0) not in rows:
                    rows[matrix == 0] = chunk_rows(left_cot if matrix == 0 else left_two, axis, chunk)
                left = rows[matrix == 0]
                mine = pl.ds(pl.multiple_of(core * WIDE_COLUMNS + column, 128), width)
                value = dot(left[:, :256], own[matrix][:, mine])
                value = value + dot(left[:, 256:], other[matrix][:, column : column + width])
                store_blocks(value, target, (slot % 2) * 4 * WIDE[kind], WIDE[kind], tile)


def split_small(value, target, at):
    high = value.astype(BF16)
    target[at, :32] = high
    target[at, 32:] = (value - high.astype(F32)).astype(BF16)


def join_small(source, at):
    return source[at, :32].astype(F32) + source[at, 32:].astype(F32)


def rounded_small(value):
    high = value.astype(BF16)
    return high.astype(F32) + (value - high.astype(F32)).astype(BF16).astype(F32)


def sum_small(value, gots, layout, axis):
    near, far, cross = (
        join_small(gots[SETS.index((axis, p))], layout[SETS.index((axis, p))][0]["small"]) for p in range(3)
    )
    return (rounded_small(value) + cross) + (near + far)


def take(refs, *counts):
    out, at = [], 0
    for count in counts:
        out.append(refs[at : at + count])
        at += count
    return out


def first_kernel(scalars, *refs):
    gots, keeps, operands, (small,), sends, wide_keeps, narrow_keeps, lefts = take(refs, 4, 4, 6, 1, 6, 4, 4, 2)
    one, one_other, low, late_other, backs, ymix = operands
    left_one, left_low = lefts
    width = one.shape[1]
    for at in range(0, width, 256):
        left_one[at : at + 256, :256] = one[:, at : at + 256].T
        left_one[at : at + 256, 256:] = one_other[:, at : at + 256].T
        left_low[at : at + 256, :256] = low[:, at : at + 256].T
        left_low[at : at + 256, 256:] = late_other[at // 256].T
    mine = pl.ds(pl.multiple_of(scalars[3] * 256, 256), 256)
    for kind in range(4):
        axis = FIRST[kind][0]
        at = position(scalars, axis)
        left, own, other = (
            (left_one, backs[kind, :, mine], late_other[4 + kind])
            if kind < 3
            else (left_low, ymix[:, mine], one_other[:, width:])
        )
        for pairing in (0, 1, 2, None):
            rows = chunk_rows(left, axis, at if pairing is None else peer(at, pairing))
            value = dot(rows[:, :256], own) + dot(rows[:, 256:], other)
            if pairing is None:
                store_blocks(value, narrow_keeps[kind], 0, 2, 0)
            else:
                place = SETS.index((axis, pairing))
                store_blocks(value, sends[place], ROUND_ONE[place][0]["narrow", kind], 2, 0)
    for kind in range(4):
        half = 4 * WIDE[kind]
        place = SETS.index(SECOND[kind])
        base = ROUND_ONE[place][0]["wide", kind]
        wide_keeps[kind][...] = (keeps[kind][:half].astype(F32) + gots[kind][:half].astype(F32)).astype(BF16)
        sends[place][base : base + half] = (
            keeps[kind][half:].astype(F32) + gots[kind][half:].astype(F32)
        ).astype(BF16)
    for pairing in range(3):
        place = SETS.index(("y", pairing))
        split_small(small[...], sends[place], ROUND_ONE[place][0]["small"])


def second_kernel(scalars, *refs):
    gots, wide_in, narrow_in, (small,), sends, wide_keeps, narrow_keeps, (new_small,) = take(refs, 6, 4, 4, 1, 6, 4, 4, 1)
    for family, tiles, keeps, new_keeps in (
        ("narrow", NARROW, narrow_in, narrow_keeps),
        ("wide", WIDE, wide_in, wide_keeps),
    ):
        for kind in range(4):
            axis, count = FIRST[kind][0], tiles[kind]
            came = [SECOND[kind]] if family == "wide" else [(axis, p) for p in range(3)]
            came = [SETS.index(entry) for entry in came]

            def total(chunk):
                value = keeps[kind][pl.ds(chunk * count, count)].astype(F32)
                for place in came:
                    base = ROUND_ONE[place][0][family, kind]
                    value = value + gots[place][pl.ds(base + chunk * count, count)].astype(F32)
                return value.astype(BF16)

            at = position(scalars, OTHER_AXIS[axis])
            new_keeps[kind][...] = total(at)
            for pairing in range(3):
                place = SETS.index((OTHER_AXIS[axis], pairing))
                base = ROUND_TWO[place][0][family, kind]
                sends[place][base : base + count] = total(peer(at, pairing))
    value = sum_small(small[...], gots, ROUND_ONE, "y")
    new_small[...] = value
    for pairing in range(3):
        place = SETS.index(("z", pairing))
        split_small(value, sends[place], ROUND_TWO[place][0]["small"])


def third_kernel(scalars, *refs):
    gots, wide_in, narrow_in, (small,), (send, keep, gain_sum) = take(refs, 6, 4, 4, 1, 3)
    here = scalars[2]
    tile = 0
    for family, tiles, keeps in (("wide", WIDE, wide_in), ("narrow", NARROW, narrow_in)):
        for kind in range(4):
            count = tiles[kind]
            value = keeps[kind][...].astype(F32)
            for pairing in range(3):
                place = SETS.index((OTHER_AXIS[FIRST[kind][0]], pairing))
                base = ROUND_TWO[place][0][family, kind]
                value = value + gots[place][base : base + count].astype(F32)
            zero, one = value[:, :32], value[:, 32:]
            keep[tile : tile + count] = jnp.where(here == 0, zero, one)
            send[tile : tile + count] = jnp.where(here == 0, one, zero).astype(BF16)
            tile += count
    value = sum_small(small[...], gots, ROUND_TWO, "z")
    high = value.astype(BF16)
    low = (value - high.astype(F32)).astype(BF16)
    send[TILES] = high
    send[TILES + 1] = low
    gain_sum[...] = high[:8].astype(F32) + low[:8].astype(F32)
    keep[TILES] = high.astype(F32)
    keep[TILES + 1] = low.astype(F32)


def cores_kernel(scalars, keep, across, skew, got, mine, away):
    core = scalars[3]
    total = keep[:TILES] + got[:TILES].astype(F32)
    zero, one = total[:, :16], total[:, 16:]
    mine[:TILES] = jnp.where(core == 0, zero, one)
    away[:TILES] = jnp.where(core == 0, one, zero)
    here = keep[TILES] + keep[TILES + 1]
    there = got[TILES].astype(F32) + got[TILES + 1].astype(F32)
    both = here + there
    gain = (here[:8] + across[...]) + (there[:8] + skew[...])
    for target in (mine, away):
        target[TILES, :8] = gain
        target[TILES, 8:] = both[8:16]
        target[TILES + 1] = both[16:]


def outputs_kernel(scalars, mine, got, down, gate, up, inner, out, gain_one, gain_two, taps):
    core = scalars[3]

    def place(target, tile, column, columns):
        zero, one = jnp.where(core == 0, mine[tile], got[tile]), jnp.where(core == 0, got[tile], mine[tile])
        target[:, column : column + 128] = zero
        target[:, columns + column : columns + column + 128] = one

    for matrix, target in enumerate((down, gate, up)):
        for column in range(0, WIDE_COLUMNS, 128):
            tile = 7 * matrix + column // 128 if column < CUT else 21 + 2 * matrix + (column - CUT) // 128
            place(target, tile, column, WIDE_COLUMNS)
    for kind in range(4):
        for column in range(2):
            place(inner.at[kind] if kind < 3 else out, 27 + 2 * kind + column, column * 128, 256)
    gains = mine[TILES] + got[TILES]
    rest = mine[TILES + 1] + got[TILES + 1]
    for at in range(8):
        lanes = slice(at * 128, at * 128 + 128)
        gain_one[:, lanes] = gains[at : at + 1]
        gain_two[:, lanes] = gains[8 + at : 9 + at]
    for lag in range(3):
        for at in range(4):
            row = 4 * lag + at
            taps[lag : lag + 1, at * 128 : at * 128 + 128] = rest[row : row + 1]


def swap_round(sends, sets):
    return [swap(value, PAIRS[entry]) for value, entry in zip(sends, sets)]


def blocks(counts):
    return [like((count, *BLOCK), BF16) for count in counts]


def on_device(
    tokens,
    starts,
    gain_one,
    in_weight,
    conv_weight,
    out_weight,
    gain_two,
    gate_weight,
    up_weight,
    down_weight,
    cotangent,
):
    at = lax.axis_index("seq")
    core = at % 2
    scalars = jnp.stack([at // 16, (at // 4) % 4, (at // 2) % 2, core, starts[0]]).astype(jnp.int32)
    run = functools.partial(call, scalars=scalars)
    rows, width = tokens.shape
    channels = conv_weight.shape[1]
    in_parts = in_weight.transpose(1, 0, 2)
    gain_one_row, gain_two_row = gain_one.reshape(1, -1), gain_two.reshape(1, -1)

    def share(value):
        return swap(value, CORES)

    tail = run(tail_kernel, operands=[tokens, gain_one_row, in_parts], outs=[like((16, channels), BF16)])[0]
    incoming = from_behind(tail, "seq", 1)
    normed_one, parts, gated = run(
        project_kernel,
        operands=[tokens, gain_one_row, in_parts],
        outs=[like((rows, width), BF16), like((3, rows, channels), F32), like((rows, channels), BF16)],
    )
    conv, ymix, shared, branch = run(
        mix_kernel,
        operands=[gated, incoming, parts, conv_weight, out_weight, normed_one],
        outs=[
            like((rows, channels), F32),
            like((rows, channels), BF16),
            like((rows, width + channels // 2), BF16),
            like((rows, width), BF16),
        ],
    )
    branch_other = swap(branch, ACROSS)
    hidden_grad = jnp.einsum("td,fd->tf", cotangent, down_weight, preferred_element_type=F32)
    cotangent_other = share(cotangent)
    shared_other = share(shared)
    branch_other, cotangent_other, shared_other, hidden_grad = lax.optimization_barrier(
        (branch_other, cotangent_other, shared_other, hidden_grad)
    )
    resid = tokens.astype(F32) + (branch.astype(F32) + branch_other.astype(F32))
    normed_two = (resid * norm_scale(resid) * gain_two).astype(BF16)
    gate_act = jnp.dot(normed_two, gate_weight, preferred_element_type=F32)
    up_act = jnp.dot(normed_two, up_weight, preferred_element_type=F32)
    sigmoid_gate = jax.nn.sigmoid(gate_act)
    swish = gate_act * sigmoid_gate
    hidden = (swish * up_act).astype(BF16)
    swish_slope = sigmoid_gate * (1.0 + gate_act * (1.0 - sigmoid_gate))
    gate_back = (hidden_grad * up_act * swish_slope).astype(BF16)
    up_back = (hidden_grad * swish).astype(BF16)
    norm_two_part = jnp.einsum("tf,df->td", gate_back, gate_weight, preferred_element_type=F32)
    norm_two_part = norm_two_part + jnp.einsum(
        "tf,df->td", up_back, up_weight, preferred_element_type=F32
    )
    norm_two_part = norm_two_part.astype(BF16)
    norm_two_other = swap(norm_two_part, ACROSS)

    results = run(
        wide_kernel,
        operands=[normed_two, share(normed_two), cotangent, cotangent_other, hidden, gate_back, up_back]
        + [share(away_half(value, core)) for value in (hidden, gate_back, up_back)],
        outs=blocks([8 * count for count in WIDE] * 2),
        scratch=[pltpu.VMEM((width, 2 * rows), BF16)] * 2,
    )
    sends, keeps = list(results[:4]), list(results[4:])
    down_part = jnp.dot(hidden, down_weight, preferred_element_type=F32).astype(BF16)
    norm_two_other, keeps[3], down_part = lax.optimization_barrier((norm_two_other, keeps[3], down_part))
    gots = swap_round(sends, FIRST)

    edge_operands = [norm_two_part, norm_two_other, resid, gain_two_row, cotangent, out_weight, parts, conv_weight]
    edge = run(edge_kernel, operands=edge_operands, outs=[like((8, channels), F32)])[0]
    returned = from_behind(edge, "seq", -1)
    resid_grad, resid_low, gain_two_grad, c_back, gated_back, tap_grads = run(
        middle_kernel,
        operands=edge_operands + [conv, gated, incoming],
        outs=[
            like((rows, width), F32),
            like((rows, width), BF16),
            like((1, width), F32),
            like((rows, channels), BF16),
            like((rows, channels), F32),
            like((3, channels), F32),
        ],
    )
    backs, shared, sums, small = run(
        last_kernel,
        operands=[gated_back, returned, parts, c_back, in_parts, tokens, gain_two_grad, tap_grads]
        + [resid_low, down_part],
        outs=[
            like((3, rows, channels), BF16),
            like((7, rows, 256), BF16),
            like((2, rows, width), BF16),
            like((32, 128), F32),
        ],
    )
    results = run(
        first_kernel,
        operands=gots
        + keeps
        + [normed_one, shared_other, resid_low, share(shared), backs, ymix]
        + [small],
        outs=blocks([total for _, total in ROUND_ONE])
        + blocks([4 * count for count in WIDE])
        + blocks([4 * count for count in NARROW]),
        scratch=[pltpu.VMEM((width, 2 * rows), BF16)] * 2,
    )
    sends, keeps = list(results[:6]), list(results[6:])
    gots = swap_round(sends, SETS)
    sums_other = swap(sums, ACROSS)
    gots[0], sums_other = lax.optimization_barrier((gots[0], sums_other))
    results = run(
        second_kernel,
        operands=gots + keeps + [small],
        outs=blocks([total for _, total in ROUND_TWO]) + blocks(WIDE) + blocks(NARROW) + [like((32, 128), F32)],
    )
    sends, keeps, small = list(results[:6]), list(results[6:14]), results[14]
    gots = swap_round(sends, SETS)
    beside, kept, gain_sum = run(
        third_kernel,
        operands=gots + keeps + [small],
        outs=[like((TILES + 2, 32, 128), BF16), like((TILES + 2, 32, 128), F32), like((8, 128), F32)],
    )
    gots = [swap(gain_sum, ACROSS), swap(gain_sum, SKEW), swap(beside, BESIDE)]
    mixed = (resid + (sums[1].astype(F32) + sums_other[1].astype(F32))).astype(BF16)
    inputs = tokens.astype(F32)
    norm_one_back = sums[0].astype(F32) + sums_other[0].astype(F32)
    tokens_grad = resid_grad + norm_backward(norm_one_back, inputs, norm_scale(inputs), gain_one)
    gots[0], mixed, tokens_grad = lax.optimization_barrier((gots[0], mixed, tokens_grad))
    mine, away = run(
        cores_kernel,
        operands=[kept] + gots,
        outs=[like((TILES + 2, 16, 128), F32)] * 2,
    )
    down_g, gate_g, up_g, in_g, out_g, gain_one_g, gain_two_g, conv_g = run(
        outputs_kernel,
        operands=[mine, swap(away, CORES)],
        outs=[like((16, 2 * WIDE_COLUMNS), F32)] * 3
        + [like((3, 16, channels), F32), like((16, channels), F32)]
        + [like((1, width), F32)] * 2
        + [like((3, channels), F32)],
    )
    in_g, gain_one_g, gain_two_g = in_g.transpose(1, 0, 2), gain_one_g.reshape(-1), gain_two_g.reshape(-1)
    return (mixed, tokens_grad, gain_one_g, in_g, conv_g, out_g.T, gain_two_g, gate_g, up_g, down_g.T)


def solution(mesh):
    return jax.shard_map(
        on_device,
        mesh=mesh,
        in_specs=(
            P("seq", None),
            P("seq"),
            P(),
            P(None, None, "tensor"),
            P(None, "tensor"),
            P("tensor", None),
            P(),
            P(None, "tensor"),
            P(None, "tensor"),
            P("tensor", None),
            P("seq", None),
        ),
        out_specs=(
            P("seq", None),
            P("seq", None),
            P(),
            P("seq", None, "tensor"),
            P(None, "tensor"),
            P("tensor", "seq"),
            P(),
            P("seq", "tensor"),
            P("seq", "tensor"),
            P("tensor", "seq"),
        ),
        check_vma=False,
    )
```

```python
import functools

import jax
import jax.numpy as jnp
from jax import lax
from jax.experimental import pallas as pl
from jax.experimental.pallas import tpu as pltpu
from jax.sharding import PartitionSpec as P

EPS = 1e-05
AXES = ("seq", "tensor")
BF16 = jnp.bfloat16
F32 = jnp.float32


def device_pairs(move):
    def number(y, z, x, core):
        return ((((y % 4) * 4 + z % 4) * 2 + x % 2) * 2 + core) * 2 + (x % 4) // 2

    return [
        (number(y, z, x, core), number(*move(y, z, x, core)))
        for y in range(4)
        for z in range(4)
        for x in range(4)
        for core in range(2)
    ]


ACROSS = device_pairs(lambda y, z, x, core: (y, z, (x + 2) % 4, core))
BESIDE = device_pairs(lambda y, z, x, core: (y, z, x ^ 1, core))
SKEW = device_pairs(lambda y, z, x, core: (y, z, (x ^ 1) ^ 2, core))
CORES = device_pairs(lambda y, z, x, core: (y, z, x, 1 - core))


def peer(at, pairing):
    return (at ^ 1, 3 - at, at ^ 2)[pairing]


FIRST = [
    device_pairs(
        functools.partial(
            lambda pairing, y, z, x, core: (y, peer(z, pairing), x, core)
            if core
            else (peer(y, pairing), z, x, core),
            pairing,
        )
    )
    for pairing in range(3)
]
SECOND = [
    device_pairs(
        functools.partial(
            lambda pairing, y, z, x, core: (peer(y, pairing), z, x, core)
            if core
            else (y, peer(z, pairing), x, core),
            pairing,
        )
    )
    for pairing in range(3)
]
WIDE_COLUMNS = 1152
WIDE_TILES = 27
WIDE = (14, 13)
NARROW = 8
BLOCK = (64, 128)
LONG = 3 * 10**10
SHORT = 8 * 10**9
TILES = WIDE_TILES + NARROW
WIDE_PIECE = (1, 0, None)
WIDE_BLOCKS = (4 * WIDE[1], 4 * WIDE[0], 0)
ROUND_ONE = tuple(count + 4 * NARROW + 1 for count in WIDE_BLOCKS)


def swap(value, pairs):
    return lax.ppermute(value, AXES, pairs)


def from_behind(value, axis, steps):
    count = lax.axis_size(axis)
    leading, last = (max(0, -steps), min(count, count - steps))
    return lax.ppermute(value, axis, [(source, source + steps) for source in range(leading, last)])


def norm_scale(values):
    return lax.rsqrt(jnp.mean(values * values, axis=1, keepdims=True) + EPS)


def norm_backward(out_grad_rows, values, scale_rows, gain):
    scaled = out_grad_rows * gain
    inner = jnp.mean(scaled * values, axis=1, keepdims=True)
    return scale_rows * (scaled - values * scale_rows * scale_rows * inner)


def like(shape, dtype):
    return jax.ShapeDtypeStruct(shape, dtype)


def call(body, *, scalars, operands, outs, scratch=(), where=pltpu.VMEM, flops=0):
    whole = pl.BlockSpec(memory_space=pltpu.VMEM)
    return pl.pallas_call(
        body,
        out_shape=tuple(outs),
        in_specs=[pl.BlockSpec(memory_space=pltpu.SMEM)] + [pl.BlockSpec(memory_space=where)] * len(operands),
        out_specs=tuple(whole for _ in outs),
        scratch_shapes=list(scratch),
        compiler_params=pltpu.CompilerParams(vmem_limit_bytes=16 * 2**20),
        cost_estimate=pl.CostEstimate(flops=flops, bytes_accessed=0, transcendentals=0),
    )(scalars, *operands)


def dot(left, right):
    return jnp.dot(left, right, preferred_element_type=F32)


def dot_rows(left, right):
    return lax.dot_general(left, right, (((1,), (1,)), ((), ())), preferred_element_type=F32)


def row_numbers(shape, first=0):
    return lax.broadcasted_iota(jnp.int32, shape, 0) + first


def valid_rows(offset, lag, shape):
    row = row_numbers(shape)
    return jnp.where((offset <= row) & (offset > row - lag), 0.0, 1.0)


def linked_rows(offset, shape, first, count):
    return jnp.where((row_numbers(shape, first) < offset) & (offset < count), 0.0, 1.0)


def tail_kernel(scalars, tokens, gain, weight, tail, token_rows, gain_row, b_weight, x_weight, done):
    rows = tokens.shape[0]
    copies = [
        pltpu.make_async_copy(source, target, done.at[at])
        for at, (source, target) in enumerate(
            (
                (tokens.at[pl.ds(rows - 16, 16)], token_rows),
                (gain, gain_row),
                (weight.at[0], b_weight),
                (weight.at[2], x_weight),
            )
        )
    ]
    for copy in copies:
        copy.start()
    for copy in copies:
        copy.wait()
    values = token_rows[...].astype(F32)
    normed = (values * norm_scale(values) * gain_row[...]).astype(BF16)
    gated = (dot(normed, b_weight[...]) * dot(normed, x_weight[...])).astype(BF16).astype(F32)
    tail[...] = (gated * linked_rows(scalars[4], gated.shape, rows - 16, rows)).astype(BF16)


def project_kernel(scalars, tokens, gain, weight, normed, parts, gated):
    values = tokens[...].astype(F32)
    normed[...] = (values * norm_scale(values) * gain[...]).astype(BF16)
    for k in range(3):
        parts[k] = dot(normed[...], weight[k])
    gated[...] = (parts[0] * parts[2]).astype(BF16)


def behind(gated, incoming, lag):
    moved = pltpu.roll(gated, lag, 0)
    row = row_numbers(gated.shape)
    for at in range(lag):
        moved = jnp.where(row == at, incoming[16 - lag + at : 17 - lag + at], moved)
    return moved


def mix_kernel(scalars, gated, incoming, parts, taps, weight, conv, ymix, branch):
    values = gated[...].astype(F32)
    before = incoming[...].astype(F32)
    total = taps[0:1] * values
    for lag in (1, 2):
        total = total + taps[lag : lag + 1] * behind(values, before, lag) * valid_rows(
            scalars[4], lag, values.shape
        )
    conv[...] = total
    ymix[...] = (parts[1] * total).astype(BF16)
    branch[...] = dot(ymix[...], weight[...]).astype(BF16)


def away_half(value, core):
    half = value.shape[-1] // 2
    return jnp.where(core == 0, value[..., half:], value[..., :half])


def hidden_kernel(scalars, cot, weight, out):
    for at in range(0, weight.shape[0], 256):
        out[:, at : at + 256] = dot_rows(cot[...], weight[at : at + 256])


def down_kernel(scalars, hidden, weight, out):
    out[...] = dot(hidden[...], weight[...]).astype(BF16)


def feed_kernel(
    scalars,
    tokens,
    branch,
    other,
    gain,
    gate,
    up,
    hidden_grad,
    normed_one,
    ymix,
    resid,
    normed,
    hidden,
    gate_back,
    up_back,
    part,
    shared,
):
    resid[...] = tokens[...].astype(F32) + (branch[...].astype(F32) + other[...].astype(F32))
    normed[...] = (resid[...] * norm_scale(resid[...]) * gain[...]).astype(BF16)
    values = normed[...]
    for at in range(0, gate.shape[1], 256):
        columns = slice(at, at + 256)
        gate_act, up_act = dot(values, gate[:, columns]), dot(values, up[:, columns])
        back = hidden_grad[:, columns]
        sigmoid_gate = jax.nn.sigmoid(gate_act)
        swish = gate_act * sigmoid_gate
        hidden[:, columns] = (swish * up_act).astype(BF16)
        up_back[:, columns] = (back * swish).astype(BF16)
        slope = sigmoid_gate * (1.0 + gate_act * (1.0 - sigmoid_gate))
        gate_back[:, columns] = (back * up_act * slope).astype(BF16)
    part[...] = (dot_rows(gate_back[...], gate[...]) + dot_rows(up_back[...], up[...])).astype(BF16)
    away = pl.ds(pl.multiple_of((1 - scalars[3]) * WIDE_COLUMNS, 128), WIDE_COLUMNS)
    for k, value in enumerate((hidden, gate_back, up_back)):
        shared[:, k * WIDE_COLUMNS : (k + 1) * WIDE_COLUMNS] = value[:, away]
    width, at = normed.shape[1], 3 * WIDE_COLUMNS
    shared[:, at : at + width] = values
    shared[:, at + width : at + 2 * width] = normed_one[...]
    shared[:, at + 2 * width :] = away_half(ymix[...], scalars[3])


def second_norm(part, other, resid, gain, cot):
    back = part.astype(F32) + other.astype(F32)
    scale = norm_scale(resid)
    return back, scale, cot.astype(F32) + norm_backward(back, resid, scale, gain)


def edge_kernel(scalars, part, other, resid, gain, cot, weight, parts, taps, edge):
    top = slice(0, 16)
    _, _, grad = second_norm(part[top], other[top], resid[top], gain[...], cot[top])
    conv_back = dot_rows(grad.astype(BF16), weight[...]) * parts[1, top]
    one = conv_back * valid_rows(scalars[4], 1, conv_back.shape) * taps[1:2]
    two = conv_back * valid_rows(scalars[4], 2, conv_back.shape) * taps[2:3]
    row = row_numbers((8, conv_back.shape[1]))
    edge[...] = jnp.where(row == 6, two[0:1], 0.0) + jnp.where(row == 7, one[0:1] + two[1:2], 0.0)


def middle_kernel(
    scalars, part, other, resid, gain, cot, weight, parts, taps, conv, gated, incoming, grad, low, gain_grad, c_back, gated_back, tap_grads
):
    back, scale, resid_grad = second_norm(part[...], other[...], resid[...], gain[...], cot[...])
    gain_grad[...] = jnp.sum(back * resid[...] * scale, axis=0, keepdims=True)
    grad[...] = resid_grad
    low[...] = resid_grad.astype(BF16)
    ymix_back = dot_rows(low[...], weight[...])
    c_back[...] = (ymix_back * conv[...]).astype(BF16)
    conv_back = ymix_back * parts[1]
    values, before = gated[...].astype(F32), incoming[...].astype(F32)
    rows = values.shape[0]
    tap_grads[0:1] = jnp.sum(conv_back * values, axis=0, keepdims=True)
    total = conv_back * taps[0:1]
    row = row_numbers(values.shape)
    for lag in (1, 2):
        term = conv_back * valid_rows(scalars[4], lag, values.shape)
        tap_grads[lag : lag + 1] = jnp.sum(term * behind(values, before, lag), axis=0, keepdims=True)
        moved = pltpu.roll(term * taps[lag : lag + 1], rows - lag, 0)
        total = total + jnp.where(row < rows - lag, moved, 0.0)
    gated_back[...] = total


def last_kernel(
    scalars,
    gated_back,
    returned,
    parts,
    c_back,
    weight,
    tokens,
    gain_two_grad,
    tap_grads,
    resid_low,
    backs,
    shared,
    part,
    small,
):
    rows = gated_back.shape[0]
    links = linked_rows(scalars[4], returned.shape, rows - 8, rows)
    end = gated_back[rows - 8 :] + returned[...] * links
    total = jnp.concatenate([gated_back[: rows - 8], end], 0)
    backs[0] = (total * parts[2]).astype(BF16)
    backs[1] = c_back[...]
    backs[2] = (total * parts[0]).astype(BF16)
    for k in range(3):
        shared[4 + k] = away_half(backs[k], scalars[3])
    for at in range(4):
        shared[at] = resid_low[:, at * 256 : at * 256 + 256]
    grad = dot_rows(backs[0], weight[0]) + dot_rows(backs[1], weight[1]) + dot_rows(backs[2], weight[2])
    part[...] = grad.astype(BF16)
    values = tokens[...].astype(F32)
    gain_grad = jnp.sum(grad * values * norm_scale(values), axis=0, keepdims=True)
    for at in range(8):
        lanes = slice(at * 128, at * 128 + 128)
        small[at : at + 1] = gain_grad[:, lanes]
        small[8 + at : 9 + at] = gain_two_grad[:, lanes]
    for lag in range(3):
        for at in range(4):
            row = 16 + 4 * lag + at
            small[row : row + 1] = tap_grads[lag : lag + 1, at * 128 : at * 128 + 128]
    small[28:32] = jnp.zeros((4, 128), F32)


def fill_transposed(left, own, other):
    for at in range(0, own.shape[1], 256):
        left[at : at + 256, :256] = own[:, at : at + 256].T
        left[at : at + 256, 256:] = other[:, at : at + 256].T


def chunk_rows(left, core, chunk):
    wide, slim = jnp.where(core == 0, 256, 64), jnp.where(core == 0, 64, 256)
    return jnp.concatenate(
        [left[pl.ds(pl.multiple_of(chunk * wide + at * slim, 64), 64)] for at in range(4)], 0
    )


def store_blocks(value, target, base, tiles, tile):
    value = value.astype(BF16)
    for chunk in range(4):
        for column in range(value.shape[1] // 128):
            target[base + chunk * tiles + tile + column] = value[
                chunk * 64 : chunk * 64 + 64, column * 128 : column * 128 + 128
            ]


def wide_runs(kind):
    at, end = (0, WIDE[0]) if kind == 0 else (WIDE[0], WIDE_TILES)
    first = at
    while at < end:
        matrix, tile = divmod(at, WIDE_COLUMNS // 128)
        count = min(2, WIDE_COLUMNS // 128 - tile, end - at)
        yield matrix, tile * 128, count * 128, at - first
        at += count


def wide_kernel(scalars, two, cot, cot_other, *refs):
    own, shared, sends, keeps = refs[:3], refs[3], refs[4:6], refs[6:8]
    left_two, left_cot = refs[8:]
    fill_transposed(left_cot, cot, cot_other)
    fill_transposed(left_two, two, shared.at[:, 3 * WIDE_COLUMNS : 3 * WIDE_COLUMNS + two.shape[1]])
    at, core = scalars[0], scalars[3]
    for kind in range(2):
        first, second = peer(at, kind), peer(at, 1 - kind)
        chunks = (at, second, first, peer(first, 1 - kind))
        for slot, chunk in enumerate(chunks):
            target = keeps[kind] if slot < 2 else sends[kind]
            rows = {}
            for matrix, column, width, tile in wide_runs(kind):
                if (matrix == 0) not in rows:
                    rows[matrix == 0] = chunk_rows(left_cot if matrix == 0 else left_two, core, chunk)
                left = rows[matrix == 0]
                mine = pl.ds(pl.multiple_of(core * WIDE_COLUMNS + column, 128), width)
                away = matrix * WIDE_COLUMNS + column
                value = dot(left[:, :256], own[matrix][:, mine])
                value = value + dot(left[:, 256:], shared[:, away : away + width])
                store_blocks(value, target, (slot % 2) * 4 * WIDE[kind], WIDE[kind], tile)


def narrow_kernel(scalars, one, shared, low, late_other, backs, ymix, out, left_one, left_low):
    width = one.shape[1]
    first = 3 * WIDE_COLUMNS + width
    one_other, ymix_other = shared.at[:, first : first + width], shared.at[:, first + width :]
    for at in range(0, width, 256):
        left_one[at : at + 256, :256] = one[:, at : at + 256].T
        left_one[at : at + 256, 256:] = one_other[:, at : at + 256].T
        left_low[at : at + 256, :256] = low[:, at : at + 256].T
        left_low[at : at + 256, 256:] = late_other[at // 256].T
    mine = pl.ds(pl.multiple_of(scalars[3] * 256, 256), 256)
    for slot in range(4):
        chunk = peer(scalars[0], slot) if slot < 3 else scalars[0]
        for kind in range(4):
            left, own, other = (
                (left_one, backs[kind, :, mine], late_other[4 + kind])
                if kind < 3
                else (left_low, ymix[:, mine], ymix_other[...])
            )
            rows = chunk_rows(left, scalars[3], chunk)
            value = dot(rows[:, :256], own) + dot(rows[:, 256:], other)
            store_blocks(value, out.at[slot], 0, NARROW, 2 * kind)


def split_small(value, target, at):
    high = value.astype(BF16)
    target[at, :32] = high
    target[at, 32:] = (value - high.astype(F32)).astype(BF16)


def join_small(source, at):
    return source[at, :32].astype(F32) + source[at, 32:].astype(F32)


def rounded_small(value):
    high = value.astype(BF16)
    return high.astype(F32) + (value - high.astype(F32)).astype(BF16).astype(F32)


def sum_small(value, gots, bases):
    near, far, cross = (join_small(got, base) for got, base in zip(gots, bases))
    return (rounded_small(value) + cross) + (near + far)


def first_kernel(scalars, *refs):
    gots, keeps, (narrow, small), sends, wide_keeps = refs[:2], refs[2:4], refs[4:6], refs[6:9], refs[9:]
    for pairing in range(3):
        base = WIDE_BLOCKS[pairing]
        sends[pairing][base : base + 4 * NARROW] = narrow[pairing]
        split_small(small[...], sends[pairing], base + 4 * NARROW)
    for kind in range(2):
        half = 4 * WIDE[kind]
        for chunk in range(4):
            at = slice(chunk * WIDE[kind], (chunk + 1) * WIDE[kind])
            after = slice(half + chunk * WIDE[kind], half + (chunk + 1) * WIDE[kind])
            wide_keeps[kind][at] = (keeps[kind][at].astype(F32) + gots[kind][at].astype(F32)).astype(BF16)
            sends[1 - kind][at] = (keeps[kind][after].astype(F32) + gots[kind][after].astype(F32)).astype(BF16)


def second_kernel(scalars, *refs):
    gots, wide_in, (narrow, small), sends, (keep, new_small) = refs[:3], refs[3:5], refs[5:7], refs[7:10], refs[10:]

    def fill(chunk, target):
        tile = 0
        for kind in range(2):
            at = pl.ds(chunk * WIDE[kind], WIDE[kind])
            value = wide_in[kind][at].astype(F32) + gots[1 - kind][at].astype(F32)
            target[tile : tile + WIDE[kind]] = value.astype(BF16)
            tile += WIDE[kind]
        value = narrow[3, pl.ds(chunk * NARROW, NARROW)].astype(F32)
        for pairing in range(3):
            value = value + gots[pairing][pl.ds(WIDE_BLOCKS[pairing] + chunk * NARROW, NARROW)].astype(F32)
        target[tile : tile + NARROW] = value.astype(BF16)

    value = sum_small(small[...], gots, [count - 1 for count in ROUND_ONE])
    new_small[...] = value
    for pairing in range(3):
        fill(peer(scalars[1], pairing), sends[pairing])
        split_small(value, sends[pairing], TILES)
    fill(scalars[1], keep)


def third_kernel(scalars, *refs):
    gots, (kept, small), (send, keep, gain_sum) = refs[:3], refs[3:5], refs[5:]
    here = scalars[2]
    for first in range(0, TILES, 7):
        at = slice(first, first + 7)
        value = kept[at].astype(F32)
        for got in gots:
            value = value + got[at].astype(F32)
        zero, one = value[:, :32], value[:, 32:]
        keep[at] = jnp.where(here == 0, zero, one)
        send[at] = jnp.where(here == 0, one, zero).astype(BF16)
    value = sum_small(small[...], gots, [TILES] * 3)
    high = value.astype(BF16)
    low = (value - high.astype(F32)).astype(BF16)
    send[TILES] = high
    send[TILES + 1] = low
    gain_sum[...] = high[:8].astype(F32) + low[:8].astype(F32)
    keep[TILES] = high.astype(F32)
    keep[TILES + 1] = low.astype(F32)


def cores_kernel(scalars, keep, across, skew, got, mine, away):
    core = scalars[3]
    total = keep[:TILES] + got[:TILES].astype(F32)
    zero, one = total[:, :16], total[:, 16:]
    mine[:TILES] = jnp.where(core == 0, zero, one)
    away[:TILES] = jnp.where(core == 0, one, zero)
    here = keep[TILES] + keep[TILES + 1]
    there = got[TILES].astype(F32) + got[TILES + 1].astype(F32)
    both = here + there
    gain = (here[:8] + across[...]) + (there[:8] + skew[...])
    for target in (mine, away):
        target[TILES, :8] = gain
        target[TILES, 8:] = both[8:16]
        target[TILES + 1] = both[16:]


def outputs_kernel(scalars, mine, got, down, gate, up, inner, out, gain_one, gain_two, taps):
    core = scalars[3]

    def place(target, tile, column, columns):
        zero, one = jnp.where(core == 0, mine[tile], got[tile]), jnp.where(core == 0, got[tile], mine[tile])
        target[:, column : column + 128] = zero
        target[:, columns + column : columns + column + 128] = one

    for matrix, target in enumerate((down, gate, up)):
        for tile in range(WIDE_COLUMNS // 128):
            place(target, matrix * (WIDE_COLUMNS // 128) + tile, tile * 128, WIDE_COLUMNS)
    for kind in range(4):
        for column in range(2):
            place(inner.at[kind] if kind < 3 else out, WIDE_TILES + 2 * kind + column, column * 128, 256)
    gains = mine[TILES] + got[TILES]
    rest = mine[TILES + 1] + got[TILES + 1]
    for at in range(8):
        lanes = slice(at * 128, at * 128 + 128)
        gain_one[:, lanes] = gains[at : at + 1]
        gain_two[:, lanes] = gains[8 + at : 9 + at]
    for lag in range(3):
        for at in range(4):
            row = 4 * lag + at
            taps[lag : lag + 1, at * 128 : at * 128 + 128] = rest[row : row + 1]


def swap_round(sends, pairings):
    return [swap(value, pairs) for value, pairs in zip(sends, pairings)]


def blocks(counts):
    return [like((count, *BLOCK), BF16) for count in counts]


def on_device(
    tokens,
    starts,
    gain_one,
    in_weight,
    conv_weight,
    out_weight,
    gain_two,
    gate_weight,
    up_weight,
    down_weight,
    cotangent,
):
    at = lax.axis_index("seq")
    core = at % 2
    y, z = at // 16, (at // 4) % 4
    scalars = jnp.stack(
        [jnp.where(core == 0, y, z), jnp.where(core == 0, z, y), (at // 2) % 2, core, starts[0]]
    ).astype(jnp.int32)
    run = functools.partial(call, scalars=scalars)
    rows, width = tokens.shape
    channels = conv_weight.shape[1]
    in_parts = in_weight.transpose(1, 0, 2)
    gain_one_row, gain_two_row = gain_one.reshape(1, -1), gain_two.reshape(1, -1)

    def share(value):
        return swap(value, CORES)

    tail = run(
        tail_kernel,
        operands=[tokens, gain_one_row, in_parts],
        outs=[like((16, channels), BF16)],
        scratch=[
            pltpu.VMEM((16, width), BF16),
            pltpu.VMEM((1, width), F32),
            pltpu.VMEM((width, channels), BF16),
            pltpu.VMEM((width, channels), BF16),
            pltpu.SemaphoreType.DMA((4,)),
        ],
        where=pltpu.HBM,
    )[0]
    incoming = from_behind(tail, "seq", 1)
    cotangent_other = share(cotangent)
    incoming, cotangent_other = lax.optimization_barrier((incoming, cotangent_other))
    normed_one, parts, gated = run(
        project_kernel,
        operands=[tokens, gain_one_row, in_parts],
        outs=[like((rows, width), BF16), like((3, rows, channels), F32), like((rows, channels), BF16)],
    )
    conv, ymix, branch = run(
        mix_kernel,
        operands=[gated, incoming, parts, conv_weight, out_weight],
        outs=[
            like((rows, channels), F32),
            like((rows, channels), BF16),
            like((rows, width), BF16),
        ],
    )
    branch, cotangent_late = lax.optimization_barrier((branch, cotangent))
    branch_other = swap(branch, ACROSS)
    units = gate_weight.shape[1]
    hidden_grad = run(
        hidden_kernel,
        operands=[cotangent_late, down_weight],
        outs=[like((rows, units), F32)],
        flops=LONG,
    )[0]
    branch_other, hidden_grad = lax.optimization_barrier((branch_other, hidden_grad))
    resid, normed_two, hidden, gate_back, up_back, norm_two_part, late_shared = run(
        feed_kernel,
        operands=[tokens, branch, branch_other, gain_two_row, gate_weight, up_weight, hidden_grad]
        + [normed_one, ymix],
        outs=[like((rows, width), F32), like((rows, width), BF16)]
        + [like((rows, units), BF16)] * 3
        + [like((rows, width), BF16), like((rows, 3 * WIDE_COLUMNS + 2 * width + channels // 2), BF16)],
    )
    norm_two_other = swap(norm_two_part, ACROSS)
    shared_other = share(late_shared)
    results = run(
        wide_kernel,
        operands=[normed_two, cotangent, cotangent_other, hidden, gate_back, up_back, shared_other],
        outs=blocks([8 * count for count in WIDE] * 2),
        scratch=[pltpu.VMEM((width, 2 * rows), BF16)] * 2,
    )
    sends, keeps = list(results[:2]), list(results[2:])
    down_part = run(down_kernel, operands=[hidden, down_weight], outs=[like((rows, width), BF16)])[0]
    norm_two_other, keeps[1], down_part = lax.optimization_barrier((norm_two_other, keeps[1], down_part))
    gots = swap_round(sends, FIRST)
    down_other = swap(down_part, ACROSS)

    edge_operands = [norm_two_part, norm_two_other, resid, gain_two_row, cotangent, out_weight, parts, conv_weight]
    edge = run(edge_kernel, operands=edge_operands, outs=[like((8, channels), F32)])[0]
    returned = from_behind(edge, "seq", -1)
    resid_grad, resid_low, gain_two_grad, c_back, gated_back, tap_grads = run(
        middle_kernel,
        operands=edge_operands + [conv, gated, incoming],
        outs=[
            like((rows, width), F32),
            like((rows, width), BF16),
            like((1, width), F32),
            like((rows, channels), BF16),
            like((rows, channels), F32),
            like((3, channels), F32),
        ],
        flops=SHORT,
    )
    backs, shared, norm_one_part, small = run(
        last_kernel,
        operands=[gated_back, returned, parts, c_back, in_parts, tokens, gain_two_grad, tap_grads]
        + [resid_low],
        outs=[
            like((3, rows, channels), BF16),
            like((7, rows, 256), BF16),
            like((rows, width), BF16),
            like((32, 128), F32),
        ],
    )
    narrow = run(
        narrow_kernel,
        operands=[normed_one, shared_other, resid_low, share(shared), backs, ymix],
        outs=[like((4, 4 * NARROW, *BLOCK), BF16)],
        scratch=[pltpu.VMEM((width, 2 * rows), BF16)] * 2,
    )[0]
    gots[0], gots[1], narrow, down_other = lax.optimization_barrier((gots[0], gots[1], narrow, down_other))
    results = run(
        first_kernel,
        operands=gots + keeps + [narrow, small],
        outs=blocks(ROUND_ONE) + blocks([4 * count for count in WIDE]),
    )
    sends, keeps = list(results[:3]), list(results[3:])
    gots = swap_round(sends, FIRST)
    norm_one_other = swap(norm_one_part, ACROSS)
    gots[0], norm_one_other = lax.optimization_barrier((gots[0], norm_one_other))
    results = run(
        second_kernel,
        operands=gots + keeps + [narrow, small],
        outs=blocks([TILES + 1] * 3 + [TILES]) + [like((32, 128), F32)],
    )
    sends, keep, small = list(results[:3]), results[3], results[4]
    gots = swap_round(sends, SECOND)
    beside, kept, gain_sum = run(
        third_kernel,
        operands=gots + [keep, small],
        outs=[like((TILES + 2, 32, 128), BF16), like((TILES + 2, 32, 128), F32), like((8, 128), F32)],
    )
    gots = [swap(gain_sum, ACROSS), swap(gain_sum, SKEW), swap(beside, BESIDE)]
    mixed = (resid + (down_part.astype(F32) + down_other.astype(F32))).astype(BF16)
    inputs = tokens.astype(F32)
    norm_one_back = norm_one_part.astype(F32) + norm_one_other.astype(F32)
    tokens_grad = resid_grad + norm_backward(norm_one_back, inputs, norm_scale(inputs), gain_one)
    gots[0], mixed, tokens_grad = lax.optimization_barrier((gots[0], mixed, tokens_grad))
    mine, away = run(
        cores_kernel,
        operands=[kept] + gots,
        outs=[like((TILES + 2, 16, 128), F32)] * 2,
    )
    down_g, gate_g, up_g, in_g, out_g, gain_one_g, gain_two_g, conv_g = run(
        outputs_kernel,
        operands=[mine, swap(away, CORES)],
        outs=[like((16, 2 * WIDE_COLUMNS), F32)] * 3
        + [like((3, 16, channels), F32), like((16, channels), F32)]
        + [like((1, width), F32)] * 2
        + [like((3, channels), F32)],
    )
    in_g, gain_one_g, gain_two_g = in_g.transpose(1, 0, 2), gain_one_g.reshape(-1), gain_two_g.reshape(-1)
    return (mixed, tokens_grad, gain_one_g, in_g, conv_g, out_g.T, gain_two_g, gate_g, up_g, down_g.T)


def solution(mesh):
    return jax.shard_map(
        on_device,
        mesh=mesh,
        in_specs=(
            P("seq", None),
            P("seq"),
            P(),
            P(None, None, "tensor"),
            P(None, "tensor"),
            P("tensor", None),
            P(),
            P(None, "tensor"),
            P(None, "tensor"),
            P("tensor", None),
            P("seq", None),
        ),
        out_specs=(
            P("seq", None),
            P("seq", None),
            P(),
            P("seq", None, "tensor"),
            P(None, "tensor"),
            P("tensor", "seq"),
            P(),
            P("seq", "tensor"),
            P("seq", "tensor"),
            P("tensor", "seq"),
        ),
        check_vma=False,
    )
```

```python
import functools

import jax
import jax.numpy as jnp
from jax import lax
from jax.experimental import pallas as pl
from jax.experimental.pallas import tpu as pltpu
from jax.sharding import PartitionSpec as P

EPS = 1e-05
AXES = ("seq", "tensor")
BF16 = jnp.bfloat16
F32 = jnp.float32


def device_pairs(move):
    def number(y, z, x, core):
        return ((((y % 4) * 4 + z % 4) * 2 + x % 2) * 2 + core) * 2 + (x % 4) // 2

    return [
        (number(y, z, x, core), number(*move(y, z, x, core)))
        for y in range(4)
        for z in range(4)
        for x in range(4)
        for core in range(2)
    ]


ACROSS = device_pairs(lambda y, z, x, core: (y, z, (x + 2) % 4, core))
BESIDE = device_pairs(lambda y, z, x, core: (y, z, x ^ 1, core))
NEAREST = device_pairs(lambda y, z, x, core: (y, z, 3 - x, core))
CORES = device_pairs(lambda y, z, x, core: (y, z, x, 1 - core))


def peer(at, pairing):
    return (at ^ 1, 3 - at, at ^ 2)[pairing]


FIRST = [
    device_pairs(
        functools.partial(
            lambda pairing, y, z, x, core: (y, peer(z, pairing), x, core)
            if core
            else (peer(y, pairing), z, x, core),
            pairing,
        )
    )
    for pairing in range(3)
]
SECOND = [
    device_pairs(
        functools.partial(
            lambda pairing, y, z, x, core: (peer(y, pairing), z, x, core)
            if core
            else (y, peer(z, pairing), x, core),
            pairing,
        )
    )
    for pairing in range(3)
]
WIDE_COLUMNS = 1152
WIDE_TILES = 27
WIDE = (14, 13)
NARROW = 8
BLOCK = (64, 128)
LONG = 3 * 10**10
SHORT = 8 * 10**9
TILES = WIDE_TILES + NARROW
WIDE_PIECE = (1, 0, None)
WIDE_BLOCKS = (4 * WIDE[1], 4 * WIDE[0], 0)
ROUND_ONE = tuple(count + 4 * NARROW + 1 for count in WIDE_BLOCKS)


def swap(value, pairs):
    return lax.ppermute(value, AXES, pairs)


def from_behind(value, axis, steps):
    count = lax.axis_size(axis)
    leading, last = (max(0, -steps), min(count, count - steps))
    return lax.ppermute(value, axis, [(source, source + steps) for source in range(leading, last)])


def norm_scale(values):
    return lax.rsqrt(jnp.mean(values * values, axis=1, keepdims=True) + EPS)


def norm_backward(out_grad_rows, values, scale_rows, gain):
    scaled = out_grad_rows * gain
    inner = jnp.mean(scaled * values, axis=1, keepdims=True)
    return scale_rows * (scaled - values * scale_rows * scale_rows * inner)


def like(shape, dtype):
    return jax.ShapeDtypeStruct(shape, dtype)


def call(body, *, scalars, operands, outs, scratch=(), where=pltpu.VMEM, flops=0, room=16):
    whole = pl.BlockSpec(memory_space=pltpu.VMEM)
    return pl.pallas_call(
        body,
        out_shape=tuple(outs),
        in_specs=[pl.BlockSpec(memory_space=pltpu.SMEM)] + [pl.BlockSpec(memory_space=where)] * len(operands),
        out_specs=tuple(whole for _ in outs),
        scratch_shapes=list(scratch),
        compiler_params=pltpu.CompilerParams(vmem_limit_bytes=room * 2**20),
        cost_estimate=pl.CostEstimate(flops=flops, bytes_accessed=0, transcendentals=0),
    )(scalars, *operands)


def dot(left, right):
    return jnp.dot(left, right, preferred_element_type=F32)


def dot_rows(left, right):
    return lax.dot_general(left, right, (((1,), (1,)), ((), ())), preferred_element_type=F32)


def row_numbers(shape, first=0):
    return lax.broadcasted_iota(jnp.int32, shape, 0) + first


def valid_rows(offset, lag, shape):
    row = row_numbers(shape)
    return jnp.where((offset <= row) & (offset > row - lag), 0.0, 1.0)


def linked_rows(offset, shape, first, count):
    return jnp.where((row_numbers(shape, first) < offset) & (offset < count), 0.0, 1.0)


def tail_kernel(scalars, tokens, gain, weight, tail, token_rows, gain_row, b_weight, x_weight, done):
    rows = tokens.shape[0]
    copies = [
        pltpu.make_async_copy(source, target, done.at[at])
        for at, (source, target) in enumerate(
            (
                (tokens.at[pl.ds(rows - 16, 16)], token_rows),
                (gain, gain_row),
                (weight.at[0], b_weight),
                (weight.at[2], x_weight),
            )
        )
    ]
    for copy in copies:
        copy.start()
    for copy in copies:
        copy.wait()
    values = token_rows[...].astype(F32)
    normed = (values * norm_scale(values) * gain_row[...]).astype(BF16)
    gated = (dot(normed, b_weight[...]) * dot(normed, x_weight[...])).astype(BF16).astype(F32)
    tail[...] = (gated * linked_rows(scalars[4], gated.shape, rows - 16, rows)).astype(BF16)


def project_kernel(scalars, tokens, gain, weight, normed, parts, gated, token_rows, gain_row, weights, done):
    pieces = [(tokens, token_rows), (gain, gain_row)] + [(weight.at[k], weights.at[k]) for k in range(3)]
    copies = [
        pltpu.make_async_copy(source, target, done.at[at]) for at, (source, target) in enumerate(pieces)
    ]
    for copy in copies:
        copy.start()
    copies[0].wait()
    copies[1].wait()
    values = token_rows[...].astype(F32)
    normed[...] = (values * norm_scale(values) * gain_row[...]).astype(BF16)
    for k in range(3):
        copies[2 + k].wait()
        parts[k] = dot(normed[...], weights[k])
    gated[...] = (parts[0] * parts[2]).astype(BF16)


def behind(gated, incoming, lag):
    moved = pltpu.roll(gated, lag, 0)
    row = row_numbers(gated.shape)
    for at in range(lag):
        moved = jnp.where(row == at, incoming[16 - lag + at : 17 - lag + at], moved)
    return moved


def mix_kernel(scalars, gated, incoming, parts, taps, conv, ymix):
    values = gated[...].astype(F32)
    before = incoming[...].astype(F32)
    total = taps[0:1] * values
    for lag in (1, 2):
        total = total + taps[lag : lag + 1] * behind(values, before, lag) * valid_rows(
            scalars[4], lag, values.shape
        )
    conv[...] = total
    ymix[...] = (parts[1] * total).astype(BF16)


def away_half(value, core):
    half = value.shape[-1] // 2
    return jnp.where(core == 0, value[..., half:], value[..., :half])


def hidden_kernel(scalars, cot, weight, out):
    for at in range(0, weight.shape[0], 256):
        out[:, at : at + 256] = dot_rows(cot[...], weight[at : at + 256])


def down_kernel(scalars, hidden, weight, out):
    out[...] = dot(hidden[...], weight[...]).astype(BF16)


def whole_kernel(scalars, weight, got, got_other, whole):
    core, side = scalars[3], scalars[5]
    half = got.shape[0]
    low, high = jnp.where(core == 0, got[...], got_other[...]), jnp.where(core == 0, got_other[...], got[...])
    whole[:half] = jnp.where(side == 0, weight[:half], low)
    whole[half : 2 * half] = jnp.where(side == 0, weight[half:], high)
    whole[2 * half : 3 * half] = jnp.where(side == 0, low, weight[:half])
    whole[3 * half :] = jnp.where(side == 0, high, weight[half:])


def feed_kernel(
    scalars,
    tokens,
    ymix,
    ymix_other,
    whole,
    gain,
    gate,
    up,
    hidden_grad,
    normed_one,
    resid,
    normed,
    hidden,
    gate_back,
    up_back,
    shared,
    shared_early,
):
    side, channels = scalars[5], ymix.shape[1]
    first, second = (
        jnp.where(side == 0, ymix[...], ymix_other[...]),
        jnp.where(side == 0, ymix_other[...], ymix[...]),
    )
    branch = dot(first, whole[:channels]) + dot(second, whole[channels:])
    resid[...] = tokens[...].astype(F32) + branch
    normed[...] = (resid[...] * norm_scale(resid[...]) * gain[...]).astype(BF16)
    values = normed[...]
    for at in range(0, gate.shape[1], 256):
        columns = slice(at, at + 256)
        gate_act, up_act = dot(values, gate[:, columns]), dot(values, up[:, columns])
        back = hidden_grad[:, columns]
        sigmoid_gate = jax.nn.sigmoid(gate_act)
        swish = gate_act * sigmoid_gate
        hidden[:, columns] = (swish * up_act).astype(BF16)
        up_back[:, columns] = (back * swish).astype(BF16)
        slope = sigmoid_gate * (1.0 + gate_act * (1.0 - sigmoid_gate))
        gate_back[:, columns] = (back * up_act * slope).astype(BF16)
    away = pl.ds(pl.multiple_of((1 - scalars[3]) * WIDE_COLUMNS, 128), WIDE_COLUMNS)
    for k, value in enumerate((hidden, gate_back, up_back)):
        shared[:, k * WIDE_COLUMNS : (k + 1) * WIDE_COLUMNS] = value[:, away]
    shared[:, 3 * WIDE_COLUMNS :] = values
    shared_early[:, : normed.shape[1]] = normed_one[...]
    shared_early[:, normed.shape[1] :] = away_half(ymix[...], scalars[3])


def part_kernel(scalars, gate_back, up_back, gate, up, part):
    part[...] = (dot_rows(gate_back[...], gate[...]) + dot_rows(up_back[...], up[...])).astype(BF16)


def second_norm(part, other, resid, gain, cot):
    back = part.astype(F32) + other.astype(F32)
    scale = norm_scale(resid)
    return back, scale, cot.astype(F32) + norm_backward(back, resid, scale, gain)


def edge_kernel(scalars, part, other, resid, gain, cot, weight, parts, taps, edge):
    top = slice(0, 16)
    _, _, grad = second_norm(part[top], other[top], resid[top], gain[...], cot[top])
    conv_back = dot_rows(grad.astype(BF16), weight[...]) * parts[1, top]
    one = conv_back * valid_rows(scalars[4], 1, conv_back.shape) * taps[1:2]
    two = conv_back * valid_rows(scalars[4], 2, conv_back.shape) * taps[2:3]
    row = row_numbers((8, conv_back.shape[1]))
    edge[...] = jnp.where(row == 6, two[0:1], 0.0) + jnp.where(row == 7, one[0:1] + two[1:2], 0.0)


def middle_kernel(
    scalars, part, other, resid, gain, cot, weight, parts, taps, conv, gated, incoming, grad, low, gain_grad, c_back, gated_back, tap_grads
):
    back, scale, resid_grad = second_norm(part[...], other[...], resid[...], gain[...], cot[...])
    gain_grad[...] = jnp.sum(back * resid[...] * scale, axis=0, keepdims=True)
    grad[...] = resid_grad
    low[...] = resid_grad.astype(BF16)
    ymix_back = dot_rows(low[...], weight[...])
    c_back[...] = (ymix_back * conv[...]).astype(BF16)
    conv_back = ymix_back * parts[1]
    values, before = gated[...].astype(F32), incoming[...].astype(F32)
    rows = values.shape[0]
    tap_grads[0:1] = jnp.sum(conv_back * values, axis=0, keepdims=True)
    total = conv_back * taps[0:1]
    row = row_numbers(values.shape)
    for lag in (1, 2):
        term = conv_back * valid_rows(scalars[4], lag, values.shape)
        tap_grads[lag : lag + 1] = jnp.sum(term * behind(values, before, lag), axis=0, keepdims=True)
        moved = pltpu.roll(term * taps[lag : lag + 1], rows - lag, 0)
        total = total + jnp.where(row < rows - lag, moved, 0.0)
    gated_back[...] = total


def last_kernel(
    scalars,
    gated_back,
    returned,
    parts,
    c_back,
    weight,
    tokens,
    gain_two_grad,
    tap_grads,
    resid_low,
    backs,
    shared,
    part,
    gain_part,
    small,
):
    rows = gated_back.shape[0]
    links = linked_rows(scalars[4], returned.shape, rows - 8, rows)
    end = gated_back[rows - 8 :] + returned[...] * links
    total = jnp.concatenate([gated_back[: rows - 8], end], 0)
    backs[0] = (total * parts[2]).astype(BF16)
    backs[1] = c_back[...]
    backs[2] = (total * parts[0]).astype(BF16)
    for k in range(3):
        shared[4 + k] = away_half(backs[k], scalars[3])
    for at in range(4):
        shared[at] = resid_low[:, at * 256 : at * 256 + 256]
    grad = dot_rows(backs[0], weight[0]) + dot_rows(backs[1], weight[1]) + dot_rows(backs[2], weight[2])
    part[...] = grad.astype(BF16)
    values = tokens[...].astype(F32)
    gain_grad = jnp.sum(grad * values * norm_scale(values), axis=0, keepdims=True)
    for at in range(8):
        lanes = slice(at * 128, at * 128 + 128)
        gain_part[at : at + 1] = gain_grad[:, lanes]
        small[8 + at : 9 + at] = gain_two_grad[:, lanes]
    for lag in range(3):
        for at in range(4):
            row = 16 + 4 * lag + at
            small[row : row + 1] = tap_grads[lag : lag + 1, at * 128 : at * 128 + 128]
    small[:8] = jnp.zeros((8, 128), F32)
    small[28:32] = jnp.zeros((4, 128), F32)


def fill_transposed(left, own, other):
    for at in range(0, own.shape[1], 256):
        left[at : at + 256, :256] = own[:, at : at + 256].T
        left[at : at + 256, 256:] = other[:, at : at + 256].T


def chunk_rows(left, core, chunk):
    wide, slim = jnp.where(core == 0, 256, 64), jnp.where(core == 0, 64, 256)
    return jnp.concatenate(
        [left[pl.ds(pl.multiple_of(chunk * wide + at * slim, 64), 64)] for at in range(4)], 0
    )


def store_blocks(value, target, base, tiles, tile):
    value = value.astype(BF16)
    for chunk in range(4):
        for column in range(value.shape[1] // 128):
            target[base + chunk * tiles + tile + column] = value[
                chunk * 64 : chunk * 64 + 64, column * 128 : column * 128 + 128
            ]


def wide_runs(kind):
    at, end = (0, WIDE[0]) if kind == 0 else (WIDE[0], WIDE_TILES)
    first = at
    while at < end:
        matrix, tile = divmod(at, WIDE_COLUMNS // 128)
        count = min(2, WIDE_COLUMNS // 128 - tile, end - at)
        yield matrix, tile * 128, count * 128, at - first
        at += count


def wide_kernel(scalars, two, cot, cot_other, *refs):
    own, shared, sends, keeps = refs[:3], refs[3], refs[4:6], refs[6:8]
    left_two, left_cot = refs[8:]
    fill_transposed(left_cot, cot, cot_other)
    fill_transposed(left_two, two, shared.at[:, 3 * WIDE_COLUMNS :])
    at, core = scalars[0], scalars[3]
    for kind in range(2):
        first, second = peer(at, kind), peer(at, 1 - kind)
        chunks = (at, second, first, peer(first, 1 - kind))
        for slot, chunk in enumerate(chunks):
            target = keeps[kind] if slot < 2 else sends[kind]
            rows = {}
            for matrix, column, width, tile in wide_runs(kind):
                if (matrix == 0) not in rows:
                    rows[matrix == 0] = chunk_rows(left_cot if matrix == 0 else left_two, core, chunk)
                left = rows[matrix == 0]
                mine = pl.ds(pl.multiple_of(core * WIDE_COLUMNS + column, 128), width)
                away = matrix * WIDE_COLUMNS + column
                value = dot(left[:, :256], own[matrix][:, mine])
                value = value + dot(left[:, 256:], shared[:, away : away + width])
                store_blocks(value, target, (slot % 2) * 4 * WIDE[kind], WIDE[kind], tile)


def narrow_kernel(scalars, one, shared, low, late_other, backs, ymix, out, left_one, left_low):
    width = one.shape[1]
    one_other, ymix_other = shared.at[:, :width], shared.at[:, width:]
    for at in range(0, width, 256):
        left_one[at : at + 256, :256] = one[:, at : at + 256].T
        left_one[at : at + 256, 256:] = one_other[:, at : at + 256].T
        left_low[at : at + 256, :256] = low[:, at : at + 256].T
        left_low[at : at + 256, 256:] = late_other[at // 256].T
    mine = pl.ds(pl.multiple_of(scalars[3] * 256, 256), 256)
    for slot in range(4):
        chunk = peer(scalars[0], slot) if slot < 3 else scalars[0]
        for kind in range(4):
            left, own, other = (
                (left_one, backs[kind, :, mine], late_other[4 + kind])
                if kind < 3
                else (left_low, ymix[:, mine], ymix_other[...])
            )
            rows = chunk_rows(left, scalars[3], chunk)
            value = dot(rows[:, :256], own) + dot(rows[:, 256:], other)
            store_blocks(value, out.at[slot], 0, NARROW, 2 * kind)


def split_small(value, target, at):
    high = value.astype(BF16)
    target[at, :32] = high
    target[at, 32:] = (value - high.astype(F32)).astype(BF16)


def join_small(source, at):
    return source[at, :32].astype(F32) + source[at, 32:].astype(F32)


def rounded_small(value):
    high = value.astype(BF16)
    return high.astype(F32) + (value - high.astype(F32)).astype(BF16).astype(F32)


def sum_small(value, gots, bases):
    near, far, cross = (join_small(got, base) for got, base in zip(gots, bases))
    return (rounded_small(value) + cross) + (near + far)


def first_kernel(scalars, *refs):
    gots, keeps, (narrow, small, gain, gain_other) = refs[:2], refs[2:4], refs[4:8]
    sends, wide_keeps, new_small = refs[8:11], refs[11:13], refs[13]
    new_small[:8] = gain[...] + gain_other[...]
    new_small[8:] = small[8:]
    for pairing in range(3):
        base = WIDE_BLOCKS[pairing]
        sends[pairing][base : base + 4 * NARROW] = narrow[pairing]
        split_small(new_small[...], sends[pairing], base + 4 * NARROW)
    for kind in range(2):
        half = 4 * WIDE[kind]
        for chunk in range(4):
            at = slice(chunk * WIDE[kind], (chunk + 1) * WIDE[kind])
            after = slice(half + chunk * WIDE[kind], half + (chunk + 1) * WIDE[kind])
            wide_keeps[kind][at] = (keeps[kind][at].astype(F32) + gots[kind][at].astype(F32)).astype(BF16)
            sends[1 - kind][at] = (keeps[kind][after].astype(F32) + gots[kind][after].astype(F32)).astype(BF16)


def second_kernel(scalars, *refs):
    gots, wide_in, (narrow, small), sends, (keep, new_small) = refs[:3], refs[3:5], refs[5:7], refs[7:10], refs[10:]

    def fill(chunk, target):
        tile = 0
        for kind in range(2):
            at = pl.ds(chunk * WIDE[kind], WIDE[kind])
            value = wide_in[kind][at].astype(F32) + gots[1 - kind][at].astype(F32)
            target[tile : tile + WIDE[kind]] = value.astype(BF16)
            tile += WIDE[kind]
        value = narrow[3, pl.ds(chunk * NARROW, NARROW)].astype(F32)
        for pairing in range(3):
            value = value + gots[pairing][pl.ds(WIDE_BLOCKS[pairing] + chunk * NARROW, NARROW)].astype(F32)
        target[tile : tile + NARROW] = value.astype(BF16)

    value = sum_small(small[...], gots, [count - 1 for count in ROUND_ONE])
    new_small[...] = value
    for pairing in range(3):
        fill(peer(scalars[1], pairing), sends[pairing])
        split_small(value, sends[pairing], TILES)
    fill(scalars[1], keep)


def third_kernel(scalars, *refs):
    gots, (kept, small), (send, keep) = refs[:3], refs[3:5], refs[5:]
    here = scalars[2]
    for first in range(0, TILES, 7):
        at = slice(first, first + 7)
        value = kept[at].astype(F32)
        for got in gots:
            value = value + got[at].astype(F32)
        zero, one = value[:, :32], value[:, 32:]
        keep[at] = jnp.where(here == 0, zero, one)
        send[at] = jnp.where(here == 0, one, zero).astype(BF16)
    value = sum_small(small[...], gots, [TILES] * 3)
    high = value.astype(BF16)
    low = (value - high.astype(F32)).astype(BF16)
    send[TILES] = high
    send[TILES + 1] = low
    keep[TILES] = high.astype(F32)
    keep[TILES + 1] = low.astype(F32)


def cores_kernel(scalars, keep, got, mine, away):
    core = scalars[3]
    total = keep[:TILES] + got[:TILES].astype(F32)
    zero, one = total[:, :16], total[:, 16:]
    mine[:TILES] = jnp.where(core == 0, zero, one)
    away[:TILES] = jnp.where(core == 0, one, zero)
    small = (keep[TILES] + keep[TILES + 1]) + (got[TILES].astype(F32) + got[TILES + 1].astype(F32))
    for target in (mine, away):
        target[TILES] = small[:16]
        target[TILES + 1] = small[16:]


def outputs_kernel(scalars, mine, got, down, gate, up, inner, out, gain_one, gain_two, taps):
    core = scalars[3]

    def place(target, tile, column, columns):
        zero, one = jnp.where(core == 0, mine[tile], got[tile]), jnp.where(core == 0, got[tile], mine[tile])
        target[:, column : column + 128] = zero
        target[:, columns + column : columns + column + 128] = one

    for matrix, target in enumerate((down, gate, up)):
        for tile in range(WIDE_COLUMNS // 128):
            place(target, matrix * (WIDE_COLUMNS // 128) + tile, tile * 128, WIDE_COLUMNS)
    for kind in range(4):
        for column in range(2):
            place(inner.at[kind] if kind < 3 else out, WIDE_TILES + 2 * kind + column, column * 128, 256)
    gains = mine[TILES] + got[TILES]
    rest = mine[TILES + 1] + got[TILES + 1]
    for at in range(8):
        lanes = slice(at * 128, at * 128 + 128)
        gain_one[:, lanes] = gains[at : at + 1]
        gain_two[:, lanes] = gains[8 + at : 9 + at]
    for lag in range(3):
        for at in range(4):
            row = 4 * lag + at
            taps[lag : lag + 1, at * 128 : at * 128 + 128] = rest[row : row + 1]


def swap_round(sends, pairings):
    return [swap(value, pairs) for value, pairs in zip(sends, pairings)]


def blocks(counts):
    return [like((count, *BLOCK), BF16) for count in counts]


def on_device(
    tokens,
    starts,
    gain_one,
    in_weight,
    conv_weight,
    out_weight,
    gain_two,
    gate_weight,
    up_weight,
    down_weight,
    cotangent,
):
    at = lax.axis_index("seq")
    core = at % 2
    y, z = at // 16, (at // 4) % 4
    scalars = jnp.stack(
        [jnp.where(core == 0, y, z), jnp.where(core == 0, z, y), (at // 2) % 2, core, starts[0]]
        + [lax.axis_index("tensor")]
    ).astype(jnp.int32)
    run = functools.partial(call, scalars=scalars)
    rows, width = tokens.shape
    channels = conv_weight.shape[1]
    in_parts = in_weight.transpose(1, 0, 2)
    gain_one_row, gain_two_row = gain_one.reshape(1, -1), gain_two.reshape(1, -1)

    def share(value):
        return swap(value, CORES)

    half = channels // 2
    weight_got = swap(jnp.where(core == 0, out_weight[:half], out_weight[half:]), NEAREST)
    tail = run(
        tail_kernel,
        operands=[tokens, gain_one_row, in_parts],
        outs=[like((16, channels), BF16)],
        scratch=[
            pltpu.VMEM((16, width), BF16),
            pltpu.VMEM((1, width), F32),
            pltpu.VMEM((width, channels), BF16),
            pltpu.VMEM((width, channels), BF16),
            pltpu.SemaphoreType.DMA((4,)),
        ],
        room=60,
        where=pltpu.HBM,
    )[0]
    incoming = from_behind(tail, "seq", 1)
    cotangent_other = share(cotangent)
    incoming, cotangent_other = lax.optimization_barrier((incoming, cotangent_other))
    normed_one, parts, gated = run(
        project_kernel,
        operands=[tokens, gain_one_row, in_parts],
        outs=[like((rows, width), BF16), like((3, rows, channels), F32), like((rows, channels), BF16)],
        scratch=[
            pltpu.VMEM((rows, width), BF16),
            pltpu.VMEM((1, width), F32),
            pltpu.VMEM((3, width, channels), BF16),
            pltpu.SemaphoreType.DMA((5,)),
        ],
        room=50,
        where=pltpu.HBM,
    )
    conv, ymix = run(
        mix_kernel,
        operands=[gated, incoming, parts, conv_weight],
        outs=[like((rows, channels), F32), like((rows, channels), BF16)],
    )
    ymix, cotangent_late = lax.optimization_barrier((ymix, cotangent))
    ymix_other = swap(ymix, ACROSS)
    units = gate_weight.shape[1]
    hidden_grad = run(
        hidden_kernel,
        operands=[cotangent_late, down_weight],
        outs=[like((rows, units), F32)],
        flops=LONG,
    )[0]
    whole_weight = run(
        whole_kernel, operands=[out_weight, weight_got, share(weight_got)], outs=[like((2 * channels, width), BF16)]
    )[0]
    ymix_other, hidden_grad, whole_weight = lax.optimization_barrier((ymix_other, hidden_grad, whole_weight))
    resid, normed_two, hidden, gate_back, up_back, shared, shared_early = run(
        feed_kernel,
        operands=[tokens, ymix, ymix_other, whole_weight, gain_two_row, gate_weight, up_weight, hidden_grad]
        + [normed_one],
        outs=[like((rows, width), F32), like((rows, width), BF16)]
        + [like((rows, units), BF16)] * 3
        + [like((rows, 3 * WIDE_COLUMNS + width), BF16), like((rows, width + channels // 2), BF16)],
    )
    shared_other = share(shared)
    norm_two_part = run(
        part_kernel, operands=[gate_back, up_back, gate_weight, up_weight], outs=[like((rows, width), BF16)]
    )[0]
    norm_two_other = swap(norm_two_part, ACROSS)
    results = run(
        wide_kernel,
        operands=[normed_two, cotangent, cotangent_other, hidden, gate_back, up_back, shared_other],
        outs=blocks([8 * count for count in WIDE] * 2),
        scratch=[pltpu.VMEM((width, 2 * rows), BF16)] * 2,
    )
    sends, keeps = list(results[:2]), list(results[2:])
    down_part = run(down_kernel, operands=[hidden, down_weight], outs=[like((rows, width), BF16)])[0]
    norm_two_other, keeps[1], down_part = lax.optimization_barrier((norm_two_other, keeps[1], down_part))
    gots = swap_round(sends, FIRST)

    edge_operands = [norm_two_part, norm_two_other, resid, gain_two_row, cotangent, out_weight, parts, conv_weight]
    edge = run(edge_kernel, operands=edge_operands, outs=[like((8, channels), F32)])[0]
    returned = from_behind(edge, "seq", -1)
    resid_grad, resid_low, gain_two_grad, c_back, gated_back, tap_grads = run(
        middle_kernel,
        operands=edge_operands + [conv, gated, incoming],
        outs=[
            like((rows, width), F32),
            like((rows, width), BF16),
            like((1, width), F32),
            like((rows, channels), BF16),
            like((rows, channels), F32),
            like((3, channels), F32),
        ],
        flops=SHORT,
    )
    backs, shared, norm_one_part, gain_part, small = run(
        last_kernel,
        operands=[gated_back, returned, parts, c_back, in_parts, tokens, gain_two_grad, tap_grads]
        + [resid_low],
        outs=[
            like((3, rows, channels), BF16),
            like((7, rows, 256), BF16),
            like((rows, width), BF16),
            like((8, 128), F32),
            like((32, 128), F32),
        ],
    )
    narrow = run(
        narrow_kernel,
        operands=[normed_one, share(shared_early), resid_low, share(shared), backs, ymix],
        outs=[like((4, 4 * NARROW, *BLOCK), BF16)],
        scratch=[pltpu.VMEM((width, 2 * rows), BF16)] * 2,
    )[0]
    gain_other = swap(gain_part, ACROSS)
    gots[0], gots[1], narrow, gain_other = lax.optimization_barrier((gots[0], gots[1], narrow, gain_other))
    results = run(
        first_kernel,
        operands=gots + keeps + [narrow, small, gain_part, gain_other],
        outs=blocks(ROUND_ONE) + blocks([4 * count for count in WIDE]) + [like((32, 128), F32)],
    )
    sends, keeps, small = list(results[:3]), list(results[3:5]), results[5]
    gots = swap_round(sends, FIRST)
    norm_one_other = swap(norm_one_part, ACROSS)
    gots[0], norm_one_other = lax.optimization_barrier((gots[0], norm_one_other))
    results = run(
        second_kernel,
        operands=gots + keeps + [narrow, small],
        outs=blocks([TILES + 1] * 3 + [TILES]) + [like((32, 128), F32)],
    )
    sends, keep, small = list(results[:3]), results[3], results[4]
    gots = swap_round(sends, SECOND)
    small, down_part = lax.optimization_barrier((small, down_part))
    down_other = swap(down_part, ACROSS)
    gots[0], down_other = lax.optimization_barrier((gots[0], down_other))
    beside, kept = run(
        third_kernel,
        operands=gots + [keep, small],
        outs=[like((TILES + 2, 32, 128), BF16), like((TILES + 2, 32, 128), F32)],
    )
    beside = swap(beside, BESIDE)
    mixed = (resid + (down_part.astype(F32) + down_other.astype(F32))).astype(BF16)
    inputs = tokens.astype(F32)
    norm_one_back = norm_one_part.astype(F32) + norm_one_other.astype(F32)
    tokens_grad = resid_grad + norm_backward(norm_one_back, inputs, norm_scale(inputs), gain_one)
    beside, mixed, tokens_grad = lax.optimization_barrier((beside, mixed, tokens_grad))
    mine, away = run(
        cores_kernel,
        operands=[kept, beside],
        outs=[like((TILES + 2, 16, 128), F32)] * 2,
    )
    down_g, gate_g, up_g, in_g, out_g, gain_one_g, gain_two_g, conv_g = run(
        outputs_kernel,
        operands=[mine, swap(away, CORES)],
        outs=[like((16, 2 * WIDE_COLUMNS), F32)] * 3
        + [like((3, 16, channels), F32), like((16, channels), F32)]
        + [like((1, width), F32)] * 2
        + [like((3, channels), F32)],
    )
    in_g, gain_one_g, gain_two_g = in_g.transpose(1, 0, 2), gain_one_g.reshape(-1), gain_two_g.reshape(-1)
    return (mixed, tokens_grad, gain_one_g, in_g, conv_g, out_g.T, gain_two_g, gate_g, up_g, down_g.T)


def solution(mesh):
    return jax.shard_map(
        on_device,
        mesh=mesh,
        in_specs=(
            P("seq", None),
            P("seq"),
            P(),
            P(None, None, "tensor"),
            P(None, "tensor"),
            P("tensor", None),
            P(),
            P(None, "tensor"),
            P(None, "tensor"),
            P("tensor", None),
            P("seq", None),
        ),
        out_specs=(
            P("seq", None),
            P("seq", None),
            P(),
            P("seq", None, "tensor"),
            P(None, "tensor"),
            P("tensor", "seq"),
            P(),
            P("seq", "tensor"),
            P("seq", "tensor"),
            P("tensor", "seq"),
        ),
        check_vma=False,
    )
```

```python
import functools

import jax
import jax.numpy as jnp
from jax import lax
from jax.experimental import pallas as pl
from jax.experimental.pallas import tpu as pltpu
from jax.sharding import PartitionSpec as P

EPS = 1e-05
AXES = ("seq", "tensor")
BF16 = jnp.bfloat16
F32 = jnp.float32


def device_pairs(move):
    def number(y, z, x, core):
        return ((((y % 4) * 4 + z % 4) * 2 + x % 2) * 2 + core) * 2 + (x % 4) // 2

    return [
        (number(y, z, x, core), number(*move(y, z, x, core)))
        for y in range(4)
        for z in range(4)
        for x in range(4)
        for core in range(2)
    ]


ACROSS = device_pairs(lambda y, z, x, core: (y, z, (x + 2) % 4, core))
BESIDE = device_pairs(lambda y, z, x, core: (y, z, x ^ 1, core))
NEAREST = device_pairs(lambda y, z, x, core: (y, z, 3 - x, core))
CORES = device_pairs(lambda y, z, x, core: (y, z, x, 1 - core))


def peer(at, pairing):
    return (at ^ 1, 3 - at, at ^ 2)[pairing]


FIRST = [
    device_pairs(
        functools.partial(
            lambda pairing, y, z, x, core: (y, peer(z, pairing), x, core)
            if core
            else (peer(y, pairing), z, x, core),
            pairing,
        )
    )
    for pairing in range(3)
]
SECOND = [
    device_pairs(
        functools.partial(
            lambda pairing, y, z, x, core: (peer(y, pairing), z, x, core)
            if core
            else (y, peer(z, pairing), x, core),
            pairing,
        )
    )
    for pairing in range(3)
]
WIDE_COLUMNS = 1152
WIDE_TILES = 27
WIDE = (14, 13)
NARROW = 8
BLOCK = (64, 128)
LONG = 3 * 10**10
SHORT = 8 * 10**9
TILES = WIDE_TILES + NARROW
WIDE_PIECE = (1, 0, None)
WIDE_BLOCKS = (4 * WIDE[1], 4 * WIDE[0], 0)
ROUND_ONE = tuple(count + 4 * NARROW + 1 for count in WIDE_BLOCKS)


def swap(value, pairs):
    return lax.ppermute(value, AXES, pairs)


def from_behind(value, axis, steps):
    count = lax.axis_size(axis)
    leading, last = (max(0, -steps), min(count, count - steps))
    return lax.ppermute(value, axis, [(source, source + steps) for source in range(leading, last)])


def norm_scale(values):
    return lax.rsqrt(jnp.mean(values * values, axis=1, keepdims=True) + EPS)


def norm_backward(out_grad_rows, values, scale_rows, gain):
    scaled = out_grad_rows * gain
    inner = jnp.mean(scaled * values, axis=1, keepdims=True)
    return scale_rows * (scaled - values * scale_rows * scale_rows * inner)


def like(shape, dtype):
    return jax.ShapeDtypeStruct(shape, dtype)


def positions(offset):
    at = lax.axis_index("seq")
    y, z, core = at // 16, (at // 4) % 4, at % 2
    first, second = jnp.where(core == 0, y, z), jnp.where(core == 0, z, y)
    return first, second, (at // 2) % 2, core, offset, lax.axis_index("tensor")


def call(body, *, operands, outs, scratch=(), offset=None, flops=0, aliases=None, where=pltpu.VMEM, scalar=None):
    whole = pl.BlockSpec(memory_space=pltpu.VMEM)
    specs = [pl.BlockSpec(memory_space=where)] * len(operands)
    if scalar is not None:
        operands, specs = [scalar, *operands], [pl.BlockSpec(memory_space=pltpu.SMEM), *specs]

    def kernel(*refs):
        if offset is None:
            body(positions(None), *refs)
        else:
            body(positions(refs[0][0:1, 0:1]), *refs[1:])

    if offset is not None:
        operands, specs = [offset, *operands], [whole, *specs]
    return pl.pallas_call(
        kernel,
        out_shape=tuple(outs),
        in_specs=specs,
        out_specs=tuple(whole for _ in outs),
        scratch_shapes=list(scratch),
        input_output_aliases=aliases or {},
        compiler_params=pltpu.CompilerParams(vmem_limit_bytes=16 * 2**20),
        cost_estimate=pl.CostEstimate(flops=flops, bytes_accessed=0, transcendentals=0),
    )(*operands)


def dot(left, right):
    return jnp.dot(left, right, preferred_element_type=F32)


def dot_rows(left, right):
    return lax.dot_general(left, right, (((1,), (1,)), ((), ())), preferred_element_type=F32)


def row_numbers(shape, first=0):
    return lax.broadcasted_iota(jnp.int32, shape, 0) + first


def valid_rows(offset, lag, shape):
    row = row_numbers(shape)
    return jnp.where((offset <= row) & (offset > row - lag), 0.0, 1.0)


def linked_rows(offset, shape, first, count):
    return jnp.where((row_numbers(shape, first) < offset) & (offset < count), 0.0, 1.0)


def half_kernel(scalars, weight, half, done):
    rows = half.shape[0]
    copy = pltpu.make_async_copy(weight.at[pl.ds(pl.multiple_of(scalars[3] * rows, 16), rows)], half, done)
    copy.start()
    copy.wait()


def load_kernel(scalars, starts, tokens, gain, weight, tail, token_rows, gain_row, weights, offset, done):
    rows, depth = tokens.shape[0], weight.shape[1] // 4
    pieces = [(gain, gain_row)]
    pieces += [(tokens.at[pl.ds(at, 128)], token_rows.at[pl.ds(at, 128)]) for at in (rows - 128, 0)]
    for k in (0, 2, 1):
        for at in range(0, weight.shape[1], depth):
            pieces.append((weight.at[k, pl.ds(at, depth)], weights.at[k, pl.ds(at, depth)]))
    copies = [
        pltpu.make_async_copy(source, target, done.at[at]) for at, (source, target) in enumerate(pieces)
    ]
    for copy in copies:
        copy.start()
    for copy in copies[:2]:
        copy.wait()
    offset[...] = jnp.full(offset.shape, starts[0], jnp.int32)
    values = token_rows[rows - 16 :].astype(F32)
    normed = (values * norm_scale(values) * gain_row[...]).astype(BF16)
    for copy in copies[2:11]:
        copy.wait()
    gated = (dot(normed, weights[0]) * dot(normed, weights[2])).astype(BF16).astype(F32)
    tail[...] = (gated * linked_rows(starts[0], gated.shape, rows - 16, rows)).astype(BF16)
    for copy in copies[11:]:
        copy.wait()


def project_kernel(scalars, tokens, gain, weights, normed, parts, gated):
    values = tokens[...].astype(F32)
    normed[...] = (values * norm_scale(values) * gain[...]).astype(BF16)
    for k in range(3):
        parts[k] = dot(normed[...], weights[k])
    gated[...] = (parts[0] * parts[2]).astype(BF16)


def behind(gated, incoming, lag):
    moved = pltpu.roll(gated, lag, 0)
    row = row_numbers(gated.shape)
    for at in range(lag):
        moved = jnp.where(row == at, incoming[16 - lag + at : 17 - lag + at], moved)
    return moved


def mix_kernel(scalars, gated, incoming, parts, taps, conv, ymix):
    values = gated[...].astype(F32)
    before = incoming[...].astype(F32)
    total = taps[0:1] * values
    for lag in (1, 2):
        total = total + taps[lag : lag + 1] * behind(values, before, lag) * valid_rows(
            scalars[4], lag, values.shape
        )
    conv[...] = total
    ymix[...] = (parts[1] * total).astype(BF16)


def away_half(value, core):
    half = value.shape[-1] // 2
    return jnp.where(core == 0, value[..., half:], value[..., :half])


def hidden_kernel(scalars, cot, weight, out):
    for at in range(0, weight.shape[0], 256):
        out[:, at : at + 256] = dot_rows(cot[...], weight[at : at + 256])


def down_kernel(scalars, hidden, weight, out):
    out[...] = dot(hidden[...], weight[...]).astype(BF16)


def whole_kernel(scalars, weight, got, got_other, whole):
    core, side = scalars[3], scalars[5]
    half = got.shape[0]
    low, high = jnp.where(core == 0, got[...], got_other[...]), jnp.where(core == 0, got_other[...], got[...])
    whole[:half] = jnp.where(side == 0, weight[:half], low)
    whole[half : 2 * half] = jnp.where(side == 0, weight[half:], high)
    whole[2 * half : 3 * half] = jnp.where(side == 0, low, weight[:half])
    whole[3 * half :] = jnp.where(side == 0, high, weight[half:])


def feed_kernel(
    scalars,
    tokens,
    ymix,
    ymix_other,
    whole,
    gain,
    gate,
    up,
    hidden_grad,
    normed_one,
    resid,
    normed,
    hidden,
    gate_back,
    up_back,
    shared,
    shared_early,
):
    side, channels = scalars[5], ymix.shape[1]
    first, second = (
        jnp.where(side == 0, ymix[...], ymix_other[...]),
        jnp.where(side == 0, ymix_other[...], ymix[...]),
    )
    branch = dot(first, whole[:channels]) + dot(second, whole[channels:])
    resid[...] = tokens[...].astype(F32) + branch
    normed[...] = (resid[...] * norm_scale(resid[...]) * gain[...]).astype(BF16)
    values = normed[...]
    for at in range(0, gate.shape[1], 256):
        columns = slice(at, at + 256)
        gate_act, up_act = dot(values, gate[:, columns]), dot(values, up[:, columns])
        back = hidden_grad[:, columns]
        sigmoid_gate = jax.nn.sigmoid(gate_act)
        swish = gate_act * sigmoid_gate
        hidden[:, columns] = (swish * up_act).astype(BF16)
        up_back[:, columns] = (back * swish).astype(BF16)
        slope = sigmoid_gate * (1.0 + gate_act * (1.0 - sigmoid_gate))
        gate_back[:, columns] = (back * up_act * slope).astype(BF16)
    away = pl.ds(pl.multiple_of((1 - scalars[3]) * WIDE_COLUMNS, 128), WIDE_COLUMNS)
    for k, value in enumerate((hidden, gate_back, up_back)):
        shared[:, k * WIDE_COLUMNS : (k + 1) * WIDE_COLUMNS] = value[:, away]
    shared[:, 3 * WIDE_COLUMNS :] = values
    shared_early[:, : normed.shape[1]] = normed_one[...]
    shared_early[:, normed.shape[1] :] = away_half(ymix[...], scalars[3])


def part_kernel(scalars, gate_back, up_back, gate, up, part):
    part[...] = (dot_rows(gate_back[...], gate[...]) + dot_rows(up_back[...], up[...])).astype(BF16)


def second_norm(part, other, resid, gain, cot):
    back = part.astype(F32) + other.astype(F32)
    scale = norm_scale(resid)
    return back, scale, cot.astype(F32) + norm_backward(back, resid, scale, gain)


def edge_kernel(scalars, part, other, resid, gain, cot, weight, parts, taps, edge):
    top = slice(0, 16)
    _, _, grad = second_norm(part[top], other[top], resid[top], gain[...], cot[top])
    conv_back = dot_rows(grad.astype(BF16), weight[...]) * parts[1, top]
    one = conv_back * valid_rows(scalars[4], 1, conv_back.shape) * taps[1:2]
    two = conv_back * valid_rows(scalars[4], 2, conv_back.shape) * taps[2:3]
    row = row_numbers((8, conv_back.shape[1]))
    edge[...] = jnp.where(row == 6, two[0:1], 0.0) + jnp.where(row == 7, one[0:1] + two[1:2], 0.0)


def middle_kernel(
    scalars, part, other, resid, gain, cot, weight, parts, taps, conv, gated, incoming, grad, low, gain_grad, c_back, gated_back, tap_grads
):
    back, scale, resid_grad = second_norm(part[...], other[...], resid[...], gain[...], cot[...])
    gain_grad[...] = jnp.sum(back * resid[...] * scale, axis=0, keepdims=True)
    grad[...] = resid_grad
    low[...] = resid_grad.astype(BF16)
    ymix_back = dot_rows(low[...], weight[...])
    c_back[...] = (ymix_back * conv[...]).astype(BF16)
    conv_back = ymix_back * parts[1]
    values, before = gated[...].astype(F32), incoming[...].astype(F32)
    rows = values.shape[0]
    tap_grads[0:1] = jnp.sum(conv_back * values, axis=0, keepdims=True)
    total = conv_back * taps[0:1]
    row = row_numbers(values.shape)
    for lag in (1, 2):
        term = conv_back * valid_rows(scalars[4], lag, values.shape)
        tap_grads[lag : lag + 1] = jnp.sum(term * behind(values, before, lag), axis=0, keepdims=True)
        moved = pltpu.roll(term * taps[lag : lag + 1], rows - lag, 0)
        total = total + jnp.where(row < rows - lag, moved, 0.0)
    gated_back[...] = total


def last_kernel(
    scalars,
    gated_back,
    returned,
    parts,
    c_back,
    weight,
    tokens,
    gain_two_grad,
    tap_grads,
    resid_low,
    backs,
    shared,
    part,
    gain_part,
    small,
):
    rows = gated_back.shape[0]
    links = linked_rows(scalars[4], returned.shape, rows - 8, rows)
    end = gated_back[rows - 8 :] + returned[...] * links
    total = jnp.concatenate([gated_back[: rows - 8], end], 0)
    backs[0] = (total * parts[2]).astype(BF16)
    backs[1] = c_back[...]
    backs[2] = (total * parts[0]).astype(BF16)
    for k in range(3):
        shared[4 + k] = away_half(backs[k], scalars[3])
    for at in range(4):
        shared[at] = resid_low[:, at * 256 : at * 256 + 256]
    grad = dot_rows(backs[0], weight[0]) + dot_rows(backs[1], weight[1]) + dot_rows(backs[2], weight[2])
    part[...] = grad.astype(BF16)
    values = tokens[...].astype(F32)
    gain_grad = jnp.sum(grad * values * norm_scale(values), axis=0, keepdims=True)
    for at in range(8):
        lanes = slice(at * 128, at * 128 + 128)
        gain_part[at : at + 1] = gain_grad[:, lanes]
        small[8 + at : 9 + at] = gain_two_grad[:, lanes]
    for lag in range(3):
        for at in range(4):
            row = 16 + 4 * lag + at
            small[row : row + 1] = tap_grads[lag : lag + 1, at * 128 : at * 128 + 128]
    small[:8] = jnp.zeros((8, 128), F32)
    small[28:32] = jnp.zeros((4, 128), F32)


def fill_transposed(left, own, other):
    for at in range(0, own.shape[1], 256):
        left[at : at + 256, :256] = own[:, at : at + 256].T
        left[at : at + 256, 256:] = other[:, at : at + 256].T


def chunk_rows(left, core, chunk):
    wide, slim = jnp.where(core == 0, 256, 64), jnp.where(core == 0, 64, 256)
    return jnp.concatenate(
        [left[pl.ds(pl.multiple_of(chunk * wide + at * slim, 64), 64)] for at in range(4)], 0
    )


def store_blocks(value, target, base, tiles, tile):
    value = value.astype(BF16)
    for chunk in range(4):
        for column in range(value.shape[1] // 128):
            target[base + chunk * tiles + tile + column] = value[
                chunk * 64 : chunk * 64 + 64, column * 128 : column * 128 + 128
            ]


def wide_runs(kind):
    at, end = (0, WIDE[0]) if kind == 0 else (WIDE[0], WIDE_TILES)
    first = at
    while at < end:
        matrix, tile = divmod(at, WIDE_COLUMNS // 128)
        count = min(2, WIDE_COLUMNS // 128 - tile, end - at)
        yield matrix, tile * 128, count * 128, at - first
        at += count


def wide_piece(scalars, kind, lefts, own, shared, send, keep):
    at, core = scalars[0], scalars[3]
    first, second = peer(at, kind), peer(at, 1 - kind)
    chunks = (at, second, first, peer(first, 1 - kind))
    for slot, chunk in enumerate(chunks):
        target = keep if slot < 2 else send
        rows = {}
        for matrix, column, width, tile in wide_runs(kind):
            if (matrix == 0) not in rows:
                rows[matrix == 0] = chunk_rows(lefts[matrix], core, chunk)
            left = rows[matrix == 0]
            mine = pl.ds(pl.multiple_of(core * WIDE_COLUMNS + column, 128), width)
            away = matrix * WIDE_COLUMNS + column
            value = dot(left[:, :256], own[matrix][:, mine])
            value = value + dot(left[:, 256:], shared[:, away : away + width])
            store_blocks(value, target, (slot % 2) * 4 * WIDE[kind], WIDE[kind], tile)


def wide_first_kernel(scalars, two, cot, cot_other, hidden, gate_back, shared, send, keep, left_two, left_cot):
    fill_transposed(left_cot, cot, cot_other)
    fill_transposed(left_two, two, shared.at[:, 3 * WIDE_COLUMNS :])
    wide_piece(scalars, 0, (left_cot, left_two), (hidden, gate_back), shared, send, keep)


def wide_second_kernel(scalars, left_two, gate_back, up_back, shared, send, keep):
    wide_piece(scalars, 1, (None, left_two, left_two), (None, gate_back, up_back), shared, send, keep)


def narrow_kernel(scalars, one, shared, low, late_other, backs, ymix, *refs):
    outs, (left_one, left_low) = refs[:4], refs[4:]
    width = one.shape[1]
    one_other, ymix_other = shared.at[:, :width], shared.at[:, width:]
    for at in range(0, width, 256):
        left_one[at : at + 256, :256] = one[:, at : at + 256].T
        left_one[at : at + 256, 256:] = one_other[:, at : at + 256].T
        left_low[at : at + 256, :256] = low[:, at : at + 256].T
        left_low[at : at + 256, 256:] = late_other[at // 256].T
    mine = pl.ds(pl.multiple_of(scalars[3] * 256, 256), 256)
    for slot in range(4):
        chunk = peer(scalars[0], slot) if slot < 3 else scalars[0]
        for kind in range(4):
            left, own, other = (
                (left_one, backs[kind, :, mine], late_other[4 + kind])
                if kind < 3
                else (left_low, ymix[:, mine], ymix_other[...])
            )
            rows = chunk_rows(left, scalars[3], chunk)
            value = dot(rows[:, :256], own) + dot(rows[:, 256:], other)
            store_blocks(value, outs[slot], WIDE_BLOCKS[slot] if slot < 3 else 0, NARROW, 2 * kind)


def split_small(value, target, at):
    high = value.astype(BF16)
    target[at, :32] = high
    target[at, 32:] = (value - high.astype(F32)).astype(BF16)


def join_small(source, at):
    return source[at, :32].astype(F32) + source[at, 32:].astype(F32)


def rounded_small(value):
    high = value.astype(BF16)
    return high.astype(F32) + (value - high.astype(F32)).astype(BF16).astype(F32)


def sum_small(value, gots, bases):
    near, far, cross = (join_small(got, base) for got, base in zip(gots, bases))
    return (rounded_small(value) + cross) + (near + far)


def first_kernel(scalars, *refs):
    gots, keeps, (small, gain, gain_other) = refs[:2], refs[2:4], refs[4:7]
    sends, wide_keeps, new_small = refs[10:13], refs[13:15], refs[15]
    new_small[:8] = gain[...] + gain_other[...]
    new_small[8:] = small[8:]
    for pairing in range(3):
        split_small(new_small[...], sends[pairing], ROUND_ONE[pairing] - 1)
    for kind in range(2):
        half = 4 * WIDE[kind]
        for chunk in range(4):
            at = slice(chunk * WIDE[kind], (chunk + 1) * WIDE[kind])
            after = slice(half + chunk * WIDE[kind], half + (chunk + 1) * WIDE[kind])
            wide_keeps[kind][at] = (keeps[kind][at].astype(F32) + gots[kind][at].astype(F32)).astype(BF16)
            sends[1 - kind][at] = (keeps[kind][after].astype(F32) + gots[kind][after].astype(F32)).astype(BF16)


def second_kernel(scalars, *refs):
    gots, wide_in, (narrow, small), sends, (keep, new_small) = refs[:3], refs[3:5], refs[5:7], refs[7:10], refs[10:]

    def fill(chunk, target):
        tile = 0
        for kind in range(2):
            at = pl.ds(chunk * WIDE[kind], WIDE[kind])
            value = wide_in[kind][at].astype(F32) + gots[1 - kind][at].astype(F32)
            target[tile : tile + WIDE[kind]] = value.astype(BF16)
            tile += WIDE[kind]
        value = narrow[pl.ds(chunk * NARROW, NARROW)].astype(F32)
        for pairing in range(3):
            value = value + gots[pairing][pl.ds(WIDE_BLOCKS[pairing] + chunk * NARROW, NARROW)].astype(F32)
        target[tile : tile + NARROW] = value.astype(BF16)

    value = sum_small(small[...], gots, [count - 1 for count in ROUND_ONE])
    new_small[...] = value
    for pairing in range(3):
        fill(peer(scalars[1], pairing), sends[pairing])
        split_small(value, sends[pairing], TILES)
    fill(scalars[1], keep)


def third_kernel(scalars, *refs):
    gots, (kept, small), (send, keep) = refs[:3], refs[3:5], refs[5:]
    here = scalars[2]
    for first in range(0, TILES, 7):
        at = slice(first, first + 7)
        value = kept[at].astype(F32)
        for got in gots:
            value = value + got[at].astype(F32)
        zero, one = value[:, :32], value[:, 32:]
        keep[at] = jnp.where(here == 0, zero, one)
        send[at] = jnp.where(here == 0, one, zero).astype(BF16)
    value = sum_small(small[...], gots, [TILES] * 3)
    high = value.astype(BF16)
    low = (value - high.astype(F32)).astype(BF16)
    send[TILES] = high
    send[TILES + 1] = low
    keep[TILES] = high.astype(F32)
    keep[TILES + 1] = low.astype(F32)


def cores_kernel(scalars, keep, got, mine, away):
    core = scalars[3]
    total = keep[:TILES] + got[:TILES].astype(F32)
    zero, one = total[:, :16], total[:, 16:]
    mine[:TILES] = jnp.where(core == 0, zero, one)
    away[:TILES] = jnp.where(core == 0, one, zero)
    small = (keep[TILES] + keep[TILES + 1]) + (got[TILES].astype(F32) + got[TILES + 1].astype(F32))
    for target in (mine, away):
        target[TILES] = small[:16]
        target[TILES + 1] = small[16:]


def outputs_kernel(scalars, mine, got, down, gate, up, inner, out, gain_one, gain_two, taps):
    core = scalars[3]

    def place(target, tile, column, columns):
        zero, one = jnp.where(core == 0, mine[tile], got[tile]), jnp.where(core == 0, got[tile], mine[tile])
        target[:, column : column + 128] = zero
        target[:, columns + column : columns + column + 128] = one

    for matrix, target in enumerate((down, gate, up)):
        for tile in range(WIDE_COLUMNS // 128):
            place(target, matrix * (WIDE_COLUMNS // 128) + tile, tile * 128, WIDE_COLUMNS)
    for kind in range(4):
        for column in range(2):
            place(inner.at[kind] if kind < 3 else out, WIDE_TILES + 2 * kind + column, column * 128, 256)
    gains = mine[TILES] + got[TILES]
    rest = mine[TILES + 1] + got[TILES + 1]
    for at in range(8):
        lanes = slice(at * 128, at * 128 + 128)
        gain_one[:, lanes] = gains[at : at + 1]
        gain_two[:, lanes] = gains[8 + at : 9 + at]
    for lag in range(3):
        for at in range(4):
            row = 4 * lag + at
            taps[lag : lag + 1, at * 128 : at * 128 + 128] = rest[row : row + 1]


def swap_round(sends, pairings):
    return [swap(value, pairs) for value, pairs in zip(sends, pairings)]


def blocks(counts):
    return [like((count, *BLOCK), BF16) for count in counts]


def on_device(
    tokens,
    starts,
    gain_one,
    in_weight,
    conv_weight,
    out_weight,
    gain_two,
    gate_weight,
    up_weight,
    down_weight,
    cotangent,
):
    core = lax.axis_index("seq") % 2
    run = call
    rows, width = tokens.shape
    channels = conv_weight.shape[1]
    in_parts = in_weight.transpose(1, 0, 2)
    gain_one_row, gain_two_row = gain_one.reshape(1, -1), gain_two.reshape(1, -1)

    def share(value):
        return swap(value, CORES)

    half = channels // 2
    whole_half = run(
        half_kernel,
        operands=[pltpu.with_memory_space_constraint(out_weight, pltpu.HBM)],
        outs=[like((half, width), BF16)],
        scratch=[pltpu.SemaphoreType.DMA],
        where=pltpu.HBM,
    )[0]
    weight_got = swap(whole_half, NEAREST)
    tail, tokens_here, gain_here, weights_here, offset = run(
        load_kernel,
        operands=[
            pltpu.with_memory_space_constraint(value, pltpu.HBM) for value in (tokens, gain_one_row, in_parts)
        ],
        scalar=starts,
        outs=[
            like((16, channels), BF16),
            like((rows, width), BF16),
            like((1, width), F32),
            like((3, width, channels), BF16),
            like((8, 128), jnp.int32),
        ],
        scratch=[pltpu.SemaphoreType.DMA((15,))],
        where=pltpu.HBM,
    )
    incoming = from_behind(tail, "seq", 1)
    cotangent_other = share(cotangent)
    incoming, cotangent_other = lax.optimization_barrier((incoming, cotangent_other))
    normed_one, parts, gated = run(
        project_kernel,
        operands=[tokens_here, gain_here, weights_here],
        outs=[like((rows, width), BF16), like((3, rows, channels), F32), like((rows, channels), BF16)],
    )
    conv, ymix = run(
        mix_kernel,
        offset=offset,
        operands=[gated, incoming, parts, conv_weight],
        outs=[like((rows, channels), F32), like((rows, channels), BF16)],
    )
    ymix, cotangent_late = lax.optimization_barrier((ymix, cotangent))
    ymix_other = swap(ymix, ACROSS)
    units = gate_weight.shape[1]
    hidden_grad = run(
        hidden_kernel,
        operands=[cotangent_late, down_weight],
        outs=[like((rows, units), F32)],
        flops=LONG,
    )[0]
    whole_weight = run(
        whole_kernel, operands=[out_weight, weight_got, share(weight_got)], outs=[like((2 * channels, width), BF16)]
    )[0]
    ymix_other, hidden_grad, whole_weight = lax.optimization_barrier((ymix_other, hidden_grad, whole_weight))
    resid, normed_two, hidden, gate_back, up_back, shared, shared_early = run(
        feed_kernel,
        operands=[tokens, ymix, ymix_other, whole_weight, gain_two_row, gate_weight, up_weight, hidden_grad]
        + [normed_one],
        outs=[like((rows, width), F32), like((rows, width), BF16)]
        + [like((rows, units), BF16)] * 3
        + [like((rows, 3 * WIDE_COLUMNS + width), BF16), like((rows, width + channels // 2), BF16)],
    )
    shared_other = share(shared)
    norm_two_part = run(
        part_kernel, operands=[gate_back, up_back, gate_weight, up_weight], outs=[like((rows, width), BF16)]
    )[0]
    norm_two_other = swap(norm_two_part, ACROSS)
    first_send, first_keep, left_two = run(
        wide_first_kernel,
        operands=[normed_two, cotangent, cotangent_other, hidden, gate_back, shared_other],
        outs=blocks([8 * WIDE[0]] * 2) + [like((width, 2 * rows), BF16)],
        scratch=[pltpu.VMEM((width, 2 * rows), BF16)],
    )
    second_send, second_keep = run(
        wide_second_kernel,
        operands=[left_two, gate_back, up_back, shared_other],
        outs=blocks([8 * WIDE[1]] * 2),
    )
    sends, keeps = [first_send, second_send], [first_keep, second_keep]
    down_part = run(down_kernel, operands=[hidden, down_weight], outs=[like((rows, width), BF16)])[0]
    early_other = share(shared_early)
    norm_two_other, keeps[1], down_part, early_other = lax.optimization_barrier(
        (norm_two_other, keeps[1], down_part, early_other)
    )
    gots = swap_round(sends, FIRST)

    edge_operands = [norm_two_part, norm_two_other, resid, gain_two_row, cotangent, out_weight, parts, conv_weight]
    edge = run(edge_kernel, offset=offset, operands=edge_operands, outs=[like((8, channels), F32)])[0]
    returned = from_behind(edge, "seq", -1)
    resid_grad, resid_low, gain_two_grad, c_back, gated_back, tap_grads = run(
        middle_kernel,
        offset=offset,
        operands=edge_operands + [conv, gated, incoming],
        outs=[
            like((rows, width), F32),
            like((rows, width), BF16),
            like((1, width), F32),
            like((rows, channels), BF16),
            like((rows, channels), F32),
            like((3, channels), F32),
        ],
        flops=SHORT,
    )
    backs, shared, norm_one_part, gain_part, small = run(
        last_kernel,
        offset=offset,
        operands=[gated_back, returned, parts, c_back, in_parts, tokens, gain_two_grad, tap_grads]
        + [resid_low],
        outs=[
            like((3, rows, channels), BF16),
            like((7, rows, 256), BF16),
            like((rows, width), BF16),
            like((8, 128), F32),
            like((32, 128), F32),
        ],
    )
    *sends, narrow = run(
        narrow_kernel,
        operands=[normed_one, early_other, resid_low, share(shared), backs, ymix],
        outs=blocks(ROUND_ONE) + blocks([4 * NARROW]),
        scratch=[pltpu.VMEM((width, 2 * rows), BF16)] * 2,
    )
    gain_other = swap(gain_part, ACROSS)
    gots[0], gots[1], narrow, gain_other = lax.optimization_barrier((gots[0], gots[1], narrow, gain_other))
    results = run(
        first_kernel,
        operands=gots + keeps + [small, gain_part, gain_other] + sends,
        aliases={7: 0, 8: 1, 9: 2},
        outs=blocks(ROUND_ONE) + blocks([4 * count for count in WIDE]) + [like((32, 128), F32)],
    )
    sends, keeps, small = list(results[:3]), list(results[3:5]), results[5]
    gots = swap_round(sends, FIRST)
    norm_one_other = swap(norm_one_part, ACROSS)
    gots[0], norm_one_other = lax.optimization_barrier((gots[0], norm_one_other))
    results = run(
        second_kernel,
        operands=gots + keeps + [narrow, small],
        outs=blocks([TILES + 1] * 3 + [TILES]) + [like((32, 128), F32)],
    )
    sends, keep, small = list(results[:3]), results[3], results[4]
    gots = swap_round(sends, SECOND)
    small, down_part = lax.optimization_barrier((small, down_part))
    down_other = swap(down_part, ACROSS)
    gots[0], down_other = lax.optimization_barrier((gots[0], down_other))
    beside, kept = run(
        third_kernel,
        operands=gots + [keep, small],
        outs=[like((TILES + 2, 32, 128), BF16), like((TILES + 2, 32, 128), F32)],
    )
    beside = swap(beside, BESIDE)
    mixed = (resid + (down_part.astype(F32) + down_other.astype(F32))).astype(BF16)
    inputs = tokens.astype(F32)
    norm_one_back = norm_one_part.astype(F32) + norm_one_other.astype(F32)
    tokens_grad = resid_grad + norm_backward(norm_one_back, inputs, norm_scale(inputs), gain_one)
    beside, mixed, tokens_grad = lax.optimization_barrier((beside, mixed, tokens_grad))
    mine, away = run(
        cores_kernel,
        operands=[kept, beside],
        outs=[like((TILES + 2, 16, 128), F32)] * 2,
    )
    down_g, gate_g, up_g, in_g, out_g, gain_one_g, gain_two_g, conv_g = run(
        outputs_kernel,
        operands=[mine, swap(away, CORES)],
        outs=[like((16, 2 * WIDE_COLUMNS), F32)] * 3
        + [like((3, 16, channels), F32), like((16, channels), F32)]
        + [like((1, width), F32)] * 2
        + [like((3, channels), F32)],
    )
    in_g, gain_one_g, gain_two_g = in_g.transpose(1, 0, 2), gain_one_g.reshape(-1), gain_two_g.reshape(-1)
    return (mixed, tokens_grad, gain_one_g, in_g, conv_g, out_g.T, gain_two_g, gate_g, up_g, down_g.T)


def solution(mesh):
    return jax.shard_map(
        on_device,
        mesh=mesh,
        in_specs=(
            P("seq", None),
            P("seq"),
            P(),
            P(None, None, "tensor"),
            P(None, "tensor"),
            P("tensor", None),
            P(),
            P(None, "tensor"),
            P(None, "tensor"),
            P("tensor", None),
            P("seq", None),
        ),
        out_specs=(
            P("seq", None),
            P("seq", None),
            P(),
            P("seq", None, "tensor"),
            P(None, "tensor"),
            P("tensor", "seq"),
            P(),
            P("seq", "tensor"),
            P("seq", "tensor"),
            P("tensor", "seq"),
        ),
        check_vma=False,
    )
```

```python
import functools

import jax
import jax.numpy as jnp
from jax import lax
from jax.experimental import pallas as pl
from jax.experimental.pallas import tpu as pltpu
from jax.sharding import PartitionSpec as P

EPS = 1e-05
AXES = ("seq", "tensor")
BF16 = jnp.bfloat16
F32 = jnp.float32


def device_pairs(move):
    def number(y, z, x, core):
        return ((((y % 4) * 4 + z % 4) * 2 + x % 2) * 2 + core) * 2 + (x % 4) // 2

    return [
        (number(y, z, x, core), number(*move(y, z, x, core)))
        for y in range(4)
        for z in range(4)
        for x in range(4)
        for core in range(2)
    ]


ACROSS = device_pairs(lambda y, z, x, core: (y, z, (x + 2) % 4, core))
BESIDE = device_pairs(lambda y, z, x, core: (y, z, x ^ 1, core))
CORES = device_pairs(lambda y, z, x, core: (y, z, x, 1 - core))


def peer(at, pairing):
    return (at ^ 1, 3 - at, at ^ 2)[pairing]


FIRST = [
    device_pairs(
        functools.partial(
            lambda pairing, y, z, x, core: (y, peer(z, pairing), x, core)
            if core
            else (peer(y, pairing), z, x, core),
            pairing,
        )
    )
    for pairing in range(3)
]
SECOND = [
    device_pairs(
        functools.partial(
            lambda pairing, y, z, x, core: (peer(y, pairing), z, x, core)
            if core
            else (y, peer(z, pairing), x, core),
            pairing,
        )
    )
    for pairing in range(3)
]
WIDE_COLUMNS = 1152
WIDE_TILES = 27
WIDE = (14, 13)
NARROW = 8
BLOCK = (64, 128)
LONG = 3 * 10**10
SHORT = 8 * 10**9
TILES = WIDE_TILES + NARROW
WIDE_BLOCKS = (4 * WIDE[1], 4 * WIDE[0], 0)
ROUND_ONE = tuple(count + 4 * NARROW + 1 for count in WIDE_BLOCKS)


def swap(value, pairs):
    return lax.ppermute(value, AXES, pairs)


def from_behind(value, axis, steps):
    count = lax.axis_size(axis)
    leading, last = (max(0, -steps), min(count, count - steps))
    return lax.ppermute(value, axis, [(source, source + steps) for source in range(leading, last)])


def norm_scale(values):
    return lax.rsqrt(jnp.mean(values * values, axis=1, keepdims=True) + EPS)


def norm_backward(out_grad_rows, values, scale_rows, gain):
    scaled = out_grad_rows * gain
    inner = jnp.mean(scaled * values, axis=1, keepdims=True)
    return scale_rows * (scaled - values * scale_rows * scale_rows * inner)


def like(shape, dtype):
    return jax.ShapeDtypeStruct(shape, dtype)


def positions(offset):
    at = lax.axis_index("seq")
    y, z, core = at // 16, (at // 4) % 4, at % 2
    first, second = jnp.where(core == 0, y, z), jnp.where(core == 0, z, y)
    return first, second, (at // 2) % 2, core, offset


def call(body, *, operands, outs, scratch=(), offset=None, flops=0, aliases=None, where=pltpu.VMEM, scalar=None):
    whole = pl.BlockSpec(memory_space=pltpu.VMEM)
    specs = [pl.BlockSpec(memory_space=where)] * len(operands)
    if scalar is not None:
        operands, specs = [scalar, *operands], [pl.BlockSpec(memory_space=pltpu.SMEM), *specs]

    def kernel(*refs):
        if offset is None:
            body(positions(None), *refs)
        else:
            body(positions(refs[0][0:1, 0:1]), *refs[1:])

    if offset is not None:
        operands, specs = [offset, *operands], [whole, *specs]
    return pl.pallas_call(
        kernel,
        out_shape=tuple(outs),
        in_specs=specs,
        out_specs=tuple(whole for _ in outs),
        scratch_shapes=list(scratch),
        input_output_aliases=aliases or {},
        compiler_params=pltpu.CompilerParams(vmem_limit_bytes=16 * 2**20),
        cost_estimate=pl.CostEstimate(flops=flops, bytes_accessed=0, transcendentals=0),
    )(*operands)


def dot(left, right):
    return jnp.dot(left, right, preferred_element_type=F32)


def dot_rows(left, right):
    return lax.dot_general(left, right, (((1,), (1,)), ((), ())), preferred_element_type=F32)


def row_numbers(shape, first=0):
    return lax.broadcasted_iota(jnp.int32, shape, 0) + first


def valid_rows(offset, lag, shape):
    row = row_numbers(shape)
    return jnp.where((offset <= row) & (offset > row - lag), 0.0, 1.0)


def linked_rows(offset, shape, first, count):
    return jnp.where((row_numbers(shape, first) < offset) & (offset < count), 0.0, 1.0)


def load_kernel(scalars, starts, tokens, gain, weight, tail, token_rows, gain_row, weights, offset, done):
    rows, depth = tokens.shape[0], weight.shape[1] // 4
    pieces = [(gain, gain_row)]
    pieces += [(tokens.at[pl.ds(at, 128)], token_rows.at[pl.ds(at, 128)]) for at in (rows - 128, 0)]
    for k in (0, 2, 1):
        for at in range(0, weight.shape[1], depth):
            pieces.append((weight.at[k, pl.ds(at, depth)], weights.at[k, pl.ds(at, depth)]))
    copies = [
        pltpu.make_async_copy(source, target, done.at[at]) for at, (source, target) in enumerate(pieces)
    ]
    for copy in copies:
        copy.start()
    for copy in copies[:2]:
        copy.wait()
    offset[...] = jnp.full(offset.shape, starts[0], jnp.int32)
    values = token_rows[rows - 16 :].astype(F32)
    normed = (values * norm_scale(values) * gain_row[...]).astype(BF16)
    for copy in copies[2:11]:
        copy.wait()
    gated = (dot(normed, weights[0]) * dot(normed, weights[2])).astype(BF16).astype(F32)
    tail[...] = (gated * linked_rows(starts[0], gated.shape, rows - 16, rows)).astype(BF16)
    for copy in copies[11:]:
        copy.wait()


def project_kernel(scalars, tokens, gain, weights, normed, parts, gated):
    values = tokens[...].astype(F32)
    normed[...] = (values * norm_scale(values) * gain[...]).astype(BF16)
    for k in range(3):
        parts[k] = dot(normed[...], weights[k])
    gated[...] = (parts[0] * parts[2]).astype(BF16)


def behind(gated, incoming, lag):
    moved = pltpu.roll(gated, lag, 0)
    row = row_numbers(gated.shape)
    for at in range(lag):
        moved = jnp.where(row == at, incoming[16 - lag + at : 17 - lag + at], moved)
    return moved


def mix_kernel(scalars, gated, incoming, parts, taps, weight, conv, ymix, branch):
    values = gated[...].astype(F32)
    before = incoming[...].astype(F32)
    total = taps[0:1] * values
    for lag in (1, 2):
        total = total + taps[lag : lag + 1] * behind(values, before, lag) * valid_rows(
            scalars[4], lag, values.shape
        )
    conv[...] = total
    ymix[...] = (parts[1] * total).astype(BF16)
    branch[...] = dot(ymix[...], weight[...]).astype(BF16)


def away_half(value, core):
    half = value.shape[-1] // 2
    return jnp.where(core == 0, value[..., half:], value[..., :half])


def hidden_kernel(scalars, cot, weight, out):
    for at in range(0, weight.shape[0], 256):
        out[:, at : at + 256] = dot_rows(cot[...], weight[at : at + 256])


def down_kernel(scalars, hidden, weight, out):
    out[...] = dot(hidden[...], weight[...]).astype(BF16)


def feed_kernel(
    scalars,
    tokens,
    branch,
    other,
    gain,
    gate,
    up,
    hidden_grad,
    normed_one,
    ymix,
    resid,
    normed,
    hidden,
    gate_back,
    up_back,
    shared,
    shared_early,
):
    resid[...] = tokens[...].astype(F32) + (branch[...].astype(F32) + other[...].astype(F32))
    normed[...] = (resid[...] * norm_scale(resid[...]) * gain[...]).astype(BF16)
    values = normed[...]
    for at in range(0, gate.shape[1], 256):
        columns = slice(at, at + 256)
        gate_act, up_act = dot(values, gate[:, columns]), dot(values, up[:, columns])
        back = hidden_grad[:, columns]
        sigmoid_gate = jax.nn.sigmoid(gate_act)
        swish = gate_act * sigmoid_gate
        hidden[:, columns] = (swish * up_act).astype(BF16)
        up_back[:, columns] = (back * swish).astype(BF16)
        slope = sigmoid_gate * (1.0 + gate_act * (1.0 - sigmoid_gate))
        gate_back[:, columns] = (back * up_act * slope).astype(BF16)
    away = pl.ds(pl.multiple_of((1 - scalars[3]) * WIDE_COLUMNS, 128), WIDE_COLUMNS)
    for k, value in enumerate((hidden, gate_back, up_back)):
        shared[:, k * WIDE_COLUMNS : (k + 1) * WIDE_COLUMNS] = value[:, away]
    shared[:, 3 * WIDE_COLUMNS :] = values
    shared_early[:, : normed.shape[1]] = normed_one[...]
    shared_early[:, normed.shape[1] :] = away_half(ymix[...], scalars[3])


def part_kernel(scalars, gate_back, up_back, gate, up, part):
    part[...] = (dot_rows(gate_back[...], gate[...]) + dot_rows(up_back[...], up[...])).astype(BF16)


def second_norm(part, other, resid, gain, cot):
    back = part.astype(F32) + other.astype(F32)
    scale = norm_scale(resid)
    return back, scale, cot.astype(F32) + norm_backward(back, resid, scale, gain)


def edge_kernel(scalars, part, other, resid, gain, cot, weight, parts, taps, edge):
    top = slice(0, 16)
    _, _, grad = second_norm(part[top], other[top], resid[top], gain[...], cot[top])
    conv_back = dot_rows(grad.astype(BF16), weight[...]) * parts[1, top]
    one = conv_back * valid_rows(scalars[4], 1, conv_back.shape) * taps[1:2]
    two = conv_back * valid_rows(scalars[4], 2, conv_back.shape) * taps[2:3]
    row = row_numbers((8, conv_back.shape[1]))
    edge[...] = jnp.where(row == 6, two[0:1], 0.0) + jnp.where(row == 7, one[0:1] + two[1:2], 0.0)


def middle_kernel(
    scalars, part, other, resid, gain, cot, weight, parts, taps, conv, gated, incoming, grad, low, gain_grad, c_back, gated_back, tap_grads
):
    back, scale, resid_grad = second_norm(part[...], other[...], resid[...], gain[...], cot[...])
    gain_grad[...] = jnp.sum(back * resid[...] * scale, axis=0, keepdims=True)
    grad[...] = resid_grad
    low[...] = resid_grad.astype(BF16)
    ymix_back = dot_rows(low[...], weight[...])
    c_back[...] = (ymix_back * conv[...]).astype(BF16)
    conv_back = ymix_back * parts[1]
    values, before = gated[...].astype(F32), incoming[...].astype(F32)
    rows = values.shape[0]
    tap_grads[0:1] = jnp.sum(conv_back * values, axis=0, keepdims=True)
    total = conv_back * taps[0:1]
    row = row_numbers(values.shape)
    for lag in (1, 2):
        term = conv_back * valid_rows(scalars[4], lag, values.shape)
        tap_grads[lag : lag + 1] = jnp.sum(term * behind(values, before, lag), axis=0, keepdims=True)
        moved = pltpu.roll(term * taps[lag : lag + 1], rows - lag, 0)
        total = total + jnp.where(row < rows - lag, moved, 0.0)
    gated_back[...] = total


def last_kernel(
    scalars,
    gated_back,
    returned,
    parts,
    c_back,
    weight,
    tokens,
    gain_two_grad,
    tap_grads,
    resid_low,
    backs,
    shared,
    part,
    gain_part,
    small,
):
    rows = gated_back.shape[0]
    links = linked_rows(scalars[4], returned.shape, rows - 8, rows)
    end = gated_back[rows - 8 :] + returned[...] * links
    total = jnp.concatenate([gated_back[: rows - 8], end], 0)
    backs[0] = (total * parts[2]).astype(BF16)
    backs[1] = c_back[...]
    backs[2] = (total * parts[0]).astype(BF16)
    for k in range(3):
        shared[4 + k] = away_half(backs[k], scalars[3])
    for at in range(4):
        shared[at] = resid_low[:, at * 256 : at * 256 + 256]
    grad = dot_rows(backs[0], weight[0]) + dot_rows(backs[1], weight[1]) + dot_rows(backs[2], weight[2])
    part[...] = grad.astype(BF16)
    values = tokens[...].astype(F32)
    gain_grad = jnp.sum(grad * values * norm_scale(values), axis=0, keepdims=True)
    for at in range(8):
        lanes = slice(at * 128, at * 128 + 128)
        gain_part[at : at + 1] = gain_grad[:, lanes]
        small[8 + at : 9 + at] = gain_two_grad[:, lanes]
    for lag in range(3):
        for at in range(4):
            row = 16 + 4 * lag + at
            small[row : row + 1] = tap_grads[lag : lag + 1, at * 128 : at * 128 + 128]
    small[:8] = jnp.zeros((8, 128), F32)
    small[28:32] = jnp.zeros((4, 128), F32)


def fill_transposed(left, own, other):
    for at in range(0, own.shape[1], 256):
        left[at : at + 256, :256] = own[:, at : at + 256].T
        left[at : at + 256, 256:] = other[:, at : at + 256].T


def chunk_rows(left, core, chunk):
    wide, slim = jnp.where(core == 0, 256, 64), jnp.where(core == 0, 64, 256)
    return jnp.concatenate(
        [left[pl.ds(pl.multiple_of(chunk * wide + at * slim, 64), 64)] for at in range(4)], 0
    )


def store_blocks(value, target, base, tiles, tile):
    value = value.astype(BF16)
    for chunk in range(4):
        for column in range(value.shape[1] // 128):
            target[base + chunk * tiles + tile + column] = value[
                chunk * 64 : chunk * 64 + 64, column * 128 : column * 128 + 128
            ]


def wide_runs(kind):
    at, end = (0, WIDE[0]) if kind == 0 else (WIDE[0], WIDE_TILES)
    first = at
    while at < end:
        matrix, tile = divmod(at, WIDE_COLUMNS // 128)
        count = min(2, WIDE_COLUMNS // 128 - tile, end - at)
        yield matrix, tile * 128, count * 128, at - first
        at += count


def wide_piece(scalars, kind, lefts, own, shared, send, keep):
    at, core = scalars[0], scalars[3]
    first, second = peer(at, kind), peer(at, 1 - kind)
    chunks = (at, second, first, peer(first, 1 - kind))
    for slot, chunk in enumerate(chunks):
        target = keep if slot < 2 else send
        rows = {}
        for matrix, column, width, tile in wide_runs(kind):
            if (matrix == 0) not in rows:
                rows[matrix == 0] = chunk_rows(lefts[matrix], core, chunk)
            left = rows[matrix == 0]
            mine = pl.ds(pl.multiple_of(core * WIDE_COLUMNS + column, 128), width)
            away = matrix * WIDE_COLUMNS + column
            value = dot(left[:, :256], own[matrix][:, mine])
            value = value + dot(left[:, 256:], shared[:, away : away + width])
            store_blocks(value, target, (slot % 2) * 4 * WIDE[kind], WIDE[kind], tile)


def wide_first_kernel(scalars, two, cot, cot_other, hidden, gate_back, shared, send, keep, left_two, left_cot):
    fill_transposed(left_cot, cot, cot_other)
    fill_transposed(left_two, two, shared.at[:, 3 * WIDE_COLUMNS :])
    wide_piece(scalars, 0, (left_cot, left_two), (hidden, gate_back), shared, send, keep)


def wide_second_kernel(scalars, left_two, gate_back, up_back, shared, send, keep):
    wide_piece(scalars, 1, (None, left_two, left_two), (None, gate_back, up_back), shared, send, keep)


def narrow_kernel(scalars, one, shared, low, late_other, backs, ymix, *refs):
    (small, gain, gain_other), outs, (new_small, left_one, left_low) = refs[:3], refs[3:7], refs[7:]
    new_small[:8] = gain[...] + gain_other[...]
    new_small[8:] = small[8:]
    for pairing in range(3):
        split_small(new_small[...], outs[pairing], ROUND_ONE[pairing] - 1)
    width = one.shape[1]
    one_other, ymix_other = shared.at[:, :width], shared.at[:, width:]
    for at in range(0, width, 256):
        left_one[at : at + 256, :256] = one[:, at : at + 256].T
        left_one[at : at + 256, 256:] = one_other[:, at : at + 256].T
        left_low[at : at + 256, :256] = low[:, at : at + 256].T
        left_low[at : at + 256, 256:] = late_other[at // 256].T
    mine = pl.ds(pl.multiple_of(scalars[3] * 256, 256), 256)
    for slot in range(4):
        chunk = peer(scalars[0], slot) if slot < 3 else scalars[0]
        for kind in range(4):
            left, own, other = (
                (left_one, backs[kind, :, mine], late_other[4 + kind])
                if kind < 3
                else (left_low, ymix[:, mine], ymix_other[...])
            )
            rows = chunk_rows(left, scalars[3], chunk)
            value = dot(rows[:, :256], own) + dot(rows[:, 256:], other)
            store_blocks(value, outs[slot], WIDE_BLOCKS[slot] if slot < 3 else 0, NARROW, 2 * kind)


def split_small(value, target, at):
    high = value.astype(BF16)
    target[at, :32] = high
    target[at, 32:] = (value - high.astype(F32)).astype(BF16)


def join_small(source, at):
    return source[at, :32].astype(F32) + source[at, 32:].astype(F32)


def rounded_small(value):
    high = value.astype(BF16)
    return high.astype(F32) + (value - high.astype(F32)).astype(BF16).astype(F32)


def sum_small(value, near, far, cross):
    return (rounded_small(value) + cross) + (near + far)


def far_kernel(scalars, mine, got, total, small):
    total[...] = mine[...].astype(F32) + got[: 4 * NARROW].astype(F32)
    small[...] = join_small(got, 4 * NARROW)


def first_kernel(scalars, *refs):
    gots, keeps, sends, wide_keeps = refs[:2], refs[2:4], refs[6:8], refs[8:]
    for kind in range(2):
        half = 4 * WIDE[kind]
        for chunk in range(4):
            at = slice(chunk * WIDE[kind], (chunk + 1) * WIDE[kind])
            after = slice(half + chunk * WIDE[kind], half + (chunk + 1) * WIDE[kind])
            wide_keeps[kind][at] = (keeps[kind][at].astype(F32) + gots[kind][at].astype(F32)).astype(BF16)
            sends[1 - kind][at] = (keeps[kind][after].astype(F32) + gots[kind][after].astype(F32)).astype(BF16)


def second_kernel(scalars, *refs):
    gots, wide_in, (narrow, small, cross) = refs[:2], refs[2:4], refs[4:7]
    sends, (keep, new_small) = refs[7:10], refs[10:]

    def fill(chunk, target):
        tile = 0
        for kind in range(2):
            at = pl.ds(chunk * WIDE[kind], WIDE[kind])
            value = wide_in[kind][at].astype(F32) + gots[1 - kind][at].astype(F32)
            target[tile : tile + WIDE[kind]] = value.astype(BF16)
            tile += WIDE[kind]
        value = narrow[pl.ds(chunk * NARROW, NARROW)]
        for pairing in range(2):
            value = value + gots[pairing][pl.ds(WIDE_BLOCKS[pairing] + chunk * NARROW, NARROW)].astype(F32)
        target[tile : tile + NARROW] = value.astype(BF16)

    near, far = (join_small(got, count - 1) for got, count in zip(gots, ROUND_ONE))
    value = sum_small(small[...], near, far, cross[...])
    new_small[...] = value
    for pairing in range(3):
        fill(peer(scalars[1], pairing), sends[pairing])
        split_small(value, sends[pairing], TILES)
    fill(scalars[1], keep)


def third_kernel(scalars, *refs):
    gots, (kept, small), (send, keep) = refs[:3], refs[3:5], refs[5:]
    here = scalars[2]
    for first in range(0, TILES, 7):
        at = slice(first, first + 7)
        value = kept[at].astype(F32)
        for got in gots:
            value = value + got[at].astype(F32)
        zero, one = value[:, :32], value[:, 32:]
        keep[at] = jnp.where(here == 0, zero, one)
        send[at] = jnp.where(here == 0, one, zero).astype(BF16)
    value = sum_small(small[...], *(join_small(got, TILES) for got in gots))
    high = value.astype(BF16)
    low = (value - high.astype(F32)).astype(BF16)
    send[TILES] = high
    send[TILES + 1] = low
    keep[TILES] = high.astype(F32)
    keep[TILES + 1] = low.astype(F32)


def cores_kernel(scalars, keep, got, mine, away):
    core = scalars[3]
    total = keep[:TILES] + got[:TILES].astype(F32)
    zero, one = total[:, :16], total[:, 16:]
    mine[:TILES] = jnp.where(core == 0, zero, one)
    away[:TILES] = jnp.where(core == 0, one, zero)
    small = (keep[TILES] + keep[TILES + 1]) + (got[TILES].astype(F32) + got[TILES + 1].astype(F32))
    for target in (mine, away):
        target[TILES] = small[:16]
        target[TILES + 1] = small[16:]


def outputs_kernel(scalars, mine, got, down, gate, up, inner, out, gain_one, gain_two, taps):
    core = scalars[3]

    def place(target, tile, column, columns):
        zero, one = jnp.where(core == 0, mine[tile], got[tile]), jnp.where(core == 0, got[tile], mine[tile])
        target[:, column : column + 128] = zero
        target[:, columns + column : columns + column + 128] = one

    for matrix, target in enumerate((down, gate, up)):
        for tile in range(WIDE_COLUMNS // 128):
            place(target, matrix * (WIDE_COLUMNS // 128) + tile, tile * 128, WIDE_COLUMNS)
    for kind in range(4):
        for column in range(2):
            place(inner.at[kind] if kind < 3 else out, WIDE_TILES + 2 * kind + column, column * 128, 256)
    gains = mine[TILES] + got[TILES]
    rest = mine[TILES + 1] + got[TILES + 1]
    for at in range(8):
        lanes = slice(at * 128, at * 128 + 128)
        gain_one[:, lanes] = gains[at : at + 1]
        gain_two[:, lanes] = gains[8 + at : 9 + at]
    for lag in range(3):
        for at in range(4):
            row = 4 * lag + at
            taps[lag : lag + 1, at * 128 : at * 128 + 128] = rest[row : row + 1]


def swap_round(sends, pairings):
    return [swap(value, pairs) for value, pairs in zip(sends, pairings)]


def blocks(counts):
    return [like((count, *BLOCK), BF16) for count in counts]


def on_device(
    tokens,
    starts,
    gain_one,
    in_weight,
    conv_weight,
    out_weight,
    gain_two,
    gate_weight,
    up_weight,
    down_weight,
    cotangent,
):
    core = lax.axis_index("seq") % 2
    run = call
    rows, width = tokens.shape
    channels = conv_weight.shape[1]
    in_parts = in_weight.transpose(1, 0, 2)
    gain_one_row, gain_two_row = gain_one.reshape(1, -1), gain_two.reshape(1, -1)

    def share(value):
        return swap(value, CORES)

    tail, tokens_here, gain_here, weights_here, offset = run(
        load_kernel,
        operands=[
            pltpu.with_memory_space_constraint(value, pltpu.HBM) for value in (tokens, gain_one_row, in_parts)
        ],
        scalar=starts,
        outs=[
            like((16, channels), BF16),
            like((rows, width), BF16),
            like((1, width), F32),
            like((3, width, channels), BF16),
            like((8, 128), jnp.int32),
        ],
        scratch=[pltpu.SemaphoreType.DMA((15,))],
        where=pltpu.HBM,
    )
    incoming = from_behind(tail, "seq", 1)
    cotangent_other = share(cotangent)
    incoming, cotangent_other = lax.optimization_barrier((incoming, cotangent_other))
    normed_one, parts, gated = run(
        project_kernel,
        operands=[tokens_here, gain_here, weights_here],
        outs=[like((rows, width), BF16), like((3, rows, channels), F32), like((rows, channels), BF16)],
    )
    conv, ymix, branch = run(
        mix_kernel,
        offset=offset,
        operands=[gated, incoming, parts, conv_weight, out_weight],
        outs=[like((rows, channels), F32), like((rows, channels), BF16), like((rows, width), BF16)],
    )
    branch, cotangent_late = lax.optimization_barrier((branch, cotangent))
    branch_other = swap(branch, ACROSS)
    units = gate_weight.shape[1]
    hidden_grad = run(
        hidden_kernel,
        operands=[cotangent_late, down_weight],
        outs=[like((rows, units), F32)],
        flops=LONG,
    )[0]
    branch_other, hidden_grad = lax.optimization_barrier((branch_other, hidden_grad))
    resid, normed_two, hidden, gate_back, up_back, shared, shared_early = run(
        feed_kernel,
        operands=[tokens, branch, branch_other, gain_two_row, gate_weight, up_weight, hidden_grad]
        + [normed_one, ymix],
        outs=[like((rows, width), F32), like((rows, width), BF16)]
        + [like((rows, units), BF16)] * 3
        + [like((rows, 3 * WIDE_COLUMNS + width), BF16), like((rows, width + channels // 2), BF16)],
    )
    shared_other = share(shared)
    norm_two_part = run(
        part_kernel, operands=[gate_back, up_back, gate_weight, up_weight], outs=[like((rows, width), BF16)]
    )[0]
    norm_two_other = swap(norm_two_part, ACROSS)
    first_send, first_keep, left_two = run(
        wide_first_kernel,
        operands=[normed_two, cotangent, cotangent_other, hidden, gate_back, shared_other],
        outs=blocks([8 * WIDE[0]] * 2) + [like((width, 2 * rows), BF16)],
        scratch=[pltpu.VMEM((width, 2 * rows), BF16)],
    )
    second_send, second_keep = run(
        wide_second_kernel,
        operands=[left_two, gate_back, up_back, shared_other],
        outs=blocks([8 * WIDE[1]] * 2),
    )
    sends, keeps = [first_send, second_send], [first_keep, second_keep]
    down_part = run(down_kernel, operands=[hidden, down_weight], outs=[like((rows, width), BF16)])[0]
    early_other = share(shared_early)
    norm_two_other, keeps[1], down_part, early_other = lax.optimization_barrier(
        (norm_two_other, keeps[1], down_part, early_other)
    )
    gots = swap_round(sends, FIRST)

    edge_operands = [norm_two_part, norm_two_other, resid, gain_two_row, cotangent, out_weight, parts, conv_weight]
    edge = run(edge_kernel, offset=offset, operands=edge_operands, outs=[like((8, channels), F32)])[0]
    returned = from_behind(edge, "seq", -1)
    resid_grad, resid_low, gain_two_grad, c_back, gated_back, tap_grads = run(
        middle_kernel,
        offset=offset,
        operands=edge_operands + [conv, gated, incoming],
        outs=[
            like((rows, width), F32),
            like((rows, width), BF16),
            like((1, width), F32),
            like((rows, channels), BF16),
            like((rows, channels), F32),
            like((3, channels), F32),
        ],
        flops=SHORT,
    )
    backs, shared, norm_one_part, gain_part, small = run(
        last_kernel,
        offset=offset,
        operands=[gated_back, returned, parts, c_back, in_parts, tokens, gain_two_grad, tap_grads]
        + [resid_low],
        outs=[
            like((3, rows, channels), BF16),
            like((7, rows, 256), BF16),
            like((rows, width), BF16),
            like((8, 128), F32),
            like((32, 128), F32),
        ],
    )
    gain_other = swap(gain_part, ACROSS)
    *sends, narrow, small = run(
        narrow_kernel,
        operands=[normed_one, early_other, resid_low, share(shared), backs, ymix, small, gain_part, gain_other],
        outs=blocks(ROUND_ONE) + blocks([4 * NARROW]) + [like((32, 128), F32)],
        scratch=[pltpu.VMEM((width, 2 * rows), BF16)] * 2,
    )
    narrow, cross = run(
        far_kernel,
        operands=[narrow, swap(sends.pop(), FIRST[2])],
        outs=[like((4 * NARROW, *BLOCK), F32), like((32, 128), F32)],
        flops=LONG,
    )
    results = run(
        first_kernel,
        operands=gots + keeps + sends,
        aliases={4: 0, 5: 1},
        outs=blocks(ROUND_ONE[:2]) + blocks([4 * count for count in WIDE]),
    )
    sends, keeps = list(results[:2]), list(results[2:])
    gots = swap_round(sends, FIRST)
    norm_one_other = swap(norm_one_part, ACROSS)
    gots[0], norm_one_other = lax.optimization_barrier((gots[0], norm_one_other))
    results = run(
        second_kernel,
        operands=gots + keeps + [narrow, small, cross],
        outs=blocks([TILES + 1] * 3 + [TILES]) + [like((32, 128), F32)],
    )
    sends, keep, small = list(results[:3]), results[3], results[4]
    gots = swap_round(sends, SECOND)
    small, down_part = lax.optimization_barrier((small, down_part))
    down_other = swap(down_part, ACROSS)
    gots[0], down_other = lax.optimization_barrier((gots[0], down_other))
    beside, kept = run(
        third_kernel,
        operands=gots + [keep, small],
        outs=[like((TILES + 2, 32, 128), BF16), like((TILES + 2, 32, 128), F32)],
    )
    beside = swap(beside, BESIDE)
    mixed = (resid + (down_part.astype(F32) + down_other.astype(F32))).astype(BF16)
    inputs = tokens.astype(F32)
    norm_one_back = norm_one_part.astype(F32) + norm_one_other.astype(F32)
    tokens_grad = resid_grad + norm_backward(norm_one_back, inputs, norm_scale(inputs), gain_one)
    beside, mixed, tokens_grad = lax.optimization_barrier((beside, mixed, tokens_grad))
    mine, away = run(
        cores_kernel,
        operands=[kept, beside],
        outs=[like((TILES + 2, 16, 128), F32)] * 2,
    )
    down_g, gate_g, up_g, in_g, out_g, gain_one_g, gain_two_g, conv_g = run(
        outputs_kernel,
        operands=[mine, swap(away, CORES)],
        outs=[like((16, 2 * WIDE_COLUMNS), F32)] * 3
        + [like((3, 16, channels), F32), like((16, channels), F32)]
        + [like((1, width), F32)] * 2
        + [like((3, channels), F32)],
    )
    in_g, gain_one_g, gain_two_g = in_g.transpose(1, 0, 2), gain_one_g.reshape(-1), gain_two_g.reshape(-1)
    return (mixed, tokens_grad, gain_one_g, in_g, conv_g, out_g.T, gain_two_g, gate_g, up_g, down_g.T)


def solution(mesh):
    return jax.shard_map(
        on_device,
        mesh=mesh,
        in_specs=(
            P("seq", None),
            P("seq"),
            P(),
            P(None, None, "tensor"),
            P(None, "tensor"),
            P("tensor", None),
            P(),
            P(None, "tensor"),
            P(None, "tensor"),
            P("tensor", None),
            P("seq", None),
        ),
        out_specs=(
            P("seq", None),
            P("seq", None),
            P(),
            P("seq", None, "tensor"),
            P(None, "tensor"),
            P("tensor", "seq"),
            P(),
            P("seq", "tensor"),
            P("seq", "tensor"),
            P("tensor", "seq"),
        ),
        check_vma=False,
    )
```

```python
import functools

import jax
import jax.numpy as jnp
from jax import lax
from jax.experimental import pallas as pl
from jax.experimental.pallas import tpu as pltpu
from jax.sharding import PartitionSpec as P

EPS = 1e-05
AXES = ("seq", "tensor")
BF16 = jnp.bfloat16
F32 = jnp.float32


def device_pairs(move):
    def number(y, z, x, core):
        return ((((y % 4) * 4 + z % 4) * 2 + x % 2) * 2 + core) * 2 + (x % 4) // 2

    return [
        (number(y, z, x, core), number(*move(y, z, x, core)))
        for y in range(4)
        for z in range(4)
        for x in range(4)
        for core in range(2)
    ]


ACROSS = device_pairs(lambda y, z, x, core: (y, z, (x + 2) % 4, core))
BESIDE = device_pairs(lambda y, z, x, core: (y, z, x ^ 1, core))
SKEW = device_pairs(lambda y, z, x, core: (y, z, (x ^ 1) ^ 2, core))
CORES = device_pairs(lambda y, z, x, core: (y, z, x, 1 - core))


def peer(at, pairing):
    return (at ^ 1, 3 - at, at ^ 2)[pairing]


FIRST = [
    device_pairs(
        functools.partial(
            lambda pairing, y, z, x, core: (y, peer(z, pairing), x, core)
            if core
            else (peer(y, pairing), z, x, core),
            pairing,
        )
    )
    for pairing in range(3)
]
SECOND = [
    device_pairs(
        functools.partial(
            lambda pairing, y, z, x, core: (peer(y, pairing), z, x, core)
            if core
            else (y, peer(z, pairing), x, core),
            pairing,
        )
    )
    for pairing in range(3)
]
WIDE_COLUMNS = 1152
WIDE_TILES = 27
WIDE = (14, 13)
NARROW = 8
BLOCK = (64, 128)
LONG = 3 * 10**10
SHORT = 8 * 10**9
TILES = WIDE_TILES + NARROW
WIDE_BLOCKS = (4 * WIDE[1], 4 * WIDE[0], 0)
ROUND_ONE = tuple(count + 4 * NARROW + 1 for count in WIDE_BLOCKS)


def swap(value, pairs):
    return lax.ppermute(value, AXES, pairs)


def from_behind(value, axis, steps):
    count = lax.axis_size(axis)
    leading, last = (max(0, -steps), min(count, count - steps))
    return lax.ppermute(value, axis, [(source, source + steps) for source in range(leading, last)])


def norm_scale(values):
    return lax.rsqrt(jnp.mean(values * values, axis=1, keepdims=True) + EPS)


def norm_backward(out_grad_rows, values, scale_rows, gain):
    scaled = out_grad_rows * gain
    inner = jnp.mean(scaled * values, axis=1, keepdims=True)
    return scale_rows * (scaled - values * scale_rows * scale_rows * inner)


def like(shape, dtype):
    return jax.ShapeDtypeStruct(shape, dtype)


def positions(offset):
    at = lax.axis_index("seq")
    y, z, core = at // 16, (at // 4) % 4, at % 2
    first, second = jnp.where(core == 0, y, z), jnp.where(core == 0, z, y)
    return first, second, (at // 2) % 2, core, offset


def call(body, *, operands, outs, scratch=(), offset=None, flops=0, aliases=None, where=pltpu.VMEM, scalar=None):
    whole = pl.BlockSpec(memory_space=pltpu.VMEM)
    specs = [pl.BlockSpec(memory_space=where)] * len(operands)
    if scalar is not None:
        operands, specs = [scalar, *operands], [pl.BlockSpec(memory_space=pltpu.SMEM), *specs]

    def kernel(*refs):
        if offset is None:
            body(positions(None), *refs)
        else:
            body(positions(refs[0][0:1, 0:1]), *refs[1:])

    if offset is not None:
        operands, specs = [offset, *operands], [whole, *specs]
    return pl.pallas_call(
        kernel,
        out_shape=tuple(outs),
        in_specs=specs,
        out_specs=tuple(whole for _ in outs),
        scratch_shapes=list(scratch),
        input_output_aliases=aliases or {},
        compiler_params=pltpu.CompilerParams(vmem_limit_bytes=16 * 2**20),
        cost_estimate=pl.CostEstimate(flops=flops, bytes_accessed=0, transcendentals=0),
    )(*operands)


def dot(left, right):
    return jnp.dot(left, right, preferred_element_type=F32)


def dot_rows(left, right):
    return lax.dot_general(left, right, (((1,), (1,)), ((), ())), preferred_element_type=F32)


def row_numbers(shape, first=0):
    return lax.broadcasted_iota(jnp.int32, shape, 0) + first


def valid_rows(offset, lag, shape):
    row = row_numbers(shape)
    return jnp.where((offset <= row) & (offset > row - lag), 0.0, 1.0)


def linked_rows(offset, shape, first, count):
    return jnp.where((row_numbers(shape, first) < offset) & (offset < count), 0.0, 1.0)


def load_kernel(scalars, starts, tokens, gain, weight, tail, token_rows, gain_row, weights, offset, done):
    rows, depth = tokens.shape[0], weight.shape[1] // 4
    pieces = [(gain, gain_row)]
    pieces += [(tokens.at[pl.ds(at, 128)], token_rows.at[pl.ds(at, 128)]) for at in (rows - 128, 0)]
    for k in (0, 2, 1):
        for at in range(0, weight.shape[1], depth):
            pieces.append((weight.at[k, pl.ds(at, depth)], weights.at[k, pl.ds(at, depth)]))
    copies = [
        pltpu.make_async_copy(source, target, done.at[at]) for at, (source, target) in enumerate(pieces)
    ]
    for copy in copies:
        copy.start()
    for copy in copies[:2]:
        copy.wait()
    offset[...] = jnp.full(offset.shape, starts[0], jnp.int32)
    values = token_rows[rows - 16 :].astype(F32)
    normed = (values * norm_scale(values) * gain_row[...]).astype(BF16)
    for copy in copies[2:11]:
        copy.wait()
    gated = (dot(normed, weights[0]) * dot(normed, weights[2])).astype(BF16).astype(F32)
    tail[...] = (gated * linked_rows(starts[0], gated.shape, rows - 16, rows)).astype(BF16)
    for copy in copies[11:]:
        copy.wait()


def project_kernel(scalars, tokens, gain, weights, normed, parts, gated):
    values = tokens[...].astype(F32)
    normed[...] = (values * norm_scale(values) * gain[...]).astype(BF16)
    for k in range(3):
        parts[k] = dot(normed[...], weights[k])
    gated[...] = (parts[0] * parts[2]).astype(BF16)


def behind(gated, incoming, lag):
    moved = pltpu.roll(gated, lag, 0)
    row = row_numbers(gated.shape)
    for at in range(lag):
        moved = jnp.where(row == at, incoming[16 - lag + at : 17 - lag + at], moved)
    return moved


def mix_kernel(scalars, gated, incoming, parts, taps, weight, conv, ymix, branch):
    values = gated[...].astype(F32)
    before = incoming[...].astype(F32)
    total = taps[0:1] * values
    for lag in (1, 2):
        total = total + taps[lag : lag + 1] * behind(values, before, lag) * valid_rows(
            scalars[4], lag, values.shape
        )
    conv[...] = total
    ymix[...] = (parts[1] * total).astype(BF16)
    branch[...] = dot(ymix[...], weight[...]).astype(BF16)


def away_half(value, core):
    half = value.shape[-1] // 2
    return jnp.where(core == 0, value[..., half:], value[..., :half])


def hidden_kernel(scalars, cot, weight, out):
    for at in range(0, weight.shape[0], 256):
        out[:, at : at + 256] = dot_rows(cot[...], weight[at : at + 256])


def down_kernel(scalars, hidden, weight, out):
    out[...] = dot(hidden[...], weight[...]).astype(BF16)


def feed_kernel(
    scalars,
    tokens,
    branch,
    other,
    gain,
    gate,
    up,
    hidden_grad,
    normed_one,
    ymix,
    resid,
    normed,
    hidden,
    gate_back,
    up_back,
    shared,
    shared_early,
):
    resid[...] = tokens[...].astype(F32) + (branch[...].astype(F32) + other[...].astype(F32))
    normed[...] = (resid[...] * norm_scale(resid[...]) * gain[...]).astype(BF16)
    values = normed[...]
    for at in range(0, gate.shape[1], 256):
        columns = slice(at, at + 256)
        gate_act, up_act = dot(values, gate[:, columns]), dot(values, up[:, columns])
        back = hidden_grad[:, columns]
        sigmoid_gate = jax.nn.sigmoid(gate_act)
        swish = gate_act * sigmoid_gate
        hidden[:, columns] = (swish * up_act).astype(BF16)
        up_back[:, columns] = (back * swish).astype(BF16)
        slope = sigmoid_gate * (1.0 + gate_act * (1.0 - sigmoid_gate))
        gate_back[:, columns] = (back * up_act * slope).astype(BF16)
    away = pl.ds(pl.multiple_of((1 - scalars[3]) * WIDE_COLUMNS, 128), WIDE_COLUMNS)
    for k, value in enumerate((hidden, gate_back, up_back)):
        shared[:, k * WIDE_COLUMNS : (k + 1) * WIDE_COLUMNS] = value[:, away]
    shared[:, 3 * WIDE_COLUMNS :] = values
    shared_early[:, : normed.shape[1]] = normed_one[...]
    shared_early[:, normed.shape[1] :] = away_half(ymix[...], scalars[3])


def part_kernel(scalars, gate_back, up_back, gate, up, part):
    part[...] = (dot_rows(gate_back[...], gate[...]) + dot_rows(up_back[...], up[...])).astype(BF16)


def second_norm(part, other, resid, gain, cot):
    back = part.astype(F32) + other.astype(F32)
    scale = norm_scale(resid)
    return back, scale, cot.astype(F32) + norm_backward(back, resid, scale, gain)


def edge_kernel(scalars, part, other, resid, gain, cot, weight, parts, taps, edge):
    top = slice(0, 16)
    _, _, grad = second_norm(part[top], other[top], resid[top], gain[...], cot[top])
    conv_back = dot_rows(grad.astype(BF16), weight[...]) * parts[1, top]
    one = conv_back * valid_rows(scalars[4], 1, conv_back.shape) * taps[1:2]
    two = conv_back * valid_rows(scalars[4], 2, conv_back.shape) * taps[2:3]
    row = row_numbers((8, conv_back.shape[1]))
    edge[...] = jnp.where(row == 6, two[0:1], 0.0) + jnp.where(row == 7, one[0:1] + two[1:2], 0.0)


def middle_kernel(
    scalars, part, other, resid, gain, cot, weight, parts, taps, conv, gated, incoming, grad, low, gain_grad, c_back, gated_back, tap_grads
):
    back, scale, resid_grad = second_norm(part[...], other[...], resid[...], gain[...], cot[...])
    gain_grad[...] = jnp.sum(back * resid[...] * scale, axis=0, keepdims=True)
    grad[...] = resid_grad
    low[...] = resid_grad.astype(BF16)
    ymix_back = dot_rows(low[...], weight[...])
    c_back[...] = (ymix_back * conv[...]).astype(BF16)
    conv_back = ymix_back * parts[1]
    values, before = gated[...].astype(F32), incoming[...].astype(F32)
    rows = values.shape[0]
    tap_grads[0:1] = jnp.sum(conv_back * values, axis=0, keepdims=True)
    total = conv_back * taps[0:1]
    row = row_numbers(values.shape)
    for lag in (1, 2):
        term = conv_back * valid_rows(scalars[4], lag, values.shape)
        tap_grads[lag : lag + 1] = jnp.sum(term * behind(values, before, lag), axis=0, keepdims=True)
        moved = pltpu.roll(term * taps[lag : lag + 1], rows - lag, 0)
        total = total + jnp.where(row < rows - lag, moved, 0.0)
    gated_back[...] = total


def last_kernel(
    scalars,
    gated_back,
    returned,
    parts,
    c_back,
    weight,
    tokens,
    gain_two_grad,
    tap_grads,
    resid_low,
    backs,
    shared,
    part,
    small,
):
    rows = gated_back.shape[0]
    links = linked_rows(scalars[4], returned.shape, rows - 8, rows)
    end = gated_back[rows - 8 :] + returned[...] * links
    total = jnp.concatenate([gated_back[: rows - 8], end], 0)
    backs[0] = (total * parts[2]).astype(BF16)
    backs[1] = c_back[...]
    backs[2] = (total * parts[0]).astype(BF16)
    for k in range(3):
        shared[4 + k] = away_half(backs[k], scalars[3])
    for at in range(4):
        shared[at] = resid_low[:, at * 256 : at * 256 + 256]
    grad = dot_rows(backs[0], weight[0]) + dot_rows(backs[1], weight[1]) + dot_rows(backs[2], weight[2])
    part[...] = grad.astype(BF16)
    values = tokens[...].astype(F32)
    gain_grad = jnp.sum(grad * values * norm_scale(values), axis=0, keepdims=True)
    for at in range(8):
        lanes = slice(at * 128, at * 128 + 128)
        small[at : at + 1] = gain_grad[:, lanes]
        small[8 + at : 9 + at] = gain_two_grad[:, lanes]
    for lag in range(3):
        for at in range(4):
            row = 16 + 4 * lag + at
            small[row : row + 1] = tap_grads[lag : lag + 1, at * 128 : at * 128 + 128]
    small[28:32] = jnp.zeros((4, 128), F32)


def fill_transposed(left, own, other):
    for at in range(0, own.shape[1], 256):
        left[at : at + 256, :256] = own[:, at : at + 256].T
        left[at : at + 256, 256:] = other[:, at : at + 256].T


def chunk_rows(left, core, chunk):
    wide, slim = jnp.where(core == 0, 256, 64), jnp.where(core == 0, 64, 256)
    return jnp.concatenate(
        [left[pl.ds(pl.multiple_of(chunk * wide + at * slim, 64), 64)] for at in range(4)], 0
    )


def store_blocks(value, target, base, tiles, tile):
    value = value.astype(BF16)
    for chunk in range(4):
        for column in range(value.shape[1] // 128):
            target[base + chunk * tiles + tile + column] = value[
                chunk * 64 : chunk * 64 + 64, column * 128 : column * 128 + 128
            ]


def wide_runs(kind):
    at, end = (0, WIDE[0]) if kind == 0 else (WIDE[0], WIDE_TILES)
    first = at
    while at < end:
        matrix, tile = divmod(at, WIDE_COLUMNS // 128)
        count = min(2, WIDE_COLUMNS // 128 - tile, end - at)
        yield matrix, tile * 128, count * 128, at - first
        at += count


def wide_piece(scalars, kind, lefts, own, shared, send, keep):
    at, core = scalars[0], scalars[3]
    first, second = peer(at, kind), peer(at, 1 - kind)
    chunks = (at, second, first, peer(first, 1 - kind))
    for slot, chunk in enumerate(chunks):
        target = keep if slot < 2 else send
        rows = {}
        for matrix, column, width, tile in wide_runs(kind):
            if (matrix == 0) not in rows:
                rows[matrix == 0] = chunk_rows(lefts[matrix], core, chunk)
            left = rows[matrix == 0]
            mine = pl.ds(pl.multiple_of(core * WIDE_COLUMNS + column, 128), width)
            away = matrix * WIDE_COLUMNS + column
            value = dot(left[:, :256], own[matrix][:, mine])
            value = value + dot(left[:, 256:], shared[:, away : away + width])
            store_blocks(value, target, (slot % 2) * 4 * WIDE[kind], WIDE[kind], tile)


def wide_first_kernel(scalars, two, cot, cot_other, hidden, gate_back, shared, send, keep, left_two, left_cot):
    fill_transposed(left_cot, cot, cot_other)
    fill_transposed(left_two, two, shared.at[:, 3 * WIDE_COLUMNS :])
    wide_piece(scalars, 0, (left_cot, left_two), (hidden, gate_back), shared, send, keep)


def wide_second_kernel(scalars, left_two, gate_back, up_back, shared, send, keep):
    wide_piece(scalars, 1, (None, left_two, left_two), (None, gate_back, up_back), shared, send, keep)


def narrow_kernel(scalars, one, shared, low, late_other, backs, ymix, *refs):
    small, outs, (left_one, left_low) = refs[0], refs[1:5], refs[5:]
    for pairing in range(3):
        split_small(small[...], outs[pairing], ROUND_ONE[pairing] - 1)
    width = one.shape[1]
    one_other, ymix_other = shared.at[:, :width], shared.at[:, width:]
    for at in range(0, width, 256):
        left_one[at : at + 256, :256] = one[:, at : at + 256].T
        left_one[at : at + 256, 256:] = one_other[:, at : at + 256].T
        left_low[at : at + 256, :256] = low[:, at : at + 256].T
        left_low[at : at + 256, 256:] = late_other[at // 256].T
    mine = pl.ds(pl.multiple_of(scalars[3] * 256, 256), 256)
    for slot in range(4):
        chunk = peer(scalars[0], slot) if slot < 3 else scalars[0]
        for kind in range(4):
            left, own, other = (
                (left_one, backs[kind, :, mine], late_other[4 + kind])
                if kind < 3
                else (left_low, ymix[:, mine], ymix_other[...])
            )
            rows = chunk_rows(left, scalars[3], chunk)
            value = dot(rows[:, :256], own) + dot(rows[:, 256:], other)
            store_blocks(value, outs[slot], WIDE_BLOCKS[slot] if slot < 3 else 0, NARROW, 2 * kind)


def split_small(value, target, at):
    high = value.astype(BF16)
    target[at, :32] = high
    target[at, 32:] = (value - high.astype(F32)).astype(BF16)


def join_small(source, at):
    return source[at, :32].astype(F32) + source[at, 32:].astype(F32)


def rounded_small(value):
    high = value.astype(BF16)
    return high.astype(F32) + (value - high.astype(F32)).astype(BF16).astype(F32)


def sum_small(value, near, far, cross):
    return (rounded_small(value) + cross) + (near + far)


def far_kernel(scalars, mine, got, total, small):
    total[...] = mine[...].astype(F32) + got[: 4 * NARROW].astype(F32)
    small[...] = join_small(got, 4 * NARROW)


def first_kernel(scalars, *refs):
    gots, keeps, sends, wide_keeps = refs[:2], refs[2:4], refs[6:8], refs[8:]
    for kind in range(2):
        half = 4 * WIDE[kind]
        for chunk in range(4):
            at = slice(chunk * WIDE[kind], (chunk + 1) * WIDE[kind])
            after = slice(half + chunk * WIDE[kind], half + (chunk + 1) * WIDE[kind])
            wide_keeps[kind][at] = (keeps[kind][at].astype(F32) + gots[kind][at].astype(F32)).astype(BF16)
            sends[1 - kind][at] = (keeps[kind][after].astype(F32) + gots[kind][after].astype(F32)).astype(BF16)


def second_kernel(scalars, *refs):
    gots, wide_in, (narrow, small, cross) = refs[:2], refs[2:4], refs[4:7]
    sends, (keep, new_small) = refs[7:10], refs[10:]

    def fill(chunk, target):
        tile = 0
        for kind in range(2):
            at = pl.ds(chunk * WIDE[kind], WIDE[kind])
            value = wide_in[kind][at].astype(F32) + gots[1 - kind][at].astype(F32)
            target[tile : tile + WIDE[kind]] = value.astype(BF16)
            tile += WIDE[kind]
        value = narrow[pl.ds(chunk * NARROW, NARROW)]
        for pairing in range(2):
            value = value + gots[pairing][pl.ds(WIDE_BLOCKS[pairing] + chunk * NARROW, NARROW)].astype(F32)
        target[tile : tile + NARROW] = value.astype(BF16)

    near, far = (join_small(got, count - 1) for got, count in zip(gots, ROUND_ONE))
    value = sum_small(small[...], near, far, cross[...])
    new_small[...] = value
    for pairing in range(3):
        fill(peer(scalars[1], pairing), sends[pairing])
        split_small(value, sends[pairing], TILES)
    fill(scalars[1], keep)


def third_kernel(scalars, *refs):
    gots, (kept, small), (send, keep, gain) = refs[:3], refs[3:5], refs[5:]
    here = scalars[2]
    for first in range(0, TILES, 7):
        at = slice(first, first + 7)
        value = kept[at].astype(F32)
        for got in gots:
            value = value + got[at].astype(F32)
        zero, one = value[:, :32], value[:, 32:]
        keep[at] = jnp.where(here == 0, zero, one)
        send[at] = jnp.where(here == 0, one, zero).astype(BF16)
    value = sum_small(small[...], *(join_small(got, TILES) for got in gots))
    high = value.astype(BF16)
    low = (value - high.astype(F32)).astype(BF16)
    send[TILES] = high
    send[TILES + 1] = low
    gain[...] = high[:8].astype(F32) + low[:8].astype(F32)
    keep[TILES] = high.astype(F32)
    keep[TILES + 1] = low.astype(F32)


def finish_kernel(
    scalars, resid, down, down_other, part, other, tokens, resid_grad, gain, mixed, tokens_grad
):
    mixed[...] = (resid[...] + (down[...].astype(F32) + down_other[...].astype(F32))).astype(BF16)
    values = tokens[...].astype(F32)
    back = part[...].astype(F32) + other[...].astype(F32)
    tokens_grad[...] = resid_grad[...] + norm_backward(back, values, norm_scale(values), gain[...])


def cores_kernel(scalars, keep, got, across, skew, mine, away):
    core = scalars[3]
    total = keep[:TILES] + got[:TILES].astype(F32)
    zero, one = total[:, :16], total[:, 16:]
    mine[:TILES] = jnp.where(core == 0, zero, one)
    away[:TILES] = jnp.where(core == 0, one, zero)
    here = keep[TILES] + keep[TILES + 1]
    there = got[TILES].astype(F32) + got[TILES + 1].astype(F32)
    small = here + there
    for target in (mine, away):
        target[TILES, :8] = (here[:8] + across[...]) + (there[:8] + skew[...])
        target[TILES, 8:] = small[8:16]
        target[TILES + 1] = small[16:]


def outputs_kernel(scalars, mine, got, down, gate, up, inner, out, gain_one, gain_two, taps):
    core = scalars[3]

    def place(target, tile, column, columns):
        zero, one = jnp.where(core == 0, mine[tile], got[tile]), jnp.where(core == 0, got[tile], mine[tile])
        target[:, column : column + 128] = zero
        target[:, columns + column : columns + column + 128] = one

    for matrix, target in enumerate((down, gate, up)):
        for tile in range(WIDE_COLUMNS // 128):
            place(target, matrix * (WIDE_COLUMNS // 128) + tile, tile * 128, WIDE_COLUMNS)
    for kind in range(4):
        for column in range(2):
            place(inner.at[kind] if kind < 3 else out, WIDE_TILES + 2 * kind + column, column * 128, 256)
    gains = mine[TILES] + got[TILES]
    rest = mine[TILES + 1] + got[TILES + 1]
    for at in range(8):
        lanes = slice(at * 128, at * 128 + 128)
        gain_one[:, lanes] = gains[at : at + 1]
        gain_two[:, lanes] = gains[8 + at : 9 + at]
    for lag in range(3):
        for at in range(4):
            row = 4 * lag + at
            taps[lag : lag + 1, at * 128 : at * 128 + 128] = rest[row : row + 1]


def swap_round(sends, pairings):
    return [swap(value, pairs) for value, pairs in zip(sends, pairings)]


def blocks(counts):
    return [like((count, *BLOCK), BF16) for count in counts]


def on_device(
    tokens,
    starts,
    gain_one,
    in_weight,
    conv_weight,
    out_weight,
    gain_two,
    gate_weight,
    up_weight,
    down_weight,
    cotangent,
):
    core = lax.axis_index("seq") % 2
    run = call
    rows, width = tokens.shape
    channels = conv_weight.shape[1]
    in_parts = in_weight.transpose(1, 0, 2)
    gain_one_row, gain_two_row = gain_one.reshape(1, -1), gain_two.reshape(1, -1)

    def share(value):
        return swap(value, CORES)

    tail, tokens_here, gain_here, weights_here, offset = run(
        load_kernel,
        operands=[
            pltpu.with_memory_space_constraint(value, pltpu.HBM) for value in (tokens, gain_one_row, in_parts)
        ],
        scalar=starts,
        outs=[
            like((16, channels), BF16),
            like((rows, width), BF16),
            like((1, width), F32),
            like((3, width, channels), BF16),
            like((8, 128), jnp.int32),
        ],
        scratch=[pltpu.SemaphoreType.DMA((15,))],
        where=pltpu.HBM,
    )
    incoming = from_behind(tail, "seq", 1)
    cotangent_other = share(cotangent)
    incoming, cotangent_other = lax.optimization_barrier((incoming, cotangent_other))
    normed_one, parts, gated = run(
        project_kernel,
        operands=[tokens_here, gain_here, weights_here],
        outs=[like((rows, width), BF16), like((3, rows, channels), F32), like((rows, channels), BF16)],
    )
    conv, ymix, branch = run(
        mix_kernel,
        offset=offset,
        operands=[gated, incoming, parts, conv_weight, out_weight],
        outs=[like((rows, channels), F32), like((rows, channels), BF16), like((rows, width), BF16)],
    )
    branch, cotangent_late = lax.optimization_barrier((branch, cotangent))
    branch_other = swap(branch, ACROSS)
    units = gate_weight.shape[1]
    hidden_grad = run(
        hidden_kernel,
        operands=[cotangent_late, down_weight],
        outs=[like((rows, units), F32)],
        flops=LONG,
    )[0]
    branch_other, hidden_grad = lax.optimization_barrier((branch_other, hidden_grad))
    resid, normed_two, hidden, gate_back, up_back, shared, shared_early = run(
        feed_kernel,
        operands=[tokens, branch, branch_other, gain_two_row, gate_weight, up_weight, hidden_grad]
        + [normed_one, ymix],
        outs=[like((rows, width), F32), like((rows, width), BF16)]
        + [like((rows, units), BF16)] * 3
        + [like((rows, 3 * WIDE_COLUMNS + width), BF16), like((rows, width + channels // 2), BF16)],
    )
    shared_other = share(shared)
    norm_two_part = run(
        part_kernel, operands=[gate_back, up_back, gate_weight, up_weight], outs=[like((rows, width), BF16)]
    )[0]
    norm_two_other = swap(norm_two_part, ACROSS)
    first_send, first_keep, left_two = run(
        wide_first_kernel,
        operands=[normed_two, cotangent, cotangent_other, hidden, gate_back, shared_other],
        outs=blocks([8 * WIDE[0]] * 2) + [like((width, 2 * rows), BF16)],
        scratch=[pltpu.VMEM((width, 2 * rows), BF16)],
    )
    second_send, second_keep = run(
        wide_second_kernel,
        operands=[left_two, gate_back, up_back, shared_other],
        outs=blocks([8 * WIDE[1]] * 2),
    )
    sends, keeps = [first_send, second_send], [first_keep, second_keep]
    hidden, sends[1] = lax.optimization_barrier((hidden, sends[1]))
    down_part = run(down_kernel, operands=[hidden, down_weight], outs=[like((rows, width), BF16)])[0]
    early_other = share(shared_early)
    norm_two_other, keeps[1], down_part, early_other = lax.optimization_barrier(
        (norm_two_other, keeps[1], down_part, early_other)
    )
    gots = swap_round(sends, FIRST)

    edge_operands = [norm_two_part, norm_two_other, resid, gain_two_row, cotangent, out_weight, parts, conv_weight]
    edge = run(edge_kernel, offset=offset, operands=edge_operands, outs=[like((8, channels), F32)])[0]
    returned = from_behind(edge, "seq", -1)
    resid_grad, resid_low, gain_two_grad, c_back, gated_back, tap_grads = run(
        middle_kernel,
        offset=offset,
        operands=edge_operands + [conv, gated, incoming],
        outs=[
            like((rows, width), F32),
            like((rows, width), BF16),
            like((1, width), F32),
            like((rows, channels), BF16),
            like((rows, channels), F32),
            like((3, channels), F32),
        ],
        flops=SHORT,
    )
    backs, shared, norm_one_part, small = run(
        last_kernel,
        offset=offset,
        operands=[gated_back, returned, parts, c_back, in_parts, tokens, gain_two_grad, tap_grads]
        + [resid_low],
        outs=[
            like((3, rows, channels), BF16),
            like((7, rows, 256), BF16),
            like((rows, width), BF16),
            like((32, 128), F32),
        ],
    )
    *sends, narrow = run(
        narrow_kernel,
        operands=[normed_one, early_other, resid_low, share(shared), backs, ymix, small],
        outs=blocks(ROUND_ONE) + blocks([4 * NARROW]),
        scratch=[pltpu.VMEM((width, 2 * rows), BF16)] * 2,
    )
    narrow, cross = run(
        far_kernel,
        operands=[narrow, swap(sends.pop(), FIRST[2])],
        outs=[like((4 * NARROW, *BLOCK), F32), like((32, 128), F32)],
        flops=LONG,
    )
    results = run(
        first_kernel,
        operands=gots + keeps + sends,
        aliases={4: 0, 5: 1},
        outs=blocks(ROUND_ONE[:2]) + blocks([4 * count for count in WIDE]),
    )
    sends, keeps = list(results[:2]), list(results[2:])
    gots = swap_round(sends, FIRST)
    norm_one_other = swap(norm_one_part, ACROSS)
    down_other = swap(down_part, ACROSS)
    results = run(
        second_kernel,
        operands=gots + keeps + [narrow, small, cross],
        outs=blocks([TILES + 1] * 3 + [TILES]) + [like((32, 128), F32)],
    )
    sends, keep, small = list(results[:3]), results[3], results[4]
    gots = swap_round(sends, SECOND)
    mixed, tokens_grad = run(
        finish_kernel,
        operands=[resid, down_part, down_other, norm_one_part, norm_one_other, tokens, resid_grad, gain_one_row],
        outs=[like((rows, width), BF16), like((rows, width), F32)],
        flops=LONG,
    )
    gots[0], mixed, tokens_grad = lax.optimization_barrier((gots[0], mixed, tokens_grad))
    beside, kept, gain = run(
        third_kernel,
        operands=gots + [keep, small],
        outs=[like((TILES + 2, 32, 128), BF16), like((TILES + 2, 32, 128), F32), like((8, 128), F32)],
    )
    mine, away = run(
        cores_kernel,
        operands=[kept, swap(beside, BESIDE), swap(gain, ACROSS), swap(gain, SKEW)],
        outs=[like((TILES + 2, 16, 128), F32)] * 2,
    )
    down_g, gate_g, up_g, in_g, out_g, gain_one_g, gain_two_g, conv_g = run(
        outputs_kernel,
        operands=[mine, swap(away, CORES)],
        outs=[like((16, 2 * WIDE_COLUMNS), F32)] * 3
        + [like((3, 16, channels), F32), like((16, channels), F32)]
        + [like((1, width), F32)] * 2
        + [like((3, channels), F32)],
    )
    in_g, gain_one_g, gain_two_g = in_g.transpose(1, 0, 2), gain_one_g.reshape(-1), gain_two_g.reshape(-1)
    return (mixed, tokens_grad, gain_one_g, in_g, conv_g, out_g.T, gain_two_g, gate_g, up_g, down_g.T)


def solution(mesh):
    return jax.shard_map(
        on_device,
        mesh=mesh,
        in_specs=(
            P("seq", None),
            P("seq"),
            P(),
            P(None, None, "tensor"),
            P(None, "tensor"),
            P("tensor", None),
            P(),
            P(None, "tensor"),
            P(None, "tensor"),
            P("tensor", None),
            P("seq", None),
        ),
        out_specs=(
            P("seq", None),
            P("seq", None),
            P(),
            P("seq", None, "tensor"),
            P(None, "tensor"),
            P("tensor", "seq"),
            P(),
            P("seq", "tensor"),
            P("seq", "tensor"),
            P("tensor", "seq"),
        ),
        check_vma=False,
    )
```

```python
import functools

import jax
import jax.numpy as jnp
from jax import lax
from jax.experimental import pallas as pl
from jax.experimental.pallas import tpu as pltpu
from jax.sharding import PartitionSpec as P

EPS = 1e-05
AXES = ("seq", "tensor")
BF16 = jnp.bfloat16
F32 = jnp.float32


def device_pairs(move):
    def number(y, z, x, core):
        return ((((y % 4) * 4 + z % 4) * 2 + x % 2) * 2 + core) * 2 + (x % 4) // 2

    return [
        (number(y, z, x, core), number(*move(y, z, x, core)))
        for y in range(4)
        for z in range(4)
        for x in range(4)
        for core in range(2)
    ]


ACROSS = device_pairs(lambda y, z, x, core: (y, z, (x + 2) % 4, core))
BESIDE = device_pairs(lambda y, z, x, core: (y, z, x ^ 1, core))
CORES = device_pairs(lambda y, z, x, core: (y, z, x, 1 - core))


def peer(at, pairing):
    return (at ^ 1, 3 - at, at ^ 2)[pairing]


FIRST = [
    device_pairs(
        functools.partial(
            lambda pairing, y, z, x, core: (y, peer(z, pairing), x, core)
            if core
            else (peer(y, pairing), z, x, core),
            pairing,
        )
    )
    for pairing in range(3)
]
SECOND = [
    device_pairs(
        functools.partial(
            lambda pairing, y, z, x, core: (peer(y, pairing), z, x, core)
            if core
            else (y, peer(z, pairing), x, core),
            pairing,
        )
    )
    for pairing in range(3)
]
WIDE_COLUMNS = 1152
WIDE_TILES = 27
WIDE = (14, 13)
NARROW = 8
BLOCK = (64, 128)
LONG = 3 * 10**10
SHORT = 8 * 10**9
TILES = WIDE_TILES + NARROW
WIDE_BLOCKS = (4 * WIDE[1], 4 * WIDE[0], 0)
ROUND_ONE = tuple(count + 4 * NARROW + 1 for count in WIDE_BLOCKS)


def swap(value, pairs):
    return lax.ppermute(value, AXES, pairs)


def from_behind(value, axis, steps):
    count = lax.axis_size(axis)
    leading, last = (max(0, -steps), min(count, count - steps))
    return lax.ppermute(value, axis, [(source, source + steps) for source in range(leading, last)])


def norm_scale(values):
    return lax.rsqrt(jnp.mean(values * values, axis=1, keepdims=True) + EPS)


def norm_backward(out_grad_rows, values, scale_rows, gain):
    scaled = out_grad_rows * gain
    inner = jnp.mean(scaled * values, axis=1, keepdims=True)
    return scale_rows * (scaled - values * scale_rows * scale_rows * inner)


def like(shape, dtype):
    return jax.ShapeDtypeStruct(shape, dtype)


def positions(offset):
    at = lax.axis_index("seq")
    y, z, core = at // 16, (at // 4) % 4, at % 2
    first, second = jnp.where(core == 0, y, z), jnp.where(core == 0, z, y)
    return first, second, (at // 2) % 2, core, offset


def call(body, *, operands, outs, scratch=(), offset=None, flops=0, aliases=None, where=pltpu.VMEM, scalar=None):
    whole = pl.BlockSpec(memory_space=pltpu.VMEM)
    specs = [pl.BlockSpec(memory_space=where)] * len(operands)
    if scalar is not None:
        operands, specs = [scalar, *operands], [pl.BlockSpec(memory_space=pltpu.SMEM), *specs]

    def kernel(*refs):
        if offset is None:
            body(positions(None), *refs)
        else:
            body(positions(refs[0][0:1, 0:1]), *refs[1:])

    if offset is not None:
        operands, specs = [offset, *operands], [whole, *specs]
    return pl.pallas_call(
        kernel,
        out_shape=tuple(outs),
        in_specs=specs,
        out_specs=tuple(whole for _ in outs),
        scratch_shapes=list(scratch),
        input_output_aliases=aliases or {},
        compiler_params=pltpu.CompilerParams(vmem_limit_bytes=16 * 2**20),
        cost_estimate=pl.CostEstimate(flops=flops, bytes_accessed=0, transcendentals=0),
    )(*operands)


def dot(left, right):
    return jnp.dot(left, right, preferred_element_type=F32)


def dot_rows(left, right):
    return lax.dot_general(left, right, (((1,), (1,)), ((), ())), preferred_element_type=F32)


def row_numbers(shape, first=0):
    return lax.broadcasted_iota(jnp.int32, shape, 0) + first


def valid_rows(offset, lag, shape):
    row = row_numbers(shape)
    return jnp.where((offset <= row) & (offset > row - lag), 0.0, 1.0)


def linked_rows(offset, shape, first, count):
    return jnp.where((row_numbers(shape, first) < offset) & (offset < count), 0.0, 1.0)


def load_kernel(scalars, starts, tokens, gain, weight, tail, token_rows, gain_row, weights, offset, done):
    rows, depth = tokens.shape[0], weight.shape[1] // 4
    pieces = [(gain, gain_row)]
    pieces += [(tokens.at[pl.ds(at, 128)], token_rows.at[pl.ds(at, 128)]) for at in (rows - 128, 0)]
    for k in (0, 2, 1):
        for at in range(0, weight.shape[1], depth):
            pieces.append((weight.at[k, pl.ds(at, depth)], weights.at[k, pl.ds(at, depth)]))
    copies = [
        pltpu.make_async_copy(source, target, done.at[at]) for at, (source, target) in enumerate(pieces)
    ]
    for copy in copies:
        copy.start()
    for copy in copies[:2]:
        copy.wait()
    offset[...] = jnp.full(offset.shape, starts[0], jnp.int32)
    values = token_rows[rows - 16 :].astype(F32)
    normed = (values * norm_scale(values) * gain_row[...]).astype(BF16)
    for copy in copies[2:11]:
        copy.wait()
    gated = (dot(normed, weights[0]) * dot(normed, weights[2])).astype(BF16).astype(F32)
    tail[...] = (gated * linked_rows(starts[0], gated.shape, rows - 16, rows)).astype(BF16)
    for copy in copies[11:]:
        copy.wait()


def project_kernel(scalars, tokens, gain, weights, normed, parts, gated):
    values = tokens[...].astype(F32)
    normed[...] = (values * norm_scale(values) * gain[...]).astype(BF16)
    for k in range(3):
        parts[k] = dot(normed[...], weights[k])
    gated[...] = (parts[0] * parts[2]).astype(BF16)


def behind(gated, incoming, lag):
    moved = pltpu.roll(gated, lag, 0)
    row = row_numbers(gated.shape)
    for at in range(lag):
        moved = jnp.where(row == at, incoming[16 - lag + at : 17 - lag + at], moved)
    return moved


def mix_kernel(scalars, gated, incoming, parts, taps, weight, conv, ymix, branch):
    values = gated[...].astype(F32)
    before = incoming[...].astype(F32)
    total = taps[0:1] * values
    for lag in (1, 2):
        total = total + taps[lag : lag + 1] * behind(values, before, lag) * valid_rows(
            scalars[4], lag, values.shape
        )
    conv[...] = total
    ymix[...] = (parts[1] * total).astype(BF16)
    branch[...] = dot(ymix[...], weight[...]).astype(BF16)


def away_half(value, core):
    half = value.shape[-1] // 2
    return jnp.where(core == 0, value[..., half:], value[..., :half])


def hidden_kernel(scalars, cot, weight, out):
    for at in range(0, weight.shape[0], 256):
        out[:, at : at + 256] = dot_rows(cot[...], weight[at : at + 256])


def down_kernel(scalars, hidden, weight, out):
    out[...] = dot(hidden[...], weight[...]).astype(BF16)


def feed_kernel(
    scalars,
    tokens,
    branch,
    other,
    gain,
    gate,
    up,
    hidden_grad,
    normed_one,
    ymix,
    resid,
    normed,
    hidden,
    gate_back,
    up_back,
    shared,
    shared_early,
):
    resid[...] = tokens[...].astype(F32) + (branch[...].astype(F32) + other[...].astype(F32))
    normed[...] = (resid[...] * norm_scale(resid[...]) * gain[...]).astype(BF16)
    values = normed[...]
    for at in range(0, gate.shape[1], 256):
        columns = slice(at, at + 256)
        gate_act, up_act = dot(values, gate[:, columns]), dot(values, up[:, columns])
        back = hidden_grad[:, columns]
        sigmoid_gate = jax.nn.sigmoid(gate_act)
        swish = gate_act * sigmoid_gate
        hidden[:, columns] = (swish * up_act).astype(BF16)
        up_back[:, columns] = (back * swish).astype(BF16)
        slope = sigmoid_gate * (1.0 + gate_act * (1.0 - sigmoid_gate))
        gate_back[:, columns] = (back * up_act * slope).astype(BF16)
    away = pl.ds(pl.multiple_of((1 - scalars[3]) * WIDE_COLUMNS, 128), WIDE_COLUMNS)
    for k, value in enumerate((hidden, gate_back, up_back)):
        shared[:, k * WIDE_COLUMNS : (k + 1) * WIDE_COLUMNS] = value[:, away]
    shared[:, 3 * WIDE_COLUMNS :] = values
    shared_early[:, : normed.shape[1]] = normed_one[...]
    shared_early[:, normed.shape[1] :] = away_half(ymix[...], scalars[3])


def part_kernel(scalars, gate_back, up_back, gate, up, part):
    part[...] = (dot_rows(gate_back[...], gate[...]) + dot_rows(up_back[...], up[...])).astype(BF16)


def second_norm(part, other, resid, gain, cot):
    back = part.astype(F32) + other.astype(F32)
    scale = norm_scale(resid)
    return back, scale, cot.astype(F32) + norm_backward(back, resid, scale, gain)


def edge_kernel(scalars, part, other, resid, gain, cot, weight, parts, taps, edge):
    top = slice(0, 16)
    _, _, grad = second_norm(part[top], other[top], resid[top], gain[...], cot[top])
    conv_back = dot_rows(grad.astype(BF16), weight[...]) * parts[1, top]
    one = conv_back * valid_rows(scalars[4], 1, conv_back.shape) * taps[1:2]
    two = conv_back * valid_rows(scalars[4], 2, conv_back.shape) * taps[2:3]
    row = row_numbers((8, conv_back.shape[1]))
    edge[...] = jnp.where(row == 6, two[0:1], 0.0) + jnp.where(row == 7, one[0:1] + two[1:2], 0.0)


def middle_kernel(
    scalars, part, other, resid, gain, cot, weight, parts, taps, conv, gated, incoming, grad, low, gain_grad, c_back, gated_back, tap_grads
):
    back, scale, resid_grad = second_norm(part[...], other[...], resid[...], gain[...], cot[...])
    gain_grad[...] = jnp.sum(back * resid[...] * scale, axis=0, keepdims=True)
    grad[...] = resid_grad
    low[...] = resid_grad.astype(BF16)
    ymix_back = dot_rows(low[...], weight[...])
    c_back[...] = (ymix_back * conv[...]).astype(BF16)
    conv_back = ymix_back * parts[1]
    values, before = gated[...].astype(F32), incoming[...].astype(F32)
    rows = values.shape[0]
    tap_grads[0:1] = jnp.sum(conv_back * values, axis=0, keepdims=True)
    total = conv_back * taps[0:1]
    row = row_numbers(values.shape)
    for lag in (1, 2):
        term = conv_back * valid_rows(scalars[4], lag, values.shape)
        tap_grads[lag : lag + 1] = jnp.sum(term * behind(values, before, lag), axis=0, keepdims=True)
        moved = pltpu.roll(term * taps[lag : lag + 1], rows - lag, 0)
        total = total + jnp.where(row < rows - lag, moved, 0.0)
    gated_back[...] = total


def last_kernel(
    scalars,
    gated_back,
    returned,
    parts,
    c_back,
    weight,
    tokens,
    gain_two_grad,
    tap_grads,
    resid_low,
    backs,
    shared,
    part,
    gain_part,
    small,
):
    rows = gated_back.shape[0]
    links = linked_rows(scalars[4], returned.shape, rows - 8, rows)
    end = gated_back[rows - 8 :] + returned[...] * links
    total = jnp.concatenate([gated_back[: rows - 8], end], 0)
    backs[0] = (total * parts[2]).astype(BF16)
    backs[1] = c_back[...]
    backs[2] = (total * parts[0]).astype(BF16)
    for k in range(3):
        shared[4 + k] = away_half(backs[k], scalars[3])
    for at in range(4):
        shared[at] = resid_low[:, at * 256 : at * 256 + 256]
    grad = dot_rows(backs[0], weight[0]) + dot_rows(backs[1], weight[1]) + dot_rows(backs[2], weight[2])
    part[...] = grad.astype(BF16)
    values = tokens[...].astype(F32)
    gain_grad = jnp.sum(grad * values * norm_scale(values), axis=0, keepdims=True)
    for at in range(8):
        lanes = slice(at * 128, at * 128 + 128)
        gain_part[at : at + 1] = gain_grad[:, lanes]
        small[8 + at : 9 + at] = gain_two_grad[:, lanes]
    for lag in range(3):
        for at in range(4):
            row = 16 + 4 * lag + at
            small[row : row + 1] = tap_grads[lag : lag + 1, at * 128 : at * 128 + 128]
    small[:8] = jnp.zeros((8, 128), F32)
    small[28:32] = jnp.zeros((4, 128), F32)


def fill_transposed(left, own, other):
    for at in range(0, own.shape[1], 256):
        left[at : at + 256, :256] = own[:, at : at + 256].T
        left[at : at + 256, 256:] = other[:, at : at + 256].T


def chunk_rows(left, core, chunk):
    wide, slim = jnp.where(core == 0, 256, 64), jnp.where(core == 0, 64, 256)
    return jnp.concatenate(
        [left[pl.ds(pl.multiple_of(chunk * wide + at * slim, 64), 64)] for at in range(4)], 0
    )


def store_blocks(value, target, base, tiles, tile):
    value = value.astype(BF16)
    for chunk in range(4):
        for column in range(value.shape[1] // 128):
            target[base + chunk * tiles + tile + column] = value[
                chunk * 64 : chunk * 64 + 64, column * 128 : column * 128 + 128
            ]


def wide_runs(kind):
    at, end = (0, WIDE[0]) if kind == 0 else (WIDE[0], WIDE_TILES)
    first = at
    while at < end:
        matrix, tile = divmod(at, WIDE_COLUMNS // 128)
        count = min(2, WIDE_COLUMNS // 128 - tile, end - at)
        yield matrix, tile * 128, count * 128, at - first
        at += count


def wide_piece(scalars, kind, lefts, own, shared, send, keep):
    at, core = scalars[0], scalars[3]
    first, second = peer(at, kind), peer(at, 1 - kind)
    chunks = (at, second, first, peer(first, 1 - kind))
    for slot, chunk in enumerate(chunks):
        target = keep if slot < 2 else send
        rows = {}
        for matrix, column, width, tile in wide_runs(kind):
            if (matrix == 0) not in rows:
                rows[matrix == 0] = chunk_rows(lefts[matrix], core, chunk)
            left = rows[matrix == 0]
            mine = pl.ds(pl.multiple_of(core * WIDE_COLUMNS + column, 128), width)
            away = matrix * WIDE_COLUMNS + column
            value = dot(left[:, :256], own[matrix][:, mine])
            value = value + dot(left[:, 256:], shared[:, away : away + width])
            store_blocks(value, target, (slot % 2) * 4 * WIDE[kind], WIDE[kind], tile)


def wide_first_kernel(scalars, two, cot, cot_other, hidden, gate_back, shared, send, keep, left_two, left_cot):
    fill_transposed(left_cot, cot, cot_other)
    fill_transposed(left_two, two, shared.at[:, 3 * WIDE_COLUMNS :])
    wide_piece(scalars, 0, (left_cot, left_two), (hidden, gate_back), shared, send, keep)


def wide_second_kernel(scalars, left_two, gate_back, up_back, shared, send, keep):
    wide_piece(scalars, 1, (None, left_two, left_two), (None, gate_back, up_back), shared, send, keep)


def narrow_kernel(scalars, one, shared, low, late_other, backs, ymix, *refs):
    (small, gain, gain_other), outs, (new_small, left_one, left_low) = refs[:3], refs[3:7], refs[7:]
    new_small[:8] = gain[...] + gain_other[...]
    new_small[8:] = small[8:]
    for pairing in range(3):
        split_small(new_small[...], outs[pairing], ROUND_ONE[pairing] - 1)
    width = one.shape[1]
    one_other, ymix_other = shared.at[:, :width], shared.at[:, width:]
    for at in range(0, width, 256):
        left_one[at : at + 256, :256] = one[:, at : at + 256].T
        left_one[at : at + 256, 256:] = one_other[:, at : at + 256].T
        left_low[at : at + 256, :256] = low[:, at : at + 256].T
        left_low[at : at + 256, 256:] = late_other[at // 256].T
    mine = pl.ds(pl.multiple_of(scalars[3] * 256, 256), 256)
    for slot in range(4):
        chunk = peer(scalars[0], slot) if slot < 3 else scalars[0]
        for kind in range(4):
            left, own, other = (
                (left_one, backs[kind, :, mine], late_other[4 + kind])
                if kind < 3
                else (left_low, ymix[:, mine], ymix_other[...])
            )
            rows = chunk_rows(left, scalars[3], chunk)
            value = dot(rows[:, :256], own) + dot(rows[:, 256:], other)
            store_blocks(value, outs[slot], WIDE_BLOCKS[slot] if slot < 3 else 0, NARROW, 2 * kind)


def split_small(value, target, at):
    high = value.astype(BF16)
    target[at, :32] = high
    target[at, 32:] = (value - high.astype(F32)).astype(BF16)


def join_small(source, at):
    return source[at, :32].astype(F32) + source[at, 32:].astype(F32)


def rounded_small(value):
    high = value.astype(BF16)
    return high.astype(F32) + (value - high.astype(F32)).astype(BF16).astype(F32)


def sum_small(value, near, far, cross):
    return (rounded_small(value) + cross) + (near + far)


def far_kernel(scalars, mine, got, total, small):
    total[...] = mine[...].astype(F32) + got[: 4 * NARROW].astype(F32)
    small[...] = join_small(got, 4 * NARROW)


def first_kernel(scalars, *refs):
    gots, keeps, sends, wide_keeps = refs[:2], refs[2:4], refs[6:8], refs[8:]
    for kind in range(2):
        half = 4 * WIDE[kind]
        for chunk in range(4):
            at = slice(chunk * WIDE[kind], (chunk + 1) * WIDE[kind])
            after = slice(half + chunk * WIDE[kind], half + (chunk + 1) * WIDE[kind])
            wide_keeps[kind][at] = (keeps[kind][at].astype(F32) + gots[kind][at].astype(F32)).astype(BF16)
            sends[1 - kind][at] = (keeps[kind][after].astype(F32) + gots[kind][after].astype(F32)).astype(BF16)


def second_kernel(scalars, *refs):
    gots, wide_in, (narrow, small, cross) = refs[:2], refs[2:4], refs[4:7]
    sends, (keep, new_small) = refs[7:10], refs[10:]

    def fill(chunk, target):
        tile = 0
        for kind in range(2):
            at = pl.ds(chunk * WIDE[kind], WIDE[kind])
            value = wide_in[kind][at].astype(F32) + gots[1 - kind][at].astype(F32)
            target[tile : tile + WIDE[kind]] = value.astype(BF16)
            tile += WIDE[kind]
        value = narrow[pl.ds(chunk * NARROW, NARROW)]
        for pairing in range(2):
            value = value + gots[pairing][pl.ds(WIDE_BLOCKS[pairing] + chunk * NARROW, NARROW)].astype(F32)
        target[tile : tile + NARROW] = value.astype(BF16)

    near, far = (join_small(got, count - 1) for got, count in zip(gots, ROUND_ONE))
    value = sum_small(small[...], near, far, cross[...])
    new_small[...] = value
    for pairing in range(3):
        fill(peer(scalars[1], pairing), sends[pairing])
        split_small(value, sends[pairing], TILES)
    fill(scalars[1], keep)


def third_kernel(scalars, *refs):
    gots, (kept, small), (send, keep) = refs[:3], refs[3:5], refs[5:]
    here = scalars[2]
    for first in range(0, TILES, 7):
        at = slice(first, first + 7)
        value = kept[at].astype(F32)
        for got in gots:
            value = value + got[at].astype(F32)
        zero, one = value[:, :32], value[:, 32:]
        keep[at] = jnp.where(here == 0, zero, one)
        send[at] = jnp.where(here == 0, one, zero).astype(BF16)
    value = sum_small(small[...], *(join_small(got, TILES) for got in gots))
    high = value.astype(BF16)
    low = (value - high.astype(F32)).astype(BF16)
    send[TILES] = high
    send[TILES + 1] = low
    keep[TILES] = high.astype(F32)
    keep[TILES + 1] = low.astype(F32)


def finish_kernel(
    scalars, resid, down, down_other, part, other, tokens, resid_grad, gain, mixed, tokens_grad
):
    mixed[...] = (resid[...] + (down[...].astype(F32) + down_other[...].astype(F32))).astype(BF16)
    values = tokens[...].astype(F32)
    back = part[...].astype(F32) + other[...].astype(F32)
    tokens_grad[...] = resid_grad[...] + norm_backward(back, values, norm_scale(values), gain[...])


def cores_kernel(scalars, keep, got, mine, away):
    core = scalars[3]
    total = keep[:TILES] + got[:TILES].astype(F32)
    zero, one = total[:, :16], total[:, 16:]
    mine[:TILES] = jnp.where(core == 0, zero, one)
    away[:TILES] = jnp.where(core == 0, one, zero)
    small = (keep[TILES] + keep[TILES + 1]) + (got[TILES].astype(F32) + got[TILES + 1].astype(F32))
    for target in (mine, away):
        target[TILES] = small[:16]
        target[TILES + 1] = small[16:]


def outputs_kernel(scalars, mine, got, down, gate, up, inner, out, gain_one, gain_two, taps):
    core = scalars[3]

    def place(target, tile, column, columns):
        zero, one = jnp.where(core == 0, mine[tile], got[tile]), jnp.where(core == 0, got[tile], mine[tile])
        target[:, column : column + 128] = zero
        target[:, columns + column : columns + column + 128] = one

    for matrix, target in enumerate((down, gate, up)):
        for tile in range(WIDE_COLUMNS // 128):
            place(target, matrix * (WIDE_COLUMNS // 128) + tile, tile * 128, WIDE_COLUMNS)
    for kind in range(4):
        for column in range(2):
            place(inner.at[kind] if kind < 3 else out, WIDE_TILES + 2 * kind + column, column * 128, 256)
    gains = mine[TILES] + got[TILES]
    rest = mine[TILES + 1] + got[TILES + 1]
    for at in range(8):
        lanes = slice(at * 128, at * 128 + 128)
        gain_one[:, lanes] = gains[at : at + 1]
        gain_two[:, lanes] = gains[8 + at : 9 + at]
    for lag in range(3):
        for at in range(4):
            row = 4 * lag + at
            taps[lag : lag + 1, at * 128 : at * 128 + 128] = rest[row : row + 1]


def swap_round(sends, pairings):
    return [swap(value, pairs) for value, pairs in zip(sends, pairings)]


def blocks(counts):
    return [like((count, *BLOCK), BF16) for count in counts]


def on_device(
    tokens,
    starts,
    gain_one,
    in_weight,
    conv_weight,
    out_weight,
    gain_two,
    gate_weight,
    up_weight,
    down_weight,
    cotangent,
):
    core = lax.axis_index("seq") % 2
    run = call
    rows, width = tokens.shape
    channels = conv_weight.shape[1]
    in_parts = in_weight.transpose(1, 0, 2)
    gain_one_row, gain_two_row = gain_one.reshape(1, -1), gain_two.reshape(1, -1)

    def share(value):
        return swap(value, CORES)

    tail, tokens_here, gain_here, weights_here, offset = run(
        load_kernel,
        operands=[
            pltpu.with_memory_space_constraint(value, pltpu.HBM) for value in (tokens, gain_one_row, in_parts)
        ],
        scalar=starts,
        outs=[
            like((16, channels), BF16),
            like((rows, width), BF16),
            like((1, width), F32),
            like((3, width, channels), BF16),
            like((8, 128), jnp.int32),
        ],
        scratch=[pltpu.SemaphoreType.DMA((15,))],
        where=pltpu.HBM,
    )
    incoming = from_behind(tail, "seq", 1)
    cotangent_other = share(cotangent)
    incoming, cotangent_other = lax.optimization_barrier((incoming, cotangent_other))
    normed_one, parts, gated = run(
        project_kernel,
        operands=[tokens_here, gain_here, weights_here],
        outs=[like((rows, width), BF16), like((3, rows, channels), F32), like((rows, channels), BF16)],
    )
    conv, ymix, branch = run(
        mix_kernel,
        offset=offset,
        operands=[gated, incoming, parts, conv_weight, out_weight],
        outs=[like((rows, channels), F32), like((rows, channels), BF16), like((rows, width), BF16)],
    )
    branch, cotangent_late = lax.optimization_barrier((branch, cotangent))
    branch_other = swap(branch, ACROSS)
    units = gate_weight.shape[1]
    hidden_grad = run(
        hidden_kernel,
        operands=[cotangent_late, down_weight],
        outs=[like((rows, units), F32)],
        flops=LONG,
    )[0]
    branch_other, hidden_grad = lax.optimization_barrier((branch_other, hidden_grad))
    resid, normed_two, hidden, gate_back, up_back, shared, shared_early = run(
        feed_kernel,
        operands=[tokens, branch, branch_other, gain_two_row, gate_weight, up_weight, hidden_grad]
        + [normed_one, ymix],
        outs=[like((rows, width), F32), like((rows, width), BF16)]
        + [like((rows, units), BF16)] * 3
        + [like((rows, 3 * WIDE_COLUMNS + width), BF16), like((rows, width + channels // 2), BF16)],
    )
    shared_other = share(shared)
    norm_two_part = run(
        part_kernel, operands=[gate_back, up_back, gate_weight, up_weight], outs=[like((rows, width), BF16)]
    )[0]
    norm_two_other = swap(norm_two_part, ACROSS)
    first_send, first_keep, left_two = run(
        wide_first_kernel,
        operands=[normed_two, cotangent, cotangent_other, hidden, gate_back, shared_other],
        outs=blocks([8 * WIDE[0]] * 2) + [like((width, 2 * rows), BF16)],
        scratch=[pltpu.VMEM((width, 2 * rows), BF16)],
    )
    second_send, second_keep = run(
        wide_second_kernel,
        operands=[left_two, gate_back, up_back, shared_other],
        outs=blocks([8 * WIDE[1]] * 2),
    )
    sends, keeps = [first_send, second_send], [first_keep, second_keep]
    hidden, sends[1] = lax.optimization_barrier((hidden, sends[1]))
    down_part = run(down_kernel, operands=[hidden, down_weight], outs=[like((rows, width), BF16)])[0]
    early_other = share(shared_early)
    norm_two_other, keeps[1], down_part, early_other = lax.optimization_barrier(
        (norm_two_other, keeps[1], down_part, early_other)
    )
    gots = swap_round(sends, FIRST)

    edge_operands = [norm_two_part, norm_two_other, resid, gain_two_row, cotangent, out_weight, parts, conv_weight]
    edge = run(edge_kernel, offset=offset, operands=edge_operands, outs=[like((8, channels), F32)])[0]
    returned = from_behind(edge, "seq", -1)
    resid_grad, resid_low, gain_two_grad, c_back, gated_back, tap_grads = run(
        middle_kernel,
        offset=offset,
        operands=edge_operands + [conv, gated, incoming],
        outs=[
            like((rows, width), F32),
            like((rows, width), BF16),
            like((1, width), F32),
            like((rows, channels), BF16),
            like((rows, channels), F32),
            like((3, channels), F32),
        ],
        flops=SHORT,
    )
    backs, shared, norm_one_part, gain_part, small = run(
        last_kernel,
        offset=offset,
        operands=[gated_back, returned, parts, c_back, in_parts, tokens, gain_two_grad, tap_grads]
        + [resid_low],
        outs=[
            like((3, rows, channels), BF16),
            like((7, rows, 256), BF16),
            like((rows, width), BF16),
            like((8, 128), F32),
            like((32, 128), F32),
        ],
    )
    gain_other = swap(gain_part, ACROSS)
    *sends, narrow, small = run(
        narrow_kernel,
        operands=[normed_one, early_other, resid_low, share(shared), backs, ymix, small, gain_part, gain_other],
        outs=blocks(ROUND_ONE) + blocks([4 * NARROW]) + [like((32, 128), F32)],
        scratch=[pltpu.VMEM((width, 2 * rows), BF16)] * 2,
    )
    far_send = sends.pop()
    results = run(
        first_kernel,
        operands=gots + keeps + sends,
        aliases={4: 0, 5: 1},
        outs=blocks(ROUND_ONE[:2]) + blocks([4 * count for count in WIDE]),
    )
    sends, keeps = list(results[:2]), list(results[2:])
    keeps[0], far_send = lax.optimization_barrier((keeps[0], far_send))
    narrow, cross = run(
        far_kernel,
        operands=[narrow, swap(far_send, FIRST[2])],
        outs=[like((4 * NARROW, *BLOCK), F32), like((32, 128), F32)],
    )
    gots = swap_round(sends, FIRST)
    down_other = swap(down_part, ACROSS)
    norm_one_other = swap(norm_one_part, ACROSS)
    results = run(
        second_kernel,
        operands=gots + keeps + [narrow, small, cross],
        outs=blocks([TILES + 1] * 3 + [TILES]) + [like((32, 128), F32)],
    )
    sends, keep, small = list(results[:3]), results[3], results[4]
    gots = swap_round(sends, SECOND)
    mixed, tokens_grad = run(
        finish_kernel,
        operands=[resid, down_part, down_other, norm_one_part, norm_one_other, tokens, resid_grad, gain_one_row],
        outs=[like((rows, width), BF16), like((rows, width), F32)],
        flops=LONG,
    )
    gots[0], mixed, tokens_grad = lax.optimization_barrier((gots[0], mixed, tokens_grad))
    beside, kept = run(
        third_kernel,
        operands=gots + [keep, small],
        outs=[like((TILES + 2, 32, 128), BF16), like((TILES + 2, 32, 128), F32)],
    )
    beside = swap(beside, BESIDE)
    mine, away = run(
        cores_kernel,
        operands=[kept, beside],
        outs=[like((TILES + 2, 16, 128), F32)] * 2,
    )
    down_g, gate_g, up_g, in_g, out_g, gain_one_g, gain_two_g, conv_g = run(
        outputs_kernel,
        operands=[mine, swap(away, CORES)],
        outs=[like((16, 2 * WIDE_COLUMNS), F32)] * 3
        + [like((3, 16, channels), F32), like((16, channels), F32)]
        + [like((1, width), F32)] * 2
        + [like((3, channels), F32)],
    )
    in_g, gain_one_g, gain_two_g = in_g.transpose(1, 0, 2), gain_one_g.reshape(-1), gain_two_g.reshape(-1)
    return (mixed, tokens_grad, gain_one_g, in_g, conv_g, out_g.T, gain_two_g, gate_g, up_g, down_g.T)


def solution(mesh):
    return jax.shard_map(
        on_device,
        mesh=mesh,
        in_specs=(
            P("seq", None),
            P("seq"),
            P(),
            P(None, None, "tensor"),
            P(None, "tensor"),
            P("tensor", None),
            P(),
            P(None, "tensor"),
            P(None, "tensor"),
            P("tensor", None),
            P("seq", None),
        ),
        out_specs=(
            P("seq", None),
            P("seq", None),
            P(),
            P("seq", None, "tensor"),
            P(None, "tensor"),
            P("tensor", "seq"),
            P(),
            P("seq", "tensor"),
            P("seq", "tensor"),
            P("tensor", "seq"),
        ),
        check_vma=False,
    )
```

```python
import functools

import jax
import jax.numpy as jnp
from jax import lax
from jax.experimental import pallas as pl
from jax.experimental.pallas import tpu as pltpu
from jax.sharding import PartitionSpec as P

EPS = 1e-05
AXES = ("seq", "tensor")
BF16 = jnp.bfloat16
F32 = jnp.float32


def device_pairs(move):
    def number(y, z, x, core):
        return ((((y % 4) * 4 + z % 4) * 2 + x % 2) * 2 + core) * 2 + (x % 4) // 2

    return [
        (number(y, z, x, core), number(*move(y, z, x, core)))
        for y in range(4)
        for z in range(4)
        for x in range(4)
        for core in range(2)
    ]


ACROSS = device_pairs(lambda y, z, x, core: (y, z, (x + 2) % 4, core))
BESIDE = device_pairs(lambda y, z, x, core: (y, z, x ^ 1, core))
BESIDE_OTHER = device_pairs(lambda y, z, x, core: (y, z, x ^ 1, 1 - core))
CORES = device_pairs(lambda y, z, x, core: (y, z, x, 1 - core))


def peer(at, pairing):
    return (at ^ 1, 3 - at, at ^ 2)[pairing]


FIRST = [
    device_pairs(
        functools.partial(
            lambda pairing, y, z, x, core: (y, peer(z, pairing), x, core)
            if core
            else (peer(y, pairing), z, x, core),
            pairing,
        )
    )
    for pairing in range(3)
]
SECOND = [
    device_pairs(
        functools.partial(
            lambda pairing, y, z, x, core: (peer(y, pairing), z, x, core)
            if core
            else (y, peer(z, pairing), x, core),
            pairing,
        )
    )
    for pairing in range(3)
]
WIDE_COLUMNS = 1152
WIDE_TILES = 27
WIDE = (14, 13)
NARROW = 8
BLOCK = (64, 128)
LONG = 3 * 10**10
SHORT = 8 * 10**9
TILES = WIDE_TILES + NARROW
WIDE_BLOCKS = (4 * WIDE[1], 4 * WIDE[0], 0)
ROUND_ONE = tuple(count + 4 * NARROW + 1 for count in WIDE_BLOCKS)


def swap(value, pairs):
    return lax.ppermute(value, AXES, pairs)


def from_behind(value, axis, steps):
    count = lax.axis_size(axis)
    leading, last = (max(0, -steps), min(count, count - steps))
    return lax.ppermute(value, axis, [(source, source + steps) for source in range(leading, last)])


def norm_scale(values):
    return lax.rsqrt(jnp.mean(values * values, axis=1, keepdims=True) + EPS)


def norm_backward(out_grad_rows, values, scale_rows, gain):
    scaled = out_grad_rows * gain
    inner = jnp.mean(scaled * values, axis=1, keepdims=True)
    return scale_rows * (scaled - values * scale_rows * scale_rows * inner)


def like(shape, dtype):
    return jax.ShapeDtypeStruct(shape, dtype)


def positions(offset):
    at = lax.axis_index("seq")
    y, z, core = at // 16, (at // 4) % 4, at % 2
    first, second = jnp.where(core == 0, y, z), jnp.where(core == 0, z, y)
    return first, second, (at // 2) % 2, core, offset


def call(body, *, operands, outs, scratch=(), offset=None, flops=0, aliases=None, where=pltpu.VMEM, scalar=None):
    whole = pl.BlockSpec(memory_space=pltpu.VMEM)
    specs = [pl.BlockSpec(memory_space=where)] * len(operands)
    if scalar is not None:
        operands, specs = [scalar, *operands], [pl.BlockSpec(memory_space=pltpu.SMEM), *specs]

    def kernel(*refs):
        if offset is None:
            body(positions(None), *refs)
        else:
            body(positions(refs[0][0:1, 0:1]), *refs[1:])

    if offset is not None:
        operands, specs = [offset, *operands], [whole, *specs]
    return pl.pallas_call(
        kernel,
        out_shape=tuple(outs),
        in_specs=specs,
        out_specs=tuple(whole for _ in outs),
        scratch_shapes=list(scratch),
        input_output_aliases=aliases or {},
        compiler_params=pltpu.CompilerParams(vmem_limit_bytes=16 * 2**20),
        cost_estimate=pl.CostEstimate(flops=flops, bytes_accessed=0, transcendentals=0),
    )(*operands)


def dot(left, right):
    return jnp.dot(left, right, preferred_element_type=F32)


def dot_rows(left, right):
    return lax.dot_general(left, right, (((1,), (1,)), ((), ())), preferred_element_type=F32)


def row_numbers(shape, first=0):
    return lax.broadcasted_iota(jnp.int32, shape, 0) + first


def valid_rows(offset, lag, shape):
    row = row_numbers(shape)
    return jnp.where((offset <= row) & (offset > row - lag), 0.0, 1.0)


def linked_rows(offset, shape, first, count):
    return jnp.where((row_numbers(shape, first) < offset) & (offset < count), 0.0, 1.0)


def load_kernel(scalars, starts, tokens, gain, weight, tail, token_rows, gain_row, weights, offset, done):
    rows, depth = tokens.shape[0], weight.shape[1] // 4
    pieces = [(gain, gain_row)]
    pieces += [(tokens.at[pl.ds(at, 128)], token_rows.at[pl.ds(at, 128)]) for at in (rows - 128, 0)]
    for k in (0, 2, 1):
        for at in range(0, weight.shape[1], depth):
            pieces.append((weight.at[k, pl.ds(at, depth)], weights.at[k, pl.ds(at, depth)]))
    copies = [
        pltpu.make_async_copy(source, target, done.at[at]) for at, (source, target) in enumerate(pieces)
    ]
    for copy in copies:
        copy.start()
    for copy in copies[:2]:
        copy.wait()
    offset[...] = jnp.full(offset.shape, starts[0], jnp.int32)
    values = token_rows[rows - 16 :].astype(F32)
    normed = (values * norm_scale(values) * gain_row[...]).astype(BF16)
    for copy in copies[2:11]:
        copy.wait()
    gated = (dot(normed, weights[0]) * dot(normed, weights[2])).astype(BF16).astype(F32)
    tail[...] = (gated * linked_rows(starts[0], gated.shape, rows - 16, rows)).astype(BF16)
    for copy in copies[11:]:
        copy.wait()


def project_kernel(scalars, tokens, gain, weights, normed, parts, gated):
    values = tokens[...].astype(F32)
    normed[...] = (values * norm_scale(values) * gain[...]).astype(BF16)
    for k in range(3):
        parts[k] = dot(normed[...], weights[k])
    gated[...] = (parts[0] * parts[2]).astype(BF16)


def behind(gated, incoming, lag):
    moved = pltpu.roll(gated, lag, 0)
    row = row_numbers(gated.shape)
    for at in range(lag):
        moved = jnp.where(row == at, incoming[16 - lag + at : 17 - lag + at], moved)
    return moved


def mix_kernel(scalars, gated, incoming, parts, taps, weight, conv, ymix, branch):
    values = gated[...].astype(F32)
    before = incoming[...].astype(F32)
    total = taps[0:1] * values
    for lag in (1, 2):
        total = total + taps[lag : lag + 1] * behind(values, before, lag) * valid_rows(
            scalars[4], lag, values.shape
        )
    conv[...] = total
    ymix[...] = (parts[1] * total).astype(BF16)
    branch[...] = dot(ymix[...], weight[...]).astype(BF16)


def away_half(value, core):
    half = value.shape[-1] // 2
    return jnp.where(core == 0, value[..., half:], value[..., :half])


def hidden_kernel(scalars, cot, weight, out):
    for at in range(0, weight.shape[0], 256):
        out[:, at : at + 256] = dot_rows(cot[...], weight[at : at + 256])


def down_kernel(scalars, hidden, weight, out):
    out[...] = dot(hidden[...], weight[...]).astype(BF16)


def feed_kernel(
    scalars,
    tokens,
    branch,
    other,
    gain,
    gate,
    up,
    hidden_grad,
    normed_one,
    ymix,
    resid,
    normed,
    hidden,
    gate_back,
    up_back,
    shared,
    shared_early,
):
    resid[...] = tokens[...].astype(F32) + (branch[...].astype(F32) + other[...].astype(F32))
    normed[...] = (resid[...] * norm_scale(resid[...]) * gain[...]).astype(BF16)
    values = normed[...]
    for at in range(0, gate.shape[1], 256):
        columns = slice(at, at + 256)
        gate_act, up_act = dot(values, gate[:, columns]), dot(values, up[:, columns])
        back = hidden_grad[:, columns]
        sigmoid_gate = jax.nn.sigmoid(gate_act)
        swish = gate_act * sigmoid_gate
        hidden[:, columns] = (swish * up_act).astype(BF16)
        up_back[:, columns] = (back * swish).astype(BF16)
        slope = sigmoid_gate * (1.0 + gate_act * (1.0 - sigmoid_gate))
        gate_back[:, columns] = (back * up_act * slope).astype(BF16)
    away = pl.ds(pl.multiple_of((1 - scalars[3]) * WIDE_COLUMNS, 128), WIDE_COLUMNS)
    for k, value in enumerate((hidden, gate_back, up_back)):
        shared[:, k * WIDE_COLUMNS : (k + 1) * WIDE_COLUMNS] = value[:, away]
    shared[:, 3 * WIDE_COLUMNS :] = values
    shared_early[:, : normed.shape[1]] = normed_one[...]
    shared_early[:, normed.shape[1] :] = away_half(ymix[...], scalars[3])


def part_kernel(scalars, gate_back, up_back, gate, up, part):
    part[...] = (dot_rows(gate_back[...], gate[...]) + dot_rows(up_back[...], up[...])).astype(BF16)


def second_norm(part, other, resid, gain, cot):
    back = part.astype(F32) + other.astype(F32)
    scale = norm_scale(resid)
    return back, scale, cot.astype(F32) + norm_backward(back, resid, scale, gain)


def edge_kernel(scalars, part, other, resid, gain, cot, weight, parts, taps, edge):
    top = slice(0, 16)
    _, _, grad = second_norm(part[top], other[top], resid[top], gain[...], cot[top])
    conv_back = dot_rows(grad.astype(BF16), weight[...]) * parts[1, top]
    one = conv_back * valid_rows(scalars[4], 1, conv_back.shape) * taps[1:2]
    two = conv_back * valid_rows(scalars[4], 2, conv_back.shape) * taps[2:3]
    row = row_numbers((8, conv_back.shape[1]))
    edge[...] = jnp.where(row == 6, two[0:1], 0.0) + jnp.where(row == 7, one[0:1] + two[1:2], 0.0)


def middle_kernel(
    scalars, part, other, resid, gain, cot, weight, parts, taps, conv, gated, incoming, grad, low, gain_grad, c_back, gated_back, tap_grads
):
    back, scale, resid_grad = second_norm(part[...], other[...], resid[...], gain[...], cot[...])
    gain_grad[...] = jnp.sum(back * resid[...] * scale, axis=0, keepdims=True)
    grad[...] = resid_grad
    low[...] = resid_grad.astype(BF16)
    ymix_back = dot_rows(low[...], weight[...])
    c_back[...] = (ymix_back * conv[...]).astype(BF16)
    conv_back = ymix_back * parts[1]
    values, before = gated[...].astype(F32), incoming[...].astype(F32)
    rows = values.shape[0]
    tap_grads[0:1] = jnp.sum(conv_back * values, axis=0, keepdims=True)
    total = conv_back * taps[0:1]
    row = row_numbers(values.shape)
    for lag in (1, 2):
        term = conv_back * valid_rows(scalars[4], lag, values.shape)
        tap_grads[lag : lag + 1] = jnp.sum(term * behind(values, before, lag), axis=0, keepdims=True)
        moved = pltpu.roll(term * taps[lag : lag + 1], rows - lag, 0)
        total = total + jnp.where(row < rows - lag, moved, 0.0)
    gated_back[...] = total


def last_kernel(
    scalars,
    gated_back,
    returned,
    parts,
    c_back,
    weight,
    tokens,
    gain_two_grad,
    tap_grads,
    resid_low,
    backs,
    shared,
    part,
    gain_part,
    small,
):
    rows = gated_back.shape[0]
    links = linked_rows(scalars[4], returned.shape, rows - 8, rows)
    end = gated_back[rows - 8 :] + returned[...] * links
    total = jnp.concatenate([gated_back[: rows - 8], end], 0)
    backs[0] = (total * parts[2]).astype(BF16)
    backs[1] = c_back[...]
    backs[2] = (total * parts[0]).astype(BF16)
    for k in range(3):
        shared[4 + k] = away_half(backs[k], scalars[3])
    for at in range(4):
        shared[at] = resid_low[:, at * 256 : at * 256 + 256]
    grad = dot_rows(backs[0], weight[0]) + dot_rows(backs[1], weight[1]) + dot_rows(backs[2], weight[2])
    part[...] = grad.astype(BF16)
    values = tokens[...].astype(F32)
    gain_grad = jnp.sum(grad * values * norm_scale(values), axis=0, keepdims=True)
    for at in range(8):
        lanes = slice(at * 128, at * 128 + 128)
        gain_part[at : at + 1] = gain_grad[:, lanes]
        small[8 + at : 9 + at] = gain_two_grad[:, lanes]
    for lag in range(3):
        for at in range(4):
            row = 16 + 4 * lag + at
            small[row : row + 1] = tap_grads[lag : lag + 1, at * 128 : at * 128 + 128]
    small[:8] = jnp.zeros((8, 128), F32)
    small[28:32] = jnp.zeros((4, 128), F32)


def fill_transposed(left, own, other):
    for at in range(0, own.shape[1], 256):
        left[at : at + 256, :256] = own[:, at : at + 256].T
        left[at : at + 256, 256:] = other[:, at : at + 256].T


def chunk_rows(left, core, chunk):
    wide, slim = jnp.where(core == 0, 256, 64), jnp.where(core == 0, 64, 256)
    return jnp.concatenate(
        [left[pl.ds(pl.multiple_of(chunk * wide + at * slim, 64), 64)] for at in range(4)], 0
    )


def store_blocks(value, target, base, tiles, tile):
    value = value.astype(BF16)
    for chunk in range(4):
        for column in range(value.shape[1] // 128):
            target[base + chunk * tiles + tile + column] = value[
                chunk * 64 : chunk * 64 + 64, column * 128 : column * 128 + 128
            ]


def wide_runs(kind):
    at, end = (0, WIDE[0]) if kind == 0 else (WIDE[0], WIDE_TILES)
    first = at
    while at < end:
        matrix, tile = divmod(at, WIDE_COLUMNS // 128)
        count = min(2, WIDE_COLUMNS // 128 - tile, end - at)
        yield matrix, tile * 128, count * 128, at - first
        at += count


def wide_piece(scalars, kind, lefts, own, shared, send, keep):
    at, core = scalars[0], scalars[3]
    first, second = peer(at, kind), peer(at, 1 - kind)
    chunks = (at, second, first, peer(first, 1 - kind))
    for slot, chunk in enumerate(chunks):
        target = keep if slot < 2 else send
        rows = {}
        for matrix, column, width, tile in wide_runs(kind):
            if (matrix == 0) not in rows:
                rows[matrix == 0] = chunk_rows(lefts[matrix], core, chunk)
            left = rows[matrix == 0]
            mine = pl.ds(pl.multiple_of(core * WIDE_COLUMNS + column, 128), width)
            away = matrix * WIDE_COLUMNS + column
            value = dot(left[:, :256], own[matrix][:, mine])
            value = value + dot(left[:, 256:], shared[:, away : away + width])
            store_blocks(value, target, (slot % 2) * 4 * WIDE[kind], WIDE[kind], tile)


def wide_first_kernel(scalars, two, cot, cot_other, hidden, gate_back, shared, send, keep, left_two, left_cot):
    fill_transposed(left_cot, cot, cot_other)
    fill_transposed(left_two, two, shared.at[:, 3 * WIDE_COLUMNS :])
    wide_piece(scalars, 0, (left_cot, left_two), (hidden, gate_back), shared, send, keep)


def wide_second_kernel(scalars, left_two, gate_back, up_back, shared, send, keep):
    wide_piece(scalars, 1, (None, left_two, left_two), (None, gate_back, up_back), shared, send, keep)


def narrow_kernel(scalars, one, shared, low, late_other, backs, ymix, *refs):
    (small, gain, gain_other), outs, (new_small, left_one, left_low) = refs[:3], refs[3:7], refs[7:]
    new_small[:8] = gain[...] + gain_other[...]
    new_small[8:] = small[8:]
    for pairing in range(3):
        split_small(new_small[...], outs[pairing], ROUND_ONE[pairing] - 1)
    width = one.shape[1]
    one_other, ymix_other = shared.at[:, :width], shared.at[:, width:]
    for at in range(0, width, 256):
        left_one[at : at + 256, :256] = one[:, at : at + 256].T
        left_one[at : at + 256, 256:] = one_other[:, at : at + 256].T
        left_low[at : at + 256, :256] = low[:, at : at + 256].T
        left_low[at : at + 256, 256:] = late_other[at // 256].T
    mine = pl.ds(pl.multiple_of(scalars[3] * 256, 256), 256)
    for slot in range(4):
        chunk = peer(scalars[0], slot) if slot < 3 else scalars[0]
        for kind in range(4):
            left, own, other = (
                (left_one, backs[kind, :, mine], late_other[4 + kind])
                if kind < 3
                else (left_low, ymix[:, mine], ymix_other[...])
            )
            rows = chunk_rows(left, scalars[3], chunk)
            value = dot(rows[:, :256], own) + dot(rows[:, 256:], other)
            store_blocks(value, outs[slot], WIDE_BLOCKS[slot] if slot < 3 else 0, NARROW, 2 * kind)


def split_small(value, target, at):
    high = value.astype(BF16)
    target[at, :32] = high
    target[at, 32:] = (value - high.astype(F32)).astype(BF16)


def join_small(source, at):
    return source[at, :32].astype(F32) + source[at, 32:].astype(F32)


def rounded_small(value):
    high = value.astype(BF16)
    return high.astype(F32) + (value - high.astype(F32)).astype(BF16).astype(F32)


def sum_small(value, near, far, cross):
    return (rounded_small(value) + cross) + (near + far)


def far_kernel(scalars, mine, got, total, small):
    total[...] = mine[...].astype(F32) + got[: 4 * NARROW].astype(F32)
    small[...] = join_small(got, 4 * NARROW)


def first_kernel(scalars, *refs):
    gots, keeps, sends, wide_keeps = refs[:2], refs[2:4], refs[6:8], refs[8:]
    for kind in range(2):
        half = 4 * WIDE[kind]
        for chunk in range(4):
            at = slice(chunk * WIDE[kind], (chunk + 1) * WIDE[kind])
            after = slice(half + chunk * WIDE[kind], half + (chunk + 1) * WIDE[kind])
            wide_keeps[kind][at] = (keeps[kind][at].astype(F32) + gots[kind][at].astype(F32)).astype(BF16)
            sends[1 - kind][at] = (keeps[kind][after].astype(F32) + gots[kind][after].astype(F32)).astype(BF16)


def second_kernel(scalars, *refs):
    gots, wide_in, (narrow, small, cross) = refs[:2], refs[2:4], refs[4:7]
    sends, (keep, new_small) = refs[7:10], refs[10:]

    def fill(chunk, target):
        tile = 0
        for kind in range(2):
            at = pl.ds(chunk * WIDE[kind], WIDE[kind])
            value = wide_in[kind][at].astype(F32) + gots[1 - kind][at].astype(F32)
            target[tile : tile + WIDE[kind]] = value.astype(BF16)
            tile += WIDE[kind]
        value = narrow[pl.ds(chunk * NARROW, NARROW)]
        for pairing in range(2):
            value = value + gots[pairing][pl.ds(WIDE_BLOCKS[pairing] + chunk * NARROW, NARROW)].astype(F32)
        target[tile : tile + NARROW] = value.astype(BF16)

    near, far = (join_small(got, count - 1) for got, count in zip(gots, ROUND_ONE))
    value = sum_small(small[...], near, far, cross[...])
    new_small[...] = value
    for pairing in range(3):
        fill(peer(scalars[1], pairing), sends[pairing])
        split_small(value, sends[pairing], TILES)
    fill(scalars[1], keep)


def third_kernel(scalars, *refs):
    gots, (kept, small), (mine, away, near, far, new_small) = refs[:3], refs[3:5], refs[5:]
    here, core = scalars[2], scalars[3]
    for first in range(0, TILES, 7):
        at = slice(first, first + 7)
        value = kept[at].astype(F32)
        for got in gots:
            value = value + got[at].astype(F32)
        zero, one = value[:, :32], value[:, 32:]
        stay, leave = jnp.where(here == 0, zero, one), jnp.where(here == 0, one, zero)
        mine[at] = jnp.where(core == 0, stay[:, :16], stay[:, 16:])
        away[at] = jnp.where(core == 0, stay[:, 16:], stay[:, :16])
        near[at] = jnp.where(core == 0, leave[:, :16], leave[:, 16:]).astype(BF16)
        far[at] = jnp.where(core == 0, leave[:, 16:], leave[:, :16]).astype(BF16)
    value = sum_small(small[...], *(join_small(got, TILES) for got in gots))
    high = value.astype(BF16)
    low = (value - high.astype(F32)).astype(BF16)
    new_small[...] = high.astype(F32) + low.astype(F32)
    for at in range(2):
        rows = slice(16 * at, 16 * at + 16)
        away[TILES + at] = new_small[rows]
        for target in (near, far):
            target[TILES + at] = high[rows]
            target[TILES + 2 + at] = low[rows]


def finish_kernel(
    scalars, resid, down, down_other, part, other, tokens, resid_grad, gain, mixed, tokens_grad
):
    mixed[...] = (resid[...] + (down[...].astype(F32) + down_other[...].astype(F32))).astype(BF16)
    values = tokens[...].astype(F32)
    back = part[...].astype(F32) + other[...].astype(F32)
    tokens_grad[...] = resid_grad[...] + norm_backward(back, values, norm_scale(values), gain[...])


def outputs_kernel(scalars, mine, away, near, far, small, down, gate, up, inner, out, gain_one, gain_two, taps):
    core = scalars[3]

    def place(target, tile, column, columns):
        own = mine[tile] + near[tile].astype(F32)
        other = away[tile] + far[tile].astype(F32)
        target[:, column : column + 128] = jnp.where(core == 0, own, other)
        target[:, columns + column : columns + column + 128] = jnp.where(core == 0, other, own)

    for matrix, target in enumerate((down, gate, up)):
        for tile in range(WIDE_COLUMNS // 128):
            place(target, matrix * (WIDE_COLUMNS // 128) + tile, tile * 128, WIDE_COLUMNS)
    for kind in range(4):
        for column in range(2):
            place(inner.at[kind] if kind < 3 else out, WIDE_TILES + 2 * kind + column, column * 128, 256)
    sums = []
    for at in range(2):
        own = small[16 * at : 16 * at + 16] + (near[TILES + at].astype(F32) + near[TILES + 2 + at].astype(F32))
        other = away[TILES + at] + (far[TILES + at].astype(F32) + far[TILES + 2 + at].astype(F32))
        sums.append(own + other)
    gains, rest = sums
    for at in range(8):
        lanes = slice(at * 128, at * 128 + 128)
        gain_one[:, lanes] = gains[at : at + 1]
        gain_two[:, lanes] = gains[8 + at : 9 + at]
    for lag in range(3):
        for at in range(4):
            row = 4 * lag + at
            taps[lag : lag + 1, at * 128 : at * 128 + 128] = rest[row : row + 1]


def swap_round(sends, pairings):
    return [swap(value, pairs) for value, pairs in zip(sends, pairings)]


def blocks(counts):
    return [like((count, *BLOCK), BF16) for count in counts]


def on_device(
    tokens,
    starts,
    gain_one,
    in_weight,
    conv_weight,
    out_weight,
    gain_two,
    gate_weight,
    up_weight,
    down_weight,
    cotangent,
):
    core = lax.axis_index("seq") % 2
    run = call
    rows, width = tokens.shape
    channels = conv_weight.shape[1]
    in_parts = in_weight.transpose(1, 0, 2)
    gain_one_row, gain_two_row = gain_one.reshape(1, -1), gain_two.reshape(1, -1)

    def share(value):
        return swap(value, CORES)

    tail, tokens_here, gain_here, weights_here, offset = run(
        load_kernel,
        operands=[
            pltpu.with_memory_space_constraint(value, pltpu.HBM) for value in (tokens, gain_one_row, in_parts)
        ],
        scalar=starts,
        outs=[
            like((16, channels), BF16),
            like((rows, width), BF16),
            like((1, width), F32),
            like((3, width, channels), BF16),
            like((8, 128), jnp.int32),
        ],
        scratch=[pltpu.SemaphoreType.DMA((15,))],
        where=pltpu.HBM,
    )
    incoming = from_behind(tail, "seq", 1)
    cotangent_other = share(cotangent)
    incoming, cotangent_other = lax.optimization_barrier((incoming, cotangent_other))
    normed_one, parts, gated = run(
        project_kernel,
        operands=[tokens_here, gain_here, weights_here],
        outs=[like((rows, width), BF16), like((3, rows, channels), F32), like((rows, channels), BF16)],
    )
    conv, ymix, branch = run(
        mix_kernel,
        offset=offset,
        operands=[gated, incoming, parts, conv_weight, out_weight],
        outs=[like((rows, channels), F32), like((rows, channels), BF16), like((rows, width), BF16)],
    )
    branch, cotangent_late = lax.optimization_barrier((branch, cotangent))
    branch_other = swap(branch, ACROSS)
    units = gate_weight.shape[1]
    hidden_grad = run(
        hidden_kernel,
        operands=[cotangent_late, down_weight],
        outs=[like((rows, units), F32)],
        flops=LONG,
    )[0]
    branch_other, hidden_grad = lax.optimization_barrier((branch_other, hidden_grad))
    resid, normed_two, hidden, gate_back, up_back, shared, shared_early = run(
        feed_kernel,
        operands=[tokens, branch, branch_other, gain_two_row, gate_weight, up_weight, hidden_grad]
        + [normed_one, ymix],
        outs=[like((rows, width), F32), like((rows, width), BF16)]
        + [like((rows, units), BF16)] * 3
        + [like((rows, 3 * WIDE_COLUMNS + width), BF16), like((rows, width + channels // 2), BF16)],
    )
    shared_other = share(shared)
    norm_two_part = run(
        part_kernel, operands=[gate_back, up_back, gate_weight, up_weight], outs=[like((rows, width), BF16)]
    )[0]
    norm_two_other = swap(norm_two_part, ACROSS)
    first_send, first_keep, left_two = run(
        wide_first_kernel,
        operands=[normed_two, cotangent, cotangent_other, hidden, gate_back, shared_other],
        outs=blocks([8 * WIDE[0]] * 2) + [like((width, 2 * rows), BF16)],
        scratch=[pltpu.VMEM((width, 2 * rows), BF16)],
    )
    second_send, second_keep = run(
        wide_second_kernel,
        operands=[left_two, gate_back, up_back, shared_other],
        outs=blocks([8 * WIDE[1]] * 2),
    )
    sends, keeps = [first_send, second_send], [first_keep, second_keep]
    hidden, sends[1] = lax.optimization_barrier((hidden, sends[1]))
    down_part = run(down_kernel, operands=[hidden, down_weight], outs=[like((rows, width), BF16)])[0]
    early_other = share(shared_early)
    norm_two_other, keeps[1], down_part, early_other = lax.optimization_barrier(
        (norm_two_other, keeps[1], down_part, early_other)
    )
    gots = swap_round(sends, FIRST)

    edge_operands = [norm_two_part, norm_two_other, resid, gain_two_row, cotangent, out_weight, parts, conv_weight]
    edge = run(edge_kernel, offset=offset, operands=edge_operands, outs=[like((8, channels), F32)])[0]
    returned = from_behind(edge, "seq", -1)
    resid_grad, resid_low, gain_two_grad, c_back, gated_back, tap_grads = run(
        middle_kernel,
        offset=offset,
        operands=edge_operands + [conv, gated, incoming],
        outs=[
            like((rows, width), F32),
            like((rows, width), BF16),
            like((1, width), F32),
            like((rows, channels), BF16),
            like((rows, channels), F32),
            like((3, channels), F32),
        ],
        flops=SHORT,
    )
    backs, shared, norm_one_part, gain_part, small = run(
        last_kernel,
        offset=offset,
        operands=[gated_back, returned, parts, c_back, in_parts, tokens, gain_two_grad, tap_grads]
        + [resid_low],
        outs=[
            like((3, rows, channels), BF16),
            like((7, rows, 256), BF16),
            like((rows, width), BF16),
            like((8, 128), F32),
            like((32, 128), F32),
        ],
    )
    gain_other = swap(gain_part, ACROSS)
    *sends, narrow, small = run(
        narrow_kernel,
        operands=[normed_one, early_other, resid_low, share(shared), backs, ymix, small, gain_part, gain_other],
        outs=blocks(ROUND_ONE) + blocks([4 * NARROW]) + [like((32, 128), F32)],
        scratch=[pltpu.VMEM((width, 2 * rows), BF16)] * 2,
    )
    far_send = sends.pop()
    results = run(
        first_kernel,
        operands=gots + keeps + sends,
        aliases={4: 0, 5: 1},
        outs=blocks(ROUND_ONE[:2]) + blocks([4 * count for count in WIDE]),
    )
    sends, keeps = list(results[:2]), list(results[2:])
    keeps[0], far_send = lax.optimization_barrier((keeps[0], far_send))
    narrow, cross = run(
        far_kernel,
        operands=[narrow, swap(far_send, FIRST[2])],
        outs=[like((4 * NARROW, *BLOCK), F32), like((32, 128), F32)],
    )
    gots = swap_round(sends, FIRST)
    down_other = swap(down_part, ACROSS)
    norm_one_other = swap(norm_one_part, ACROSS)
    results = run(
        second_kernel,
        operands=gots + keeps + [narrow, small, cross],
        outs=blocks([TILES + 1] * 3 + [TILES]) + [like((32, 128), F32)],
    )
    sends, keep, small = list(results[:3]), results[3], results[4]
    gots = swap_round(sends, SECOND)
    mixed, tokens_grad = run(
        finish_kernel,
        operands=[resid, down_part, down_other, norm_one_part, norm_one_other, tokens, resid_grad, gain_one_row],
        outs=[like((rows, width), BF16), like((rows, width), F32)],
        flops=LONG,
    )
    gots[0], mixed, tokens_grad = lax.optimization_barrier((gots[0], mixed, tokens_grad))
    mine, away, near, far, small = run(
        third_kernel,
        operands=gots + [keep, small],
        outs=[like((TILES, 16, 128), F32), like((TILES + 2, 16, 128), F32)]
        + [like((TILES + 4, 16, 128), BF16)] * 2
        + [like((32, 128), F32)],
    )
    down_g, gate_g, up_g, in_g, out_g, gain_one_g, gain_two_g, conv_g = run(
        outputs_kernel,
        operands=[mine, swap(away, CORES), swap(near, BESIDE), swap(far, BESIDE_OTHER), small],
        outs=[like((16, 2 * WIDE_COLUMNS), F32)] * 3
        + [like((3, 16, channels), F32), like((16, channels), F32)]
        + [like((1, width), F32)] * 2
        + [like((3, channels), F32)],
    )
    in_g, gain_one_g, gain_two_g = in_g.transpose(1, 0, 2), gain_one_g.reshape(-1), gain_two_g.reshape(-1)
    return (mixed, tokens_grad, gain_one_g, in_g, conv_g, out_g.T, gain_two_g, gate_g, up_g, down_g.T)


def solution(mesh):
    return jax.shard_map(
        on_device,
        mesh=mesh,
        in_specs=(
            P("seq", None),
            P("seq"),
            P(),
            P(None, None, "tensor"),
            P(None, "tensor"),
            P("tensor", None),
            P(),
            P(None, "tensor"),
            P(None, "tensor"),
            P("tensor", None),
            P("seq", None),
        ),
        out_specs=(
            P("seq", None),
            P("seq", None),
            P(),
            P("seq", None, "tensor"),
            P(None, "tensor"),
            P("tensor", "seq"),
            P(),
            P("seq", "tensor"),
            P("seq", "tensor"),
            P("tensor", "seq"),
        ),
        check_vma=False,
    )
```

```python
import functools

import jax
import jax.numpy as jnp
from jax import lax
from jax.experimental import pallas as pl
from jax.experimental.pallas import tpu as pltpu
from jax.sharding import PartitionSpec as P

EPS = 1e-05
AXES = ("seq", "tensor")
BF16 = jnp.bfloat16
F32 = jnp.float32


def device_pairs(move):
    def number(y, z, x, core):
        return ((((y % 4) * 4 + z % 4) * 2 + x % 2) * 2 + core) * 2 + (x % 4) // 2

    return [
        (number(y, z, x, core), number(*move(y, z, x, core)))
        for y in range(4)
        for z in range(4)
        for x in range(4)
        for core in range(2)
    ]


ACROSS = device_pairs(lambda y, z, x, core: (y, z, (x + 2) % 4, core))
BESIDE = device_pairs(lambda y, z, x, core: (y, z, x ^ 1, core))
BESIDE_OTHER = device_pairs(lambda y, z, x, core: (y, z, x ^ 1, 1 - core))
CORES = device_pairs(lambda y, z, x, core: (y, z, x, 1 - core))


def peer(at, pairing):
    return (at ^ 1, 3 - at, at ^ 2)[pairing]


FIRST = [
    device_pairs(
        functools.partial(
            lambda pairing, y, z, x, core: (y, peer(z, pairing), x, core)
            if core
            else (peer(y, pairing), z, x, core),
            pairing,
        )
    )
    for pairing in range(3)
]
SECOND = [
    device_pairs(
        functools.partial(
            lambda pairing, y, z, x, core: (peer(y, pairing), z, x, core)
            if core
            else (y, peer(z, pairing), x, core),
            pairing,
        )
    )
    for pairing in range(3)
]
WIDE_COLUMNS = 1152
WIDE_TILES = 27
WIDE = (14, 13)
NARROW = 8
BLOCK = (64, 128)
LONG = 3 * 10**10
SHORT = 8 * 10**9
MIDDLE = 12 * 10**9
TILES = WIDE_TILES + NARROW
WIDE_BLOCKS = (4 * WIDE[1], 4 * WIDE[0], 0)
ROUND_ONE = tuple(count + 4 * NARROW + 1 for count in WIDE_BLOCKS)


def swap(value, pairs):
    return lax.ppermute(value, AXES, pairs)


def from_behind(value, axis, steps):
    count = lax.axis_size(axis)
    leading, last = (max(0, -steps), min(count, count - steps))
    return lax.ppermute(value, axis, [(source, source + steps) for source in range(leading, last)])


def norm_scale(values):
    return lax.rsqrt(jnp.mean(values * values, axis=1, keepdims=True) + EPS)


def norm_backward(out_grad_rows, values, scale_rows, gain):
    scaled = out_grad_rows * gain
    inner = jnp.mean(scaled * values, axis=1, keepdims=True)
    return scale_rows * (scaled - values * scale_rows * scale_rows * inner)


def like(shape, dtype):
    return jax.ShapeDtypeStruct(shape, dtype)


def positions(offset):
    at = lax.axis_index("seq")
    y, z, core = at // 16, (at // 4) % 4, at % 2
    first, second = jnp.where(core == 0, y, z), jnp.where(core == 0, z, y)
    return first, second, (at // 2) % 2, core, offset


def call(body, *, operands, outs, scratch=(), offset=None, flops=0, aliases=None, where=pltpu.VMEM, scalar=None):
    whole = pl.BlockSpec(memory_space=pltpu.VMEM)
    specs = [pl.BlockSpec(memory_space=where)] * len(operands)
    if scalar is not None:
        operands, specs = [scalar, *operands], [pl.BlockSpec(memory_space=pltpu.SMEM), *specs]

    def kernel(*refs):
        if offset is None:
            body(positions(None), *refs)
        else:
            body(positions(refs[0][0:1, 0:1]), *refs[1:])

    if offset is not None:
        operands, specs = [offset, *operands], [whole, *specs]
    return pl.pallas_call(
        kernel,
        out_shape=tuple(outs),
        in_specs=specs,
        out_specs=tuple(whole for _ in outs),
        scratch_shapes=list(scratch),
        input_output_aliases=aliases or {},
        compiler_params=pltpu.CompilerParams(vmem_limit_bytes=16 * 2**20),
        cost_estimate=pl.CostEstimate(flops=flops, bytes_accessed=0, transcendentals=0),
    )(*operands)


def dot(left, right):
    return jnp.dot(left, right, preferred_element_type=F32)


def dot_rows(left, right):
    return lax.dot_general(left, right, (((1,), (1,)), ((), ())), preferred_element_type=F32)


def row_numbers(shape, first=0):
    return lax.broadcasted_iota(jnp.int32, shape, 0) + first


def valid_rows(offset, lag, shape):
    row = row_numbers(shape)
    return jnp.where((offset <= row) & (offset > row - lag), 0.0, 1.0)


def linked_rows(offset, shape, first, count):
    return jnp.where((row_numbers(shape, first) < offset) & (offset < count), 0.0, 1.0)


def load_kernel(scalars, starts, tokens, gain, weight, tail, token_rows, gain_row, weights, offset, done):
    rows, depth = tokens.shape[0], weight.shape[1] // 4
    pieces = [(gain, gain_row)]
    pieces += [(tokens.at[pl.ds(at, 128)], token_rows.at[pl.ds(at, 128)]) for at in (rows - 128, 0)]
    for k in (0, 2, 1):
        for at in range(0, weight.shape[1], depth):
            pieces.append((weight.at[k, pl.ds(at, depth)], weights.at[k, pl.ds(at, depth)]))
    copies = [
        pltpu.make_async_copy(source, target, done.at[at]) for at, (source, target) in enumerate(pieces)
    ]
    for copy in copies:
        copy.start()
    for copy in copies[:2]:
        copy.wait()
    offset[...] = jnp.full(offset.shape, starts[0], jnp.int32)
    values = token_rows[rows - 16 :].astype(F32)
    normed = (values * norm_scale(values) * gain_row[...]).astype(BF16)
    for copy in copies[2:11]:
        copy.wait()
    gated = (dot(normed, weights[0]) * dot(normed, weights[2])).astype(BF16).astype(F32)
    tail[...] = (gated * linked_rows(starts[0], gated.shape, rows - 16, rows)).astype(BF16)
    for copy in copies[11:]:
        copy.wait()


def project_kernel(scalars, tokens, gain, weights, normed, parts, gated):
    values = tokens[...].astype(F32)
    normed[...] = (values * norm_scale(values) * gain[...]).astype(BF16)
    for k in range(3):
        parts[k] = dot(normed[...], weights[k])
    gated[...] = (parts[0] * parts[2]).astype(BF16)


def behind(gated, incoming, lag):
    moved = pltpu.roll(gated, lag, 0)
    row = row_numbers(gated.shape)
    for at in range(lag):
        moved = jnp.where(row == at, incoming[16 - lag + at : 17 - lag + at], moved)
    return moved


def mix_kernel(scalars, gated, incoming, parts, taps, weight, conv, ymix, branch):
    values = gated[...].astype(F32)
    before = incoming[...].astype(F32)
    total = taps[0:1] * values
    for lag in (1, 2):
        total = total + taps[lag : lag + 1] * behind(values, before, lag) * valid_rows(
            scalars[4], lag, values.shape
        )
    conv[...] = total
    ymix[...] = (parts[1] * total).astype(BF16)
    branch[...] = dot(ymix[...], weight[...]).astype(BF16)


def away_half(value, core):
    half = value.shape[-1] // 2
    return jnp.where(core == 0, value[..., half:], value[..., :half])


def hidden_kernel(scalars, cot, weight, out):
    for at in range(0, weight.shape[0], 256):
        out[:, at : at + 256] = dot_rows(cot[...], weight[at : at + 256])


def down_kernel(scalars, hidden, weight, out):
    out[...] = dot(hidden[...], weight[...]).astype(BF16)


def feed_kernel(
    scalars,
    tokens,
    branch,
    other,
    gain,
    gate,
    up,
    hidden_grad,
    normed_one,
    ymix,
    resid,
    normed,
    hidden,
    gate_back,
    up_back,
    shared,
    shared_early,
):
    resid[...] = tokens[...].astype(F32) + (branch[...].astype(F32) + other[...].astype(F32))
    normed[...] = (resid[...] * norm_scale(resid[...]) * gain[...]).astype(BF16)
    values = normed[...]
    for at in range(0, gate.shape[1], 256):
        columns = slice(at, at + 256)
        gate_act, up_act = dot(values, gate[:, columns]), dot(values, up[:, columns])
        back = hidden_grad[:, columns]
        sigmoid_gate = jax.nn.sigmoid(gate_act)
        swish = gate_act * sigmoid_gate
        hidden[:, columns] = (swish * up_act).astype(BF16)
        up_back[:, columns] = (back * swish).astype(BF16)
        slope = sigmoid_gate * (1.0 + gate_act * (1.0 - sigmoid_gate))
        gate_back[:, columns] = (back * up_act * slope).astype(BF16)
    away = pl.ds(pl.multiple_of((1 - scalars[3]) * WIDE_COLUMNS, 128), WIDE_COLUMNS)
    for k, value in enumerate((hidden, gate_back, up_back)):
        shared[:, k * WIDE_COLUMNS : (k + 1) * WIDE_COLUMNS] = value[:, away]
    shared[:, 3 * WIDE_COLUMNS :] = values
    shared_early[:, : normed.shape[1]] = normed_one[...]
    shared_early[:, normed.shape[1] :] = away_half(ymix[...], scalars[3])


def part_kernel(scalars, gate_back, up_back, gate, up, part):
    part[...] = (dot_rows(gate_back[...], gate[...]) + dot_rows(up_back[...], up[...])).astype(BF16)


def second_norm(part, other, resid, gain, cot):
    back = part.astype(F32) + other.astype(F32)
    scale = norm_scale(resid)
    return back, scale, cot.astype(F32) + norm_backward(back, resid, scale, gain)


def edge_kernel(scalars, part, other, resid, gain, cot, weight, parts, taps, edge):
    top = slice(0, 16)
    _, _, grad = second_norm(part[top], other[top], resid[top], gain[...], cot[top])
    conv_back = dot_rows(grad.astype(BF16), weight[...]) * parts[1, top]
    one = conv_back * valid_rows(scalars[4], 1, conv_back.shape) * taps[1:2]
    two = conv_back * valid_rows(scalars[4], 2, conv_back.shape) * taps[2:3]
    row = row_numbers((8, conv_back.shape[1]))
    edge[...] = jnp.where(row == 6, two[0:1], 0.0) + jnp.where(row == 7, one[0:1] + two[1:2], 0.0)


def middle_kernel(
    scalars, part, other, resid, gain, cot, weight, parts, taps, conv, gated, incoming, grad, low, gain_grad, c_back, gated_back, tap_grads
):
    back, scale, resid_grad = second_norm(part[...], other[...], resid[...], gain[...], cot[...])
    gain_grad[...] = jnp.sum(back * resid[...] * scale, axis=0, keepdims=True)
    grad[...] = resid_grad
    low[...] = resid_grad.astype(BF16)
    ymix_back = dot_rows(low[...], weight[...])
    c_back[...] = (ymix_back * conv[...]).astype(BF16)
    conv_back = ymix_back * parts[1]
    values, before = gated[...].astype(F32), incoming[...].astype(F32)
    rows = values.shape[0]
    tap_grads[0:1] = jnp.sum(conv_back * values, axis=0, keepdims=True)
    total = conv_back * taps[0:1]
    row = row_numbers(values.shape)
    for lag in (1, 2):
        term = conv_back * valid_rows(scalars[4], lag, values.shape)
        tap_grads[lag : lag + 1] = jnp.sum(term * behind(values, before, lag), axis=0, keepdims=True)
        moved = pltpu.roll(term * taps[lag : lag + 1], rows - lag, 0)
        total = total + jnp.where(row < rows - lag, moved, 0.0)
    gated_back[...] = total


def last_kernel(
    scalars,
    gated_back,
    returned,
    parts,
    c_back,
    weight,
    tokens,
    gain_two_grad,
    tap_grads,
    resid_low,
    backs,
    shared,
    part,
    gain_part,
    small,
):
    rows = gated_back.shape[0]
    links = linked_rows(scalars[4], returned.shape, rows - 8, rows)
    end = gated_back[rows - 8 :] + returned[...] * links
    total = jnp.concatenate([gated_back[: rows - 8], end], 0)
    backs[0] = (total * parts[2]).astype(BF16)
    backs[1] = c_back[...]
    backs[2] = (total * parts[0]).astype(BF16)
    for k in range(3):
        shared[4 + k] = away_half(backs[k], scalars[3])
    for at in range(4):
        shared[at] = resid_low[:, at * 256 : at * 256 + 256]
    grad = dot_rows(backs[0], weight[0]) + dot_rows(backs[1], weight[1]) + dot_rows(backs[2], weight[2])
    part[...] = grad.astype(BF16)
    values = tokens[...].astype(F32)
    gain_grad = jnp.sum(grad * values * norm_scale(values), axis=0, keepdims=True)
    for at in range(8):
        lanes = slice(at * 128, at * 128 + 128)
        gain_part[at : at + 1] = gain_grad[:, lanes]
        small[8 + at : 9 + at] = gain_two_grad[:, lanes]
    for lag in range(3):
        for at in range(4):
            row = 16 + 4 * lag + at
            small[row : row + 1] = tap_grads[lag : lag + 1, at * 128 : at * 128 + 128]
    small[:8] = jnp.zeros((8, 128), F32)
    small[28:32] = jnp.zeros((4, 128), F32)


def fill_transposed(left, own, other):
    for at in range(0, own.shape[1], 256):
        left[at : at + 256, :256] = own[:, at : at + 256].T
        left[at : at + 256, 256:] = other[:, at : at + 256].T


def chunk_rows(left, core, chunk):
    wide, slim = jnp.where(core == 0, 256, 64), jnp.where(core == 0, 64, 256)
    return jnp.concatenate(
        [left[pl.ds(pl.multiple_of(chunk * wide + at * slim, 64), 64)] for at in range(4)], 0
    )


def store_blocks(value, target, base, tiles, tile):
    value = value.astype(BF16)
    for chunk in range(4):
        for column in range(value.shape[1] // 128):
            target[base + chunk * tiles + tile + column] = value[
                chunk * 64 : chunk * 64 + 64, column * 128 : column * 128 + 128
            ]


def wide_runs(kind):
    at, end = (0, WIDE[0]) if kind == 0 else (WIDE[0], WIDE_TILES)
    first = at
    while at < end:
        matrix, tile = divmod(at, WIDE_COLUMNS // 128)
        count = min(2, WIDE_COLUMNS // 128 - tile, end - at)
        yield matrix, tile * 128, count * 128, at - first
        at += count


def wide_piece(scalars, kind, lefts, own, shared, send, keep):
    at, core = scalars[0], scalars[3]
    first, second = peer(at, kind), peer(at, 1 - kind)
    chunks = (at, second, first, peer(first, 1 - kind))
    for slot, chunk in enumerate(chunks):
        target = keep if slot < 2 else send
        rows = {}
        for matrix, column, width, tile in wide_runs(kind):
            if (matrix == 0) not in rows:
                rows[matrix == 0] = chunk_rows(lefts[matrix], core, chunk)
            left = rows[matrix == 0]
            mine = pl.ds(pl.multiple_of(core * WIDE_COLUMNS + column, 128), width)
            away = matrix * WIDE_COLUMNS + column
            value = dot(left[:, :256], own[matrix][:, mine])
            value = value + dot(left[:, 256:], shared[:, away : away + width])
            store_blocks(value, target, (slot % 2) * 4 * WIDE[kind], WIDE[kind], tile)


def wide_first_kernel(scalars, two, cot, cot_other, hidden, gate_back, shared, send, keep, left_two, left_cot):
    fill_transposed(left_cot, cot, cot_other)
    fill_transposed(left_two, two, shared.at[:, 3 * WIDE_COLUMNS :])
    wide_piece(scalars, 0, (left_cot, left_two), (hidden, gate_back), shared, send, keep)


def wide_second_kernel(scalars, left_two, gate_back, up_back, shared, send, keep):
    wide_piece(scalars, 1, (None, left_two, left_two), (None, gate_back, up_back), shared, send, keep)


def narrow_kernel(scalars, one, shared, low, late_other, backs, ymix, *refs):
    (small, gain, gain_other), outs, (new_small, left_one, left_low) = refs[:3], refs[3:7], refs[7:]
    new_small[:8] = gain[...] + gain_other[...]
    new_small[8:] = small[8:]
    for pairing in range(3):
        split_small(new_small[...], outs[pairing], ROUND_ONE[pairing] - 1)
    width = one.shape[1]
    one_other, ymix_other = shared.at[:, :width], shared.at[:, width:]
    for at in range(0, width, 256):
        left_one[at : at + 256, :256] = one[:, at : at + 256].T
        left_one[at : at + 256, 256:] = one_other[:, at : at + 256].T
        left_low[at : at + 256, :256] = low[:, at : at + 256].T
        left_low[at : at + 256, 256:] = late_other[at // 256].T
    mine = pl.ds(pl.multiple_of(scalars[3] * 256, 256), 256)
    for slot in range(4):
        chunk = peer(scalars[0], slot) if slot < 3 else scalars[0]
        for kind in range(4):
            left, own, other = (
                (left_one, backs[kind, :, mine], late_other[4 + kind])
                if kind < 3
                else (left_low, ymix[:, mine], ymix_other[...])
            )
            rows = chunk_rows(left, scalars[3], chunk)
            value = dot(rows[:, :256], own) + dot(rows[:, 256:], other)
            store_blocks(value, outs[slot], WIDE_BLOCKS[slot] if slot < 3 else 0, NARROW, 2 * kind)


def split_small(value, target, at):
    high = value.astype(BF16)
    target[at, :32] = high
    target[at, 32:] = (value - high.astype(F32)).astype(BF16)


def join_small(source, at):
    return source[at, :32].astype(F32) + source[at, 32:].astype(F32)


def rounded_small(value):
    high = value.astype(BF16)
    return high.astype(F32) + (value - high.astype(F32)).astype(BF16).astype(F32)


def sum_small(value, near, far, cross):
    return (rounded_small(value) + cross) + (near + far)


def far_kernel(scalars, mine, got, total, small):
    total[...] = mine[...].astype(F32) + got[: 4 * NARROW].astype(F32)
    small[...] = join_small(got, 4 * NARROW)


def first_kernel(scalars, *refs):
    gots, keeps, sends, wide_keeps = refs[:2], refs[2:4], refs[6:8], refs[8:]
    for kind in range(2):
        half = 4 * WIDE[kind]
        for chunk in range(4):
            at = slice(chunk * WIDE[kind], (chunk + 1) * WIDE[kind])
            after = slice(half + chunk * WIDE[kind], half + (chunk + 1) * WIDE[kind])
            wide_keeps[kind][at] = (keeps[kind][at].astype(F32) + gots[kind][at].astype(F32)).astype(BF16)
            sends[1 - kind][at] = (keeps[kind][after].astype(F32) + gots[kind][after].astype(F32)).astype(BF16)


def second_kernel(scalars, *refs):
    gots, wide_in, (narrow, small, cross) = refs[:2], refs[2:4], refs[4:7]
    sends, (keep, new_small) = refs[7:10], refs[10:]

    def fill(chunk, target):
        tile = 0
        for kind in range(2):
            at = pl.ds(chunk * WIDE[kind], WIDE[kind])
            value = wide_in[kind][at].astype(F32) + gots[1 - kind][at].astype(F32)
            target[tile : tile + WIDE[kind]] = value.astype(BF16)
            tile += WIDE[kind]
        value = narrow[pl.ds(chunk * NARROW, NARROW)]
        for pairing in range(2):
            value = value + gots[pairing][pl.ds(WIDE_BLOCKS[pairing] + chunk * NARROW, NARROW)].astype(F32)
        target[tile : tile + NARROW] = value.astype(BF16)

    near, far = (join_small(got, count - 1) for got, count in zip(gots, ROUND_ONE))
    value = sum_small(small[...], near, far, cross[...])
    new_small[...] = value
    for pairing in range(3):
        fill(peer(scalars[1], pairing), sends[pairing])
        split_small(value, sends[pairing], TILES)
    fill(scalars[1], keep)


def third_kernel(scalars, *refs):
    gots, (kept, small), (mine, away, near, far, new_small) = refs[:3], refs[3:5], refs[5:]
    here, core = scalars[2], scalars[3]
    for first in range(0, TILES, 7):
        at = slice(first, first + 7)
        value = kept[at].astype(F32)
        for got in gots:
            value = value + got[at].astype(F32)
        zero, one = value[:, :32], value[:, 32:]
        stay, leave = jnp.where(here == 0, zero, one), jnp.where(here == 0, one, zero)
        mine[at] = jnp.where(core == 0, stay[:, :16], stay[:, 16:])
        away[at] = jnp.where(core == 0, stay[:, 16:], stay[:, :16]).astype(BF16)
        near[at] = jnp.where(core == 0, leave[:, :16], leave[:, 16:]).astype(BF16)
        far[at] = jnp.where(core == 0, leave[:, 16:], leave[:, :16]).astype(BF16)
    value = sum_small(small[...], *(join_small(got, TILES) for got in gots))
    high = value.astype(BF16)
    low = (value - high.astype(F32)).astype(BF16)
    new_small[...] = high.astype(F32) + low.astype(F32)
    for at in range(2):
        rows = slice(16 * at, 16 * at + 16)
        for target in (away, near, far):
            target[TILES + at] = high[rows]
            target[TILES + 2 + at] = low[rows]
    for target in (near, far):
        target[TILES + 4] = jnp.zeros((16, 128), BF16)


def finish_kernel(
    scalars, resid, down, down_other, part, other, tokens, resid_grad, gain, mixed, tokens_grad
):
    mixed[...] = (resid[...] + (down[...].astype(F32) + down_other[...].astype(F32))).astype(BF16)
    values = tokens[...].astype(F32)
    back = part[...].astype(F32) + other[...].astype(F32)
    tokens_grad[...] = resid_grad[...] + norm_backward(back, values, norm_scale(values), gain[...])


def outputs_kernel(scalars, mine, away, near, far, small, down, gate, up, inner, out, gain_one, gain_two, taps):
    core = scalars[3]

    def place(target, tile, column, columns):
        own = mine[tile] + near[tile].astype(F32)
        other = away[tile].astype(F32) + far[tile].astype(F32)
        target[:, column : column + 128] = jnp.where(core == 0, own, other)
        target[:, columns + column : columns + column + 128] = jnp.where(core == 0, other, own)

    for matrix, target in enumerate((down, gate, up)):
        for tile in range(WIDE_COLUMNS // 128):
            place(target, matrix * (WIDE_COLUMNS // 128) + tile, tile * 128, WIDE_COLUMNS)
    for kind in range(4):
        for column in range(2):
            place(inner.at[kind] if kind < 3 else out, WIDE_TILES + 2 * kind + column, column * 128, 256)
    sums = []
    for at in range(2):
        came = [part[TILES + at].astype(F32) + part[TILES + 2 + at].astype(F32) for part in (near, away, far)]
        sums.append((small[16 * at : 16 * at + 16] + came[0]) + (came[1] + came[2]))
    gains, rest = sums
    for at in range(8):
        lanes = slice(at * 128, at * 128 + 128)
        gain_one[:, lanes] = gains[at : at + 1]
        gain_two[:, lanes] = gains[8 + at : 9 + at]
    for lag in range(3):
        for at in range(4):
            row = 4 * lag + at
            taps[lag : lag + 1, at * 128 : at * 128 + 128] = rest[row : row + 1]


def swap_round(sends, pairings):
    return [swap(value, pairs) for value, pairs in zip(sends, pairings)]


def blocks(counts):
    return [like((count, *BLOCK), BF16) for count in counts]


def on_device(
    tokens,
    starts,
    gain_one,
    in_weight,
    conv_weight,
    out_weight,
    gain_two,
    gate_weight,
    up_weight,
    down_weight,
    cotangent,
):
    core = lax.axis_index("seq") % 2
    run = call
    rows, width = tokens.shape
    channels = conv_weight.shape[1]
    in_parts = in_weight.transpose(1, 0, 2)
    gain_one_row, gain_two_row = gain_one.reshape(1, -1), gain_two.reshape(1, -1)

    def share(value):
        return swap(value, CORES)

    tail, tokens_here, gain_here, weights_here, offset = run(
        load_kernel,
        operands=[
            pltpu.with_memory_space_constraint(value, pltpu.HBM) for value in (tokens, gain_one_row, in_parts)
        ],
        scalar=starts,
        outs=[
            like((16, channels), BF16),
            like((rows, width), BF16),
            like((1, width), F32),
            like((3, width, channels), BF16),
            like((8, 128), jnp.int32),
        ],
        scratch=[pltpu.SemaphoreType.DMA((15,))],
        where=pltpu.HBM,
    )
    incoming = from_behind(tail, "seq", 1)
    cotangent_other = share(cotangent)
    incoming, cotangent_other = lax.optimization_barrier((incoming, cotangent_other))
    normed_one, parts, gated = run(
        project_kernel,
        operands=[tokens_here, gain_here, weights_here],
        outs=[like((rows, width), BF16), like((3, rows, channels), F32), like((rows, channels), BF16)],
    )
    conv, ymix, branch = run(
        mix_kernel,
        offset=offset,
        operands=[gated, incoming, parts, conv_weight, out_weight],
        outs=[like((rows, channels), F32), like((rows, channels), BF16), like((rows, width), BF16)],
    )
    branch, cotangent_late = lax.optimization_barrier((branch, cotangent))
    branch_other = swap(branch, ACROSS)
    units = gate_weight.shape[1]
    hidden_grad = run(
        hidden_kernel,
        operands=[cotangent_late, down_weight],
        outs=[like((rows, units), F32)],
        flops=LONG,
    )[0]
    branch_other, hidden_grad = lax.optimization_barrier((branch_other, hidden_grad))
    resid, normed_two, hidden, gate_back, up_back, shared, shared_early = run(
        feed_kernel,
        operands=[tokens, branch, branch_other, gain_two_row, gate_weight, up_weight, hidden_grad]
        + [normed_one, ymix],
        outs=[like((rows, width), F32), like((rows, width), BF16)]
        + [like((rows, units), BF16)] * 3
        + [like((rows, 3 * WIDE_COLUMNS + width), BF16), like((rows, width + channels // 2), BF16)],
    )
    shared_other = share(shared)
    norm_two_part = run(
        part_kernel, operands=[gate_back, up_back, gate_weight, up_weight], outs=[like((rows, width), BF16)]
    )[0]
    norm_two_other = swap(norm_two_part, ACROSS)
    first_send, first_keep, left_two = run(
        wide_first_kernel,
        operands=[normed_two, cotangent, cotangent_other, hidden, gate_back, shared_other],
        outs=blocks([8 * WIDE[0]] * 2) + [like((width, 2 * rows), BF16)],
        scratch=[pltpu.VMEM((width, 2 * rows), BF16)],
    )
    second_send, second_keep = run(
        wide_second_kernel,
        operands=[left_two, gate_back, up_back, shared_other],
        outs=blocks([8 * WIDE[1]] * 2),
    )
    sends, keeps = [first_send, second_send], [first_keep, second_keep]
    hidden, sends[1] = lax.optimization_barrier((hidden, sends[1]))
    down_part = run(down_kernel, operands=[hidden, down_weight], outs=[like((rows, width), BF16)])[0]
    early_other = share(shared_early)
    norm_two_other, keeps[1], down_part, early_other = lax.optimization_barrier(
        (norm_two_other, keeps[1], down_part, early_other)
    )
    gots = swap_round(sends, FIRST)

    edge_operands = [norm_two_part, norm_two_other, resid, gain_two_row, cotangent, out_weight, parts, conv_weight]
    edge = run(edge_kernel, offset=offset, operands=edge_operands, outs=[like((8, channels), F32)])[0]
    returned = from_behind(edge, "seq", -1)
    resid_grad, resid_low, gain_two_grad, c_back, gated_back, tap_grads = run(
        middle_kernel,
        offset=offset,
        operands=edge_operands + [conv, gated, incoming],
        outs=[
            like((rows, width), F32),
            like((rows, width), BF16),
            like((1, width), F32),
            like((rows, channels), BF16),
            like((rows, channels), F32),
            like((3, channels), F32),
        ],
        flops=SHORT,
    )
    backs, shared, norm_one_part, gain_part, small = run(
        last_kernel,
        offset=offset,
        operands=[gated_back, returned, parts, c_back, in_parts, tokens, gain_two_grad, tap_grads]
        + [resid_low],
        outs=[
            like((3, rows, channels), BF16),
            like((7, rows, 256), BF16),
            like((rows, width), BF16),
            like((8, 128), F32),
            like((32, 128), F32),
        ],
    )
    gain_other = swap(gain_part, ACROSS)
    *sends, narrow, small = run(
        narrow_kernel,
        operands=[normed_one, early_other, resid_low, share(shared), backs, ymix, small, gain_part, gain_other],
        outs=blocks(ROUND_ONE) + blocks([4 * NARROW]) + [like((32, 128), F32)],
        scratch=[pltpu.VMEM((width, 2 * rows), BF16)] * 2,
    )
    far_send = sends.pop()
    results = run(
        first_kernel,
        operands=gots + keeps + sends,
        aliases={4: 0, 5: 1},
        outs=blocks(ROUND_ONE[:2]) + blocks([4 * count for count in WIDE]),
    )
    sends, keeps = list(results[:2]), list(results[2:])
    keeps[0], far_send = lax.optimization_barrier((keeps[0], far_send))
    narrow, cross = run(
        far_kernel,
        operands=[narrow, swap(far_send, FIRST[2])],
        outs=[like((4 * NARROW, *BLOCK), F32), like((32, 128), F32)],
        flops=MIDDLE,
    )
    gots = swap_round(sends, FIRST)
    down_other = swap(down_part, ACROSS)
    norm_one_other = swap(norm_one_part, ACROSS)
    results = run(
        second_kernel,
        operands=gots + keeps + [narrow, small, cross],
        outs=blocks([TILES + 1] * 3 + [TILES]) + [like((32, 128), F32)],
    )
    sends, keep, small = list(results[:3]), results[3], results[4]
    gots = swap_round(sends, SECOND)
    mixed, tokens_grad = run(
        finish_kernel,
        operands=[resid, down_part, down_other, norm_one_part, norm_one_other, tokens, resid_grad, gain_one_row],
        outs=[like((rows, width), BF16), like((rows, width), F32)],
        flops=LONG,
    )
    gots[0], mixed, tokens_grad = lax.optimization_barrier((gots[0], mixed, tokens_grad))
    mine, away, near, far, small = run(
        third_kernel,
        operands=gots + [keep, small],
        outs=[like((TILES, 16, 128), F32), like((TILES + 4, 16, 128), BF16)]
        + [like((TILES + 5, 16, 128), BF16)] * 2
        + [like((32, 128), F32)],
    )
    down_g, gate_g, up_g, in_g, out_g, gain_one_g, gain_two_g, conv_g = run(
        outputs_kernel,
        operands=[mine, swap(away, CORES), swap(near, BESIDE), swap(far, BESIDE_OTHER), small],
        outs=[like((16, 2 * WIDE_COLUMNS), F32)] * 3
        + [like((3, 16, channels), F32), like((16, channels), F32)]
        + [like((1, width), F32)] * 2
        + [like((3, channels), F32)],
    )
    in_g, gain_one_g, gain_two_g = in_g.transpose(1, 0, 2), gain_one_g.reshape(-1), gain_two_g.reshape(-1)
    return (mixed, tokens_grad, gain_one_g, in_g, conv_g, out_g.T, gain_two_g, gate_g, up_g, down_g.T)


def solution(mesh):
    return jax.shard_map(
        on_device,
        mesh=mesh,
        in_specs=(
            P("seq", None),
            P("seq"),
            P(),
            P(None, None, "tensor"),
            P(None, "tensor"),
            P("tensor", None),
            P(),
            P(None, "tensor"),
            P(None, "tensor"),
            P("tensor", None),
            P("seq", None),
        ),
        out_specs=(
            P("seq", None),
            P("seq", None),
            P(),
            P("seq", None, "tensor"),
            P(None, "tensor"),
            P("tensor", "seq"),
            P(),
            P("seq", "tensor"),
            P("seq", "tensor"),
            P("tensor", "seq"),
        ),
        check_vma=False,
    )
```

```python
import functools

import jax
import jax.numpy as jnp
from jax import lax
from jax.experimental import pallas as pl
from jax.experimental.pallas import tpu as pltpu
from jax.sharding import PartitionSpec as P

EPS = 1e-05
AXES = ("seq", "tensor")
BF16 = jnp.bfloat16
F32 = jnp.float32


def device_pairs(move):
    def number(y, z, x, core):
        return ((((y % 4) * 4 + z % 4) * 2 + x % 2) * 2 + core) * 2 + (x % 4) // 2

    return [
        (number(y, z, x, core), number(*move(y, z, x, core)))
        for y in range(4)
        for z in range(4)
        for x in range(4)
        for core in range(2)
    ]


ACROSS = device_pairs(lambda y, z, x, core: (y, z, (x + 2) % 4, core))
BESIDE = device_pairs(lambda y, z, x, core: (y, z, x ^ 1, core))
BESIDE_OTHER = device_pairs(lambda y, z, x, core: (y, z, x ^ 1, 1 - core))
CORES = device_pairs(lambda y, z, x, core: (y, z, x, 1 - core))


def peer(at, pairing):
    return (at ^ 1, 3 - at, at ^ 2)[pairing]


FIRST = [
    device_pairs(
        functools.partial(
            lambda pairing, y, z, x, core: (y, peer(z, pairing), x, core)
            if core
            else (peer(y, pairing), z, x, core),
            pairing,
        )
    )
    for pairing in range(3)
]
SECOND = [
    device_pairs(
        functools.partial(
            lambda pairing, y, z, x, core: (peer(y, pairing), z, x, core)
            if core
            else (y, peer(z, pairing), x, core),
            pairing,
        )
    )
    for pairing in range(3)
]
WIDE_COLUMNS = 1152
WIDE_TILES = 27
WIDE = (15, 12)
NARROW = 8
BLOCK = (64, 128)
LONG = 3 * 10**10
SHORT = 8 * 10**9
MIDDLE = 12 * 10**9
TILES = WIDE_TILES + NARROW
WIDE_BLOCKS = (4 * WIDE[1], 4 * WIDE[0], 0)
ROUND_ONE = tuple(count + 4 * NARROW + 1 for count in WIDE_BLOCKS)


def swap(value, pairs):
    return lax.ppermute(value, AXES, pairs)


def from_behind(value, axis, steps):
    count = lax.axis_size(axis)
    leading, last = (max(0, -steps), min(count, count - steps))
    return lax.ppermute(value, axis, [(source, source + steps) for source in range(leading, last)])


def norm_scale(values):
    return lax.rsqrt(jnp.mean(values * values, axis=1, keepdims=True) + EPS)


def norm_backward(out_grad_rows, values, scale_rows, gain):
    scaled = out_grad_rows * gain
    inner = jnp.mean(scaled * values, axis=1, keepdims=True)
    return scale_rows * (scaled - values * scale_rows * scale_rows * inner)


def like(shape, dtype):
    return jax.ShapeDtypeStruct(shape, dtype)


def positions(offset):
    at = lax.axis_index("seq")
    y, z, core = at // 16, (at // 4) % 4, at % 2
    first, second = jnp.where(core == 0, y, z), jnp.where(core == 0, z, y)
    return first, second, (at // 2) % 2, core, offset


def call(body, *, operands, outs, scratch=(), offset=None, flops=0, aliases=None, where=pltpu.VMEM, scalar=None):
    whole = pl.BlockSpec(memory_space=pltpu.VMEM)
    specs = [pl.BlockSpec(memory_space=where)] * len(operands)
    if scalar is not None:
        operands, specs = [scalar, *operands], [pl.BlockSpec(memory_space=pltpu.SMEM), *specs]

    def kernel(*refs):
        if offset is None:
            body(positions(None), *refs)
        else:
            body(positions(refs[0][0:1, 0:1]), *refs[1:])

    if offset is not None:
        operands, specs = [offset, *operands], [whole, *specs]
    return pl.pallas_call(
        kernel,
        out_shape=tuple(outs),
        in_specs=specs,
        out_specs=tuple(whole for _ in outs),
        scratch_shapes=list(scratch),
        input_output_aliases=aliases or {},
        compiler_params=pltpu.CompilerParams(vmem_limit_bytes=16 * 2**20),
        cost_estimate=pl.CostEstimate(flops=flops, bytes_accessed=0, transcendentals=0),
    )(*operands)


def dot(left, right):
    return jnp.dot(left, right, preferred_element_type=F32)


def dot_rows(left, right):
    return lax.dot_general(left, right, (((1,), (1,)), ((), ())), preferred_element_type=F32)


def row_numbers(shape, first=0):
    return lax.broadcasted_iota(jnp.int32, shape, 0) + first


def valid_rows(offset, lag, shape):
    row = row_numbers(shape)
    return jnp.where((offset <= row) & (offset > row - lag), 0.0, 1.0)


def linked_rows(offset, shape, first, count):
    return jnp.where((row_numbers(shape, first) < offset) & (offset < count), 0.0, 1.0)


def load_kernel(scalars, starts, tokens, gain, weight, tail, token_rows, gain_row, weights, offset, done):
    rows, depth = tokens.shape[0], weight.shape[1] // 4
    pieces = [(gain, gain_row)]
    pieces += [(tokens.at[pl.ds(at, 128)], token_rows.at[pl.ds(at, 128)]) for at in (rows - 128, 0)]
    for k in (0, 2, 1):
        for at in range(0, weight.shape[1], depth):
            pieces.append((weight.at[k, pl.ds(at, depth)], weights.at[k, pl.ds(at, depth)]))
    copies = [
        pltpu.make_async_copy(source, target, done.at[at]) for at, (source, target) in enumerate(pieces)
    ]
    for copy in copies:
        copy.start()
    for copy in copies[:2]:
        copy.wait()
    offset[...] = jnp.full(offset.shape, starts[0], jnp.int32)
    values = token_rows[rows - 16 :].astype(F32)
    normed = (values * norm_scale(values) * gain_row[...]).astype(BF16)
    for copy in copies[2:11]:
        copy.wait()
    gated = (dot(normed, weights[0]) * dot(normed, weights[2])).astype(BF16).astype(F32)
    tail[...] = (gated * linked_rows(starts[0], gated.shape, rows - 16, rows)).astype(BF16)
    for copy in copies[11:]:
        copy.wait()


def project_kernel(scalars, tokens, gain, weights, normed, parts, gated):
    values = tokens[...].astype(F32)
    normed[...] = (values * norm_scale(values) * gain[...]).astype(BF16)
    for k in range(3):
        parts[k] = dot(normed[...], weights[k])
    gated[...] = (parts[0] * parts[2]).astype(BF16)


def behind(gated, incoming, lag):
    moved = pltpu.roll(gated, lag, 0)
    row = row_numbers(gated.shape)
    for at in range(lag):
        moved = jnp.where(row == at, incoming[16 - lag + at : 17 - lag + at], moved)
    return moved


def mix_kernel(scalars, gated, incoming, parts, taps, weight, conv, ymix, branch):
    values = gated[...].astype(F32)
    before = incoming[...].astype(F32)
    total = taps[0:1] * values
    for lag in (1, 2):
        total = total + taps[lag : lag + 1] * behind(values, before, lag) * valid_rows(
            scalars[4], lag, values.shape
        )
    conv[...] = total
    ymix[...] = (parts[1] * total).astype(BF16)
    branch[...] = dot(ymix[...], weight[...]).astype(BF16)


def away_half(value, core):
    half = value.shape[-1] // 2
    return jnp.where(core == 0, value[..., half:], value[..., :half])


def hidden_kernel(scalars, cot, weight, out):
    for at in range(0, weight.shape[0], 256):
        out[:, at : at + 256] = dot_rows(cot[...], weight[at : at + 256])


def down_kernel(scalars, hidden, weight, out):
    out[...] = dot(hidden[...], weight[...]).astype(BF16)


def feed_kernel(
    scalars,
    tokens,
    branch,
    other,
    gain,
    gate,
    up,
    hidden_grad,
    normed_one,
    ymix,
    resid,
    normed,
    hidden,
    gate_back,
    up_back,
    shared,
    shared_early,
):
    resid[...] = tokens[...].astype(F32) + (branch[...].astype(F32) + other[...].astype(F32))
    normed[...] = (resid[...] * norm_scale(resid[...]) * gain[...]).astype(BF16)
    values = normed[...]
    for at in range(0, gate.shape[1], 256):
        columns = slice(at, at + 256)
        gate_act, up_act = dot(values, gate[:, columns]), dot(values, up[:, columns])
        back = hidden_grad[:, columns]
        sigmoid_gate = jax.nn.sigmoid(gate_act)
        swish = gate_act * sigmoid_gate
        hidden[:, columns] = (swish * up_act).astype(BF16)
        up_back[:, columns] = (back * swish).astype(BF16)
        slope = sigmoid_gate * (1.0 + gate_act * (1.0 - sigmoid_gate))
        gate_back[:, columns] = (back * up_act * slope).astype(BF16)
    away = pl.ds(pl.multiple_of((1 - scalars[3]) * WIDE_COLUMNS, 128), WIDE_COLUMNS)
    for k, value in enumerate((hidden, gate_back, up_back)):
        shared[:, k * WIDE_COLUMNS : (k + 1) * WIDE_COLUMNS] = value[:, away]
    shared[:, 3 * WIDE_COLUMNS :] = values
    shared_early[:, : normed.shape[1]] = normed_one[...]
    shared_early[:, normed.shape[1] :] = away_half(ymix[...], scalars[3])


def part_kernel(scalars, gate_back, up_back, gate, up, part):
    part[...] = (dot_rows(gate_back[...], gate[...]) + dot_rows(up_back[...], up[...])).astype(BF16)


def second_norm(part, other, resid, gain, cot):
    back = part.astype(F32) + other.astype(F32)
    scale = norm_scale(resid)
    return back, scale, cot.astype(F32) + norm_backward(back, resid, scale, gain)


def edge_kernel(scalars, part, other, resid, gain, cot, weight, parts, taps, edge):
    top = slice(0, 16)
    _, _, grad = second_norm(part[top], other[top], resid[top], gain[...], cot[top])
    conv_back = dot_rows(grad.astype(BF16), weight[...]) * parts[1, top]
    one = conv_back * valid_rows(scalars[4], 1, conv_back.shape) * taps[1:2]
    two = conv_back * valid_rows(scalars[4], 2, conv_back.shape) * taps[2:3]
    row = row_numbers((8, conv_back.shape[1]))
    edge[...] = jnp.where(row == 6, two[0:1], 0.0) + jnp.where(row == 7, one[0:1] + two[1:2], 0.0)


def middle_kernel(
    scalars, part, other, resid, gain, cot, weight, parts, taps, conv, gated, incoming, grad, low, gain_grad, c_back, gated_back, tap_grads
):
    back, scale, resid_grad = second_norm(part[...], other[...], resid[...], gain[...], cot[...])
    gain_grad[...] = jnp.sum(back * resid[...] * scale, axis=0, keepdims=True)
    grad[...] = resid_grad
    low[...] = resid_grad.astype(BF16)
    ymix_back = dot_rows(low[...], weight[...])
    c_back[...] = (ymix_back * conv[...]).astype(BF16)
    conv_back = ymix_back * parts[1]
    values, before = gated[...].astype(F32), incoming[...].astype(F32)
    rows = values.shape[0]
    tap_grads[0:1] = jnp.sum(conv_back * values, axis=0, keepdims=True)
    total = conv_back * taps[0:1]
    row = row_numbers(values.shape)
    for lag in (1, 2):
        term = conv_back * valid_rows(scalars[4], lag, values.shape)
        tap_grads[lag : lag + 1] = jnp.sum(term * behind(values, before, lag), axis=0, keepdims=True)
        moved = pltpu.roll(term * taps[lag : lag + 1], rows - lag, 0)
        total = total + jnp.where(row < rows - lag, moved, 0.0)
    gated_back[...] = total


def last_kernel(
    scalars,
    gated_back,
    returned,
    parts,
    c_back,
    weight,
    tokens,
    gain_two_grad,
    tap_grads,
    resid_low,
    backs,
    shared,
    part,
    gain_part,
    small,
):
    rows = gated_back.shape[0]
    links = linked_rows(scalars[4], returned.shape, rows - 8, rows)
    end = gated_back[rows - 8 :] + returned[...] * links
    total = jnp.concatenate([gated_back[: rows - 8], end], 0)
    backs[0] = (total * parts[2]).astype(BF16)
    backs[1] = c_back[...]
    backs[2] = (total * parts[0]).astype(BF16)
    for k in range(3):
        shared[4 + k] = away_half(backs[k], scalars[3])
    for at in range(4):
        shared[at] = resid_low[:, at * 256 : at * 256 + 256]
    grad = dot_rows(backs[0], weight[0]) + dot_rows(backs[1], weight[1]) + dot_rows(backs[2], weight[2])
    part[...] = grad.astype(BF16)
    values = tokens[...].astype(F32)
    gain_grad = jnp.sum(grad * values * norm_scale(values), axis=0, keepdims=True)
    for at in range(8):
        lanes = slice(at * 128, at * 128 + 128)
        gain_part[at : at + 1] = gain_grad[:, lanes]
        small[8 + at : 9 + at] = gain_two_grad[:, lanes]
    for lag in range(3):
        for at in range(4):
            row = 16 + 4 * lag + at
            small[row : row + 1] = tap_grads[lag : lag + 1, at * 128 : at * 128 + 128]
    small[:8] = jnp.zeros((8, 128), F32)
    small[28:32] = jnp.zeros((4, 128), F32)


def fill_transposed(left, own, other):
    for at in range(0, own.shape[1], 256):
        left[at : at + 256, :256] = own[:, at : at + 256].T
        left[at : at + 256, 256:] = other[:, at : at + 256].T


def chunk_rows(left, core, chunk):
    wide, slim = jnp.where(core == 0, 256, 64), jnp.where(core == 0, 64, 256)
    return jnp.concatenate(
        [left[pl.ds(pl.multiple_of(chunk * wide + at * slim, 64), 64)] for at in range(4)], 0
    )


def store_blocks(value, target, base, tiles, tile):
    value = value.astype(BF16)
    for chunk in range(4):
        for column in range(value.shape[1] // 128):
            target[base + chunk * tiles + tile + column] = value[
                chunk * 64 : chunk * 64 + 64, column * 128 : column * 128 + 128
            ]


def wide_runs(kind):
    at, end = (0, WIDE[0]) if kind == 0 else (WIDE[0], WIDE_TILES)
    first = at
    while at < end:
        matrix, tile = divmod(at, WIDE_COLUMNS // 128)
        count = min(2, WIDE_COLUMNS // 128 - tile, end - at)
        yield matrix, tile * 128, count * 128, at - first
        at += count


def wide_piece(scalars, kind, lefts, own, shared, send, keep):
    at, core = scalars[0], scalars[3]
    first, second = peer(at, kind), peer(at, 1 - kind)
    chunks = (at, second, first, peer(first, 1 - kind))
    for slot, chunk in enumerate(chunks):
        target = keep if slot < 2 else send
        rows = {}
        for matrix, column, width, tile in wide_runs(kind):
            if (matrix == 0) not in rows:
                rows[matrix == 0] = chunk_rows(lefts[matrix], core, chunk)
            left = rows[matrix == 0]
            mine = pl.ds(pl.multiple_of(core * WIDE_COLUMNS + column, 128), width)
            away = matrix * WIDE_COLUMNS + column
            value = dot(left[:, :256], own[matrix][:, mine])
            value = value + dot(left[:, 256:], shared[:, away : away + width])
            store_blocks(value, target, (slot % 2) * 4 * WIDE[kind], WIDE[kind], tile)


def wide_first_kernel(scalars, two, cot, cot_other, hidden, gate_back, shared, send, keep, left_two, left_cot):
    fill_transposed(left_cot, cot, cot_other)
    fill_transposed(left_two, two, shared.at[:, 3 * WIDE_COLUMNS :])
    wide_piece(scalars, 0, (left_cot, left_two), (hidden, gate_back), shared, send, keep)


def wide_second_kernel(scalars, left_two, gate_back, up_back, shared, send, keep):
    wide_piece(scalars, 1, (None, left_two, left_two), (None, gate_back, up_back), shared, send, keep)


def narrow_kernel(scalars, one, shared, low, late_other, backs, ymix, *refs):
    outs, (left_one, left_low) = refs[:4], refs[4:]
    width = one.shape[1]
    one_other, ymix_other = shared.at[:, :width], shared.at[:, width:]
    for at in range(0, width, 256):
        left_one[at : at + 256, :256] = one[:, at : at + 256].T
        left_one[at : at + 256, 256:] = one_other[:, at : at + 256].T
        left_low[at : at + 256, :256] = low[:, at : at + 256].T
        left_low[at : at + 256, 256:] = late_other[at // 256].T
    mine = pl.ds(pl.multiple_of(scalars[3] * 256, 256), 256)
    for slot in range(4):
        chunk = peer(scalars[0], slot) if slot < 3 else scalars[0]
        for kind in range(4):
            left, own, other = (
                (left_one, backs[kind, :, mine], late_other[4 + kind])
                if kind < 3
                else (left_low, ymix[:, mine], ymix_other[...])
            )
            rows = chunk_rows(left, scalars[3], chunk)
            value = dot(rows[:, :256], own) + dot(rows[:, 256:], other)
            store_blocks(value, outs[slot], WIDE_BLOCKS[slot] if slot < 3 else 0, NARROW, 2 * kind)


def split_small(value, target, at):
    high = value.astype(BF16)
    target[at, :32] = high
    target[at, 32:] = (value - high.astype(F32)).astype(BF16)


def join_small(source, at):
    return source[at, :32].astype(F32) + source[at, 32:].astype(F32)


def rounded_small(value):
    high = value.astype(BF16)
    return high.astype(F32) + (value - high.astype(F32)).astype(BF16).astype(F32)


def sum_small(value, near, far, cross):
    return (rounded_small(value) + cross) + (near + far)


def far_kernel(scalars, mine, got, total, small):
    total[...] = mine[...].astype(F32) + got[: 4 * NARROW].astype(F32)
    small[...] = join_small(got, 4 * NARROW)


def first_kernel(scalars, *refs):
    gots, keeps, (small, gain, gain_other) = refs[:2], refs[2:4], refs[4:7]
    sends, wide_keeps, new_small = refs[10:13], refs[13:15], refs[15]
    new_small[:8] = gain[...] + gain_other[...]
    new_small[8:] = small[8:]
    for pairing in range(3):
        split_small(new_small[...], sends[pairing], ROUND_ONE[pairing] - 1)
    for kind in range(2):
        half = 4 * WIDE[kind]
        for chunk in range(4):
            at = slice(chunk * WIDE[kind], (chunk + 1) * WIDE[kind])
            after = slice(half + chunk * WIDE[kind], half + (chunk + 1) * WIDE[kind])
            wide_keeps[kind][at] = (keeps[kind][at].astype(F32) + gots[kind][at].astype(F32)).astype(BF16)
            sends[1 - kind][at] = (keeps[kind][after].astype(F32) + gots[kind][after].astype(F32)).astype(BF16)


def second_kernel(scalars, *refs):
    gots, wide_in, (narrow, small, cross) = refs[:2], refs[2:4], refs[4:7]
    sends, (keep, new_small) = refs[7:10], refs[10:]

    def fill(chunk, target):
        tile = 0
        for kind in range(2):
            at = pl.ds(chunk * WIDE[kind], WIDE[kind])
            value = wide_in[kind][at].astype(F32) + gots[1 - kind][at].astype(F32)
            target[tile : tile + WIDE[kind]] = value.astype(BF16)
            tile += WIDE[kind]
        value = narrow[pl.ds(chunk * NARROW, NARROW)]
        for pairing in range(2):
            value = value + gots[pairing][pl.ds(WIDE_BLOCKS[pairing] + chunk * NARROW, NARROW)].astype(F32)
        target[tile : tile + NARROW] = value.astype(BF16)

    near, far = (join_small(got, count - 1) for got, count in zip(gots, ROUND_ONE))
    value = sum_small(small[...], near, far, cross[...])
    new_small[...] = value
    for pairing in range(3):
        fill(peer(scalars[1], pairing), sends[pairing])
        split_small(value, sends[pairing], TILES)
    fill(scalars[1], keep)


def third_kernel(scalars, *refs):
    gots, (kept, small), (mine, away, near, far, new_small) = refs[:3], refs[3:5], refs[5:]
    here, core = scalars[2], scalars[3]
    for first in range(0, TILES, 7):
        at = slice(first, first + 7)
        value = kept[at].astype(F32)
        for got in gots:
            value = value + got[at].astype(F32)
        zero, one = value[:, :32], value[:, 32:]
        stay, leave = jnp.where(here == 0, zero, one), jnp.where(here == 0, one, zero)
        mine[at] = jnp.where(core == 0, stay[:, :16], stay[:, 16:])
        away[at] = jnp.where(core == 0, stay[:, 16:], stay[:, :16]).astype(BF16)
        near[at] = jnp.where(core == 0, leave[:, :16], leave[:, 16:]).astype(BF16)
        far[at] = jnp.where(core == 0, leave[:, 16:], leave[:, :16]).astype(BF16)
    value = sum_small(small[...], *(join_small(got, TILES) for got in gots))
    high = value.astype(BF16)
    low = (value - high.astype(F32)).astype(BF16)
    new_small[...] = high.astype(F32) + low.astype(F32)
    for at in range(2):
        rows = slice(16 * at, 16 * at + 16)
        for target in (away, near, far):
            target[TILES + at] = high[rows]
            target[TILES + 2 + at] = low[rows]
    for target in (near, far):
        target[TILES + 4] = jnp.zeros((16, 128), BF16)


def finish_kernel(
    scalars, resid, down, down_other, part, other, tokens, resid_grad, gain, mixed, tokens_grad
):
    mixed[...] = (resid[...] + (down[...].astype(F32) + down_other[...].astype(F32))).astype(BF16)
    values = tokens[...].astype(F32)
    back = part[...].astype(F32) + other[...].astype(F32)
    tokens_grad[...] = resid_grad[...] + norm_backward(back, values, norm_scale(values), gain[...])


def outputs_kernel(scalars, mine, away, near, far, small, down, gate, up, inner, out, gain_one, gain_two, taps):
    core = scalars[3]

    def place(target, tile, column, columns):
        own = mine[tile] + near[tile].astype(F32)
        other = away[tile].astype(F32) + far[tile].astype(F32)
        target[:, column : column + 128] = jnp.where(core == 0, own, other)
        target[:, columns + column : columns + column + 128] = jnp.where(core == 0, other, own)

    for matrix, target in enumerate((down, gate, up)):
        for tile in range(WIDE_COLUMNS // 128):
            place(target, matrix * (WIDE_COLUMNS // 128) + tile, tile * 128, WIDE_COLUMNS)
    for kind in range(4):
        for column in range(2):
            place(inner.at[kind] if kind < 3 else out, WIDE_TILES + 2 * kind + column, column * 128, 256)
    sums = []
    for at in range(2):
        came = [part[TILES + at].astype(F32) + part[TILES + 2 + at].astype(F32) for part in (near, away, far)]
        sums.append((small[16 * at : 16 * at + 16] + came[0]) + (came[1] + came[2]))
    gains, rest = sums
    for at in range(8):
        lanes = slice(at * 128, at * 128 + 128)
        gain_one[:, lanes] = gains[at : at + 1]
        gain_two[:, lanes] = gains[8 + at : 9 + at]
    for lag in range(3):
        for at in range(4):
            row = 4 * lag + at
            taps[lag : lag + 1, at * 128 : at * 128 + 128] = rest[row : row + 1]


def swap_round(sends, pairings):
    return [swap(value, pairs) for value, pairs in zip(sends, pairings)]


def blocks(counts):
    return [like((count, *BLOCK), BF16) for count in counts]


def on_device(
    tokens,
    starts,
    gain_one,
    in_weight,
    conv_weight,
    out_weight,
    gain_two,
    gate_weight,
    up_weight,
    down_weight,
    cotangent,
):
    core = lax.axis_index("seq") % 2
    run = call
    rows, width = tokens.shape
    channels = conv_weight.shape[1]
    in_parts = in_weight.transpose(1, 0, 2)
    gain_one_row, gain_two_row = gain_one.reshape(1, -1), gain_two.reshape(1, -1)

    def share(value):
        return swap(value, CORES)

    tail, tokens_here, gain_here, weights_here, offset = run(
        load_kernel,
        operands=[
            pltpu.with_memory_space_constraint(value, pltpu.HBM) for value in (tokens, gain_one_row, in_parts)
        ],
        scalar=starts,
        outs=[
            like((16, channels), BF16),
            like((rows, width), BF16),
            like((1, width), F32),
            like((3, width, channels), BF16),
            like((8, 128), jnp.int32),
        ],
        scratch=[pltpu.SemaphoreType.DMA((15,))],
        where=pltpu.HBM,
    )
    incoming = from_behind(tail, "seq", 1)
    cotangent_other = share(cotangent)
    incoming, cotangent_other = lax.optimization_barrier((incoming, cotangent_other))
    normed_one, parts, gated = run(
        project_kernel,
        operands=[tokens_here, gain_here, weights_here],
        outs=[like((rows, width), BF16), like((3, rows, channels), F32), like((rows, channels), BF16)],
    )
    conv, ymix, branch = run(
        mix_kernel,
        offset=offset,
        operands=[gated, incoming, parts, conv_weight, out_weight],
        outs=[like((rows, channels), F32), like((rows, channels), BF16), like((rows, width), BF16)],
    )
    branch, cotangent_late = lax.optimization_barrier((branch, cotangent))
    branch_other = swap(branch, ACROSS)
    units = gate_weight.shape[1]
    hidden_grad = run(
        hidden_kernel,
        operands=[cotangent_late, down_weight],
        outs=[like((rows, units), F32)],
        flops=LONG,
    )[0]
    branch_other, hidden_grad = lax.optimization_barrier((branch_other, hidden_grad))
    resid, normed_two, hidden, gate_back, up_back, shared, shared_early = run(
        feed_kernel,
        operands=[tokens, branch, branch_other, gain_two_row, gate_weight, up_weight, hidden_grad]
        + [normed_one, ymix],
        outs=[like((rows, width), F32), like((rows, width), BF16)]
        + [like((rows, units), BF16)] * 3
        + [like((rows, 3 * WIDE_COLUMNS + width), BF16), like((rows, width + channels // 2), BF16)],
    )
    shared_other = share(shared)
    norm_two_part = run(
        part_kernel, operands=[gate_back, up_back, gate_weight, up_weight], outs=[like((rows, width), BF16)]
    )[0]
    norm_two_other = swap(norm_two_part, ACROSS)
    first_send, first_keep, left_two = run(
        wide_first_kernel,
        operands=[normed_two, cotangent, cotangent_other, hidden, gate_back, shared_other],
        outs=blocks([8 * WIDE[0]] * 2) + [like((width, 2 * rows), BF16)],
        scratch=[pltpu.VMEM((width, 2 * rows), BF16)],
    )
    second_send, second_keep = run(
        wide_second_kernel,
        operands=[left_two, gate_back, up_back, shared_other],
        outs=blocks([8 * WIDE[1]] * 2),
    )
    sends, keeps = [first_send, second_send], [first_keep, second_keep]
    hidden, sends[1] = lax.optimization_barrier((hidden, sends[1]))
    down_part = run(down_kernel, operands=[hidden, down_weight], outs=[like((rows, width), BF16)])[0]
    early_other = share(shared_early)
    norm_two_other, keeps[1], down_part, early_other = lax.optimization_barrier(
        (norm_two_other, keeps[1], down_part, early_other)
    )
    gots = swap_round(sends, FIRST)

    edge_operands = [norm_two_part, norm_two_other, resid, gain_two_row, cotangent, out_weight, parts, conv_weight]
    edge = run(edge_kernel, offset=offset, operands=edge_operands, outs=[like((8, channels), F32)])[0]
    returned = from_behind(edge, "seq", -1)
    resid_grad, resid_low, gain_two_grad, c_back, gated_back, tap_grads = run(
        middle_kernel,
        offset=offset,
        operands=edge_operands + [conv, gated, incoming],
        outs=[
            like((rows, width), F32),
            like((rows, width), BF16),
            like((1, width), F32),
            like((rows, channels), BF16),
            like((rows, channels), F32),
            like((3, channels), F32),
        ],
        flops=SHORT,
    )
    backs, shared, norm_one_part, gain_part, small = run(
        last_kernel,
        offset=offset,
        operands=[gated_back, returned, parts, c_back, in_parts, tokens, gain_two_grad, tap_grads]
        + [resid_low],
        outs=[
            like((3, rows, channels), BF16),
            like((7, rows, 256), BF16),
            like((rows, width), BF16),
            like((8, 128), F32),
            like((32, 128), F32),
        ],
    )
    gain_other = swap(gain_part, ACROSS)
    *sends, narrow = run(
        narrow_kernel,
        operands=[normed_one, early_other, resid_low, share(shared), backs, ymix],
        outs=blocks(ROUND_ONE) + blocks([4 * NARROW]),
        scratch=[pltpu.VMEM((width, 2 * rows), BF16)] * 2,
    )
    results = run(
        first_kernel,
        operands=gots + keeps + [small, gain_part, gain_other] + sends,
        aliases={7: 0, 8: 1, 9: 2},
        outs=blocks(ROUND_ONE) + blocks([4 * count for count in WIDE]) + [like((32, 128), F32)],
    )
    *sends, far_send = results[:3]
    keeps, small = list(results[3:5]), results[5]
    narrow, cross = run(
        far_kernel,
        operands=[narrow, swap(far_send, FIRST[2])],
        outs=[like((4 * NARROW, *BLOCK), F32), like((32, 128), F32)],
        flops=MIDDLE,
    )
    gots = swap_round(sends, FIRST)
    down_other = swap(down_part, ACROSS)
    norm_one_other = swap(norm_one_part, ACROSS)
    results = run(
        second_kernel,
        operands=gots + keeps + [narrow, small, cross],
        outs=blocks([TILES + 1] * 3 + [TILES]) + [like((32, 128), F32)],
    )
    sends, keep, small = list(results[:3]), results[3], results[4]
    gots = swap_round(sends, SECOND)
    mixed, tokens_grad = run(
        finish_kernel,
        operands=[resid, down_part, down_other, norm_one_part, norm_one_other, tokens, resid_grad, gain_one_row],
        outs=[like((rows, width), BF16), like((rows, width), F32)],
        flops=LONG,
    )
    gots[0], mixed, tokens_grad = lax.optimization_barrier((gots[0], mixed, tokens_grad))
    mine, away, near, far, small = run(
        third_kernel,
        operands=gots + [keep, small],
        outs=[like((TILES, 16, 128), F32), like((TILES + 4, 16, 128), BF16)]
        + [like((TILES + 5, 16, 128), BF16)] * 2
        + [like((32, 128), F32)],
    )
    down_g, gate_g, up_g, in_g, out_g, gain_one_g, gain_two_g, conv_g = run(
        outputs_kernel,
        operands=[mine, swap(away, CORES), swap(near, BESIDE), swap(far, BESIDE_OTHER), small],
        outs=[like((16, 2 * WIDE_COLUMNS), F32)] * 3
        + [like((3, 16, channels), F32), like((16, channels), F32)]
        + [like((1, width), F32)] * 2
        + [like((3, channels), F32)],
    )
    in_g, gain_one_g, gain_two_g = in_g.transpose(1, 0, 2), gain_one_g.reshape(-1), gain_two_g.reshape(-1)
    return (mixed, tokens_grad, gain_one_g, in_g, conv_g, out_g.T, gain_two_g, gate_g, up_g, down_g.T)


def solution(mesh):
    return jax.shard_map(
        on_device,
        mesh=mesh,
        in_specs=(
            P("seq", None),
            P("seq"),
            P(),
            P(None, None, "tensor"),
            P(None, "tensor"),
            P("tensor", None),
            P(),
            P(None, "tensor"),
            P(None, "tensor"),
            P("tensor", None),
            P("seq", None),
        ),
        out_specs=(
            P("seq", None),
            P("seq", None),
            P(),
            P("seq", None, "tensor"),
            P(None, "tensor"),
            P("tensor", "seq"),
            P(),
            P("seq", "tensor"),
            P("seq", "tensor"),
            P("tensor", "seq"),
        ),
        check_vma=False,
    )
```

```python
import functools

import jax
import jax.numpy as jnp
from jax import lax
from jax.experimental import pallas as pl
from jax.experimental.pallas import tpu as pltpu
from jax.sharding import PartitionSpec as P

EPS = 1e-05
AXES = ("seq", "tensor")
BF16 = jnp.bfloat16
F32 = jnp.float32


def device_pairs(move):
    def number(y, z, x, core):
        return ((((y % 4) * 4 + z % 4) * 2 + x % 2) * 2 + core) * 2 + (x % 4) // 2

    return [
        (number(y, z, x, core), number(*move(y, z, x, core)))
        for y in range(4)
        for z in range(4)
        for x in range(4)
        for core in range(2)
    ]


ACROSS = device_pairs(lambda y, z, x, core: (y, z, (x + 2) % 4, core))
BESIDE = device_pairs(lambda y, z, x, core: (y, z, x ^ 1, core))
BESIDE_OTHER = device_pairs(lambda y, z, x, core: (y, z, x ^ 1, 1 - core))
CORES = device_pairs(lambda y, z, x, core: (y, z, x, 1 - core))


def peer(at, pairing):
    return (at ^ 1, 3 - at, at ^ 2)[pairing]


FIRST = [
    device_pairs(
        functools.partial(
            lambda pairing, y, z, x, core: (y, peer(z, pairing), x, core)
            if core
            else (peer(y, pairing), z, x, core),
            pairing,
        )
    )
    for pairing in range(3)
]
SECOND = [
    device_pairs(
        functools.partial(
            lambda pairing, y, z, x, core: (peer(y, pairing), z, x, core)
            if core
            else (y, peer(z, pairing), x, core),
            pairing,
        )
    )
    for pairing in range(3)
]
WIDE_COLUMNS = 1152
WIDE_TILES = 27
WIDE = (14, 13)
NARROW = 8
BLOCK = (64, 128)
LONG = 3 * 10**10
SHORT = 8 * 10**9
MIDDLE = 12 * 10**9
TILES = WIDE_TILES + NARROW
WIDE_BLOCKS = (4 * WIDE[1], 4 * WIDE[0], 0)
ROUND_ONE = tuple(count + 4 * NARROW + 1 for count in WIDE_BLOCKS)


def swap(value, pairs):
    return lax.ppermute(value, AXES, pairs)


def from_behind(value, axis, steps):
    count = lax.axis_size(axis)
    leading, last = (max(0, -steps), min(count, count - steps))
    return lax.ppermute(value, axis, [(source, source + steps) for source in range(leading, last)])


def norm_scale(values):
    return lax.rsqrt(jnp.mean(values * values, axis=1, keepdims=True) + EPS)


def norm_backward(out_grad_rows, values, scale_rows, gain):
    scaled = out_grad_rows * gain
    inner = jnp.mean(scaled * values, axis=1, keepdims=True)
    return scale_rows * (scaled - values * scale_rows * scale_rows * inner)


def like(shape, dtype):
    return jax.ShapeDtypeStruct(shape, dtype)


def positions(offset):
    at = lax.axis_index("seq")
    y, z, core = at // 16, (at // 4) % 4, at % 2
    first, second = jnp.where(core == 0, y, z), jnp.where(core == 0, z, y)
    return first, second, (at // 2) % 2, core, offset


def call(body, *, operands, outs, scratch=(), offset=None, flops=0, aliases=None, where=pltpu.VMEM, scalar=None):
    whole = pl.BlockSpec(memory_space=pltpu.VMEM)
    specs = [pl.BlockSpec(memory_space=where)] * len(operands)
    if scalar is not None:
        operands, specs = [scalar, *operands], [pl.BlockSpec(memory_space=pltpu.SMEM), *specs]

    def kernel(*refs):
        if offset is None:
            body(positions(None), *refs)
        else:
            body(positions(refs[0][0:1, 0:1]), *refs[1:])

    if offset is not None:
        operands, specs = [offset, *operands], [whole, *specs]
    return pl.pallas_call(
        kernel,
        out_shape=tuple(outs),
        in_specs=specs,
        out_specs=tuple(whole for _ in outs),
        scratch_shapes=list(scratch),
        input_output_aliases=aliases or {},
        compiler_params=pltpu.CompilerParams(vmem_limit_bytes=16 * 2**20),
        cost_estimate=pl.CostEstimate(flops=flops, bytes_accessed=0, transcendentals=0),
    )(*operands)


def dot(left, right):
    return jnp.dot(left, right, preferred_element_type=F32)


def dot_rows(left, right):
    return lax.dot_general(left, right, (((1,), (1,)), ((), ())), preferred_element_type=F32)


def row_numbers(shape, first=0):
    return lax.broadcasted_iota(jnp.int32, shape, 0) + first


def valid_rows(offset, lag, shape):
    row = row_numbers(shape)
    return jnp.where((offset <= row) & (offset > row - lag), 0.0, 1.0)


def linked_rows(offset, shape, first, count):
    return jnp.where((row_numbers(shape, first) < offset) & (offset < count), 0.0, 1.0)


def load_kernel(scalars, starts, tokens, gain, weight, tail, token_rows, gain_row, weights, offset, done):
    rows, depth = tokens.shape[0], weight.shape[1] // 4
    pieces = [(gain, gain_row)]
    pieces += [(tokens.at[pl.ds(at, 128)], token_rows.at[pl.ds(at, 128)]) for at in (rows - 128, 0)]
    for k in (0, 2, 1):
        for at in range(0, weight.shape[1], depth):
            pieces.append((weight.at[k, pl.ds(at, depth)], weights.at[k, pl.ds(at, depth)]))
    copies = [
        pltpu.make_async_copy(source, target, done.at[at]) for at, (source, target) in enumerate(pieces)
    ]
    for copy in copies:
        copy.start()
    for copy in copies[:2]:
        copy.wait()
    offset[...] = jnp.full(offset.shape, starts[0], jnp.int32)
    values = token_rows[rows - 16 :].astype(F32)
    normed = (values * norm_scale(values) * gain_row[...]).astype(BF16)
    for copy in copies[2:11]:
        copy.wait()
    gated = (dot(normed, weights[0]) * dot(normed, weights[2])).astype(BF16).astype(F32)
    tail[...] = (gated * linked_rows(starts[0], gated.shape, rows - 16, rows)).astype(BF16)
    for copy in copies[11:]:
        copy.wait()


def project_kernel(scalars, tokens, gain, weights, normed, parts, gated):
    values = tokens[...].astype(F32)
    normed[...] = (values * norm_scale(values) * gain[...]).astype(BF16)
    for k in range(3):
        parts[k] = dot(normed[...], weights[k])
    gated[...] = (parts[0] * parts[2]).astype(BF16)


def behind(gated, incoming, lag):
    moved = pltpu.roll(gated, lag, 0)
    row = row_numbers(gated.shape)
    for at in range(lag):
        moved = jnp.where(row == at, incoming[16 - lag + at : 17 - lag + at], moved)
    return moved


def mix_kernel(scalars, gated, incoming, parts, taps, weight, conv, ymix, branch):
    values = gated[...].astype(F32)
    before = incoming[...].astype(F32)
    total = taps[0:1] * values
    for lag in (1, 2):
        total = total + taps[lag : lag + 1] * behind(values, before, lag) * valid_rows(
            scalars[4], lag, values.shape
        )
    conv[...] = total
    ymix[...] = (parts[1] * total).astype(BF16)
    branch[...] = dot(ymix[...], weight[...]).astype(BF16)


def away_half(value, core):
    half = value.shape[-1] // 2
    return jnp.where(core == 0, value[..., half:], value[..., :half])


def hidden_kernel(scalars, cot, weight, out):
    for at in range(0, weight.shape[0], 256):
        out[:, at : at + 256] = dot_rows(cot[...], weight[at : at + 256])


def down_kernel(scalars, hidden, weight, out):
    out[...] = dot(hidden[...], weight[...]).astype(BF16)


def feed_kernel(
    scalars,
    tokens,
    branch,
    other,
    gain,
    gate,
    up,
    hidden_grad,
    normed_one,
    ymix,
    resid,
    normed,
    hidden,
    gate_back,
    up_back,
    shared,
    shared_early,
):
    resid[...] = tokens[...].astype(F32) + (branch[...].astype(F32) + other[...].astype(F32))
    normed[...] = (resid[...] * norm_scale(resid[...]) * gain[...]).astype(BF16)
    values = normed[...]
    for at in range(0, gate.shape[1], 256):
        columns = slice(at, at + 256)
        gate_act, up_act = dot(values, gate[:, columns]), dot(values, up[:, columns])
        back = hidden_grad[:, columns]
        sigmoid_gate = jax.nn.sigmoid(gate_act)
        swish = gate_act * sigmoid_gate
        hidden[:, columns] = (swish * up_act).astype(BF16)
        up_back[:, columns] = (back * swish).astype(BF16)
        slope = sigmoid_gate * (1.0 + gate_act * (1.0 - sigmoid_gate))
        gate_back[:, columns] = (back * up_act * slope).astype(BF16)
    away = pl.ds(pl.multiple_of((1 - scalars[3]) * WIDE_COLUMNS, 128), WIDE_COLUMNS)
    for k, value in enumerate((hidden, gate_back, up_back)):
        shared[:, k * WIDE_COLUMNS : (k + 1) * WIDE_COLUMNS] = value[:, away]
    shared[:, 3 * WIDE_COLUMNS :] = values
    shared_early[:, : normed.shape[1]] = normed_one[...]
    shared_early[:, normed.shape[1] :] = away_half(ymix[...], scalars[3])


def part_kernel(scalars, gate_back, up_back, gate, up, part):
    part[...] = (dot_rows(gate_back[...], gate[...]) + dot_rows(up_back[...], up[...])).astype(BF16)


def second_norm(part, other, resid, gain, cot):
    back = part.astype(F32) + other.astype(F32)
    scale = norm_scale(resid)
    return back, scale, cot.astype(F32) + norm_backward(back, resid, scale, gain)


def edge_kernel(scalars, part, other, resid, gain, cot, weight, parts, taps, edge):
    top = slice(0, 16)
    _, _, grad = second_norm(part[top], other[top], resid[top], gain[...], cot[top])
    conv_back = dot_rows(grad.astype(BF16), weight[...]) * parts[1, top]
    one = conv_back * valid_rows(scalars[4], 1, conv_back.shape) * taps[1:2]
    two = conv_back * valid_rows(scalars[4], 2, conv_back.shape) * taps[2:3]
    row = row_numbers((8, conv_back.shape[1]))
    edge[...] = jnp.where(row == 6, two[0:1], 0.0) + jnp.where(row == 7, one[0:1] + two[1:2], 0.0)


def middle_kernel(
    scalars, part, other, resid, gain, cot, weight, parts, taps, conv, gated, incoming, grad, low, gain_grad, c_back, gated_back, tap_grads
):
    back, scale, resid_grad = second_norm(part[...], other[...], resid[...], gain[...], cot[...])
    gain_grad[...] = jnp.sum(back * resid[...] * scale, axis=0, keepdims=True)
    grad[...] = resid_grad
    low[...] = resid_grad.astype(BF16)
    ymix_back = dot_rows(low[...], weight[...])
    c_back[...] = (ymix_back * conv[...]).astype(BF16)
    conv_back = ymix_back * parts[1]
    values, before = gated[...].astype(F32), incoming[...].astype(F32)
    rows = values.shape[0]
    tap_grads[0:1] = jnp.sum(conv_back * values, axis=0, keepdims=True)
    total = conv_back * taps[0:1]
    row = row_numbers(values.shape)
    for lag in (1, 2):
        term = conv_back * valid_rows(scalars[4], lag, values.shape)
        tap_grads[lag : lag + 1] = jnp.sum(term * behind(values, before, lag), axis=0, keepdims=True)
        moved = pltpu.roll(term * taps[lag : lag + 1], rows - lag, 0)
        total = total + jnp.where(row < rows - lag, moved, 0.0)
    gated_back[...] = total


def last_kernel(
    scalars,
    gated_back,
    returned,
    parts,
    c_back,
    weight,
    tokens,
    gain_two_grad,
    tap_grads,
    resid_low,
    backs,
    shared,
    part,
    gain_part,
    small,
):
    rows = gated_back.shape[0]
    links = linked_rows(scalars[4], returned.shape, rows - 8, rows)
    end = gated_back[rows - 8 :] + returned[...] * links
    total = jnp.concatenate([gated_back[: rows - 8], end], 0)
    backs[0] = (total * parts[2]).astype(BF16)
    backs[1] = c_back[...]
    backs[2] = (total * parts[0]).astype(BF16)
    for k in range(3):
        shared[4 + k] = away_half(backs[k], scalars[3])
    for at in range(4):
        shared[at] = resid_low[:, at * 256 : at * 256 + 256]
    grad = dot_rows(backs[0], weight[0]) + dot_rows(backs[1], weight[1]) + dot_rows(backs[2], weight[2])
    part[...] = grad.astype(BF16)
    values = tokens[...].astype(F32)
    gain_grad = jnp.sum(grad * values * norm_scale(values), axis=0, keepdims=True)
    for at in range(8):
        lanes = slice(at * 128, at * 128 + 128)
        gain_part[at : at + 1] = gain_grad[:, lanes]
        small[8 + at : 9 + at] = gain_two_grad[:, lanes]
    for lag in range(3):
        for at in range(4):
            row = 16 + 4 * lag + at
            small[row : row + 1] = tap_grads[lag : lag + 1, at * 128 : at * 128 + 128]
    small[:8] = jnp.zeros((8, 128), F32)
    small[28:32] = jnp.zeros((4, 128), F32)


def fill_transposed(left, own, other):
    for at in range(0, own.shape[1], 256):
        left[at : at + 256, :256] = own[:, at : at + 256].T
        left[at : at + 256, 256:] = other[:, at : at + 256].T


def chunk_rows(left, core, chunk):
    wide, slim = jnp.where(core == 0, 256, 64), jnp.where(core == 0, 64, 256)
    return jnp.concatenate(
        [left[pl.ds(pl.multiple_of(chunk * wide + at * slim, 64), 64)] for at in range(4)], 0
    )


def store_blocks(value, target, base, tiles, tile):
    value = value.astype(BF16)
    for chunk in range(4):
        for column in range(value.shape[1] // 128):
            target[base + chunk * tiles + tile + column] = value[
                chunk * 64 : chunk * 64 + 64, column * 128 : column * 128 + 128
            ]


def wide_runs(kind):
    at, end = (0, WIDE[0]) if kind == 0 else (WIDE[0], WIDE_TILES)
    first = at
    while at < end:
        matrix, tile = divmod(at, WIDE_COLUMNS // 128)
        count = min(2, WIDE_COLUMNS // 128 - tile, end - at)
        yield matrix, tile * 128, count * 128, at - first
        at += count


def wide_piece(scalars, kind, lefts, own, shared, send, keep):
    at, core = scalars[0], scalars[3]
    first, second = peer(at, kind), peer(at, 1 - kind)
    chunks = (at, second, first, peer(first, 1 - kind))
    for slot, chunk in enumerate(chunks):
        target = keep if slot < 2 else send
        rows = {}
        for matrix, column, width, tile in wide_runs(kind):
            if (matrix == 0) not in rows:
                rows[matrix == 0] = chunk_rows(lefts[matrix], core, chunk)
            left = rows[matrix == 0]
            mine = pl.ds(pl.multiple_of(core * WIDE_COLUMNS + column, 128), width)
            away = matrix * WIDE_COLUMNS + column
            value = dot(left[:, :256], own[matrix][:, mine])
            value = value + dot(left[:, 256:], shared[:, away : away + width])
            store_blocks(value, target, (slot % 2) * 4 * WIDE[kind], WIDE[kind], tile)


def wide_first_kernel(scalars, two, cot, cot_other, hidden, gate_back, shared, send, keep, left_two, left_cot):
    fill_transposed(left_cot, cot, cot_other)
    fill_transposed(left_two, two, shared.at[:, 3 * WIDE_COLUMNS :])
    wide_piece(scalars, 0, (left_cot, left_two), (hidden, gate_back), shared, send, keep)


def wide_second_kernel(scalars, left_two, gate_back, up_back, shared, send, keep):
    wide_piece(scalars, 1, (None, left_two, left_two), (None, gate_back, up_back), shared, send, keep)


def narrow_kernel(scalars, one, shared, low, late_other, backs, ymix, *refs):
    (small, gain, gain_other), outs, (new_small, left_one, left_low) = refs[:3], refs[3:7], refs[7:]
    new_small[:8] = gain[...] + gain_other[...]
    new_small[8:] = small[8:]
    for pairing in range(3):
        split_small(new_small[...], outs[pairing], ROUND_ONE[pairing] - 1)
    width = one.shape[1]
    one_other, ymix_other = shared.at[:, :width], shared.at[:, width:]
    for at in range(0, width, 256):
        left_one[at : at + 256, :256] = one[:, at : at + 256].T
        left_one[at : at + 256, 256:] = one_other[:, at : at + 256].T
        left_low[at : at + 256, :256] = low[:, at : at + 256].T
        left_low[at : at + 256, 256:] = late_other[at // 256].T
    mine = pl.ds(pl.multiple_of(scalars[3] * 256, 256), 256)
    for slot in range(4):
        chunk = peer(scalars[0], slot) if slot < 3 else scalars[0]
        for kind in range(4):
            left, own, other = (
                (left_one, backs[kind, :, mine], late_other[4 + kind])
                if kind < 3
                else (left_low, ymix[:, mine], ymix_other[...])
            )
            rows = chunk_rows(left, scalars[3], chunk)
            value = dot(rows[:, :256], own) + dot(rows[:, 256:], other)
            store_blocks(value, outs[slot], WIDE_BLOCKS[slot] if slot < 3 else 0, NARROW, 2 * kind)


def split_small(value, target, at):
    high = value.astype(BF16)
    target[at, :32] = high
    target[at, 32:] = (value - high.astype(F32)).astype(BF16)


def join_small(source, at):
    return source[at, :32].astype(F32) + source[at, 32:].astype(F32)


def rounded_small(value):
    high = value.astype(BF16)
    return high.astype(F32) + (value - high.astype(F32)).astype(BF16).astype(F32)


def sum_small(value, near, far, cross):
    return (rounded_small(value) + cross) + (near + far)


def far_kernel(scalars, mine, got, total, small):
    total[...] = mine[...].astype(F32) + got[: 4 * NARROW].astype(F32)
    small[...] = join_small(got, 4 * NARROW)


def first_kernel(scalars, *refs):
    gots, keeps, sends, wide_keeps = refs[:2], refs[2:4], refs[6:8], refs[8:]
    for kind in range(2):
        half = 4 * WIDE[kind]
        for chunk in range(4):
            at = slice(chunk * WIDE[kind], (chunk + 1) * WIDE[kind])
            after = slice(half + chunk * WIDE[kind], half + (chunk + 1) * WIDE[kind])
            wide_keeps[kind][at] = (keeps[kind][at].astype(F32) + gots[kind][at].astype(F32)).astype(BF16)
            sends[1 - kind][at] = (keeps[kind][after].astype(F32) + gots[kind][after].astype(F32)).astype(BF16)


def second_kernel(scalars, *refs):
    gots, wide_in, (narrow, small, cross) = refs[:2], refs[2:4], refs[4:7]
    sends, (keep, new_small) = refs[7:10], refs[10:]

    def fill(chunk, target):
        tile = 0
        for kind in range(2):
            at = pl.ds(chunk * WIDE[kind], WIDE[kind])
            value = wide_in[kind][at].astype(F32) + gots[1 - kind][at].astype(F32)
            target[tile : tile + WIDE[kind]] = value.astype(BF16)
            tile += WIDE[kind]
        value = narrow[pl.ds(chunk * NARROW, NARROW)]
        for pairing in range(2):
            value = value + gots[pairing][pl.ds(WIDE_BLOCKS[pairing] + chunk * NARROW, NARROW)].astype(F32)
        target[tile : tile + NARROW] = value.astype(BF16)

    near, far = (join_small(got, count - 1) for got, count in zip(gots, ROUND_ONE))
    value = sum_small(small[...], near, far, cross[...])
    new_small[...] = value
    for pairing in range(3):
        fill(peer(scalars[1], pairing), sends[pairing])
        split_small(value, sends[pairing], TILES)
    fill(scalars[1], keep)


def third_kernel(scalars, *refs):
    gots, (kept, small), (mine, away, near, far, new_small) = refs[:3], refs[3:5], refs[5:]
    here, core = scalars[2], scalars[3]
    for first in range(0, TILES, 7):
        at = slice(first, first + 7)
        value = kept[at].astype(F32)
        for got in gots:
            value = value + got[at].astype(F32)
        zero, one = value[:, :32], value[:, 32:]
        stay, leave = jnp.where(here == 0, zero, one), jnp.where(here == 0, one, zero)
        mine[at] = jnp.where(core == 0, stay[:, :16], stay[:, 16:])
        away[at] = jnp.where(core == 0, stay[:, 16:], stay[:, :16]).astype(BF16)
        near[at] = jnp.where(core == 0, leave[:, :16], leave[:, 16:]).astype(BF16)
        far[at] = jnp.where(core == 0, leave[:, 16:], leave[:, :16]).astype(BF16)
    value = sum_small(small[...], *(join_small(got, TILES) for got in gots))
    high = value.astype(BF16)
    low = (value - high.astype(F32)).astype(BF16)
    new_small[...] = high.astype(F32) + low.astype(F32)
    for at in range(2):
        rows = slice(16 * at, 16 * at + 16)
        for target in (away, near, far):
            target[TILES + at] = high[rows]
            target[TILES + 2 + at] = low[rows]
    for target in (near, far):
        target[TILES + 4] = jnp.zeros((16, 128), BF16)


def finish_kernel(
    scalars, resid, down, down_other, part, other, tokens, resid_grad, gain, mixed, tokens_grad
):
    mixed[...] = (resid[...] + (down[...].astype(F32) + down_other[...].astype(F32))).astype(BF16)
    values = tokens[...].astype(F32)
    back = part[...].astype(F32) + other[...].astype(F32)
    tokens_grad[...] = resid_grad[...] + norm_backward(back, values, norm_scale(values), gain[...])


def outputs_kernel(scalars, mine, away, near, far, small, down, gate, up, inner, out, gain_one, gain_two, taps):
    core = scalars[3]

    def place(target, tile, column, columns):
        own = mine[tile] + near[tile].astype(F32)
        other = away[tile].astype(F32) + far[tile].astype(F32)
        target[:, column : column + 128] = jnp.where(core == 0, own, other)
        target[:, columns + column : columns + column + 128] = jnp.where(core == 0, other, own)

    for matrix, target in enumerate((down, gate, up)):
        for tile in range(WIDE_COLUMNS // 128):
            place(target, matrix * (WIDE_COLUMNS // 128) + tile, tile * 128, WIDE_COLUMNS)
    for kind in range(4):
        for column in range(2):
            place(inner.at[kind] if kind < 3 else out, WIDE_TILES + 2 * kind + column, column * 128, 256)
    sums = []
    for at in range(2):
        came = [part[TILES + at].astype(F32) + part[TILES + 2 + at].astype(F32) for part in (near, away, far)]
        sums.append((small[16 * at : 16 * at + 16] + came[0]) + (came[1] + came[2]))
    gains, rest = sums
    for at in range(8):
        lanes = slice(at * 128, at * 128 + 128)
        gain_one[:, lanes] = gains[at : at + 1]
        gain_two[:, lanes] = gains[8 + at : 9 + at]
    for lag in range(3):
        for at in range(4):
            row = 4 * lag + at
            taps[lag : lag + 1, at * 128 : at * 128 + 128] = rest[row : row + 1]


def swap_round(sends, pairings):
    return [swap(value, pairs) for value, pairs in zip(sends, pairings)]


def blocks(counts):
    return [like((count, *BLOCK), BF16) for count in counts]


def on_device(
    tokens,
    starts,
    gain_one,
    in_weight,
    conv_weight,
    out_weight,
    gain_two,
    gate_weight,
    up_weight,
    down_weight,
    cotangent,
):
    core = lax.axis_index("seq") % 2
    run = call
    rows, width = tokens.shape
    channels = conv_weight.shape[1]
    in_parts = in_weight.transpose(1, 0, 2)
    gain_one_row, gain_two_row = gain_one.reshape(1, -1), gain_two.reshape(1, -1)

    def share(value):
        return swap(value, CORES)

    tail, tokens_here, gain_here, weights_here, offset = run(
        load_kernel,
        operands=[
            pltpu.with_memory_space_constraint(value, pltpu.HBM) for value in (tokens, gain_one_row, in_parts)
        ],
        scalar=starts,
        outs=[
            like((16, channels), BF16),
            like((rows, width), BF16),
            like((1, width), F32),
            like((3, width, channels), BF16),
            like((8, 128), jnp.int32),
        ],
        scratch=[pltpu.SemaphoreType.DMA((15,))],
        where=pltpu.HBM,
    )
    incoming = from_behind(tail, "seq", 1)
    cotangent_other = share(cotangent)
    incoming, cotangent_other = lax.optimization_barrier((incoming, cotangent_other))
    normed_one, parts, gated = run(
        project_kernel,
        operands=[tokens_here, gain_here, weights_here],
        outs=[like((rows, width), BF16), like((3, rows, channels), F32), like((rows, channels), BF16)],
    )
    conv, ymix, branch = run(
        mix_kernel,
        offset=offset,
        operands=[gated, incoming, parts, conv_weight, out_weight],
        outs=[like((rows, channels), F32), like((rows, channels), BF16), like((rows, width), BF16)],
    )
    branch, cotangent_late = lax.optimization_barrier((branch, cotangent))
    branch_other = swap(branch, ACROSS)
    units = gate_weight.shape[1]
    hidden_grad = run(
        hidden_kernel,
        operands=[cotangent_late, down_weight],
        outs=[like((rows, units), F32)],
        flops=LONG,
    )[0]
    branch_other, hidden_grad = lax.optimization_barrier((branch_other, hidden_grad))
    resid, normed_two, hidden, gate_back, up_back, shared, shared_early = run(
        feed_kernel,
        operands=[tokens, branch, branch_other, gain_two_row, gate_weight, up_weight, hidden_grad]
        + [normed_one, ymix],
        outs=[like((rows, width), F32), like((rows, width), BF16)]
        + [like((rows, units), BF16)] * 3
        + [like((rows, 3 * WIDE_COLUMNS + width), BF16), like((rows, width + channels // 2), BF16)],
    )
    shared_other = share(shared)
    norm_two_part = run(
        part_kernel, operands=[gate_back, up_back, gate_weight, up_weight], outs=[like((rows, width), BF16)]
    )[0]
    norm_two_other = swap(norm_two_part, ACROSS)
    first_send, first_keep, left_two = run(
        wide_first_kernel,
        operands=[normed_two, cotangent, cotangent_other, hidden, gate_back, shared_other],
        outs=blocks([8 * WIDE[0]] * 2) + [like((width, 2 * rows), BF16)],
        scratch=[pltpu.VMEM((width, 2 * rows), BF16)],
    )
    second_send, second_keep = run(
        wide_second_kernel,
        operands=[left_two, gate_back, up_back, shared_other],
        outs=blocks([8 * WIDE[1]] * 2),
    )
    sends, keeps = [first_send, second_send], [first_keep, second_keep]
    hidden, sends[1] = lax.optimization_barrier((hidden, sends[1]))
    down_part = run(down_kernel, operands=[hidden, down_weight], outs=[like((rows, width), BF16)])[0]
    early_other = share(shared_early)
    norm_two_other, keeps[1], down_part, early_other = lax.optimization_barrier(
        (norm_two_other, keeps[1], down_part, early_other)
    )
    gots = swap_round(sends, FIRST)

    edge_operands = [norm_two_part, norm_two_other, resid, gain_two_row, cotangent, out_weight, parts, conv_weight]
    edge = run(edge_kernel, offset=offset, operands=edge_operands, outs=[like((8, channels), F32)])[0]
    returned = from_behind(edge, "seq", -1)
    resid_grad, resid_low, gain_two_grad, c_back, gated_back, tap_grads = run(
        middle_kernel,
        offset=offset,
        operands=edge_operands + [conv, gated, incoming],
        outs=[
            like((rows, width), F32),
            like((rows, width), BF16),
            like((1, width), F32),
            like((rows, channels), BF16),
            like((rows, channels), F32),
            like((3, channels), F32),
        ],
        flops=SHORT,
    )
    backs, shared, norm_one_part, gain_part, small = run(
        last_kernel,
        offset=offset,
        operands=[gated_back, returned, parts, c_back, in_parts, tokens, gain_two_grad, tap_grads]
        + [resid_low],
        outs=[
            like((3, rows, channels), BF16),
            like((7, rows, 256), BF16),
            like((rows, width), BF16),
            like((8, 128), F32),
            like((32, 128), F32),
        ],
    )
    gain_other = swap(gain_part, ACROSS)
    *sends, narrow, small = run(
        narrow_kernel,
        operands=[normed_one, early_other, resid_low, share(shared), backs, ymix, small, gain_part, gain_other],
        outs=blocks(ROUND_ONE) + blocks([4 * NARROW]) + [like((32, 128), F32)],
        scratch=[pltpu.VMEM((width, 2 * rows), BF16)] * 2,
    )
    far_send = sends.pop()
    results = run(
        first_kernel,
        operands=gots + keeps + sends,
        aliases={4: 0, 5: 1},
        outs=blocks(ROUND_ONE[:2]) + blocks([4 * count for count in WIDE]),
    )
    sends, keeps = list(results[:2]), list(results[2:])
    keeps[0], norm_one_late, down_late = lax.optimization_barrier((keeps[0], norm_one_part, down_part))
    narrow, cross = run(
        far_kernel,
        operands=[narrow, swap(far_send, FIRST[2])],
        outs=[like((4 * NARROW, *BLOCK), F32), like((32, 128), F32)],
        flops=MIDDLE,
    )
    gots = swap_round(sends, FIRST)
    down_other = swap(down_late, ACROSS)
    norm_one_other = swap(norm_one_late, ACROSS)
    results = run(
        second_kernel,
        operands=gots + keeps + [narrow, small, cross],
        outs=blocks([TILES + 1] * 3 + [TILES]) + [like((32, 128), F32)],
    )
    sends, keep, small = list(results[:3]), results[3], results[4]
    gots = swap_round(sends, SECOND)
    mixed, tokens_grad = run(
        finish_kernel,
        operands=[resid, down_part, down_other, norm_one_part, norm_one_other, tokens, resid_grad, gain_one_row],
        outs=[like((rows, width), BF16), like((rows, width), F32)],
        flops=LONG,
    )
    gots[0], mixed, tokens_grad = lax.optimization_barrier((gots[0], mixed, tokens_grad))
    mine, away, near, far, small = run(
        third_kernel,
        operands=gots + [keep, small],
        outs=[like((TILES, 16, 128), F32), like((TILES + 4, 16, 128), BF16)]
        + [like((TILES + 5, 16, 128), BF16)] * 2
        + [like((32, 128), F32)],
    )
    down_g, gate_g, up_g, in_g, out_g, gain_one_g, gain_two_g, conv_g = run(
        outputs_kernel,
        operands=[mine, swap(away, CORES), swap(near, BESIDE), swap(far, BESIDE_OTHER), small],
        outs=[like((16, 2 * WIDE_COLUMNS), F32)] * 3
        + [like((3, 16, channels), F32), like((16, channels), F32)]
        + [like((1, width), F32)] * 2
        + [like((3, channels), F32)],
    )
    in_g, gain_one_g, gain_two_g = in_g.transpose(1, 0, 2), gain_one_g.reshape(-1), gain_two_g.reshape(-1)
    return (mixed, tokens_grad, gain_one_g, in_g, conv_g, out_g.T, gain_two_g, gate_g, up_g, down_g.T)


def solution(mesh):
    return jax.shard_map(
        on_device,
        mesh=mesh,
        in_specs=(
            P("seq", None),
            P("seq"),
            P(),
            P(None, None, "tensor"),
            P(None, "tensor"),
            P("tensor", None),
            P(),
            P(None, "tensor"),
            P(None, "tensor"),
            P("tensor", None),
            P("seq", None),
        ),
        out_specs=(
            P("seq", None),
            P("seq", None),
            P(),
            P("seq", None, "tensor"),
            P(None, "tensor"),
            P("tensor", "seq"),
            P(),
            P("seq", "tensor"),
            P("seq", "tensor"),
            P("tensor", "seq"),
        ),
        check_vma=False,
    )
```

```python
import functools

import jax
import jax.numpy as jnp
from jax import lax
from jax.experimental import pallas as pl
from jax.experimental.pallas import tpu as pltpu
from jax.sharding import PartitionSpec as P

EPS = 1e-05
AXES = ("seq", "tensor")
BF16 = jnp.bfloat16
F32 = jnp.float32


def device_pairs(move):
    def number(y, z, x, core):
        return ((((y % 4) * 4 + z % 4) * 2 + x % 2) * 2 + core) * 2 + (x % 4) // 2

    return [
        (number(y, z, x, core), number(*move(y, z, x, core)))
        for y in range(4)
        for z in range(4)
        for x in range(4)
        for core in range(2)
    ]


ACROSS = device_pairs(lambda y, z, x, core: (y, z, (x + 2) % 4, core))
BESIDE = device_pairs(lambda y, z, x, core: (y, z, x ^ 1, core))
BESIDE_OTHER = device_pairs(lambda y, z, x, core: (y, z, x ^ 1, 1 - core))
CORES = device_pairs(lambda y, z, x, core: (y, z, x, 1 - core))


def peer(at, pairing):
    return (at ^ 1, 3 - at, at ^ 2)[pairing]


FIRST = [
    device_pairs(
        functools.partial(
            lambda pairing, y, z, x, core: (y, peer(z, pairing), x, core)
            if core
            else (peer(y, pairing), z, x, core),
            pairing,
        )
    )
    for pairing in range(3)
]
SECOND = [
    device_pairs(
        functools.partial(
            lambda pairing, y, z, x, core: (peer(y, pairing), z, x, core)
            if core
            else (y, peer(z, pairing), x, core),
            pairing,
        )
    )
    for pairing in range(3)
]
WIDE_COLUMNS = 1152
WIDE_TILES = 27
WIDE = (14, 13)
NARROW = 8
BLOCK = (64, 128)
LONG = 3 * 10**10
SHORT = 8 * 10**9
MIDDLE = 12 * 10**9
TILES = WIDE_TILES + NARROW
WIDE_BLOCKS = (4 * WIDE[1], 4 * WIDE[0], 0)
ROUND_ONE = tuple(count + 4 * NARROW + 1 for count in WIDE_BLOCKS)


def swap(value, pairs):
    return lax.ppermute(value, AXES, pairs)


def from_behind(value, axis, steps):
    count = lax.axis_size(axis)
    leading, last = (max(0, -steps), min(count, count - steps))
    return lax.ppermute(value, axis, [(source, source + steps) for source in range(leading, last)])


def norm_scale(values):
    return lax.rsqrt(jnp.mean(values * values, axis=1, keepdims=True) + EPS)


def norm_backward(out_grad_rows, values, scale_rows, gain):
    scaled = out_grad_rows * gain
    inner = jnp.mean(scaled * values, axis=1, keepdims=True)
    return scale_rows * (scaled - values * scale_rows * scale_rows * inner)


def like(shape, dtype):
    return jax.ShapeDtypeStruct(shape, dtype)


def positions(offset):
    at = lax.axis_index("seq")
    y, z, core = at // 16, (at // 4) % 4, at % 2
    first, second = jnp.where(core == 0, y, z), jnp.where(core == 0, z, y)
    return first, second, (at // 2) % 2, core, offset


def call(body, *, operands, outs, scratch=(), offset=None, flops=0, aliases=None, where=pltpu.VMEM, scalar=None):
    whole = pl.BlockSpec(memory_space=pltpu.VMEM)
    specs = [pl.BlockSpec(memory_space=where)] * len(operands)
    if scalar is not None:
        operands, specs = [scalar, *operands], [pl.BlockSpec(memory_space=pltpu.SMEM), *specs]

    def kernel(*refs):
        if offset is None:
            body(positions(None), *refs)
        else:
            body(positions(refs[0][0:1, 0:1]), *refs[1:])

    if offset is not None:
        operands, specs = [offset, *operands], [whole, *specs]
    return pl.pallas_call(
        kernel,
        out_shape=tuple(outs),
        in_specs=specs,
        out_specs=tuple(whole for _ in outs),
        scratch_shapes=list(scratch),
        input_output_aliases=aliases or {},
        compiler_params=pltpu.CompilerParams(vmem_limit_bytes=16 * 2**20),
        cost_estimate=pl.CostEstimate(flops=flops, bytes_accessed=0, transcendentals=0),
    )(*operands)


def dot(left, right):
    return jnp.dot(left, right, preferred_element_type=F32)


def dot_rows(left, right):
    return lax.dot_general(left, right, (((1,), (1,)), ((), ())), preferred_element_type=F32)


def row_numbers(shape, first=0):
    return lax.broadcasted_iota(jnp.int32, shape, 0) + first


def valid_rows(offset, lag, shape):
    row = row_numbers(shape)
    return jnp.where((offset <= row) & (offset > row - lag), 0.0, 1.0)


def linked_rows(offset, shape, first, count):
    return jnp.where((row_numbers(shape, first) < offset) & (offset < count), 0.0, 1.0)


def load_kernel(scalars, starts, tokens, gain, weight, tail, token_rows, gain_row, weights, offset, done):
    rows, depth = tokens.shape[0], weight.shape[1] // 4
    pieces = [(gain, gain_row)]
    pieces += [(tokens.at[pl.ds(at, 128)], token_rows.at[pl.ds(at, 128)]) for at in (rows - 128, 0)]
    for k in (0, 2, 1):
        for at in range(0, weight.shape[1], depth):
            pieces.append((weight.at[k, pl.ds(at, depth)], weights.at[k, pl.ds(at, depth)]))
    copies = [
        pltpu.make_async_copy(source, target, done.at[at]) for at, (source, target) in enumerate(pieces)
    ]
    for copy in copies:
        copy.start()
    for copy in copies[:2]:
        copy.wait()
    offset[...] = jnp.full(offset.shape, starts[0], jnp.int32)
    values = token_rows[rows - 16 :].astype(F32)
    normed = (values * norm_scale(values) * gain_row[...]).astype(BF16)
    for copy in copies[2:11]:
        copy.wait()
    gated = (dot(normed, weights[0]) * dot(normed, weights[2])).astype(BF16).astype(F32)
    tail[...] = (gated * linked_rows(starts[0], gated.shape, rows - 16, rows)).astype(BF16)
    for copy in copies[11:]:
        copy.wait()


def project_kernel(scalars, tokens, gain, weights, normed, parts, gated):
    values = tokens[...].astype(F32)
    normed[...] = (values * norm_scale(values) * gain[...]).astype(BF16)
    for k in range(3):
        parts[k] = dot(normed[...], weights[k])
    gated[...] = (parts[0] * parts[2]).astype(BF16)


def behind(gated, incoming, lag):
    moved = pltpu.roll(gated, lag, 0)
    row = row_numbers(gated.shape)
    for at in range(lag):
        moved = jnp.where(row == at, incoming[16 - lag + at : 17 - lag + at], moved)
    return moved


def mix_kernel(scalars, gated, incoming, parts, taps, weight, conv, ymix, branch):
    values = gated[...].astype(F32)
    before = incoming[...].astype(F32)
    total = taps[0:1] * values
    for lag in (1, 2):
        total = total + taps[lag : lag + 1] * behind(values, before, lag) * valid_rows(
            scalars[4], lag, values.shape
        )
    conv[...] = total
    ymix[...] = (parts[1] * total).astype(BF16)
    branch[...] = dot(ymix[...], weight[...]).astype(BF16)


def away_half(value, core):
    half = value.shape[-1] // 2
    return jnp.where(core == 0, value[..., half:], value[..., :half])


def hidden_kernel(scalars, cot, weight, out):
    for at in range(0, weight.shape[0], 256):
        out[:, at : at + 256] = dot_rows(cot[...], weight[at : at + 256])


def down_kernel(scalars, hidden, weight, out):
    out[...] = dot(hidden[...], weight[...]).astype(BF16)


def feed_kernel(
    scalars,
    tokens,
    branch,
    other,
    gain,
    gate,
    up,
    hidden_grad,
    normed_one,
    ymix,
    resid,
    normed,
    hidden,
    gate_back,
    up_back,
    shared,
    shared_early,
):
    resid[...] = tokens[...].astype(F32) + (branch[...].astype(F32) + other[...].astype(F32))
    normed[...] = (resid[...] * norm_scale(resid[...]) * gain[...]).astype(BF16)
    values = normed[...]
    for at in range(0, gate.shape[1], 256):
        columns = slice(at, at + 256)
        gate_act, up_act = dot(values, gate[:, columns]), dot(values, up[:, columns])
        back = hidden_grad[:, columns]
        sigmoid_gate = jax.nn.sigmoid(gate_act)
        swish = gate_act * sigmoid_gate
        hidden[:, columns] = (swish * up_act).astype(BF16)
        up_back[:, columns] = (back * swish).astype(BF16)
        slope = sigmoid_gate * (1.0 + gate_act * (1.0 - sigmoid_gate))
        gate_back[:, columns] = (back * up_act * slope).astype(BF16)
    away = pl.ds(pl.multiple_of((1 - scalars[3]) * WIDE_COLUMNS, 128), WIDE_COLUMNS)
    for k, value in enumerate((hidden, gate_back, up_back)):
        shared[:, k * WIDE_COLUMNS : (k + 1) * WIDE_COLUMNS] = value[:, away]
    shared[:, 3 * WIDE_COLUMNS :] = values
    shared_early[:, : normed.shape[1]] = normed_one[...]
    shared_early[:, normed.shape[1] :] = away_half(ymix[...], scalars[3])


def part_kernel(scalars, gate_back, up_back, gate, up, part):
    part[...] = (dot_rows(gate_back[...], gate[...]) + dot_rows(up_back[...], up[...])).astype(BF16)


def second_norm(part, other, resid, gain, cot):
    back = part.astype(F32) + other.astype(F32)
    scale = norm_scale(resid)
    return back, scale, cot.astype(F32) + norm_backward(back, resid, scale, gain)


def edge_kernel(scalars, part, other, resid, gain, cot, weight, parts, taps, edge):
    top = slice(0, 16)
    _, _, grad = second_norm(part[top], other[top], resid[top], gain[...], cot[top])
    conv_back = dot_rows(grad.astype(BF16), weight[...]) * parts[1, top]
    one = conv_back * valid_rows(scalars[4], 1, conv_back.shape) * taps[1:2]
    two = conv_back * valid_rows(scalars[4], 2, conv_back.shape) * taps[2:3]
    row = row_numbers((8, conv_back.shape[1]))
    edge[...] = jnp.where(row == 6, two[0:1], 0.0) + jnp.where(row == 7, one[0:1] + two[1:2], 0.0)


def middle_kernel(
    scalars, part, other, resid, gain, cot, weight, parts, taps, conv, gated, incoming, grad, low, gain_grad, c_back, gated_back, tap_grads
):
    back, scale, resid_grad = second_norm(part[...], other[...], resid[...], gain[...], cot[...])
    gain_grad[...] = jnp.sum(back * resid[...] * scale, axis=0, keepdims=True)
    grad[...] = resid_grad
    low[...] = resid_grad.astype(BF16)
    ymix_back = dot_rows(low[...], weight[...])
    c_back[...] = (ymix_back * conv[...]).astype(BF16)
    conv_back = ymix_back * parts[1]
    values, before = gated[...].astype(F32), incoming[...].astype(F32)
    rows = values.shape[0]
    tap_grads[0:1] = jnp.sum(conv_back * values, axis=0, keepdims=True)
    total = conv_back * taps[0:1]
    row = row_numbers(values.shape)
    for lag in (1, 2):
        term = conv_back * valid_rows(scalars[4], lag, values.shape)
        tap_grads[lag : lag + 1] = jnp.sum(term * behind(values, before, lag), axis=0, keepdims=True)
        moved = pltpu.roll(term * taps[lag : lag + 1], rows - lag, 0)
        total = total + jnp.where(row < rows - lag, moved, 0.0)
    gated_back[...] = total


def last_kernel(
    scalars,
    gated_back,
    returned,
    parts,
    c_back,
    weight,
    tokens,
    gain_two_grad,
    tap_grads,
    resid_low,
    backs,
    shared,
    part,
    gain_part,
    small,
):
    rows = gated_back.shape[0]
    links = linked_rows(scalars[4], returned.shape, rows - 8, rows)
    end = gated_back[rows - 8 :] + returned[...] * links
    total = jnp.concatenate([gated_back[: rows - 8], end], 0)
    backs[0] = (total * parts[2]).astype(BF16)
    backs[1] = c_back[...]
    backs[2] = (total * parts[0]).astype(BF16)
    for k in range(3):
        shared[4 + k] = away_half(backs[k], scalars[3])
    for at in range(4):
        shared[at] = resid_low[:, at * 256 : at * 256 + 256]
    grad = dot_rows(backs[0], weight[0]) + dot_rows(backs[1], weight[1]) + dot_rows(backs[2], weight[2])
    part[...] = grad.astype(BF16)
    values = tokens[...].astype(F32)
    gain_grad = jnp.sum(grad * values * norm_scale(values), axis=0, keepdims=True)
    for at in range(8):
        lanes = slice(at * 128, at * 128 + 128)
        gain_part[at : at + 1] = gain_grad[:, lanes]
        small[8 + at : 9 + at] = gain_two_grad[:, lanes]
    for lag in range(3):
        for at in range(4):
            row = 16 + 4 * lag + at
            small[row : row + 1] = tap_grads[lag : lag + 1, at * 128 : at * 128 + 128]
    small[:8] = jnp.zeros((8, 128), F32)
    small[28:32] = jnp.zeros((4, 128), F32)


def fill_transposed(left, own, other):
    for at in range(0, own.shape[1], 256):
        left[at : at + 256, :256] = own[:, at : at + 256].T
        left[at : at + 256, 256:] = other[:, at : at + 256].T


def chunk_rows(left, core, chunk):
    wide, slim = jnp.where(core == 0, 256, 64), jnp.where(core == 0, 64, 256)
    return jnp.concatenate(
        [left[pl.ds(pl.multiple_of(chunk * wide + at * slim, 64), 64)] for at in range(4)], 0
    )


def store_blocks(value, target, base, tiles, tile):
    value = value.astype(BF16)
    for chunk in range(4):
        for column in range(value.shape[1] // 128):
            target[base + chunk * tiles + tile + column] = value[
                chunk * 64 : chunk * 64 + 64, column * 128 : column * 128 + 128
            ]


def wide_runs(kind):
    at, end = (0, WIDE[0]) if kind == 0 else (WIDE[0], WIDE_TILES)
    first = at
    while at < end:
        matrix, tile = divmod(at, WIDE_COLUMNS // 128)
        count = min(2, WIDE_COLUMNS // 128 - tile, end - at)
        yield matrix, tile * 128, count * 128, at - first
        at += count


def wide_piece(scalars, kind, lefts, own, shared, send, keep):
    at, core = scalars[0], scalars[3]
    first, second = peer(at, kind), peer(at, 1 - kind)
    chunks = (at, second, first, peer(first, 1 - kind))
    for slot, chunk in enumerate(chunks):
        target = keep if slot < 2 else send
        rows = {}
        for matrix, column, width, tile in wide_runs(kind):
            if (matrix == 0) not in rows:
                rows[matrix == 0] = chunk_rows(lefts[matrix], core, chunk)
            left = rows[matrix == 0]
            mine = pl.ds(pl.multiple_of(core * WIDE_COLUMNS + column, 128), width)
            away = matrix * WIDE_COLUMNS + column
            value = dot(left[:, :256], own[matrix][:, mine])
            value = value + dot(left[:, 256:], shared[:, away : away + width])
            store_blocks(value, target, (slot % 2) * 4 * WIDE[kind], WIDE[kind], tile)


def wide_first_kernel(scalars, two, cot, cot_other, hidden, gate_back, shared, send, keep, left_two, left_cot):
    fill_transposed(left_cot, cot, cot_other)
    fill_transposed(left_two, two, shared.at[:, 3 * WIDE_COLUMNS :])
    wide_piece(scalars, 0, (left_cot, left_two), (hidden, gate_back), shared, send, keep)


def wide_second_kernel(scalars, left_two, gate_back, up_back, shared, send, keep):
    wide_piece(scalars, 1, (None, left_two, left_two), (None, gate_back, up_back), shared, send, keep)


def narrow_kernel(scalars, one, shared, low, late_other, backs, ymix, *refs):
    (small, gain, gain_other), outs, (new_small, left_one, left_low) = refs[:3], refs[3:7], refs[7:]
    new_small[:8] = gain[...] + gain_other[...]
    new_small[8:] = small[8:]
    for pairing in range(3):
        split_small(new_small[...], outs[pairing], ROUND_ONE[pairing] - 1)
    width = one.shape[1]
    one_other, ymix_other = shared.at[:, :width], shared.at[:, width:]
    for at in range(0, width, 256):
        left_one[at : at + 256, :256] = one[:, at : at + 256].T
        left_one[at : at + 256, 256:] = one_other[:, at : at + 256].T
        left_low[at : at + 256, :256] = low[:, at : at + 256].T
        left_low[at : at + 256, 256:] = late_other[at // 256].T
    mine = pl.ds(pl.multiple_of(scalars[3] * 256, 256), 256)
    for slot in range(4):
        chunk = peer(scalars[0], slot) if slot < 3 else scalars[0]
        for kind in range(4):
            left, own, other = (
                (left_one, backs[kind, :, mine], late_other[4 + kind])
                if kind < 3
                else (left_low, ymix[:, mine], ymix_other[...])
            )
            rows = chunk_rows(left, scalars[3], chunk)
            value = dot(rows[:, :256], own) + dot(rows[:, 256:], other)
            store_blocks(value, outs[slot], WIDE_BLOCKS[slot] if slot < 3 else 0, NARROW, 2 * kind)


def split_small(value, target, at):
    high = value.astype(BF16)
    target[at, :32] = high
    target[at, 32:] = (value - high.astype(F32)).astype(BF16)


def join_small(source, at):
    return source[at, :32].astype(F32) + source[at, 32:].astype(F32)


def rounded_small(value):
    high = value.astype(BF16)
    return high.astype(F32) + (value - high.astype(F32)).astype(BF16).astype(F32)


def sum_small(value, near, far, cross):
    return (rounded_small(value) + cross) + (near + far)


def far_kernel(scalars, mine, got, total, small):
    total[...] = mine[...].astype(F32) + got[: 4 * NARROW].astype(F32)
    small[...] = join_small(got, 4 * NARROW)


def first_kernel(scalars, *refs):
    gots, keeps, sends, wide_keeps = refs[:2], refs[2:4], refs[6:8], refs[8:]
    for kind in range(2):
        half = 4 * WIDE[kind]
        for chunk in range(4):
            at = slice(chunk * WIDE[kind], (chunk + 1) * WIDE[kind])
            after = slice(half + chunk * WIDE[kind], half + (chunk + 1) * WIDE[kind])
            wide_keeps[kind][at] = (keeps[kind][at].astype(F32) + gots[kind][at].astype(F32)).astype(BF16)
            sends[1 - kind][at] = (keeps[kind][after].astype(F32) + gots[kind][after].astype(F32)).astype(BF16)


def second_kernel(scalars, *refs):
    gots, wide_in, (narrow, small, cross) = refs[:2], refs[2:4], refs[4:7]
    sends, (keep, new_small) = refs[7:10], refs[10:]

    def fill(chunk, target):
        tile = 0
        for kind in range(2):
            at = pl.ds(chunk * WIDE[kind], WIDE[kind])
            value = wide_in[kind][at].astype(F32) + gots[1 - kind][at].astype(F32)
            target[tile : tile + WIDE[kind]] = value.astype(BF16)
            tile += WIDE[kind]
        value = narrow[pl.ds(chunk * NARROW, NARROW)]
        for pairing in range(2):
            value = value + gots[pairing][pl.ds(WIDE_BLOCKS[pairing] + chunk * NARROW, NARROW)].astype(F32)
        target[tile : tile + NARROW] = value.astype(BF16)

    near, far = (join_small(got, count - 1) for got, count in zip(gots, ROUND_ONE))
    value = sum_small(small[...], near, far, cross[...])
    new_small[...] = value
    for pairing in range(3):
        fill(peer(scalars[1], pairing), sends[pairing])
        split_small(value, sends[pairing], TILES)
    fill(scalars[1], keep)


def third_kernel(scalars, *refs):
    gots, (kept, small), (mine, away, near, far, new_small) = refs[:3], refs[3:5], refs[5:]
    here, core = scalars[2], scalars[3]
    for first in range(0, TILES, 7):
        at = slice(first, first + 7)
        value = kept[at].astype(F32)
        for got in gots:
            value = value + got[at].astype(F32)
        zero, one = value[:, :32], value[:, 32:]
        stay, leave = jnp.where(here == 0, zero, one), jnp.where(here == 0, one, zero)
        mine[at] = jnp.where(core == 0, stay[:, :16], stay[:, 16:])
        away[at] = jnp.where(core == 0, stay[:, 16:], stay[:, :16]).astype(BF16)
        near[at] = jnp.where(core == 0, leave[:, :16], leave[:, 16:]).astype(BF16)
        far[at] = jnp.where(core == 0, leave[:, 16:], leave[:, :16]).astype(BF16)
    value = sum_small(small[...], *(join_small(got, TILES) for got in gots))
    high = value.astype(BF16)
    low = (value - high.astype(F32)).astype(BF16)
    new_small[...] = high.astype(F32) + low.astype(F32)
    for at in range(2):
        rows = slice(16 * at, 16 * at + 16)
        for target in (away, near, far):
            target[TILES + at] = high[rows]
            target[TILES + 2 + at] = low[rows]
    for target in (near, far):
        target[TILES + 4] = jnp.zeros((16, 128), BF16)


def finish_kernel(
    scalars, resid, down, down_other, part, other, tokens, resid_grad, gain, mixed, tokens_grad
):
    mixed[...] = (resid[...] + (down[...].astype(F32) + down_other[...].astype(F32))).astype(BF16)
    values = tokens[...].astype(F32)
    back = part[...].astype(F32) + other[...].astype(F32)
    tokens_grad[...] = resid_grad[...] + norm_backward(back, values, norm_scale(values), gain[...])


def outputs_kernel(scalars, mine, away, near, far, small, down, gate, up, inner, out, gain_one, gain_two, taps):
    core = scalars[3]

    def place(target, tile, column, columns):
        own = mine[tile] + near[tile].astype(F32)
        other = away[tile].astype(F32) + far[tile].astype(F32)
        target[:, column : column + 128] = jnp.where(core == 0, own, other)
        target[:, columns + column : columns + column + 128] = jnp.where(core == 0, other, own)

    for matrix, target in enumerate((down, gate, up)):
        for tile in range(WIDE_COLUMNS // 128):
            place(target, matrix * (WIDE_COLUMNS // 128) + tile, tile * 128, WIDE_COLUMNS)
    for kind in range(4):
        for column in range(2):
            place(inner.at[kind] if kind < 3 else out, WIDE_TILES + 2 * kind + column, column * 128, 256)
    sums = []
    for at in range(2):
        came = [part[TILES + at].astype(F32) + part[TILES + 2 + at].astype(F32) for part in (near, away, far)]
        sums.append((small[16 * at : 16 * at + 16] + came[0]) + (came[1] + came[2]))
    gains, rest = sums
    for at in range(8):
        lanes = slice(at * 128, at * 128 + 128)
        gain_one[:, lanes] = gains[at : at + 1]
        gain_two[:, lanes] = gains[8 + at : 9 + at]
    for lag in range(3):
        for at in range(4):
            row = 4 * lag + at
            taps[lag : lag + 1, at * 128 : at * 128 + 128] = rest[row : row + 1]


def swap_round(sends, pairings):
    return [swap(value, pairs) for value, pairs in zip(sends, pairings)]


def blocks(counts):
    return [like((count, *BLOCK), BF16) for count in counts]


def on_device(
    tokens,
    starts,
    gain_one,
    in_weight,
    conv_weight,
    out_weight,
    gain_two,
    gate_weight,
    up_weight,
    down_weight,
    cotangent,
):
    core = lax.axis_index("seq") % 2
    run = call
    rows, width = tokens.shape
    channels = conv_weight.shape[1]
    in_parts = in_weight.transpose(1, 0, 2)
    gain_one_row, gain_two_row = gain_one.reshape(1, -1), gain_two.reshape(1, -1)

    def share(value):
        return swap(value, CORES)

    tail, tokens_here, gain_here, weights_here, offset = run(
        load_kernel,
        operands=[
            pltpu.with_memory_space_constraint(value, pltpu.HBM) for value in (tokens, gain_one_row, in_parts)
        ],
        scalar=starts,
        outs=[
            like((16, channels), BF16),
            like((rows, width), BF16),
            like((1, width), F32),
            like((3, width, channels), BF16),
            like((8, 128), jnp.int32),
        ],
        scratch=[pltpu.SemaphoreType.DMA((15,))],
        where=pltpu.HBM,
    )
    incoming = from_behind(tail, "seq", 1)
    normed_one, parts, gated = run(
        project_kernel,
        operands=[tokens_here, gain_here, weights_here],
        outs=[like((rows, width), BF16), like((3, rows, channels), F32), like((rows, channels), BF16)],
    )
    conv, ymix, branch = run(
        mix_kernel,
        offset=offset,
        operands=[gated, incoming, parts, conv_weight, out_weight],
        outs=[like((rows, channels), F32), like((rows, channels), BF16), like((rows, width), BF16)],
    )
    branch, cotangent_late = lax.optimization_barrier((branch, cotangent))
    branch_other = swap(branch, ACROSS)
    units = gate_weight.shape[1]
    hidden_grad = run(
        hidden_kernel,
        operands=[cotangent_late, down_weight],
        outs=[like((rows, units), F32)],
        flops=LONG,
    )[0]
    cotangent_late, hidden_grad = lax.optimization_barrier((cotangent_late, hidden_grad))
    cotangent_other = share(cotangent_late)
    branch_other, hidden_grad, cotangent_other = lax.optimization_barrier(
        (branch_other, hidden_grad, cotangent_other)
    )
    resid, normed_two, hidden, gate_back, up_back, shared, shared_early = run(
        feed_kernel,
        operands=[tokens, branch, branch_other, gain_two_row, gate_weight, up_weight, hidden_grad]
        + [normed_one, ymix],
        outs=[like((rows, width), F32), like((rows, width), BF16)]
        + [like((rows, units), BF16)] * 3
        + [like((rows, 3 * WIDE_COLUMNS + width), BF16), like((rows, width + channels // 2), BF16)],
    )
    shared_other = share(shared)
    norm_two_part = run(
        part_kernel, operands=[gate_back, up_back, gate_weight, up_weight], outs=[like((rows, width), BF16)]
    )[0]
    norm_two_other = swap(norm_two_part, ACROSS)
    first_send, first_keep, left_two = run(
        wide_first_kernel,
        operands=[normed_two, cotangent, cotangent_other, hidden, gate_back, shared_other],
        outs=blocks([8 * WIDE[0]] * 2) + [like((width, 2 * rows), BF16)],
        scratch=[pltpu.VMEM((width, 2 * rows), BF16)],
    )
    second_send, second_keep = run(
        wide_second_kernel,
        operands=[left_two, gate_back, up_back, shared_other],
        outs=blocks([8 * WIDE[1]] * 2),
    )
    sends, keeps = [first_send, second_send], [first_keep, second_keep]
    hidden, sends[1] = lax.optimization_barrier((hidden, sends[1]))
    down_part = run(down_kernel, operands=[hidden, down_weight], outs=[like((rows, width), BF16)])[0]
    early_other = share(shared_early)
    norm_two_other, keeps[1], down_part, early_other = lax.optimization_barrier(
        (norm_two_other, keeps[1], down_part, early_other)
    )
    gots = swap_round(sends, FIRST)

    edge_operands = [norm_two_part, norm_two_other, resid, gain_two_row, cotangent, out_weight, parts, conv_weight]
    edge = run(edge_kernel, offset=offset, operands=edge_operands, outs=[like((8, channels), F32)])[0]
    returned = from_behind(edge, "seq", -1)
    resid_grad, resid_low, gain_two_grad, c_back, gated_back, tap_grads = run(
        middle_kernel,
        offset=offset,
        operands=edge_operands + [conv, gated, incoming],
        outs=[
            like((rows, width), F32),
            like((rows, width), BF16),
            like((1, width), F32),
            like((rows, channels), BF16),
            like((rows, channels), F32),
            like((3, channels), F32),
        ],
        flops=SHORT,
    )
    backs, shared, norm_one_part, gain_part, small = run(
        last_kernel,
        offset=offset,
        operands=[gated_back, returned, parts, c_back, in_parts, tokens, gain_two_grad, tap_grads]
        + [resid_low],
        outs=[
            like((3, rows, channels), BF16),
            like((7, rows, 256), BF16),
            like((rows, width), BF16),
            like((8, 128), F32),
            like((32, 128), F32),
        ],
    )
    gain_other = swap(gain_part, ACROSS)
    *sends, narrow, small = run(
        narrow_kernel,
        operands=[normed_one, early_other, resid_low, share(shared), backs, ymix, small, gain_part, gain_other],
        outs=blocks(ROUND_ONE) + blocks([4 * NARROW]) + [like((32, 128), F32)],
        scratch=[pltpu.VMEM((width, 2 * rows), BF16)] * 2,
    )
    far_send = sends.pop()
    results = run(
        first_kernel,
        operands=gots + keeps + sends,
        aliases={4: 0, 5: 1},
        outs=blocks(ROUND_ONE[:2]) + blocks([4 * count for count in WIDE]),
    )
    sends, keeps = list(results[:2]), list(results[2:])
    keeps[0], norm_one_late, down_late = lax.optimization_barrier((keeps[0], norm_one_part, down_part))
    narrow, cross = run(
        far_kernel,
        operands=[narrow, swap(far_send, FIRST[2])],
        outs=[like((4 * NARROW, *BLOCK), F32), like((32, 128), F32)],
        flops=MIDDLE,
    )
    gots = swap_round(sends, FIRST)
    down_other = swap(down_late, ACROSS)
    norm_one_other = swap(norm_one_late, ACROSS)
    results = run(
        second_kernel,
        operands=gots + keeps + [narrow, small, cross],
        outs=blocks([TILES + 1] * 3 + [TILES]) + [like((32, 128), F32)],
    )
    sends, keep, small = list(results[:3]), results[3], results[4]
    gots = swap_round(sends, SECOND)
    mixed, tokens_grad = run(
        finish_kernel,
        operands=[resid, down_part, down_other, norm_one_part, norm_one_other, tokens, resid_grad, gain_one_row],
        outs=[like((rows, width), BF16), like((rows, width), F32)],
        flops=LONG,
    )
    gots[0], mixed, tokens_grad = lax.optimization_barrier((gots[0], mixed, tokens_grad))
    mine, away, near, far, small = run(
        third_kernel,
        operands=gots + [keep, small],
        outs=[like((TILES, 16, 128), F32), like((TILES + 4, 16, 128), BF16)]
        + [like((TILES + 5, 16, 128), BF16)] * 2
        + [like((32, 128), F32)],
    )
    down_g, gate_g, up_g, in_g, out_g, gain_one_g, gain_two_g, conv_g = run(
        outputs_kernel,
        operands=[mine, swap(away, CORES), swap(near, BESIDE), swap(far, BESIDE_OTHER), small],
        outs=[like((16, 2 * WIDE_COLUMNS), F32)] * 3
        + [like((3, 16, channels), F32), like((16, channels), F32)]
        + [like((1, width), F32)] * 2
        + [like((3, channels), F32)],
    )
    in_g, gain_one_g, gain_two_g = in_g.transpose(1, 0, 2), gain_one_g.reshape(-1), gain_two_g.reshape(-1)
    return (mixed, tokens_grad, gain_one_g, in_g, conv_g, out_g.T, gain_two_g, gate_g, up_g, down_g.T)


def solution(mesh):
    return jax.shard_map(
        on_device,
        mesh=mesh,
        in_specs=(
            P("seq", None),
            P("seq"),
            P(),
            P(None, None, "tensor"),
            P(None, "tensor"),
            P("tensor", None),
            P(),
            P(None, "tensor"),
            P(None, "tensor"),
            P("tensor", None),
            P("seq", None),
        ),
        out_specs=(
            P("seq", None),
            P("seq", None),
            P(),
            P("seq", None, "tensor"),
            P(None, "tensor"),
            P("tensor", "seq"),
            P(),
            P("seq", "tensor"),
            P("seq", "tensor"),
            P("tensor", "seq"),
        ),
        check_vma=False,
    )
```
